32 devices in a mesh: section: 8 (over z, core), tm: 4 (over y, x).
Axes of the slice: x: 2, y: 2, z: 4, core: 2. Of those that a mesh axis runs over, the one named last changes fastest.
Arguments:
- act_in: bfloat16 [8, 512, 2048], P('section', 'tm'), may hold values from -6 to 6
- grad_in: bfloat16 [8, 512, 2048], P('section', 'tm'), may hold values from -6 to 6
- saved_inputs: bfloat16 [8, 2, 512, 2048], P('section', None, 'tm'), may hold values from -6 to 6
- kernels: bfloat16 [8, 2, 31, 2048], P('section'), may hold values from -1 to 1
- norm_gains: bfloat16 [8, 2, 2048], P('section'), may hold values from 0.099609375 to 1.8984375
- forward_lengths: int32 [8], replicated, may hold values from 256 to 512
- backward_lengths: int32 [8], replicated, may hold values from 256 to 512
- forward_slots: int32 [8, 2], replicated, may hold values from 0 to 1
- backward_slots: int32 [8, 2], replicated, may hold values from 0 to 1
Outputs:
- act_out: bfloat16 [8, 512, 2048], P('section', 'tm')
- grad_out: bfloat16 [8, 512, 2048], P('section', 'tm')
- tap_grad: float32 [8, 2, 31, 2048], P('section')
- gain_grad: float32 [8, 2, 2048], P('section')
The draws below stay inside these ranges and needn't reach their ends.
All inputs are finite; a program needn't handle non-finite values.
Results may differ from the reference program's by a relative error of at most 0.0063.
Values may be sent and summed in bfloat16 or wider, within the bound.
No kernel may reach another device: no remote copies, remote signals or barrier semaphores. Data moves between devices by JAX's collectives and lax.ppermute only.
A program may use at most 64 MiB of HBM per device.

```python
import jax
import jax.numpy as jnp
from jax import lax

D = 2048
KW = 31
RES = 2
TICKS = 2
FRAMES = 512
SECTIONS = 8


def place_ends(drawn, rng, smallest, high):
    longest = drawn.shape.index(max(drawn.shape))
    spots = []
    for shift in (0, 1):
        where = [jax.random.randint(jax.random.fold_in(rng, axis), (), 0, length) for axis, length in enumerate(drawn.shape)]
        where[longest] = (where[longest] + shift) % drawn.shape[longest]
        spots.append(tuple(where))
    return drawn.at[spots[0]].set(smallest).at[spots[1]].set(high)


def shard_levels(key, dims, cuts, smallest, largest):
    def one(position, shards_of):
        draws = jax.random.uniform(jax.random.fold_in(jax.random.fold_in(key, 6), position), (shards_of,), jnp.float32, smallest / len(cuts), largest / len(cuts))
        return jnp.repeat(jnp.exp(draws), dims[position] // shards_of).reshape((-1,) + (1,) * (len(dims) - position - 1))

    gain = one(*cuts[0])
    for cut in cuts[1:]:
        gain = gain * one(*cut)
    return gain


def noise(rng, dims, spread, reach, pieces=(), held_as=jnp.bfloat16):
    drawn = jax.random.normal(rng, dims, jnp.float32) * spread
    if len(pieces) > 0:
        drawn = shard_levels(rng, dims, pieces, -0.22, 0.18) * drawn
    return jnp.clip(drawn, min=-reach, max=reach).astype(held_as)


def setup_inputs(seed: int = 0) -> dict:
    seeds = jax.random.split(jax.random.key(seed), 10)
    return {
        "act_in": noise(seeds[0], (SECTIONS, FRAMES, D), 1.0, 6.0, ((0, 8), (1, 4))),
        "grad_in": noise(seeds[1], (SECTIONS, FRAMES, D), 1.0, 6.0, ((0, 8), (1, 4))),
        "saved_inputs": noise(seeds[2], (SECTIONS, TICKS, FRAMES, D), 1.0, 6.0, ((0, 8), (2, 4))),
        "kernels": noise(seeds[3], (SECTIONS, RES, KW, D), KW ** -0.5, 1.0, ((0, 8),)),
        "norm_gains": jnp.clip(1.0 + 0.18 * jax.random.normal(seeds[4], (SECTIONS, RES, D), jnp.float32), 0.099609375, 1.8984375).astype(jnp.bfloat16),
        "forward_lengths": place_ends(jax.random.randint(seeds[5], (SECTIONS,), FRAMES // 2, FRAMES + 1), jax.random.fold_in(seeds[5], 1), FRAMES // 2, FRAMES).astype(jnp.int32),
        "backward_lengths": place_ends(jax.random.randint(seeds[6], (SECTIONS,), FRAMES // 2, FRAMES + 1), jax.random.fold_in(seeds[6], 1), FRAMES // 2, FRAMES).astype(jnp.int32),
        "forward_slots": place_ends(jax.random.randint(seeds[7], (SECTIONS, TICKS), 0, RES), jax.random.fold_in(seeds[7], 1), 0, RES - 1).astype(jnp.int32),
        "backward_slots": place_ends(jax.random.randint(seeds[8], (SECTIONS, TICKS), 0, RES), jax.random.fold_in(seeds[8], 1), 0, RES - 1).astype(jnp.int32),
    }


epsilon = 1e-05

def normalized(inputs):
    values = inputs.astype(jnp.float32)
    center = values - lax.optimization_barrier(jnp.mean(values, axis=-1, keepdims=True))
    inverse = lax.rsqrt(lax.optimization_barrier(jnp.mean(center * center, axis=-1, keepdims=True)) + epsilon)
    return (center * inverse, inverse)

def pick_slot(lookup, slot_id):
    onehot = (jnp.arange(lookup.shape[0], dtype=jnp.int32) == slot_id).astype(jnp.float32)
    return jnp.tensordot(onehot, lookup.astype(jnp.float32), axes=1)

def rounded(values):
    return lax.optimization_barrier(values.astype(jnp.bfloat16)).astype(jnp.float32)

def conv_taps(padded, kernel, row_count):
    total = jnp.zeros((row_count, kernel.shape[1]), jnp.float32)
    for offset in range(kernel.shape[0]):
        total = total + kernel[offset] * padded[offset:offset + row_count]
    return total

def flipped_taps(padded, kernel, row_count):
    reach_back = kernel.shape[0] - 1
    total = jnp.zeros((row_count, kernel.shape[1]), jnp.float32)
    for offset in range(kernel.shape[0]):
        total = total + kernel[offset] * padded[reach_back - offset:reach_back - offset + row_count]
    return total

def tap_products(padded, grad_mixed, row_count, tap_count):
    return jnp.stack([lax.optimization_barrier(jnp.sum(padded[offset:offset + row_count] * grad_mixed, axis=0)) for offset in range(tap_count)])

def reference(act_in, grad_in, saved_inputs, kernels, norm_gains, forward_lengths, backward_lengths, forward_slots, backward_slots):
    section_ids = jnp.arange(SECTIONS, dtype=jnp.int32)
    frame_ids = jnp.arange(FRAMES, dtype=jnp.int32)
    half_width = (KW - 1) // 2
    slot_range = jnp.arange(RES, dtype=jnp.int32)

    def prepare(inputs, kernel_set, gain_set, slot_id, length):
        kernel = pick_slot(kernel_set, slot_id)
        gain_row = pick_slot(gain_set, slot_id)
        frame_mask = (frame_ids < length).astype(jnp.float32)[:, None]
        normed, inverse = normalized(inputs)
        masked = rounded(frame_mask * gain_row * normed)
        padded = jnp.pad(masked, ((half_width, half_width), (0, 0)))
        conv_out = conv_taps(padded, kernel, FRAMES)
        return (kernel, gain_row, frame_mask, normed, inverse, padded, conv_out)

    def forward_one(packed):
        inputs, kernel_set, gain_set, slot_id, length = packed
        conv_out = prepare(inputs, kernel_set, gain_set, slot_id, length)[6]
        return (inputs.astype(jnp.float32) + conv_out * jax.nn.sigmoid(conv_out)).astype(jnp.bfloat16)

    def backward_one(packed):
        inputs, upstream, kernel_set, gain_set, slot_id, length = packed
        kernel, gain_row, frame_mask, normed, inverse, padded, conv_out = prepare(inputs, kernel_set, gain_set, slot_id, length)
        gate_back = jax.nn.sigmoid(conv_out)
        grad_up = upstream.astype(jnp.float32)
        grad_mixed = rounded(grad_up * gate_back * (1.0 + conv_out * (1.0 - gate_back)))
        tap_term = tap_products(padded, grad_mixed, FRAMES, KW)
        grad_pad = jnp.pad(grad_mixed, ((half_width, half_width), (0, 0)))
        grad_masked = frame_mask * flipped_taps(grad_pad, kernel, FRAMES)
        gain_term = lax.optimization_barrier(jnp.sum(grad_masked * normed, axis=0))
        scaled = grad_masked * gain_row
        grad_norm = inverse * (scaled - lax.optimization_barrier(jnp.mean(scaled, axis=-1, keepdims=True)) - normed * lax.optimization_barrier(jnp.mean(scaled * normed, axis=-1, keepdims=True)))
        return ((grad_up + grad_norm).astype(jnp.bfloat16), tap_term, gain_term)
    carried = act_in
    returning = grad_in
    tap_total = jnp.zeros((SECTIONS, RES, KW, D), jnp.float32)
    gain_total = jnp.zeros((SECTIONS, RES, D), jnp.float32)
    for tick_step in range(TICKS):
        ahead_len = forward_lengths[(section_ids - tick_step) % SECTIONS]
        outputs = lax.map(forward_one, (carried, kernels, norm_gains, forward_slots[:, tick_step], ahead_len))
        back_len = backward_lengths[(section_ids + tick_step) % SECTIONS]
        grad_x, tap_terms, gain_terms = lax.map(backward_one, (saved_inputs[:, tick_step], returning, kernels, norm_gains, backward_slots[:, tick_step], back_len))
        onehot = (slot_range[None, :] == backward_slots[:, tick_step][:, None]).astype(jnp.float32)
        tap_total = tap_total + onehot[:, :, None, None] * tap_terms[:, None]
        gain_total = gain_total + onehot[:, :, None] * gain_terms[:, None]
        carried = jnp.roll(outputs, 1, axis=0)
        returning = jnp.roll(grad_x, -1, axis=0)
    return (carried, returning, tap_total, gain_total)
```

```python
import functools

import jax
import jax.numpy as jnp
import ml_dtypes
import numpy as np
from jax import lax
from jax.experimental import pallas as pl
from jax.experimental.pallas import tpu as pltpu
from jax.sharding import PartitionSpec as P

epsilon = 1e-05
BLOCK = 512
ROWS = 16
F32 = jnp.float32
BF16 = jnp.bfloat16


def split(matrix):
    high = matrix.astype(ml_dtypes.bfloat16)
    low = (matrix - high.astype(np.float64)).astype(ml_dtypes.bfloat16)
    return high, low


def angles(size, times):
    return 2.0 * np.pi / size * np.outer(np.arange(size // 2) + 0.5, np.asarray(times, np.float64))


def to_freq(size, times):
    phase = angles(size, times)
    return np.concatenate([np.cos(phase), -np.sin(phase)], axis=0)


def from_freq(size, times):
    phase = angles(size, times).T
    return 2.0 / size * np.concatenate([np.cos(phase), -np.sin(phase)], axis=1)


def stacked(matrix):
    return np.stack(split(matrix))


def beside(matrix):
    return np.concatenate(split(matrix), axis=1)


def tap_freq(size, taps):
    phase = angles(size, np.arange(taps) - (taps - 1) // 2)
    table = np.concatenate([np.cos(phase), np.sin(phase)], axis=0)
    return beside(np.concatenate([table, np.zeros((size, 1))], axis=1))


def dot(a, b):
    return jnp.dot(a, b, preferred_element_type=F32)


def forward_dft(table, values):
    return dot(table[0], values) + dot(table[1], values)


def inverse_dft(table, values):
    high = values.astype(BF16)
    low = (values - high.astype(F32)).astype(BF16)
    return dot(table[0], high) + (dot(table[1], high) + dot(table[0], low))


def halves(values):
    half = values.shape[0] // 2
    return values[:half], values[half:]


def product(a, b):
    ar, ai = halves(a)
    br, bi = halves(b)
    return jnp.concatenate([ar * br - ai * bi, ar * bi + ai * br], axis=0)


def product_conj(a, b):
    ar, ai = halves(a)
    br, bi = halves(b)
    return jnp.concatenate([ar * br + ai * bi, ai * br - ar * bi], axis=0)


def sigmoid(values):
    return 0.5 * jnp.tanh(0.5 * values) + 0.5


def norm_rows(pieces, gain, first, length, masked_ref, normed_ref, inverse_ref, skip):
    width = masked_ref.shape[1]
    total = sum(piece[2] for piece in pieces)
    at = 0
    for ref, start, count in pieces:
        keep = normed_ref is not None and at + count > skip and at < total - skip

        def step(i, _, ref=ref, start=start, at=at, keep=keep):
            row = pl.multiple_of(i * ROWS, ROWS)
            values = ref[pl.ds(start + row, ROWS), :].astype(F32)
            center = values - jnp.sum(values, axis=1, keepdims=True) * (1.0 / width)
            inverse = lax.rsqrt(jnp.sum(center * center, axis=1, keepdims=True) * (1.0 / width) + epsilon)
            normed = center * inverse
            frame = first + at + row + lax.broadcasted_iota(jnp.int32, (ROWS, 1), 0)
            mask = ((frame >= 0) & (frame < length)).astype(F32)
            masked_ref[pl.ds(at + row, ROWS), :] = (mask * gain * normed).astype(BF16)
            if keep:
                normed_ref[pl.ds(at + row, ROWS), :] = normed
                inverse_ref[pl.ds(at + row, ROWS), :] = jnp.broadcast_to(inverse, (ROWS, 128))
            return 0

        lax.fori_loop(0, count // ROWS, step, 0)
        at += count


def window(pieces, columns):
    parts = [ref[pl.ds(start, count), columns] for ref, start, count in pieces]
    return parts[0] if len(parts) == 1 else jnp.concatenate(parts, axis=0)


def each_block(width, body):
    def step(i, _):
        body(pl.ds(pl.multiple_of(i * BLOCK, BLOCK), BLOCK))
        return 0

    lax.fori_loop(0, width // BLOCK, step, 0)


def tap_spectrum(table, weights):
    return dot(table, jnp.concatenate([weights, weights], axis=0))


def backward_kernel(
    cut, out_rows, scalars, saved, saved_left, saved_right, grads, weights,
    m_table, q_table, c_table, go_table, gh_table, x_table, t_table,
    grad_x, taps, masked, normed, inverse, scaled, sum_a, sum_b,
):
    own, width = saved.shape
    saved_reach, saved_at, grad_reach, grad_pieces = cut(saved, saved_left, saved_right, grads)
    out_reach = (out_rows - own) // 2
    slot, length, first = scalars[0], scalars[1], scalars[2]
    gain = weights[slot, 31:32, :].astype(F32)
    norm_rows(
        saved_at, gain, first - saved_reach, length, masked, normed, inverse, saved_reach - out_reach
    )
    sum_a[...] = jnp.zeros_like(sum_a)
    sum_b[...] = jnp.zeros_like(sum_b)
    lo = saved_reach - out_reach
    frame = first - out_reach + lax.broadcasted_iota(jnp.int32, (out_rows, 1), 0)
    mask = ((frame >= 0) & (frame < length)).astype(F32)

    def block(columns):
        chosen = weights[slot, :, columns]
        q = tap_spectrum(q_table[...], chosen)
        m = forward_dft(m_table, masked[:, columns])
        conv = inverse_dft(c_table, product(m, q))
        gate = sigmoid(conv)
        upstream = window(grad_pieces, columns).astype(F32)
        mixed = (upstream * gate * (1.0 + conv * (1.0 - gate))).astype(BF16)
        inner = mixed[grad_reach : grad_reach + own]
        ends = jnp.concatenate([mixed[:grad_reach], mixed[grad_reach + own :]], axis=0)
        g_own = dot(go_table[...], jnp.concatenate([inner, inner], axis=0))
        g_all = g_own + dot(gh_table[...], jnp.concatenate([ends, ends], axis=0))
        tap = inverse_dft(t_table, product_conj(m, g_own))
        grad_masked = mask * inverse_dft(x_table, product_conj(g_all, q))
        here = normed[lo : lo + out_rows, columns]
        weighted = grad_masked * here
        gain_term = jnp.sum(weighted[out_reach : out_reach + own], axis=0, keepdims=True)
        row = lax.broadcasted_iota(jnp.int32, tap.shape, 0)
        taps[:, columns] = jnp.where(row == tap.shape[0] - 1, gain_term, tap).astype(taps.dtype)
        gain_here = chosen[31:32].astype(F32)
        by_gain = grad_masked * gain_here
        scaled[:, columns] = by_gain
        both = weighted * gain_here
        part_a = by_gain[:, :128]
        part_b = both[:, :128]
        for lane in range(128, BLOCK, 128):
            part_a = part_a + by_gain[:, lane : lane + 128]
            part_b = part_b + both[:, lane : lane + 128]
        sum_a[...] += part_a
        sum_b[...] += part_b

    each_block(width, block)

    at = 0
    skip = grad_reach - out_reach
    for ref, start, count in grad_pieces:
        begin = max(at, skip)
        end = min(at + count, skip + out_rows)

        def step(i, _, ref=ref, source=start + begin - at, begin=begin):
            row = pl.multiple_of(i * ROWS, ROWS)
            out = pl.ds(begin - skip + row, ROWS)
            inside = pl.ds(begin - skip + lo + row, ROWS)
            mean_a = jnp.sum(sum_a[out, :], axis=1, keepdims=True) * (1.0 / width)
            mean_b = jnp.sum(sum_b[out, :], axis=1, keepdims=True) * (1.0 / width)
            inv = inverse[inside, :][:, :1]
            change = inv * (scaled[out, :] - mean_a - normed[inside, :] * mean_b)
            grad_x[out, :] = (ref[pl.ds(source + row, ROWS), :].astype(F32) + change).astype(BF16)
            return 0

        lax.fori_loop(0, (end - begin) // ROWS, step, 0)
        at += count


def forward_kernel(
    offset, reach, scalars, act, left, right, weights, later,
    m0_table, q0_table, c0_table, m1_table, q1_table, c1_table,
    out, masked0, between, masked1,
):
    own, width = act.shape
    middle = reach // 2
    slot, length, first = scalars[0], scalars[1], scalars[2]
    pieces = [(left, offset, reach), (act, 0, own), (right, offset, reach)]
    inner = [(left, offset + middle, middle), (act, 0, own), (right, offset, middle)]
    gain = weights[slot, 31:32, :].astype(F32)
    norm_rows(pieces, gain, first - reach, length, masked0, None, None, 0)

    def first_layer(columns):
        q = tap_spectrum(q0_table[...], weights[slot, :, columns])
        conv = inverse_dft(c0_table, product(forward_dft(m0_table, masked0[:, columns]), q))
        between[:, columns] = (window(inner, columns).astype(F32) + conv * sigmoid(conv)).astype(BF16)

    each_block(width, first_layer)
    gain = later[31:32, :].astype(F32)
    norm_rows([(between, 0, own + 2 * middle)], gain, first - middle, length, masked1, None, None, 0)

    def second_layer(columns):
        q = tap_spectrum(q1_table[...], later[:, columns])
        conv = inverse_dft(c1_table, product(forward_dft(m1_table, masked1[:, columns]), q))
        here = between[middle : middle + own, columns].astype(F32)
        out[:, columns] = (here + conv * sigmoid(conv)).astype(BF16)

    each_block(width, second_layer)


def span(reach, own):
    return np.arange(-reach, own + reach)


VMEM = pl.BlockSpec(memory_space=pltpu.VMEM)
SMEM = pl.BlockSpec(memory_space=pltpu.SMEM)
LIMIT = 56 * 1024 * 1024


def call(kernel, outs, scratch, operands, flops):
    moved = sum(int(np.prod(x.shape)) * x.dtype.itemsize for x in operands)
    return pl.pallas_call(
        kernel,
        out_shape=outs,
        in_specs=[SMEM] + [VMEM] * (len(operands) - 1),
        out_specs=jax.tree.map(lambda _: VMEM, outs),
        scratch_shapes=scratch,
        compiler_params=pltpu.CompilerParams(vmem_limit_bytes=LIMIT),
        cost_estimate=pl.CostEstimate(flops=flops, bytes_accessed=moved, transcendentals=0),
    )(*operands)


def backward(cut, reaches, scalars, saved, left, right, grads, weights):
    saved_reach, grad_reach, out_reach = reaches
    own, width = saved.shape
    taps = weights.shape[1] - 1
    size = own + 2 * saved_reach
    out_rows = own + 2 * out_reach
    ends = np.concatenate([np.arange(-grad_reach, 0), np.arange(own, own + grad_reach)])
    tap_back = np.concatenate([from_freq(size, np.arange(taps) - (taps - 1) // 2), np.zeros((1, size))], axis=0)
    tables = [
        stacked(to_freq(size, span(saved_reach, own))),
        tap_freq(size, taps),
        stacked(from_freq(size, span(grad_reach, own))),
        beside(to_freq(size, np.arange(own))),
        beside(to_freq(size, ends)),
        stacked(from_freq(size, span(out_reach, own))),
        stacked(tap_back),
    ]
    operands = [scalars, saved, left, right, grads, weights] + [jnp.asarray(t) for t in tables]
    outs = (
        jax.ShapeDtypeStruct((out_rows, width), BF16),
        jax.ShapeDtypeStruct((taps + 1, width), BF16),
    )
    scratch = [
        pltpu.VMEM((size, width), BF16),
        pltpu.VMEM((size, width), F32),
        pltpu.VMEM((size, 128), F32),
        pltpu.VMEM((out_rows, width), F32),
        pltpu.VMEM((out_rows, 128), F32),
        pltpu.VMEM((out_rows, 128), F32),
    ]
    kernel = functools.partial(backward_kernel, cut, out_rows)
    return call(kernel, outs, scratch, operands, 12 * 2 * size * size * width)


def forward(offset, reach, scalars, act, left, right, weights, later):
    own, width = act.shape
    taps = weights.shape[1] - 1
    middle = reach // 2
    size0, size1 = own + 2 * reach, own + 2 * middle
    tables = [
        stacked(to_freq(size0, span(reach, own))),
        tap_freq(size0, taps),
        stacked(from_freq(size0, span(middle, own))),
        stacked(to_freq(size1, span(middle, own))),
        tap_freq(size1, taps),
        stacked(from_freq(size1, span(0, own))),
    ]
    operands = [scalars, act, left, right, weights, later] + [jnp.asarray(t) for t in tables]
    scratch = [
        pltpu.VMEM((size0, width), BF16),
        pltpu.VMEM((size1, width), BF16),
        pltpu.VMEM((size1, width), BF16),
    ]
    kernel = functools.partial(forward_kernel, offset, reach)
    return call(kernel, jax.ShapeDtypeStruct((own, width), BF16), scratch, operands, 10 * 2 * size0 * size0 * width)


def up16(count):
    return -(-count // 16) * 16


def local(
    act_in, grad_in, saved_inputs, kernels, norm_gains,
    forward_lengths, backward_lengths, forward_slots, backward_slots,
):
    sections = lax.axis_size("section")
    shards = lax.axis_size("tm")
    section = lax.axis_index("section")
    act, grad, saved = act_in[0], grad_in[0], saved_inputs[0]
    own = act.shape[0]
    tap_count = kernels.shape[2]
    half = (tap_count - 1) // 2
    first = lax.axis_index("tm") * own
    one, two, three = up16(half), up16(2 * half), up16(3 * half)

    def shifted(x, by):
        return lax.ppermute(x, "section", [(i, (i + by) % sections) for i in range(sections)])

    parts = [(saved[0], three), (grad, two), (saved[1], two), (act, two)]
    tail = jnp.concatenate([x[own - n :] for x, n in parts], axis=0)
    head = jnp.concatenate([x[:n] for x, n in parts], axis=0)
    left = lax.ppermute(tail, "tm", [(i, i + 1) for i in range(shards - 1)])
    right = lax.ppermute(head, "tm", [(i + 1, i) for i in range(shards - 1)])
    weights = jnp.concatenate([kernels[0], norm_gains[0][:, None, :]], axis=1)
    later = shifted(lax.dynamic_index_in_dim(weights, forward_slots[section, 1], 0, keepdims=False), -1)

    def scalars(slot, length):
        return jnp.stack([slot, length, first]).astype(jnp.int32)

    def cut0(saved_ref, left_ref, right_ref, grad_ref):
        return (
            three,
            [(left_ref, 0, three), (saved_ref, 0, own), (right_ref, 0, three)],
            two,
            [(left_ref, three, two), (grad_ref, 0, own), (right_ref, three, two)],
        )

    def cut1(saved_ref, left_ref, right_ref, grad_ref):
        at = three + two
        return (
            two,
            [(left_ref, at, two), (saved_ref, 0, own), (right_ref, at, two)],
            one,
            [(grad_ref, 0, own + 2 * one)],
        )

    slot0, slot1 = backward_slots[section, 0], backward_slots[section, 1]
    grad_mid, taps0 = backward(
        cut0, (three, two, one), scalars(slot0, backward_lengths[section]),
        saved[0], left, right, grad, weights,
    )
    grad_mid = shifted(grad_mid, -1)
    act_out = forward(
        three + 2 * two, two, scalars(forward_slots[section, 0], forward_lengths[section]),
        act, left, right, weights, later,
    )
    act_out = shifted(act_out, 2)
    grad_out, taps1 = backward(
        cut1, (two, one, 0), scalars(slot1, backward_lengths[(section + 1) % sections]),
        saved[1], left, right, grad_mid, weights,
    )
    grad_out = shifted(grad_out, -1)

    def summed(x):
        if shards & (shards - 1):
            return lax.psum(x.astype(F32), "tm")
        step = 1
        while step < shards:
            other = lax.ppermute(x, "tm", [(i, i ^ step) for i in range(shards)])
            total = x.astype(F32) + other.astype(F32)
            x = total.astype(BF16)
            step *= 2
        return total

    total0, total1 = summed(taps0), summed(taps1)
    slots = jnp.arange(kernels.shape[1], dtype=jnp.int32)[:, None, None]
    sums = jnp.where(slots == slot0, total0[None], 0.0) + jnp.where(slots == slot1, total1[None], 0.0)
    return act_out[None], grad_out[None], sums[None, :, :tap_count], sums[None, :, tap_count]


def solution(mesh):
    in_specs = (
        P("section", "tm", None),
        P("section", "tm", None),
        P("section", None, "tm", None),
        P("section", None, None, None),
        P("section", None, None),
        P(),
        P(),
        P(),
        P(),
    )
    out_specs = (
        P("section", "tm", None),
        P("section", "tm", None),
        P("section", None, None, None),
        P("section", None, None),
    )
    return jax.shard_map(local, mesh=mesh, in_specs=in_specs, out_specs=out_specs, check_vma=False)
```

```python
import functools

import jax
import jax.numpy as jnp
import ml_dtypes
import numpy as np
from jax import lax
from jax.experimental import pallas as pl
from jax.experimental.pallas import tpu as pltpu
from jax.sharding import PartitionSpec as P

epsilon = 1e-05
BLOCK = 512
LANES = 128
F32 = jnp.float32
BF16 = jnp.bfloat16


def split(matrix):
    high = matrix.astype(ml_dtypes.bfloat16)
    low = (matrix - high.astype(np.float64)).astype(ml_dtypes.bfloat16)
    return high, low


def angles(size, times):
    return 2.0 * np.pi / size * np.outer(np.arange(size // 2) + 0.5, np.asarray(times, np.float64))


def to_freq(size, times):
    phase = angles(size, times)
    return np.concatenate([np.cos(phase), -np.sin(phase)], axis=0)


def from_freq(size, times):
    phase = angles(size, times).T
    return 2.0 / size * np.concatenate([np.cos(phase), -np.sin(phase)], axis=1)


def stacked(matrix):
    return np.stack(split(matrix))


def beside(matrix):
    return np.concatenate(split(matrix), axis=1)


def tap_freq(size, taps):
    phase = angles(size, np.arange(taps) - (taps - 1) // 2)
    table = np.concatenate([np.cos(phase), np.sin(phase)], axis=0)
    return beside(np.concatenate([table, np.zeros((size, 1))], axis=1))


def dot(a, b):
    return jnp.dot(a, b, preferred_element_type=F32)


def forward_dft(table, values):
    return dot(table[0], values) + dot(table[1], values)


def inverse_dft(table, values):
    high = values.astype(BF16)
    low = (values - high.astype(F32)).astype(BF16)
    return dot(table[0], high) + (dot(table[1], high) + dot(table[0], low))


def halves(values):
    half = values.shape[0] // 2
    return values[:half], values[half:]


def product(a, b):
    ar, ai = halves(a)
    br, bi = halves(b)
    return jnp.concatenate([ar * br - ai * bi, ar * bi + ai * br], axis=0)


def product_conj(a, b):
    ar, ai = halves(a)
    br, bi = halves(b)
    return jnp.concatenate([ar * br + ai * bi, ai * br - ar * bi], axis=0)


def sigmoid(values):
    return 0.5 * jnp.tanh(0.5 * values) + 0.5


def wide(stat, count):
    return jnp.concatenate([stat] * (count // LANES), axis=1)


def norm_rows(ref, start, count, at, gain, first, length, masked_ref, mean_ref, inverse_ref):
    width = masked_ref.shape[1]
    rows = pl.ds(start, count)
    tiles = [pl.ds(i * LANES, LANES) for i in range(width // LANES)]

    def values(tile):
        return ref[rows, tile].astype(F32)

    total = values(tiles[0])
    for tile in tiles[1:]:
        total = total + values(tile)
    mean = jnp.sum(total, axis=1, keepdims=True) * (1.0 / width)
    mean = jnp.broadcast_to(mean, (count, LANES))
    square = jnp.zeros((count, LANES), F32)
    for tile in tiles:
        center = values(tile) - mean
        square = square + center * center
    var = jnp.sum(square, axis=1, keepdims=True) * (1.0 / width)
    inverse = jnp.broadcast_to(lax.rsqrt(var + epsilon), (count, LANES))
    frame = first + at + lax.broadcasted_iota(jnp.int32, (count, LANES), 0)
    mask = ((frame >= 0) & (frame < length)).astype(F32)
    scale = mask * inverse
    out = pl.ds(at, count)
    for tile in tiles:
        masked_ref[out, tile] = ((values(tile) - mean) * scale * gain(tile)).astype(BF16)
    if mean_ref is not None:
        mean_ref[out, :] = mean
        inverse_ref[out, :] = inverse


def norm_pieces(pieces, gain, first, length, masked_ref, mean_ref=None, inverse_ref=None, chunk=64):
    at = 0
    for ref, start, count in pieces:
        for begin in range(0, count, chunk):
            norm_rows(
                ref, start + begin, min(chunk, count - begin), at + begin,
                gain, first, length, masked_ref, mean_ref, inverse_ref,
            )
        at += count


def window(pieces, columns):
    parts = [ref[pl.ds(start, count), columns] for ref, start, count in pieces]
    return parts[0] if len(parts) == 1 else jnp.concatenate(parts, axis=0)


def each_block(width, body):
    def step(i, _):
        body(pl.ds(pl.multiple_of(i * BLOCK, BLOCK), BLOCK))
        return 0

    lax.fori_loop(0, width // BLOCK, step, 0)


def tap_spectrum(table, weights):
    return dot(table, jnp.concatenate([weights, weights], axis=0))


def gate_factor(conv):
    gate = sigmoid(conv)
    return gate * (1.0 + conv * (1.0 - gate))


def place(rows):
    sections = lax.axis_size("section")
    return lax.axis_index("section"), sections, lax.axis_index("tm") * rows


def lane_sum(values):
    total = values[:, :LANES]
    for lane in range(LANES, values.shape[1], LANES):
        total = total + values[:, lane : lane + LANES]
    return total


class Back:
    def __init__(self, own, reach, saved, mean, inverse, gain, mask_row, go_table, gh_table, x_table):
        self.__dict__.update(locals())

    def mixed(self, pieces, factor, columns):
        return (window(pieces, columns).astype(F32) * factor).astype(BF16)

    def spectra(self, mixed):
        own, reach = self.own, self.reach
        inner = mixed[reach : reach + own]
        ends = jnp.concatenate([mixed[:reach], mixed[reach + own :]], axis=0)
        g_own = dot(self.go_table[...], jnp.concatenate([inner, inner], axis=0))
        return g_own, g_own + dot(self.gh_table[...], jnp.concatenate([ends, ends], axis=0))

    def rest(self, g_all, q, columns, scaled, sum_a, sum_b):
        grad_masked = wide(self.mask_row, BLOCK) * inverse_dft(self.x_table, product_conj(g_all, q))
        centered = self.saved[:, columns].astype(F32) - wide(self.mean[...], BLOCK)
        weighted = grad_masked * (centered * wide(self.inverse[...], BLOCK))
        gain = self.gain(columns)
        by_gain = grad_masked * gain
        scaled[:, columns] = by_gain
        sum_a[...] += lane_sum(by_gain)
        sum_b[...] += lane_sum(weighted * gain)
        return jnp.sum(weighted, axis=0, keepdims=True)

    def finish(self, ref, start, scaled, sum_a, sum_b, outs, chunk=64):
        width = self.saved.shape[1]
        for begin in range(0, self.own, chunk):
            rows = pl.ds(begin, chunk)
            mean = self.mean[rows, :]
            inverse = self.inverse[rows, :]
            mean_a = jnp.sum(sum_a[rows, :], axis=1, keepdims=True) * (1.0 / width)
            mean_b = jnp.sum(sum_b[rows, :], axis=1, keepdims=True) * (1.0 / width)
            slope = inverse * jnp.broadcast_to(mean_b, (chunk, LANES)) * inverse
            fixed = inverse * jnp.broadcast_to(mean_a, (chunk, LANES)) - slope * mean
            for lane in range(0, width, LANES):
                tile = pl.ds(lane, LANES)
                change = inverse * scaled[rows, tile] - fixed - slope * self.saved[rows, tile].astype(F32)
                value = ref[pl.ds(start + begin, chunk), tile].astype(F32) + change
                for out, low, high in outs:
                    if low < begin + chunk and high > begin:
                        a, b = max(low, begin), min(high, begin + chunk)
                        out[pl.ds(a - low, b - a), tile] = value[a - begin : b - begin].astype(BF16)


def own_mask(own, first, length):
    frame = first + lax.broadcasted_iota(jnp.int32, (own, LANES), 0)
    return (frame < length).astype(F32)


def slot_row(weights, slot):
    last = weights.shape[1] - 1
    return lambda columns: weights[slot, last : last + 1, columns].astype(F32)


def first_backward_kernel(
    reach, lengths, slots, saved, left, right, grads, weights,
    m_table, q_table, c_table, go_table, gh_table, x_table,
    grad_x, top, bottom, masked, inner, gain_sum, mean, inverse, scaled, sum_a, sum_b,
):
    own = saved.shape[0]
    width = saved.shape[1]
    half = reach // 2
    section, sections, first = place(own)
    slot, length = slots[section, 0], lengths[section]
    gain = slot_row(weights, slot)
    pieces = [(left, 0, reach), (saved, 0, own), (right, 0, reach)]
    norm_pieces(pieces, gain, first - reach, length, masked, mean, inverse)
    grad_pieces = [(left, reach, half), (grads, 0, own), (right, reach, half)]
    middle = pl.ds(reach, own)
    back = Back(
        own, half, saved, mean.at[middle], inverse.at[middle], gain, own_mask(own, first, length),
        go_table, gh_table, x_table,
    )
    sum_a[...] = jnp.zeros_like(sum_a)
    sum_b[...] = jnp.zeros_like(sum_b)

    def block(columns):
        q = tap_spectrum(q_table[...], weights[slot, :, columns])
        m = forward_dft(m_table, masked[:, columns])
        conv = inverse_dft(c_table, product(m, q))
        mixed = back.mixed(grad_pieces, gate_factor(conv), columns)
        inner[:, columns] = mixed[half : half + own]
        gain_sum[:, columns] = back.rest(back.spectra(mixed)[1], q, columns, scaled, sum_a, sum_b)

    each_block(width, block)
    outs = [(grad_x, 0, own), (top, 0, half), (bottom, own - half, own)]
    back.finish(grads, 0, scaled, sum_a, sum_b, outs)


def first_taps_kernel(masked, inner, gain_sum, m_table, go_table, t_table, taps):
    def block(columns):
        m = forward_dft(m_table, masked[:, columns])
        mixed = inner[:, columns]
        g_own = dot(go_table[...], jnp.concatenate([mixed, mixed], axis=0))
        put_taps(taps, inverse_dft(t_table, product_conj(m, g_own)), gain_sum[:, columns], columns)

    each_block(masked.shape[1], block)


def put_taps(taps, tap, gain_sum, columns):
    row = lax.broadcasted_iota(jnp.int32, tap.shape, 0)
    taps[:, columns] = jnp.where(row == tap.shape[0] - 1, gain_sum, tap).astype(taps.dtype)


def prepare_kernel(
    reach, lengths, slots, saved, left, right, weights,
    m_table, q_table, c_table,
    m_out, q_out, factor_out, mean_out, inverse_out, masked, mean, inverse,
):
    own, width = saved.shape
    section, sections, first = place(own)
    slot, length = slots[section, 1], lengths[lax.rem(section + 1, sections)]
    gain = slot_row(weights, slot)
    pieces = [(left, 0, reach), (saved, 0, own), (right, 0, reach)]
    norm_pieces(pieces, gain, first - reach, length, masked, mean, inverse)
    mean_out[...] = mean[pl.ds(reach, own), :]
    inverse_out[...] = inverse[pl.ds(reach, own), :]

    def block(columns):
        q = tap_spectrum(q_table[...], weights[slot, :, columns])
        m = forward_dft(m_table, masked[:, columns])
        q_out[:, columns] = q
        m_out[:, columns] = m
        factor_out[:, columns] = gate_factor(inverse_dft(c_table, product(m, q)))

    each_block(width, block)


def second_backward_kernel(
    lengths, slots, saved, left, grads, right, weights, m, q, factor, mean, inverse,
    go_table, gh_table, x_table, t_table,
    grad_x, taps, scaled, sum_a, sum_b,
):
    own, width = saved.shape
    half = left.shape[0]
    section, sections, first = place(own)
    slot, length = slots[section, 1], lengths[lax.rem(section + 1, sections)]
    pieces = [(left, 0, half), (grads, 0, own), (right, 0, half)]
    back = Back(
        own, half, saved, mean, inverse, slot_row(weights, slot), own_mask(own, first, length),
        go_table, gh_table, x_table,
    )
    sum_a[...] = jnp.zeros_like(sum_a)
    sum_b[...] = jnp.zeros_like(sum_b)

    def block(columns):
        mixed = back.mixed(pieces, factor[:, columns], columns)
        g_own, g_all = back.spectra(mixed)
        tap = inverse_dft(t_table, product_conj(m[:, columns], g_own))
        gain_sum = back.rest(g_all, q[:, columns], columns, scaled, sum_a, sum_b)
        put_taps(taps, tap, gain_sum, columns)

    each_block(width, block)
    back.finish(grads, 0, scaled, sum_a, sum_b, [(grad_x, 0, own)])


def forward_kernel(
    reach, lengths, slots, act, left, right, weights, later,
    m0_table, q0_table, c0_table, m1_table, q1_table, c1_table,
    out, masked0, between, masked1,
):
    own, width = act.shape
    middle = reach // 2
    section, sections, first = place(own)
    slot, length = slots[section, 0], lengths[section]
    at = left.shape[0] - reach
    pieces = [(left, at, reach), (act, 0, own), (right, at, reach)]
    inner = [(left, at + middle, middle), (act, 0, own), (right, at, middle)]
    norm_pieces(pieces, slot_row(weights, slot), first - reach, length, masked0)

    def first_layer(columns):
        q = tap_spectrum(q0_table[...], weights[slot, :, columns])
        conv = inverse_dft(c0_table, product(forward_dft(m0_table, masked0[:, columns]), q))
        between[:, columns] = (window(inner, columns).astype(F32) + conv * sigmoid(conv)).astype(BF16)

    each_block(width, first_layer)
    last = later.shape[0] - 1
    norm_pieces([(between, 0, own + 2 * middle)], lambda tile: later[last : last + 1, tile].astype(F32), first - middle, length, masked1)

    def second_layer(columns):
        q = tap_spectrum(q1_table[...], later[:, columns])
        conv = inverse_dft(c1_table, product(forward_dft(m1_table, masked1[:, columns]), q))
        here = between[middle : middle + own, columns].astype(F32)
        out[:, columns] = (here + conv * sigmoid(conv)).astype(BF16)

    each_block(width, second_layer)


def pack_kernel(count, refs):
    sems = refs[-1]
    copies = [
        pltpu.make_async_copy(refs[a].at[i].at[pl.ds(s, n)], refs[b].at[pl.ds(t, n)], sems.at[k])
        for k, (a, i, s, n, b, t) in enumerate(count)
    ]
    for copy in copies:
        copy.start()
    for copy in copies:
        copy.wait()


def final_kernel(slots, mine0, other0, mine1, other1, act, grad, act_out, grad_out, taps, gains, sems):
    copies = [
        pltpu.make_async_copy(act, act_out, sems.at[0]),
        pltpu.make_async_copy(grad, grad_out, sems.at[1]),
    ]
    for copy in copies:
        copy.start()
    section = lax.axis_index("section")
    count = taps.shape[0]
    total0 = mine0[...].astype(F32) + other0[...].astype(F32)
    total1 = mine1[...].astype(F32) + other1[...].astype(F32)
    for slot in range(taps.shape[1]):
        use0 = (slots[section, 0] == slot).astype(F32)
        use1 = (slots[section, 1] == slot).astype(F32)
        total = use0 * total0 + use1 * total1
        taps[:, slot, :] = total[:count]
        gains[slot : slot + 1, :] = total[count:]
    for copy in copies:
        copy.wait()


def span(reach, own):
    return np.arange(-reach, own + reach)


VMEM = pl.BlockSpec(memory_space=pltpu.VMEM)
SMEM = pl.BlockSpec(memory_space=pltpu.SMEM)
ANY = pl.BlockSpec(memory_space=pl.ANY)
LIMIT = 24 * 1024 * 1024


def call(kernel, outs, scratch, operands, flops, specs=None, out_specs=None):
    moved = sum(int(np.prod(x.shape)) * x.dtype.itemsize for x in operands)
    if specs is None:
        specs = [SMEM if x.dtype == jnp.int32 else VMEM for x in operands]
    return pl.pallas_call(
        kernel,
        out_shape=outs,
        in_specs=specs,
        out_specs=jax.tree.map(lambda _: VMEM, outs) if out_specs is None else out_specs,
        scratch_shapes=scratch,
        compiler_params=pltpu.CompilerParams(vmem_limit_bytes=LIMIT),
        cost_estimate=pl.CostEstimate(flops=flops, bytes_accessed=moved, transcendentals=0),
    )(*operands)


def like(rows, width, dtype):
    return jax.ShapeDtypeStruct((rows, width), dtype)


def up16(count):
    return -(-count // 16) * 16


def local(
    act_in, grad_in, saved_inputs, kernels, norm_gains,
    forward_lengths, backward_lengths, forward_slots, backward_slots,
):
    sections = lax.axis_size("section")
    shards = lax.axis_size("tm")
    section = lax.axis_index("section")
    act, grad, saved = act_in[0], grad_in[0], saved_inputs[0]
    own, width = act.shape
    tap_count = kernels.shape[2]
    half = (tap_count - 1) // 2
    one, two = up16(half), up16(2 * half)
    size = own + 2 * two
    small = own + 2 * one

    def shifted(x, by):
        return lax.ppermute(x, "section", [(i, (i + by) % sections) for i in range(sections)])

    def to_neighbour(x, by, along):
        pairs = [
            (s * shards + t, (s + by) % sections * shards + t + along)
            for s in range(sections)
            for t in range(shards)
            if 0 <= t + along < shards
        ]
        return lax.ppermute(x, ("section", "tm"), pairs)

    end, end2 = own - one, own - two
    plan = [
        (0, 0, end2, two, 3, 0), (1, 0, end, one, 3, two), (0, 0, 0, two, 4, 0), (1, 0, 0, one, 4, two),
        (0, 1, end2, two, 5, 0), (2, 0, end2, two, 5, two), (0, 1, 0, two, 6, 0), (2, 0, 0, two, 6, two),
    ]
    tail0, head0, tail1, head1 = call(
        lambda *refs: pack_kernel(plan, refs),
        tuple(like(n, width, BF16) for n in (two + one, two + one, 2 * two, 2 * two)),
        [pltpu.SemaphoreType.DMA((len(plan),))],
        (saved, grad_in, act_in),
        0, [ANY] * 3, (ANY,) * 4,
    )
    up = [(i, i + 1) for i in range(shards - 1)]
    down = [(i + 1, i) for i in range(shards - 1)]
    left0, right0 = lax.ppermute(tail0, "tm", up), lax.ppermute(head0, "tm", down)
    left1, right1 = lax.ppermute(tail1, "tm", up), lax.ppermute(head1, "tm", down)
    weights = jnp.concatenate([kernels[0], norm_gains[0][:, None, :]], axis=1)
    later = shifted(lax.dynamic_index_in_dim(weights, forward_slots[section, 1], 0, keepdims=False), -1)

    ends = np.concatenate([np.arange(-one, 0), np.arange(own, own + one)])
    tap_back = np.concatenate([from_freq(size, np.arange(tap_count) - half), np.zeros((1, size))], axis=0)
    m_table = stacked(to_freq(size, span(two, own)))
    q_table = tap_freq(size, tap_count)
    c_table = stacked(from_freq(size, span(one, own)))
    go_table = beside(to_freq(size, np.arange(own)))
    gh_table = beside(to_freq(size, ends))
    x_table = stacked(from_freq(size, span(0, own)))
    t_table = stacked(tap_back)
    work = 2 * size * size * width

    def run(kernel, outs, scratch, operands, flops):
        return call(kernel, outs, scratch, [jnp.asarray(x) for x in operands], flops)

    rows = [pltpu.VMEM((own, width), F32)] + [pltpu.VMEM((own, LANES), F32)] * 2
    stats = [pltpu.VMEM((size, LANES), F32)] * 2
    grad_mid, top, bottom, masked0, inner0, gain0 = run(
        functools.partial(first_backward_kernel, two),
        (
            like(own, width, BF16), like(one, width, BF16), like(one, width, BF16),
            like(size, width, BF16), like(own, width, BF16), like(1, width, F32),
        ),
        stats + rows,
        [
            backward_lengths, backward_slots, saved[0], left0, right0, grad, weights,
            m_table, q_table, c_table, go_table, gh_table, x_table,
        ],
        9 * work,
    )
    mid_right = to_neighbour(top, -1, -1)
    mid_left = to_neighbour(bottom, -1, 1)
    grad_mid = shifted(grad_mid, -1)
    taps0 = run(
        first_taps_kernel, like(tap_count + 1, width, BF16), [],
        [masked0, inner0, gain0, m_table, go_table, t_table], 3 * work,
    )
    act_out = run(
        functools.partial(forward_kernel, two),
        like(own, width, BF16),
        [pltpu.VMEM((size, width), BF16), pltpu.VMEM((small, width), BF16), pltpu.VMEM((small, width), BF16)],
        [
            forward_lengths, forward_slots, act, left1, right1, weights, later,
            m_table, q_table, c_table,
            stacked(to_freq(small, span(one, own))), tap_freq(small, tap_count), stacked(from_freq(small, span(0, own))),
        ],
        10 * work,
    )
    act_out = shifted(act_out, 2)
    prepared = run(
        functools.partial(prepare_kernel, two),
        (
            like(size, width, F32), like(size, width, F32), like(small, width, F32),
            like(own, LANES, F32), like(own, LANES, F32),
        ),
        [pltpu.VMEM((size, width), BF16)] + stats,
        [backward_lengths, backward_slots, saved[1], left1, right1, weights, m_table, q_table, c_table],
        6 * work,
    )
    grad_out, taps1 = run(
        second_backward_kernel,
        (like(own, width, BF16), like(tap_count + 1, width, BF16)),
        rows,
        [
            backward_lengths, backward_slots, saved[1], mid_left, grad_mid, mid_right, weights, *prepared,
            go_table, gh_table, x_table, t_table,
        ],
        6 * work,
    )

    def summed(x):
        step = 1
        while True:
            other = lax.ppermute(x, "tm", [(i, i ^ step) for i in range(shards)])
            step *= 2
            if step >= shards:
                return x, other
            x = (x.astype(F32) + other.astype(F32)).astype(BF16)

    grad_out = shifted(grad_out, -1)
    sums = summed(taps0) + summed(taps1)
    slots = kernels.shape[1]
    act_out, grad_out, taps, gains = call(
        final_kernel,
        (
            like(own, width, BF16), like(own, width, BF16),
            jax.ShapeDtypeStruct((tap_count, slots, width), F32), like(slots, width, F32),
        ),
        [pltpu.SemaphoreType.DMA((2,))],
        (backward_slots, *sums, act_out, grad_out),
        0, [SMEM] + [VMEM] * 4 + [ANY] * 2, (ANY, ANY, VMEM, VMEM),
    )
    return act_out[None], grad_out[None], taps.transpose(1, 0, 2)[None], gains[None]


def solution(mesh):
    in_specs = (
        P("section", "tm", None),
        P("section", "tm", None),
        P("section", None, "tm", None),
        P("section", None, None, None),
        P("section", None, None),
        P(),
        P(),
        P(),
        P(),
    )
    out_specs = (
        P("section", "tm", None),
        P("section", "tm", None),
        P("section", None, None, None),
        P("section", None, None),
    )
    return jax.shard_map(local, mesh=mesh, in_specs=in_specs, out_specs=out_specs, check_vma=False)
```

```python
import functools

import jax
import jax.numpy as jnp
import ml_dtypes
import numpy as np
from jax import lax
from jax.experimental import pallas as pl
from jax.experimental.pallas import tpu as pltpu
from jax.sharding import PartitionSpec as P

epsilon = 1e-05
BLOCK = 512
LANES = 128
F32 = jnp.float32
BF16 = jnp.bfloat16


def split(matrix):
    high = matrix.astype(ml_dtypes.bfloat16)
    low = (matrix - high.astype(np.float64)).astype(ml_dtypes.bfloat16)
    return high, low


def angles(size, times):
    return 2.0 * np.pi / size * np.outer(np.arange(size // 2) + 0.5, np.asarray(times, np.float64))


def to_freq(size, times):
    phase = angles(size, times)
    return np.concatenate([np.cos(phase), -np.sin(phase)], axis=0)


def from_freq(size, times):
    phase = angles(size, times).T
    return 2.0 / size * np.concatenate([np.cos(phase), -np.sin(phase)], axis=1)


def stacked(matrix):
    return np.concatenate(split(matrix), axis=0)


def beside(matrix):
    return np.concatenate(split(matrix), axis=1)


def tap_freq(size, taps):
    phase = angles(size, np.arange(taps) - (taps - 1) // 2)
    table = np.concatenate([np.cos(phase), np.sin(phase)], axis=0)
    return beside(np.concatenate([table, np.zeros((size, 1))], axis=1))


def dot(a, b):
    return jnp.dot(a, b, preferred_element_type=F32)


def transform(table, values):
    return sum(halves(dot(table[...], values.astype(BF16))))


def halves(values):
    half = values.shape[0] // 2
    return values[:half], values[half:]


def product(a, b):
    ar, ai = halves(a)
    br, bi = halves(b)
    return jnp.concatenate([ar * br - ai * bi, ar * bi + ai * br], axis=0)


def product_conj(a, b):
    ar, ai = halves(a)
    br, bi = halves(b)
    return jnp.concatenate([ar * br + ai * bi, ai * br - ar * bi], axis=0)


def sigmoid(values):
    return 0.5 * jnp.tanh(0.5 * values) + 0.5


def wide(stat, count):
    return jnp.concatenate([stat] * (count // LANES), axis=1)


def norm_rows(ref, start, count, at, gain, first, length, masked_ref, mean_ref, inverse_ref):
    width = masked_ref.shape[1]
    rows = pl.ds(start, count)
    tiles = [pl.ds(i * LANES, LANES) for i in range(width // LANES)]

    def values(tile):
        return ref[rows, tile].astype(F32)

    total = values(tiles[0])
    for tile in tiles[1:]:
        total = total + values(tile)
    mean = jnp.sum(total, axis=1, keepdims=True) * (1.0 / width)
    mean = jnp.broadcast_to(mean, (count, LANES))
    square = jnp.zeros((count, LANES), F32)
    for tile in tiles:
        center = values(tile) - mean
        square = square + center * center
    var = jnp.sum(square, axis=1, keepdims=True) * (1.0 / width)
    inverse = jnp.broadcast_to(lax.rsqrt(var + epsilon), (count, LANES))
    frame = first + at + lax.broadcasted_iota(jnp.int32, (count, LANES), 0)
    mask = ((frame >= 0) & (frame < length)).astype(F32)
    scale = mask * inverse
    out = pl.ds(at, count)
    for tile in tiles:
        masked_ref[out, tile] = ((values(tile) - mean) * scale * gain(tile)).astype(BF16)
    if mean_ref is not None:
        mean_ref[out, :] = mean
        inverse_ref[out, :] = inverse


def norm_pieces(pieces, gain, first, length, masked_ref, mean_ref=None, inverse_ref=None, chunk=64):
    at = 0
    for ref, start, count in pieces:
        for begin in range(0, count, chunk):
            norm_rows(
                ref, start + begin, min(chunk, count - begin), at + begin,
                gain, first, length, masked_ref, mean_ref, inverse_ref,
            )
        at += count


def window(pieces, columns):
    parts = [ref[pl.ds(start, count), columns] for ref, start, count in pieces]
    return parts[0] if len(parts) == 1 else jnp.concatenate(parts, axis=0)


def each_block(width, body):
    def step(i, _):
        body(pl.ds(pl.multiple_of(i * BLOCK, BLOCK), BLOCK))
        return 0

    lax.fori_loop(0, width // BLOCK, step, 0)


def tap_spectrum(table, weights):
    return dot(table, jnp.concatenate([weights, weights], axis=0))


def gate_factor(conv):
    gate = sigmoid(conv)
    return gate * (1.0 + conv * (1.0 - gate))


def place(rows):
    sections = lax.axis_size("section")
    return lax.axis_index("section"), sections, lax.axis_index("tm") * rows


def lane_sum(values):
    total = values[:, :LANES]
    for lane in range(LANES, values.shape[1], LANES):
        total = total + values[:, lane : lane + LANES]
    return total


class Back:
    def __init__(self, own, reach, saved, mean, inverse, gain, mask_row, go_table, gh_table, x_table):
        self.__dict__.update(locals())

    def mixed(self, pieces, factor, columns):
        return (window(pieces, columns).astype(F32) * factor).astype(BF16)

    def spectra(self, mixed):
        own, reach = self.own, self.reach
        inner = mixed[reach : reach + own]
        ends = jnp.concatenate([mixed[:reach], mixed[reach + own :]], axis=0)
        g_own = dot(self.go_table[...], jnp.concatenate([inner, inner], axis=0))
        return g_own, g_own + dot(self.gh_table[...], jnp.concatenate([ends, ends], axis=0))

    def rest(self, g_all, q, columns, scaled, sum_a, sum_b):
        grad_masked = wide(self.mask_row, BLOCK) * transform(self.x_table, product_conj(g_all, q))
        centered = self.saved[:, columns].astype(F32) - wide(self.mean[...], BLOCK)
        weighted = grad_masked * (centered * wide(self.inverse[...], BLOCK))
        gain = self.gain(columns)
        by_gain = grad_masked * gain
        scaled[:, columns] = by_gain
        sum_a[...] += lane_sum(by_gain)
        sum_b[...] += lane_sum(weighted * gain)
        return jnp.sum(weighted, axis=0, keepdims=True)

    def finish(self, ref, start, scaled, sum_a, sum_b, outs, chunk=64):
        width = self.saved.shape[1]
        for begin in range(0, self.own, chunk):
            rows = pl.ds(begin, chunk)
            mean = self.mean[rows, :]
            inverse = self.inverse[rows, :]
            mean_a = jnp.sum(sum_a[rows, :], axis=1, keepdims=True) * (1.0 / width)
            mean_b = jnp.sum(sum_b[rows, :], axis=1, keepdims=True) * (1.0 / width)
            slope = inverse * jnp.broadcast_to(mean_b, (chunk, LANES)) * inverse
            fixed = inverse * jnp.broadcast_to(mean_a, (chunk, LANES)) - slope * mean
            for lane in range(0, width, LANES):
                tile = pl.ds(lane, LANES)
                change = inverse * scaled[rows, tile] - fixed - slope * self.saved[rows, tile].astype(F32)
                value = ref[pl.ds(start + begin, chunk), tile].astype(F32) + change
                for out, low, high in outs:
                    if low < begin + chunk and high > begin:
                        a, b = max(low, begin), min(high, begin + chunk)
                        out[pl.ds(a - low, b - a), tile] = value[a - begin : b - begin].astype(BF16)


def own_mask(own, first, length):
    frame = first + lax.broadcasted_iota(jnp.int32, (own, LANES), 0)
    return (frame < length).astype(F32)


def slot_row(weights, slot):
    last = weights.shape[1] - 1
    return lambda columns: weights[slot, last : last + 1, columns].astype(F32)


def prepare_kernel(
    reach, lengths, slots, later_slots, kernels, gains, saved, q_table,
    weights, later, masked, mean, inverse, q,
):
    own, width = saved.shape[1:]
    count = kernels.shape[0]
    for slot in range(kernels.shape[1]):
        weights[slot, :count, :] = kernels[:, slot, :]
        weights[slot, count:, :] = gains[slot : slot + 1, :]
    section, sections, first = place(own)
    later[...] = weights[later_slots[1, section]]
    slot = slots[0, section]
    gain = slot_row(weights, slot)
    norm_pieces([(saved.at[0], 0, own)], gain, first, lengths[section], masked, mean, inverse)

    def block(columns):
        q[:, columns] = tap_spectrum(q_table[...], weights[slot, :, columns])

    each_block(width, block)


def joined(halo, own, columns):
    reach = halo.shape[0] // 2
    return jnp.concatenate([halo[:reach, columns], own[:, columns], halo[reach:, columns]], axis=0)


def first_backward_kernel(
    reach, lengths, slots, saved, left, right, grads, weights, later, masked, mean, inverse, q,
    m_table, c_table, go_table, gh_table, x_table,
    grad_x, top, bottom, halo, inner, gain_sum, scaled, sum_a, sum_b,
):
    own, width = saved.shape[1:]
    half = reach // 2
    section, sections, first = place(own)
    slot, length = slots[0, section], lengths[section]
    gain = slot_row(weights, slot)
    norm_pieces([(left, 0, reach)], gain, first - reach, length, halo)
    norm_pieces([(right, 0, reach)], gain, first + own, length, halo.at[pl.ds(reach, reach)])
    grad_pieces = [(left, reach, half), (grads, 0, own), (right, reach, half)]
    back = Back(
        own, half, saved.at[0], mean, inverse, gain, own_mask(own, first, length), go_table, gh_table, x_table
    )
    sum_a[...] = jnp.zeros_like(sum_a)
    sum_b[...] = jnp.zeros_like(sum_b)

    def block(columns):
        m = transform(m_table, joined(halo, masked, columns))
        conv = transform(c_table, product(m, q[:, columns]))
        mixed = back.mixed(grad_pieces, gate_factor(conv), columns)
        inner[:, columns] = mixed[half : half + own]
        gain_sum[:, columns] = back.rest(back.spectra(mixed)[1], q[:, columns], columns, scaled, sum_a, sum_b)

    each_block(width, block)
    outs = [(grad_x, 0, own), (top, 0, half), (bottom, own - half, own)]
    back.finish(grads, 0, scaled, sum_a, sum_b, outs)


def first_taps_kernel(halo, masked, inner, gain_sum, m_table, go_table, t_table, taps):
    def block(columns):
        m = transform(m_table, joined(halo, masked, columns))
        mixed = inner[:, columns]
        g_own = dot(go_table[...], jnp.concatenate([mixed, mixed], axis=0))
        put_taps(taps, transform(t_table, product_conj(m, g_own)), gain_sum[:, columns], columns)

    each_block(masked.shape[1], block)


def add_kernel(mine, other, out):
    out[...] = (mine[...].astype(F32) + other[...].astype(F32)).astype(out.dtype)


def put_taps(taps, tap, gain_sum, columns):
    row = lax.broadcasted_iota(jnp.int32, tap.shape, 0)
    taps[:, columns] = jnp.where(row == tap.shape[0] - 1, gain_sum, tap).astype(taps.dtype)


def second_ready_kernel(
    reach, lengths, slots, saved, left, right, weights,
    m_table, q_table, c_table,
    m_out, q_out, factor_out, mean_out, inverse_out, masked, mean, inverse,
):
    own, width = saved.shape[1:]
    section, sections, first = place(own)
    slot, length = slots[1, section], lengths[lax.rem(section + 1, sections)]
    gain = slot_row(weights, slot)
    pieces = [(left, 0, reach), (saved.at[1], 0, own), (right, 0, reach)]
    norm_pieces(pieces, gain, first - reach, length, masked, mean, inverse)
    mean_out[...] = mean[pl.ds(reach, own), :]
    inverse_out[...] = inverse[pl.ds(reach, own), :]

    def block(columns):
        q = tap_spectrum(q_table[...], weights[slot, :, columns])
        m = transform(m_table, masked[:, columns])
        q_out[:, columns] = q
        m_out[:, columns] = m
        factor_out[:, columns] = gate_factor(transform(c_table, product(m, q)))

    each_block(width, block)


def second_backward_kernel(
    lengths, slots, saved, left, grads, right, weights, m, q, factor, mean, inverse, ready,
    go_table, gh_table, x_table, t_table,
    grad_x, taps, scaled, sum_a, sum_b,
):
    own, width = saved.shape[1:]
    half = left.shape[0]
    section, sections, first = place(own)
    slot, length = slots[1, section], lengths[lax.rem(section + 1, sections)]
    pieces = [(left, 0, half), (grads, 0, own), (right, 0, half)]
    back = Back(
        own, half, saved.at[1], mean, inverse, slot_row(weights, slot), own_mask(own, first, length),
        go_table, gh_table, x_table,
    )
    sum_a[...] = jnp.zeros_like(sum_a)
    sum_b[...] = jnp.zeros_like(sum_b)

    def block(columns):
        mixed = back.mixed(pieces, factor[:, columns], columns)
        g_own, g_all = back.spectra(mixed)
        tap = transform(t_table, product_conj(m[:, columns], g_own))
        gain_sum = back.rest(g_all, q[:, columns], columns, scaled, sum_a, sum_b)
        put_taps(taps, tap, gain_sum, columns)

    each_block(width, block)
    back.finish(grads, 0, scaled, sum_a, sum_b, [(grad_x, 0, own)])


def forward_kernel(
    reach, lengths, slots, act, left, right, weights, later,
    m0_table, q0_table, c0_table, m1_table, q1_table, c1_table,
    out, masked0, between, masked1,
):
    own, width = act.shape
    middle = reach // 2
    section, sections, first = place(own)
    slot, length = slots[0, section], lengths[section]
    at = left.shape[0] - reach
    pieces = [(left, at, reach), (act, 0, own), (right, at, reach)]
    inner = [(left, at + middle, middle), (act, 0, own), (right, at, middle)]
    norm_pieces(pieces, slot_row(weights, slot), first - reach, length, masked0)

    def first_layer(columns):
        q = tap_spectrum(q0_table[...], weights[slot, :, columns])
        conv = transform(c0_table, product(transform(m0_table, masked0[:, columns]), q))
        between[:, columns] = (window(inner, columns).astype(F32) + conv * sigmoid(conv)).astype(BF16)

    each_block(width, first_layer)
    last = later.shape[0] - 1
    norm_pieces([(between, 0, own + 2 * middle)], lambda tile: later[last : last + 1, tile].astype(F32), first - middle, length, masked1)

    def second_layer(columns):
        q = tap_spectrum(q1_table[...], later[:, columns])
        conv = transform(c1_table, product(transform(m1_table, masked1[:, columns]), q))
        here = between[middle : middle + own, columns].astype(F32)
        out[:, columns] = (here + conv * sigmoid(conv)).astype(BF16)

    each_block(width, second_layer)


def pack_kernel(count, refs):
    sems = refs[-1]
    copies = [
        pltpu.make_async_copy(refs[a].at[i].at[pl.ds(s, n)], refs[b].at[pl.ds(t, n)], sems.at[k])
        for k, (a, i, s, n, b, t) in enumerate(count)
    ]
    for copy in copies:
        copy.start()
    for copy in copies:
        copy.wait()


def final_kernel(slots, mine0, other0, mine1, other1, act, grad, act_out, grad_out, taps, gains, sems):
    copies = [
        pltpu.make_async_copy(act, act_out, sems.at[0]),
        pltpu.make_async_copy(grad, grad_out, sems.at[1]),
    ]
    for copy in copies:
        copy.start()
    section = lax.axis_index("section")
    count = taps.shape[0]
    total0 = mine0[...].astype(F32) + other0[...].astype(F32)
    total1 = mine1[...].astype(F32) + other1[...].astype(F32)
    for slot in range(taps.shape[1]):
        use0 = (slots[0, section] == slot).astype(F32)
        use1 = (slots[1, section] == slot).astype(F32)
        total = use0 * total0 + use1 * total1
        taps[:, slot, :] = total[:count]
        gains[slot : slot + 1, :] = total[count:]
    for copy in copies:
        copy.wait()


def span(reach, own):
    return np.arange(-reach, own + reach)


VMEM = pl.BlockSpec(memory_space=pltpu.VMEM)
SMEM = pl.BlockSpec(memory_space=pltpu.SMEM)
ANY = pl.BlockSpec(memory_space=pl.ANY)
HBM = pl.BlockSpec(memory_space=pltpu.HBM)
LIMIT = 24 * 1024 * 1024
FULL = 127 * 512 * 1024


def call(kernel, outs, scratch, operands, flops, specs=None, out_specs=None, limit=LIMIT):
    moved = sum(int(np.prod(x.shape)) * x.dtype.itemsize for x in operands)
    if specs is None:
        specs = [SMEM if x.dtype == jnp.int32 else VMEM for x in operands]
    return pl.pallas_call(
        kernel,
        out_shape=outs,
        in_specs=specs,
        out_specs=jax.tree.map(lambda _: VMEM, outs) if out_specs is None else out_specs,
        scratch_shapes=scratch,
        compiler_params=pltpu.CompilerParams(vmem_limit_bytes=limit),
        cost_estimate=pl.CostEstimate(flops=flops, bytes_accessed=moved, transcendentals=0),
    )(*operands)


def like(rows, width, dtype):
    return jax.ShapeDtypeStruct((rows, width), dtype)


def up16(count):
    return -(-count // 16) * 16


def local(
    act_in, grad_in, saved_inputs, kernels, norm_gains,
    forward_lengths, backward_lengths, forward_slots, backward_slots,
):
    sections = lax.axis_size("section")
    shards = lax.axis_size("tm")
    act, grad, saved = act_in[0], grad_in[0], saved_inputs[0]
    own, width = act.shape
    tap_count = kernels.shape[2]
    half = (tap_count - 1) // 2
    one, two = up16(half), up16(2 * half)
    size = own + 2 * two
    small = own + 2 * one

    def shifted(x, by):
        return lax.ppermute(x, "section", [(i, (i + by) % sections) for i in range(sections)])

    def to_neighbour(x, by, along):
        pairs = [
            (s * shards + t, (s + by) % sections * shards + t + along)
            for s in range(sections)
            for t in range(shards)
            if 0 <= t + along < shards
        ]
        return lax.ppermute(x, ("section", "tm"), pairs)

    end, end2 = own - one, own - two
    plan = [
        (0, 0, end2, two, 3, 0), (1, 0, end, one, 3, two), (0, 0, 0, two, 4, 0), (1, 0, 0, one, 4, two),
        (0, 1, end2, two, 5, 0), (2, 0, end2, two, 5, two), (0, 1, 0, two, 6, 0), (2, 0, 0, two, 6, two),
    ]
    tail0, head0, tail1, head1 = call(
        lambda *refs: pack_kernel(plan, refs),
        tuple(like(n, width, BF16) for n in (two + one, two + one, 2 * two, 2 * two)),
        [pltpu.SemaphoreType.DMA((len(plan),))],
        (saved, grad_in, act_in),
        0, [HBM] * 3, (ANY,) * 4, FULL,
    )
    up = [(i, i + 1) for i in range(shards - 1)]
    down = [(i + 1, i) for i in range(shards - 1)]
    left0, right0 = lax.ppermute(tail0, "tm", up), lax.ppermute(head0, "tm", down)
    left1, right1 = lax.ppermute(tail1, "tm", up), lax.ppermute(head1, "tm", down)
    ends = np.concatenate([np.arange(-one, 0), np.arange(own, own + one)])
    tap_back = np.concatenate([from_freq(size, np.arange(tap_count) - half), np.zeros((1, size))], axis=0)
    m_table = stacked(to_freq(size, span(two, own)))
    q_table = tap_freq(size, tap_count)
    c_table = stacked(from_freq(size, span(one, own)))
    go_table = beside(to_freq(size, np.arange(own)))
    gh_table = beside(to_freq(size, ends))
    x_table = stacked(from_freq(size, span(0, own)))
    t_table = stacked(tap_back)
    work = 2 * size * size * width

    def run(kernel, outs, scratch, operands, flops):
        return call(kernel, outs, scratch, [jnp.asarray(x) for x in operands], flops)

    rows = [pltpu.VMEM((own, width), F32)] + [pltpu.VMEM((own, LANES), F32)] * 2
    stats = [pltpu.VMEM((size, LANES), F32)] * 2
    forward_slots, backward_slots = forward_slots.T, backward_slots.T
    weights, later, masked0, mean0, inverse0, q0 = run(
        functools.partial(prepare_kernel, two),
        (
            jax.ShapeDtypeStruct((kernels.shape[1], tap_count + 1, width), BF16), like(tap_count + 1, width, BF16),
            like(own, width, BF16), like(own, LANES, F32), like(own, LANES, F32), like(size, width, F32),
        ),
        [],
        [
            backward_lengths, backward_slots, forward_slots,
            kernels[0].transpose(1, 0, 2), norm_gains[0], saved, q_table,
        ],
        work,
    )
    later = shifted(later, -1)
    grad_mid, top, bottom, halo0, inner0, gain0 = run(
        functools.partial(first_backward_kernel, two),
        (
            like(own, width, BF16), like(one, width, BF16), like(one, width, BF16),
            like(2 * two, width, BF16), like(own, width, BF16), like(1, width, F32),
        ),
        rows,
        [
            backward_lengths, backward_slots, saved, left0, right0, grad, weights, later, masked0, mean0, inverse0, q0,
            m_table, c_table, go_table, gh_table, x_table,
        ],
        9 * work,
    )
    mid_right = to_neighbour(top, -1, -1)
    mid_left = to_neighbour(bottom, -1, 1)
    grad_mid = shifted(grad_mid, -1)
    taps0 = run(
        first_taps_kernel, like(tap_count + 1, width, BF16), [],
        [halo0, masked0, inner0, gain0, m_table, go_table, t_table], 3 * work,
    )
    act_out = run(
        functools.partial(forward_kernel, two),
        like(own, width, BF16),
        [pltpu.VMEM((size, width), BF16), pltpu.VMEM((small, width), BF16), pltpu.VMEM((small, width), BF16)],
        [
            forward_lengths, forward_slots, act, left1, right1, weights, later,
            m_table, q_table, c_table,
            stacked(to_freq(small, span(one, own))), tap_freq(small, tap_count), stacked(from_freq(small, span(0, own))),
        ],
        10 * work,
    )
    act_out = shifted(act_out, 2)
    prepared = run(
        functools.partial(second_ready_kernel, two),
        (
            like(size, width, F32), like(size, width, F32), like(small, width, F32),
            like(own, LANES, F32), like(own, LANES, F32),
        ),
        [pltpu.VMEM((size, width), BF16)] + stats,
        [backward_lengths, backward_slots, saved, left1, right1, weights, m_table, q_table, c_table],
        6 * work,
    )
    def summed(x):
        step = 1
        while True:
            other = lax.ppermute(x, "tm", [(i, i ^ step) for i in range(shards)])
            step *= 2
            if step >= shards:
                return x, other
            x = call(add_kernel, like(*x.shape, BF16), [], (x, other), 0)

    mine0, other0 = summed(taps0)
    grad_out, taps1 = run(
        second_backward_kernel,
        (like(own, width, BF16), like(tap_count + 1, width, BF16)),
        rows,
        [
            backward_lengths, backward_slots, saved, mid_left, grad_mid, mid_right, weights, *prepared, mine0,
            go_table, gh_table, x_table, t_table,
        ],
        6 * work,
    )

    grad_out = shifted(grad_out, -1)
    sums = (mine0, other0) + summed(taps1)
    slots = kernels.shape[1]
    act_out, grad_out, taps, gains = call(
        final_kernel,
        (
            like(own, width, BF16), like(own, width, BF16),
            jax.ShapeDtypeStruct((tap_count, slots, width), F32), like(slots, width, F32),
        ),
        [pltpu.SemaphoreType.DMA((2,))],
        (backward_slots, *sums, act_out, grad_out),
        0, [SMEM] + [VMEM] * 4 + [ANY] * 2, (ANY, ANY, VMEM, VMEM),
    )
    return act_out[None], grad_out[None], taps.transpose(1, 0, 2)[None], gains[None]


def solution(mesh):
    in_specs = (
        P("section", "tm", None),
        P("section", "tm", None),
        P("section", None, "tm", None),
        P("section", None, None, None),
        P("section", None, None),
        P(),
        P(),
        P(),
        P(),
    )
    out_specs = (
        P("section", "tm", None),
        P("section", "tm", None),
        P("section", None, None, None),
        P("section", None, None),
    )
    return jax.shard_map(local, mesh=mesh, in_specs=in_specs, out_specs=out_specs, check_vma=False)
```

```python
import functools

import jax
import jax.numpy as jnp
import ml_dtypes
import numpy as np
from jax import lax
from jax.experimental import pallas as pl
from jax.experimental.pallas import tpu as pltpu
from jax.sharding import PartitionSpec as P

epsilon = 1e-05
BLOCK = 512
LANES = 128
F32 = jnp.float32
BF16 = jnp.bfloat16


def split(matrix):
    high = matrix.astype(ml_dtypes.bfloat16)
    low = (matrix - high.astype(np.float64)).astype(ml_dtypes.bfloat16)
    return high, low


def angles(size, times):
    return 2.0 * np.pi / size * np.outer(np.arange(size // 2) + 0.5, np.asarray(times, np.float64))


def to_freq(size, times):
    phase = angles(size, times)
    return np.concatenate([np.cos(phase), -np.sin(phase)], axis=0)


def from_freq(size, times):
    phase = angles(size, times).T
    return 2.0 / size * np.concatenate([np.cos(phase), -np.sin(phase)], axis=1)


def stacked(matrix):
    return np.concatenate(split(matrix), axis=0)


def beside(matrix):
    return np.concatenate(split(matrix), axis=1)


def tap_freq(size, taps):
    phase = angles(size, np.arange(taps) - (taps - 1) // 2)
    table = np.concatenate([np.cos(phase), np.sin(phase)], axis=0)
    return beside(np.concatenate([table, np.zeros((size, 1))], axis=1))


def dot(a, b):
    return jnp.dot(a, b, preferred_element_type=F32)


def transform(table, values):
    return sum(halves(dot(table[...], values.astype(BF16))))


def halves(values):
    half = values.shape[0] // 2
    return values[:half], values[half:]


def product(a, b):
    ar, ai = halves(a)
    br, bi = halves(b)
    return jnp.concatenate([ar * br - ai * bi, ar * bi + ai * br], axis=0)


def product_conj(a, b):
    ar, ai = halves(a)
    br, bi = halves(b)
    return jnp.concatenate([ar * br + ai * bi, ai * br - ar * bi], axis=0)


def sigmoid(values):
    return 0.5 * jnp.tanh(0.5 * values) + 0.5


def wide(stat, count):
    return jnp.concatenate([stat] * (count // LANES), axis=1)


def norm_rows(ref, start, count, at, gain, first, length, masked_ref, mean_ref, inverse_ref):
    width = masked_ref.shape[1]
    rows = pl.ds(start, count)
    tiles = [pl.ds(i * LANES, LANES) for i in range(width // LANES)]

    def values(tile):
        return ref[rows, tile].astype(F32)

    total = values(tiles[0])
    for tile in tiles[1:]:
        total = total + values(tile)
    mean = jnp.sum(total, axis=1, keepdims=True) * (1.0 / width)
    mean = jnp.broadcast_to(mean, (count, LANES))
    square = jnp.zeros((count, LANES), F32)
    for tile in tiles:
        center = values(tile) - mean
        square = square + center * center
    var = jnp.sum(square, axis=1, keepdims=True) * (1.0 / width)
    inverse = jnp.broadcast_to(lax.rsqrt(var + epsilon), (count, LANES))
    frame = first + at + lax.broadcasted_iota(jnp.int32, (count, LANES), 0)
    mask = ((frame >= 0) & (frame < length)).astype(F32)
    scale = mask * inverse
    out = pl.ds(at, count)
    for tile in tiles:
        masked_ref[out, tile] = ((values(tile) - mean) * scale * gain(tile)).astype(BF16)
    if mean_ref is not None:
        mean_ref[out, :] = mean
        inverse_ref[out, :] = inverse


def norm_pieces(pieces, gain, first, length, masked_ref, mean_ref=None, inverse_ref=None, chunk=64):
    at = 0
    for ref, start, count in pieces:
        for begin in range(0, count, chunk):
            norm_rows(
                ref, start + begin, min(chunk, count - begin), at + begin,
                gain, first, length, masked_ref, mean_ref, inverse_ref,
            )
        at += count


def window(pieces, columns):
    parts = [ref[pl.ds(start, count), columns] for ref, start, count in pieces]
    return parts[0] if len(parts) == 1 else jnp.concatenate(parts, axis=0)


def each_block(width, body):
    def step(i, _):
        body(pl.ds(pl.multiple_of(i * BLOCK, BLOCK), BLOCK))
        return 0

    lax.fori_loop(0, width // BLOCK, step, 0)


def tap_spectrum(table, weights):
    return dot(table, jnp.concatenate([weights, weights], axis=0))


def gate_factor(conv):
    gate = sigmoid(conv)
    return gate * (1.0 + conv * (1.0 - gate))


def place(rows):
    sections = lax.axis_size("section")
    return lax.axis_index("section"), sections, lax.axis_index("tm") * rows


def lane_sum(values):
    total = values[:, :LANES]
    for lane in range(LANES, values.shape[1], LANES):
        total = total + values[:, lane : lane + LANES]
    return total


class Back:
    def __init__(self, own, saved, mean, inverse, gain, mask_row, g_table, x_table):
        self.__dict__.update(locals())

    def rest(self, mixed, q, columns, scaled, sum_a, sum_b):
        grad_masked = wide(self.mask_row, BLOCK) * transform(
            self.x_table, product_conj(transform(self.g_table, mixed), q)
        )
        centered = self.saved[:, columns].astype(F32) - wide(self.mean[...], BLOCK)
        weighted = grad_masked * (centered * wide(self.inverse[...], BLOCK))
        gain = self.gain(columns)
        by_gain = grad_masked * gain
        scaled[:, columns] = by_gain
        sum_a[...] += lane_sum(by_gain)
        sum_b[...] += lane_sum(weighted * gain)
        return jnp.sum(weighted, axis=0, keepdims=True)

    def finish(self, ref, start, scaled, sum_a, sum_b, outs, chunk=64):
        width = self.saved.shape[1]
        for begin in range(0, self.own, chunk):
            rows = pl.ds(begin, chunk)
            mean = self.mean[rows, :]
            inverse = self.inverse[rows, :]
            mean_a = jnp.sum(sum_a[rows, :], axis=1, keepdims=True) * (1.0 / width)
            mean_b = jnp.sum(sum_b[rows, :], axis=1, keepdims=True) * (1.0 / width)
            slope = inverse * jnp.broadcast_to(mean_b, (chunk, LANES)) * inverse
            fixed = inverse * jnp.broadcast_to(mean_a, (chunk, LANES)) - slope * mean
            for lane in range(0, width, LANES):
                tile = pl.ds(lane, LANES)
                change = inverse * scaled[rows, tile] - fixed - slope * self.saved[rows, tile].astype(F32)
                value = ref[pl.ds(start + begin, chunk), tile].astype(F32) + change
                for out, low, high in outs:
                    if low < begin + chunk and high > begin:
                        a, b = max(low, begin), min(high, begin + chunk)
                        out[pl.ds(a - low, b - a), tile] = value[a - begin : b - begin].astype(BF16)


def own_mask(own, first, length):
    frame = first + lax.broadcasted_iota(jnp.int32, (own, LANES), 0)
    return (frame < length).astype(F32)


def slot_row(weights, slot):
    last = weights.shape[1] - 1
    return lambda columns: weights[slot, last : last + 1, columns].astype(F32)


def prepare_kernel(
    reach, back_lengths, ahead_lengths, back_slots, ahead_slots, kernels, gains, saved, act, ready, q_table,
    weights, later, tail, head, *outs,
):
    own, width = act.shape
    for x, at in ((saved.at[1], 0), (act, reach)):
        tail[pl.ds(at, reach), :] = x[pl.ds(own - reach, reach), :]
        head[pl.ds(at, reach), :] = x[pl.ds(0, reach), :]
    count = kernels.shape[0]
    for slot in range(kernels.shape[1]):
        weights[slot, :count, :] = kernels[:, slot, :]
        weights[slot, count:, :] = gains[slot : slot + 1, :]
    section, sections, first = place(own)
    later[...] = weights[ahead_slots[1, section]]
    layers = [
        (saved.at[0], back_slots[0, section], back_lengths[section]),
        (saved.at[1], back_slots[1, section], back_lengths[lax.rem(section + 1, sections)]),
        (act, ahead_slots[0, section], ahead_lengths[section]),
    ]
    for (x, slot, length), (masked, mean, inverse, q) in zip(layers, (outs[:4], outs[4:8], outs[8:])):
        norm_pieces([(x, 0, own)], slot_row(weights, slot), first, length, masked, mean, inverse)

        def block(columns, slot=slot, q=q):
            q[:, columns] = tap_spectrum(q_table[...], weights[slot, :, columns])

        each_block(width, block)


def norm_halo(left, right, at, reach, own, gain, first, length, halo):
    norm_pieces([(left, at, reach)], gain, first - reach, length, halo)
    norm_pieces([(right, at, reach)], gain, first + own, length, halo.at[pl.ds(reach, reach)])


def joined(halo, own, columns):
    reach = halo.shape[0] // 2
    return jnp.concatenate([halo[:reach, columns], own[:, columns], halo[reach:, columns]], axis=0)


def first_backward_kernel(
    reach, lengths, slots, saved, left, right, grads, weights, later, masked, mean, inverse, q,
    m_table, c_table, g_table, x_table,
    grad_x, top, bottom, halo, inner, gain_sum, scaled, sum_a, sum_b,
):
    own, width = grads.shape
    half = reach // 2
    section, sections, first = place(own)
    slot, length = slots[0, section], lengths[section]
    gain = slot_row(weights, slot)
    norm_halo(left, right, 0, reach, own, gain, first, length, halo)
    grad_pieces = [(left, reach, half), (grads, 0, own), (right, reach, half)]
    back = Back(own, saved.at[0], mean, inverse, gain, own_mask(own, first, length), g_table, x_table)
    sum_a[...] = jnp.zeros_like(sum_a)
    sum_b[...] = jnp.zeros_like(sum_b)
    grad_x[pl.ds(own, later.shape[0]), :] = later[...]

    def block(columns):
        m = transform(m_table, joined(halo, masked, columns))
        conv = transform(c_table, product(m, q[:, columns]))
        mixed = (window(grad_pieces, columns).astype(F32) * gate_factor(conv)).astype(BF16)
        inner[:, columns] = mixed[half : half + own]
        gain_sum[:, columns] = back.rest(mixed, q[:, columns], columns, scaled, sum_a, sum_b)

    each_block(width, block)
    outs = [(grad_x, 0, own), (top, 0, half), (bottom, own - half, own)]
    back.finish(grads, 0, scaled, sum_a, sum_b, outs)


def tap_term(go_table, t_table, m, mixed):
    g_own = dot(go_table[...], jnp.concatenate([mixed, mixed], axis=0))
    return transform(t_table, product_conj(m, g_own))


def put_taps(taps, tap, gain_sum, columns):
    row = lax.broadcasted_iota(jnp.int32, tap.shape, 0)
    taps[:, columns] = jnp.where(row == tap.shape[0] - 1, gain_sum, tap).astype(taps.dtype)


def first_taps_kernel(halo, masked, inner, gain_sum, m_table, go_table, t_table, taps):
    def block(columns):
        m = transform(m_table, joined(halo, masked, columns))
        put_taps(taps, tap_term(go_table, t_table, m, inner[:, columns]), gain_sum[:, columns], columns)

    each_block(masked.shape[1], block)


def add_kernel(mine, other, out):
    out[...] = (mine[...].astype(F32) + other[...].astype(F32)).astype(out.dtype)


def second_ready_kernel(
    reach, lengths, slots, left, right, weights, masked, q, m_table, c_table, m_out, factor, conv_out, halo
):
    own, width = masked.shape
    section, sections, first = place(own)
    slot, length = slots[1, section], lengths[lax.rem(section + 1, sections)]
    norm_halo(left, right, 0, reach, own, slot_row(weights, slot), first, length, halo)

    def block(columns):
        m = transform(m_table, joined(halo, masked, columns))
        conv = transform(c_table, product(m, q[:, columns]))
        m_out[:, columns] = m
        factor[:, columns] = gate_factor(conv)
        edge = (conv.shape[0] - own) // 2
        conv_out[:, columns] = conv[edge : edge + own]

    each_block(width, block)


def second_taps_kernel(slots, left, grads, right, weights, m, factor, conv, ready, go_table, t_table, mixed_out, taps):
    own, width = conv.shape
    half = left.shape[0]
    section, sections, first = place(own)
    gain = slot_row(weights, slots[1, section])
    pieces = [(left, 0, half), (grads, 0, own), (right, 0, half)]

    def block(columns):
        mixed = (window(pieces, columns).astype(F32) * factor[:, columns]).astype(BF16)
        mixed_out[:, columns] = mixed
        inner = mixed[half : half + own]
        gain_sum = jnp.sum(inner.astype(F32) * conv[:, columns], axis=0, keepdims=True) / gain(columns)
        put_taps(taps, tap_term(go_table, t_table, m[:, columns], inner), gain_sum, columns)

    each_block(width, block)


def second_backward_kernel(
    lengths, slots, saved, grads, weights, mixed, q, mean, inverse, g_table, x_table, grad_x, scaled, sum_a, sum_b
):
    own, width = grad_x.shape
    section, sections, first = place(own)
    slot, length = slots[1, section], lengths[lax.rem(section + 1, sections)]
    back = Back(
        own, saved.at[1], mean, inverse, slot_row(weights, slot), own_mask(own, first, length), g_table, x_table
    )
    sum_a[...] = jnp.zeros_like(sum_a)
    sum_b[...] = jnp.zeros_like(sum_b)

    def block(columns):
        back.rest(mixed[:, columns], q[:, columns], columns, scaled, sum_a, sum_b)

    each_block(width, block)
    back.finish(grads, 0, scaled, sum_a, sum_b, [(grad_x, 0, own)])


def first_forward_kernel(
    reach, lengths, slots, act, left, right, weights, masked, q, m_table, c_table, out, halo
):
    own, width = act.shape
    middle = reach // 2
    section, sections, first = place(own)
    slot, length = slots[0, section], lengths[section]
    inner = [(left, reach + middle, middle), (act, 0, own), (right, reach, middle)]
    norm_halo(left, right, reach, reach, own, slot_row(weights, slot), first, length, halo)

    def block(columns):
        conv = transform(c_table, product(transform(m_table, joined(halo, masked, columns)), q[:, columns]))
        out[:, columns] = (window(inner, columns).astype(F32) + conv * sigmoid(conv)).astype(BF16)

    each_block(width, block)


def second_forward_kernel(lengths, between, received, m_table, q_table, c_table, out, masked):
    own, width = out.shape
    edge = (between.shape[0] - own) // 2
    section, sections, first = place(own)
    last = received.shape[0] - 1

    def gain(columns):
        return received[last : last + 1, columns].astype(F32)

    norm_pieces([(between, 0, own + 2 * edge)], gain, first - edge, lengths[section], masked)

    def block(columns):
        q = tap_spectrum(q_table[...], received[own:, columns])
        conv = transform(c_table, product(transform(m_table, masked[:, columns]), q))
        out[:, columns] = (between[edge : edge + own, columns].astype(F32) + conv * sigmoid(conv)).astype(BF16)

    each_block(width, block)


def pack_kernel(count, refs):
    sems = refs[-1]
    copies = [
        pltpu.make_async_copy(refs[a].at[i].at[pl.ds(s, n)], refs[b].at[pl.ds(t, n)], sems.at[k])
        for k, (a, i, s, n, b, t) in enumerate(count)
    ]
    for copy in copies:
        copy.start()
    for copy in copies:
        copy.wait()


def final_kernel(slots, mine0, other0, mine1, other1, act, grad, act_out, grad_out, taps, gains, sems):
    copies = [
        pltpu.make_async_copy(act, act_out, sems.at[0]),
        pltpu.make_async_copy(grad, grad_out, sems.at[1]),
    ]
    for copy in copies:
        copy.start()
    section = lax.axis_index("section")
    count = taps.shape[0]
    total0 = mine0[...].astype(F32) + other0[...].astype(F32)
    total1 = mine1[...].astype(F32) + other1[...].astype(F32)
    for slot in range(taps.shape[1]):
        use0 = (slots[0, section] == slot).astype(F32)
        use1 = (slots[1, section] == slot).astype(F32)
        total = use0 * total0 + use1 * total1
        taps[:, slot, :] = total[:count]
        gains[slot : slot + 1, :] = total[count:]
    for copy in copies:
        copy.wait()


def span(reach, own):
    return np.arange(-reach, own + reach)


VMEM = pl.BlockSpec(memory_space=pltpu.VMEM)
SMEM = pl.BlockSpec(memory_space=pltpu.SMEM)
ANY = pl.BlockSpec(memory_space=pl.ANY)
HBM = pl.BlockSpec(memory_space=pltpu.HBM)
LIMIT = 24 * 1024 * 1024
FULL = 127 * 512 * 1024


def call(kernel, outs, scratch, operands, micros, specs=None, out_specs=None, limit=LIMIT):
    if specs is None:
        specs = [SMEM if x.dtype == jnp.int32 else VMEM for x in operands]
    return pl.pallas_call(
        kernel,
        out_shape=outs,
        in_specs=specs,
        out_specs=jax.tree.map(lambda _: VMEM, outs) if out_specs is None else out_specs,
        scratch_shapes=scratch,
        compiler_params=pltpu.CompilerParams(vmem_limit_bytes=limit),
        cost_estimate=pl.CostEstimate(flops=int(micros * 1e9), bytes_accessed=0, transcendentals=0),
    )(*operands)


def like(rows, width, dtype):
    return jax.ShapeDtypeStruct((rows, width), dtype)


def up16(count):
    return -(-count // 16) * 16


def local(
    act_in, grad_in, saved_inputs, kernels, norm_gains,
    forward_lengths, backward_lengths, forward_slots, backward_slots,
):
    sections = lax.axis_size("section")
    shards = lax.axis_size("tm")
    act, grad, saved = act_in[0], grad_in[0], saved_inputs[0]
    own, width = act.shape
    tap_count = kernels.shape[2]
    half = (tap_count - 1) // 2
    one, two = up16(half), up16(2 * half)
    size = own + 2 * two
    small = own + 2 * one

    def shifted(x, by):
        return lax.ppermute(x, "section", [(i, (i + by) % sections) for i in range(sections)])

    def to_neighbour(x, by, along):
        pairs = [
            (s * shards + t, (s + by) % sections * shards + t + along)
            for s in range(sections)
            for t in range(shards)
            if 0 <= t + along < shards
        ]
        return lax.ppermute(x, ("section", "tm"), pairs)

    end, end2 = own - one, own - two
    plan = [(0, 0, end2, two, 2, 0), (1, 0, end, one, 2, two), (0, 0, 0, two, 3, 0), (1, 0, 0, one, 3, two)]
    tail0, head0 = call(
        lambda *refs: pack_kernel(plan, refs),
        (like(two + one, width, BF16),) * 2,
        [pltpu.SemaphoreType.DMA((len(plan),))],
        (saved, grad_in),
        0, [HBM] * 2, None, FULL,
    )
    up = [(i, i + 1) for i in range(shards - 1)]
    down = [(i + 1, i) for i in range(shards - 1)]
    left0, right0 = lax.ppermute(tail0, "tm", up), lax.ppermute(head0, "tm", down)
    tap_back = np.concatenate([from_freq(size, np.arange(tap_count) - half), np.zeros((1, size))], axis=0)
    m_table = stacked(to_freq(size, span(two, own)))
    q_table = tap_freq(size, tap_count)
    c_table = stacked(from_freq(size, span(one, own)))
    go_table = beside(to_freq(size, np.arange(own)))
    g_table = stacked(to_freq(size, span(one, own)))
    x_table = stacked(from_freq(size, span(0, own)))
    t_table = stacked(tap_back)

    def run(kernel, outs, scratch, operands, micros=0):
        return call(kernel, outs, scratch, [jnp.asarray(x) for x in operands], micros)

    rows = [pltpu.VMEM((own, width), F32)] + [pltpu.VMEM((own, LANES), F32)] * 2
    forward_slots, backward_slots = forward_slots.T, backward_slots.T
    layer = (like(own, width, BF16), like(own, LANES, F32), like(own, LANES, F32), like(size, width, F32))
    weights, later, tail1, head1, *layers = run(
        functools.partial(prepare_kernel, two),
        (
            jax.ShapeDtypeStruct((kernels.shape[1], tap_count + 1, width), BF16), like(tap_count + 1, width, BF16),
            like(2 * two, width, BF16), like(2 * two, width, BF16), *layer, *layer, *layer,
        ),
        [],
        [
            backward_lengths, forward_lengths, backward_slots, forward_slots,
            kernels[0].transpose(1, 0, 2), norm_gains[0], saved, act, tail0, q_table,
        ],
    )
    masked0, mean0, inverse0, q0, masked1, mean1, inverse1, q1, masked2, _, _, q2 = layers
    left1, right1 = lax.ppermute(tail1, "tm", up), lax.ppermute(head1, "tm", down)
    grad_mid, top, bottom, halo0, inner0, gain0 = run(
        functools.partial(first_backward_kernel, two),
        (
            like(own + tap_count + 1, width, BF16), like(one, width, BF16), like(one, width, BF16),
            like(2 * two, width, BF16), like(own, width, BF16), like(1, width, F32),
        ),
        rows,
        [
            backward_lengths, backward_slots, saved, left0, right0, grad, weights, later, masked0, mean0, inverse0, q0,
            m_table, c_table, g_table, x_table,
        ],
        4,
    )
    grad_mid = shifted(grad_mid, -1)
    mid_right = to_neighbour(top, -1, -1)
    mid_left = to_neighbour(bottom, -1, 1)
    taps0 = run(
        first_taps_kernel, like(tap_count + 1, width, BF16), [],
        [halo0, masked0, inner0, gain0, m_table, go_table, t_table],
        0,
    )
    between = run(
        functools.partial(first_forward_kernel, two),
        like(small, width, BF16),
        [pltpu.VMEM((2 * two, width), BF16)],
        [forward_lengths, forward_slots, act, left1, right1, weights, masked2, q2, m_table, c_table],
        3,
    )
    m1, factor1, conv1 = run(
        functools.partial(second_ready_kernel, two),
        (like(size, width, F32), like(small, width, F32), like(own, width, F32)),
        [pltpu.VMEM((2 * two, width), BF16)],
        [backward_lengths, backward_slots, left1, right1, weights, masked1, q1, m_table, c_table],
        3,
    )
    act_out = run(
        second_forward_kernel,
        like(own, width, BF16),
        [pltpu.VMEM((small, width), BF16)],
        [
            forward_lengths, between, grad_mid,
            stacked(to_freq(small, span(one, own))), tap_freq(small, tap_count), stacked(from_freq(small, span(0, own))),
        ],
        3,
    )
    act_out = shifted(act_out, 2)

    def summed(x, micros):
        step = 1
        while True:
            other = lax.ppermute(x, "tm", [(i, i ^ step) for i in range(shards)])
            step *= 2
            if step >= shards:
                return x, other
            x = call(add_kernel, like(*x.shape, BF16), [], (x, other), micros)

    mine0, other0 = summed(taps0, 0)
    mixed1, taps1 = run(
        second_taps_kernel,
        (like(small, width, BF16), like(tap_count + 1, width, BF16)),
        [],
        [backward_slots, mid_left, grad_mid, mid_right, weights, m1, factor1, conv1, other0, go_table, t_table],
        2,
    )
    grad_out = run(
        second_backward_kernel,
        like(own, width, BF16),
        rows,
        [
            backward_lengths, backward_slots, saved, grad_mid, weights, mixed1, q1, mean1, inverse1,
            g_table, x_table,
        ],
        6,
    )
    grad_out = shifted(grad_out, -1)
    sums = (mine0, other0) + summed(taps1, 6)
    slots = kernels.shape[1]
    act_out, grad_out, taps, gains = call(
        final_kernel,
        (
            like(own, width, BF16), like(own, width, BF16),
            jax.ShapeDtypeStruct((tap_count, slots, width), F32), like(slots, width, F32),
        ),
        [pltpu.SemaphoreType.DMA((2,))],
        (backward_slots, *sums, act_out, grad_out),
        0, [SMEM] + [VMEM] * 4 + [ANY] * 2, (ANY, ANY, VMEM, VMEM),
    )
    return act_out[None], grad_out[None], taps.transpose(1, 0, 2)[None], gains[None]


def solution(mesh):
    in_specs = (
        P("section", "tm", None),
        P("section", "tm", None),
        P("section", None, "tm", None),
        P("section", None, None, None),
        P("section", None, None),
        P(),
        P(),
        P(),
        P(),
    )
    out_specs = (
        P("section", "tm", None),
        P("section", "tm", None),
        P("section", None, None, None),
        P("section", None, None),
    )
    return jax.shard_map(local, mesh=mesh, in_specs=in_specs, out_specs=out_specs, check_vma=False)
```

```python
import functools

import jax
import jax.numpy as jnp
import ml_dtypes
import numpy as np
from jax import lax
from jax.experimental import pallas as pl
from jax.experimental.pallas import tpu as pltpu
from jax.sharding import PartitionSpec as P

epsilon = 1e-05
BLOCK = 512
LANES = 128
F32 = jnp.float32
BF16 = jnp.bfloat16


def split(matrix):
    high = matrix.astype(ml_dtypes.bfloat16)
    low = (matrix - high.astype(np.float64)).astype(ml_dtypes.bfloat16)
    return high, low


def angles(size, times):
    return 2.0 * np.pi / size * np.outer(np.arange(size // 2) + 0.5, np.asarray(times, np.float64))


def to_freq(size, times):
    phase = angles(size, times)
    return np.concatenate([np.cos(phase), -np.sin(phase)], axis=0)


def from_freq(size, times):
    phase = angles(size, times).T
    return 2.0 / size * np.concatenate([np.cos(phase), -np.sin(phase)], axis=1)


def stacked(matrix):
    return np.concatenate(split(matrix), axis=0)


def beside(matrix):
    return np.concatenate(split(matrix), axis=1)


def tap_freq(size, taps):
    phase = angles(size, np.arange(taps) - (taps - 1) // 2)
    table = np.concatenate([np.cos(phase), np.sin(phase)], axis=0)
    return beside(np.concatenate([table, np.zeros((size, 1))], axis=1))


def dot(a, b):
    return jnp.dot(a, b, preferred_element_type=F32)


def transform(table, values):
    return sum(halves(dot(table[...], values.astype(BF16))))


def halves(values):
    half = values.shape[0] // 2
    return values[:half], values[half:]


def product(a, b):
    ar, ai = halves(a)
    br, bi = halves(b)
    return jnp.concatenate([ar * br - ai * bi, ar * bi + ai * br], axis=0)


def product_conj(a, b):
    ar, ai = halves(a)
    br, bi = halves(b)
    return jnp.concatenate([ar * br + ai * bi, ai * br - ar * bi], axis=0)


def sigmoid(values):
    return 0.5 * jnp.tanh(0.5 * values) + 0.5


def wide(stat, count):
    return jnp.concatenate([stat] * (count // LANES), axis=1)


def norm_rows(ref, start, count, at, gain, first, length, masked_ref, mean_ref, inverse_ref):
    width = masked_ref.shape[1]
    rows = pl.ds(start, count)
    tiles = [pl.ds(i * LANES, LANES) for i in range(width // LANES)]

    def values(tile):
        return ref[rows, tile].astype(F32)

    total = values(tiles[0])
    for tile in tiles[1:]:
        total = total + values(tile)
    mean = jnp.sum(total, axis=1, keepdims=True) * (1.0 / width)
    mean = jnp.broadcast_to(mean, (count, LANES))
    square = jnp.zeros((count, LANES), F32)
    for tile in tiles:
        center = values(tile) - mean
        square = square + center * center
    var = jnp.sum(square, axis=1, keepdims=True) * (1.0 / width)
    inverse = jnp.broadcast_to(lax.rsqrt(var + epsilon), (count, LANES))
    frame = first + at + lax.broadcasted_iota(jnp.int32, (count, LANES), 0)
    mask = ((frame >= 0) & (frame < length)).astype(F32)
    scale = mask * inverse
    out = pl.ds(at, count)
    for tile in tiles:
        masked_ref[out, tile] = ((values(tile) - mean) * scale * gain(tile)).astype(BF16)
    if mean_ref is not None:
        mean_ref[out, :] = mean
        inverse_ref[out, :] = inverse


def norm_pieces(pieces, gain, first, length, masked_ref, mean_ref=None, inverse_ref=None, chunk=64):
    at = 0
    for ref, start, count in pieces:
        for begin in range(0, count, chunk):
            norm_rows(
                ref, start + begin, min(chunk, count - begin), at + begin,
                gain, first, length, masked_ref, mean_ref, inverse_ref,
            )
        at += count


def window(pieces, columns):
    parts = [ref[pl.ds(start, count), columns] for ref, start, count in pieces]
    return parts[0] if len(parts) == 1 else jnp.concatenate(parts, axis=0)


def each_block(width, body):
    def step(i, _):
        body(pl.ds(pl.multiple_of(i * BLOCK, BLOCK), BLOCK))
        return 0

    lax.fori_loop(0, width // BLOCK, step, 0)


def tap_spectrum(table, weights):
    return dot(table, jnp.concatenate([weights, weights], axis=0))


def gate_factor(conv):
    gate = sigmoid(conv)
    return gate * (1.0 + conv * (1.0 - gate))


FIRST, BACK0, BACK1, AHEAD0 = range(0, 8, 2)


def looked_up(notes, layer):
    return notes[layer], notes[layer + 1], notes[FIRST]


def sorted_halos(near, far, at, halos):
    even = lax.rem(lax.axis_index("tm") + 1, 2)
    rows = pl.ds(at, halos.shape[1])
    halos[even] = near[rows, :]
    halos[1 - even] = far[rows, :]
    return halos.at[0], halos.at[1]


def lane_sum(values):
    total = values[:, :LANES]
    for lane in range(LANES, values.shape[1], LANES):
        total = total + values[:, lane : lane + LANES]
    return total


def first_pass(pieces, mean, inverse, gain, mask, tables, mixed, q, columns, scaled, sum_a, sum_b):
    g_table, x_table = tables
    grad_masked = wide(mask, BLOCK) * transform(x_table, product_conj(transform(g_table, mixed), q))
    centered = window(pieces, columns).astype(F32) - wide(mean[...], BLOCK)
    weighted = grad_masked * (centered * wide(inverse[...], BLOCK))
    gain = gain(columns)
    by_gain = grad_masked * gain
    scaled[:, columns] = by_gain
    sum_a[...] += lane_sum(by_gain)
    sum_b[...] += lane_sum(weighted * gain)
    return weighted


def last_pass(grad_pieces, pieces, mean, inverse, scaled, sum_a, sum_b, grad_x, chunk=64):
    width = scaled.shape[1]
    at = 0
    for (ref, start, count), (saved, base, _) in zip(grad_pieces, pieces):
        for begin in range(0, count, chunk):
            here = min(chunk, count - begin)
            rows = pl.ds(at + begin, here)
            inv = inverse[rows, :]
            mean_a = jnp.sum(sum_a[rows, :], axis=1, keepdims=True) * (1.0 / width)
            mean_b = jnp.sum(sum_b[rows, :], axis=1, keepdims=True) * (1.0 / width)
            slope = inv * jnp.broadcast_to(mean_b, (here, LANES)) * inv
            fixed = inv * jnp.broadcast_to(mean_a, (here, LANES)) - slope * mean[rows, :]
            for lane in range(0, width, LANES):
                tile = pl.ds(lane, LANES)
                x = saved[pl.ds(base + begin, here), tile].astype(F32)
                change = inv * scaled[rows, tile] - fixed - slope * x
                grad_x[rows, tile] = (ref[pl.ds(start + begin, here), tile].astype(F32) + change).astype(BF16)
        at += count


def frame_mask(rows, first, length):
    frame = first + lax.broadcasted_iota(jnp.int32, (rows, LANES), 0)
    return ((frame >= 0) & (frame < length)).astype(F32)


def slot_row(weights, slot):
    last = weights.shape[1] - 1
    return lambda columns: weights[slot, last : last + 1, columns].astype(F32)


def prepare_kernel(
    reach, back_lengths, ahead_lengths, back_slots, ahead_slots, kernels, gains, saved, act, ready, q_table,
    weights, later, near, far, notes, masked, mean, inverse, q,
):
    own, width = act.shape
    section, sections = lax.axis_index("section"), lax.axis_size("section")
    for even in range(2):

        @pl.when(lax.rem(lax.axis_index("tm") + 1, 2) == even)
        def _():
            for x, at in ((saved.at[1], 0), (act, reach)):
                tail, head = (near, far) if even else (far, near)
                tail[pl.ds(at, reach), :] = x[pl.ds(own - reach, reach), :]
                head[pl.ds(at, reach), :] = x[pl.ds(0, reach), :]

    count = kernels.shape[0]
    for slot in range(kernels.shape[1]):
        weights[slot, :count, :] = kernels[:, slot, :]
        weights[slot, count:, :] = gains[slot : slot + 1, :]
    later[...] = weights[ahead_slots[1, section]]
    slot, length, first = back_slots[0, section], back_lengths[section], lax.axis_index("tm") * own
    notes[FIRST] = first
    notes[BACK0] = slot
    notes[BACK0 + 1] = length
    notes[BACK1] = back_slots[1, section]
    notes[BACK1 + 1] = back_lengths[lax.rem(section + 1, sections)]
    notes[AHEAD0] = ahead_slots[0, section]
    notes[AHEAD0 + 1] = ahead_lengths[section]
    norm_pieces([(saved.at[0], 0, own)], slot_row(weights, slot), first, length, masked, mean, inverse)

    def block(columns):
        q[:, columns] = tap_spectrum(q_table[...], weights[slot, :, columns])

    each_block(width, block)


def prepare_later_kernel(notes, saved, act, weights, q_table, *outs):
    own, width = act.shape
    for x, layer, (masked, mean, inverse, q) in ((saved.at[1], BACK1, outs[:4]), (act, AHEAD0, outs[4:])):
        slot, length, first = looked_up(notes, layer)
        norm_pieces([(x, 0, own)], slot_row(weights, slot), first, length, masked, mean, inverse)

        def block(columns, slot=slot, q=q):
            q[:, columns] = tap_spectrum(q_table[...], weights[slot, :, columns])

        each_block(width, block)


def norm_halo(left, right, own, gain, first, length, halo):
    reach = left.shape[0]
    norm_pieces([(left, 0, reach)], gain, first - reach, length, halo)
    norm_pieces([(right, 0, reach)], gain, first + own, length, halo.at[pl.ds(reach, reach)])


def joined(halo, own, columns):
    reach = halo.shape[0] // 2
    return jnp.concatenate([halo[:reach, columns], own[:, columns], halo[reach:, columns]], axis=0)


def first_backward_kernel(
    reaches, notes, saved, near, far, grads, weights, later, own_masked, own_mean, own_inverse, q,
    m_table, c_table, g_table, x_table,
    grad_x, halo, inner, gain_sum, halos, grad_halos, all_mean, all_inverse, scaled, sum_a, sum_b,
):
    own, width = grads.shape
    reach, grad_reach, out_reach = reaches
    slot, length, first = looked_up(notes, BACK0)
    gain = slot_row(weights, slot)
    left, right = sorted_halos(near, far, 0, halos)
    grad_left, grad_right = sorted_halos(near, far, reach, grad_halos)
    edge = reach - out_reach
    low, middle, high = pl.ds(0, out_reach), pl.ds(out_reach, own), pl.ds(out_reach + own, out_reach)
    bounds = ((left, first - reach, 0, edge, low), (right, first + own, reach, 0, high))
    for x, begin, at, skip, rows in bounds:
        norm_rows(x, 0, reach, 0, gain, begin, length, halo.at[pl.ds(at, reach)], sum_a, sum_b)
        all_mean[rows, :] = sum_a[pl.ds(skip, out_reach), :]
        all_inverse[rows, :] = sum_b[pl.ds(skip, out_reach), :]
    all_mean[middle, :] = own_mean[...]
    all_inverse[middle, :] = own_inverse[...]
    grad_pieces = [(grad_left, 0, grad_reach), (grads, 0, own), (grad_right, 0, grad_reach)]
    pieces = [(left, edge, out_reach), (saved.at[0], 0, own), (right, 0, out_reach)]
    out_pieces = [(grad_left, grad_reach - out_reach, out_reach), (grads, 0, own), (grad_right, 0, out_reach)]
    mask = frame_mask(own + 2 * out_reach, first - out_reach, length)
    sum_a[...] = jnp.zeros_like(sum_a)
    sum_b[...] = jnp.zeros_like(sum_b)
    grad_x[pl.ds(own + 2 * out_reach, later.shape[0]), :] = later[...]

    def block(columns):
        m = transform(m_table, joined(halo, own_masked, columns))
        conv = transform(c_table, product(m, q[:, columns]))
        mixed = (window(grad_pieces, columns).astype(F32) * gate_factor(conv)).astype(BF16)
        inner[:, columns] = mixed[grad_reach : grad_reach + own]
        weighted = first_pass(
            pieces, all_mean, all_inverse, gain, mask, (g_table, x_table), mixed, q[:, columns], columns,
            scaled, sum_a, sum_b,
        )
        gain_sum[:, columns] = jnp.sum(weighted[out_reach : out_reach + own], axis=0, keepdims=True)

    each_block(width, block)
    last_pass(out_pieces, pieces, all_mean, all_inverse, scaled, sum_a, sum_b, grad_x)


def tap_term(go_table, t_table, m, mixed):
    g_own = dot(go_table[...], jnp.concatenate([mixed, mixed], axis=0))
    return transform(t_table, product_conj(m, g_own))


def put_taps(taps, tap, gain_sum, columns):
    row = lax.broadcasted_iota(jnp.int32, tap.shape, 0)
    taps[:, columns] = jnp.where(row == tap.shape[0] - 1, gain_sum, tap).astype(taps.dtype)


def first_taps_kernel(reach, halo, masked, inner, gain_sum, m_table, go_table, t_table, taps):
    wide_reach = halo.shape[0] // 2
    own, width = masked.shape
    pieces = [(halo, wide_reach - reach, reach), (masked, 0, own), (halo, wide_reach, reach)]

    def block(columns):
        m = transform(m_table, window(pieces, columns))
        put_taps(taps, tap_term(go_table, t_table, m, inner[:, columns]), gain_sum[:, columns], columns)

    each_block(width, block)


def add_kernel(mine, other, out):
    out[...] = (mine[...].astype(F32) + other[...].astype(F32)).astype(out.dtype)


def second_ready_kernel(
    reach, notes, near, far, weights, masked, q, m_table, c_table, m_out, factor, conv_out, halo, halos
):
    own, width = masked.shape
    slot, length, first = looked_up(notes, BACK1)
    left, right = sorted_halos(near, far, 0, halos)
    norm_halo(left, right, own, slot_row(weights, slot), first, length, halo)

    def block(columns):
        m = transform(m_table, joined(halo, masked, columns))
        conv = transform(c_table, product(m, q[:, columns]))
        m_out[:, columns] = m
        factor[:, columns] = gate_factor(conv)
        edge = (conv.shape[0] - own) // 2
        conv_out[:, columns] = conv[edge : edge + own]

    each_block(width, block)


def second_taps_kernel(notes, received, weights, m, factor, conv, ready, go_table, t_table, mixed_out, taps):
    own, width = conv.shape
    rows = factor.shape[0]
    edge = (rows - own) // 2
    gain = slot_row(weights, notes[BACK1])

    def block(columns):
        mixed = (received[:rows, columns].astype(F32) * factor[:, columns]).astype(BF16)
        mixed_out[:, columns] = mixed
        inner = mixed[edge : edge + own]
        gain_sum = jnp.sum(inner.astype(F32) * conv[:, columns], axis=0, keepdims=True) / gain(columns)
        put_taps(taps, tap_term(go_table, t_table, m[:, columns], inner), gain_sum, columns)

    each_block(width, block)


def second_backward_kernel(
    notes, saved, received, weights, mixed, q, mean, inverse, g_table, x_table, grad_x, scaled, sum_a, sum_b
):
    own, width = grad_x.shape
    slot, length, first = looked_up(notes, BACK1)
    pieces = [(saved.at[1], 0, own)]
    edge = (mixed.shape[0] - own) // 2
    mask = frame_mask(own, first, length)
    sum_a[...] = jnp.zeros_like(sum_a)
    sum_b[...] = jnp.zeros_like(sum_b)

    def block(columns):
        first_pass(
            pieces, mean, inverse, slot_row(weights, slot), mask, (g_table, x_table), mixed[:, columns], q[:, columns],
            columns, scaled, sum_a, sum_b,
        )

    each_block(width, block)
    last_pass([(received, edge, own)], pieces, mean, inverse, scaled, sum_a, sum_b, grad_x)


def first_forward_kernel(reach, notes, act, near, far, weights, masked, q, m_table, c_table, out, halo, halos):
    own, width = act.shape
    middle = reach // 2
    slot, length, first = looked_up(notes, AHEAD0)
    left, right = sorted_halos(near, far, reach, halos)
    inner = [(left, middle, middle), (act, 0, own), (right, 0, middle)]
    norm_halo(left, right, own, slot_row(weights, slot), first, length, halo)

    def block(columns):
        conv = transform(c_table, product(transform(m_table, joined(halo, masked, columns)), q[:, columns]))
        out[:, columns] = (window(inner, columns).astype(F32) + conv * sigmoid(conv)).astype(BF16)

    each_block(width, block)


def second_forward_kernel(notes, between, received, m_table, q_table, c_table, out, masked):
    own, width = out.shape
    rows = between.shape[0]
    edge = (rows - own) // 2
    slot, length, first = looked_up(notes, AHEAD0)
    last = received.shape[0] - 1

    def gain(columns):
        return received[last : last + 1, columns].astype(F32)

    norm_pieces([(between, 0, rows)], gain, first - edge, length, masked)

    def block(columns):
        q = tap_spectrum(q_table[...], received[rows:, columns])
        conv = transform(c_table, product(transform(m_table, masked[:, columns]), q))
        out[:, columns] = (between[edge : edge + own, columns].astype(F32) + conv * sigmoid(conv)).astype(BF16)

    each_block(width, block)


def pack_kernel(reaches, saved, grad, near, far, ready, sems):
    own = grad.shape[1]
    even = lax.rem(lax.axis_index("tm") + 1, 2)
    copies = []
    at = 0
    for x, reach in zip((saved, grad), reaches):
        for out, tail in ((near, even), (far, 1 - even)):
            start = pl.multiple_of(tail * (own - reach), 16)
            copies.append(
                pltpu.make_async_copy(
                    x.at[0, pl.ds(start, reach)], out.at[pl.ds(at, reach)], sems.at[len(copies)]
                )
            )
        at += reach
    ready[...] = jnp.zeros_like(ready)
    for copy in copies:
        copy.start()
    for copy in copies:
        copy.wait()


def final_kernel(slots, mine0, other0, mine1, other1, act, grad, act_out, grad_out, taps, gains, sems):
    copies = [
        pltpu.make_async_copy(act, act_out, sems.at[0]),
        pltpu.make_async_copy(grad, grad_out, sems.at[1]),
    ]
    for copy in copies:
        copy.start()
    section = lax.axis_index("section")
    count = taps.shape[0]
    total0 = mine0[...].astype(F32) + other0[...].astype(F32)
    total1 = mine1[...].astype(F32) + other1[...].astype(F32)
    for slot in range(taps.shape[1]):
        use0 = (slots[0, section] == slot).astype(F32)
        use1 = (slots[1, section] == slot).astype(F32)
        total = use0 * total0 + use1 * total1
        taps[:, slot, :] = total[:count]
        gains[slot : slot + 1, :] = total[count:]
    for copy in copies:
        copy.wait()


def span(reach, own):
    return np.arange(-reach, own + reach)


VMEM = pl.BlockSpec(memory_space=pltpu.VMEM)
SMEM = pl.BlockSpec(memory_space=pltpu.SMEM)
ANY = pl.BlockSpec(memory_space=pl.ANY)
HBM = pl.BlockSpec(memory_space=pltpu.HBM)
LIMIT = 24 * 1024 * 1024
FULL = 127 * 512 * 1024


def call(kernel, outs, scratch, operands, micros, specs=None, out_specs=None, limit=LIMIT):
    if specs is None:
        specs = [SMEM if x.dtype == jnp.int32 else VMEM for x in operands]
    return pl.pallas_call(
        kernel,
        out_shape=outs,
        in_specs=specs,
        out_specs=jax.tree.map(lambda _: VMEM, outs) if out_specs is None else out_specs,
        scratch_shapes=scratch,
        compiler_params=pltpu.CompilerParams(vmem_limit_bytes=limit),
        cost_estimate=pl.CostEstimate(flops=int(micros * 1e9), bytes_accessed=0, transcendentals=0),
    )(*operands)


def like(rows, width, dtype):
    return jax.ShapeDtypeStruct((rows, width), dtype)


def up16(count):
    return -(-count // 16) * 16


def local(
    act_in, grad_in, saved_inputs, kernels, norm_gains,
    forward_lengths, backward_lengths, forward_slots, backward_slots,
):
    sections = lax.axis_size("section")
    shards = lax.axis_size("tm")
    act, grad, saved = act_in[0], grad_in[0], saved_inputs[0]
    own, width = act.shape
    tap_count = kernels.shape[2]
    half = (tap_count - 1) // 2
    one, two, three = up16(half), up16(2 * half), up16(3 * half)
    large, size, small = own + 2 * three, own + 2 * two, own + 2 * one

    def shifted(x, by):
        return lax.ppermute(x, "section", [(i, (i + by) % sections) for i in range(sections)])

    def swapped(near, far):
        results = []
        for x, begin in ((near, 0), (far, 1)):
            pairs = [(i, i + 1) for i in range(begin, shards - 1, 2)]
            results.append(lax.ppermute(x, "tm", pairs + [(b, a) for a, b in pairs]))
        return results

    near0, far0, ready = call(
        functools.partial(pack_kernel, (three, two)),
        (like(three + two, width, BF16), like(three + two, width, BF16), like(8, LANES, F32)),
        [pltpu.SemaphoreType.DMA((4,))],
        (saved, grad_in),
        0, [HBM] * 2, None, FULL,
    )
    near0, far0 = swapped(near0, far0)
    tap_back = np.concatenate([from_freq(size, np.arange(tap_count) - half), np.zeros((1, size))], axis=0)
    m_table = stacked(to_freq(size, span(two, own)))
    q_table = tap_freq(size, tap_count)
    c_table = stacked(from_freq(size, span(one, own)))
    go_table = beside(to_freq(size, np.arange(own)))
    t_table = stacked(tap_back)

    def run(kernel, outs, scratch, operands, micros=0):
        return call(kernel, outs, scratch, [jnp.asarray(x) for x in operands], micros)

    rows = [pltpu.VMEM((own, width), F32)] + [pltpu.VMEM((own, LANES), F32)] * 2
    forward_slots, backward_slots = forward_slots.T, backward_slots.T

    def layer(size):
        return like(own, width, BF16), like(own, LANES, F32), like(own, LANES, F32), like(size, width, F32)

    weights, later, near1, far1, notes, *layer0 = call(
        functools.partial(prepare_kernel, two),
        (
            jax.ShapeDtypeStruct((kernels.shape[1], tap_count + 1, width), BF16), like(tap_count + 1, width, BF16),
            like(2 * two, width, BF16), like(2 * two, width, BF16), jax.ShapeDtypeStruct((8,), jnp.int32), *layer(large),
        ),
        [],
        [
            backward_lengths, forward_lengths, backward_slots, forward_slots,
            kernels[0].transpose(1, 0, 2), norm_gains[0], saved, act, ready, jnp.asarray(tap_freq(large, tap_count)),
        ],
        0,
        None, (VMEM,) * 4 + (SMEM,) + (VMEM,) * 4,
    )
    near1, far1 = swapped(near1, far1)
    grad_mid, halo0, inner0, gain0 = run(
        functools.partial(first_backward_kernel, (three, two, one)),
        (
            like(small + tap_count + 1, width, BF16),
            like(2 * three, width, BF16), like(own, width, BF16), like(1, width, F32),
        ),
        [
            pltpu.VMEM((2, three, width), BF16), pltpu.VMEM((2, two, width), BF16),
            pltpu.VMEM((small, LANES), F32), pltpu.VMEM((small, LANES), F32),
            pltpu.VMEM((small, width), F32), pltpu.VMEM((small, LANES), F32), pltpu.VMEM((small, LANES), F32),
        ],
        [
            notes, saved, near0, far0, grad, weights, later, *layer0,
            stacked(to_freq(large, span(three, own))), stacked(from_freq(large, span(two, own))),
            stacked(to_freq(large, span(two, own))), stacked(from_freq(large, span(one, own))),
        ],
        4,
    )
    grad_mid = shifted(grad_mid, -1)
    layers = run(
        prepare_later_kernel, (*layer(size), *layer(size)), [], [notes, saved, act, weights, q_table], 0
    )
    masked1, mean1, inverse1, q1, masked2, _, _, q2 = layers
    taps0 = run(
        functools.partial(first_taps_kernel, two), like(tap_count + 1, width, BF16), [],
        [halo0, layer0[0], inner0, gain0, m_table, go_table, t_table],
        0,
    )
    halo_scratch = [pltpu.VMEM((2 * two, width), BF16), pltpu.VMEM((2, two, width), BF16)]
    between = run(
        functools.partial(first_forward_kernel, two),
        like(small, width, BF16),
        halo_scratch,
        [notes, act, near1, far1, weights, masked2, q2, m_table, c_table],
        5,
    )
    m1, factor1, conv1 = run(
        functools.partial(second_ready_kernel, two),
        (like(size, width, F32), like(small, width, F32), like(own, width, F32)),
        halo_scratch,
        [notes, near1, far1, weights, masked1, q1, m_table, c_table],
        1,
    )
    act_out = run(
        second_forward_kernel,
        like(own, width, BF16),
        [pltpu.VMEM((small, width), BF16)],
        [
            notes, between, grad_mid,
            stacked(to_freq(small, span(one, own))), tap_freq(small, tap_count), stacked(from_freq(small, span(0, own))),
        ],
        3,
    )
    act_out = shifted(act_out, 2)

    def summed(x, micros):
        step = 1
        while True:
            other = lax.ppermute(x, "tm", [(i, i ^ step) for i in range(shards)])
            step *= 2
            if step >= shards:
                return x, other
            x = call(add_kernel, like(*x.shape, BF16), [], (x, other), micros)

    mine0, other0 = summed(taps0, 0)
    mixed1, taps1 = run(
        second_taps_kernel,
        (like(small, width, BF16), like(tap_count + 1, width, BF16)),
        [],
        [notes, grad_mid, weights, m1, factor1, conv1, other0, go_table, t_table],
        2,
    )
    grad_out = run(
        second_backward_kernel,
        like(own, width, BF16),
        rows,
        [
            notes, saved, grad_mid, weights, mixed1, q1, mean1, inverse1,
            stacked(to_freq(size, span(one, own))), stacked(from_freq(size, span(0, own))),
        ],
        6,
    )
    grad_out = shifted(grad_out, -1)
    sums = (mine0, other0) + summed(taps1, 6)
    slots = kernels.shape[1]
    act_out, grad_out, taps, gains = call(
        final_kernel,
        (
            like(own, width, BF16), like(own, width, BF16),
            jax.ShapeDtypeStruct((tap_count, slots, width), F32), like(slots, width, F32),
        ),
        [pltpu.SemaphoreType.DMA((2,))],
        (backward_slots, *sums, act_out, grad_out),
        0, [SMEM] + [VMEM] * 4 + [ANY] * 2, (ANY, ANY, VMEM, VMEM),
    )
    return act_out[None], grad_out[None], taps.transpose(1, 0, 2)[None], gains[None]


def solution(mesh):
    in_specs = (
        P("section", "tm", None),
        P("section", "tm", None),
        P("section", None, "tm", None),
        P("section", None, None, None),
        P("section", None, None),
        P(),
        P(),
        P(),
        P(),
    )
    out_specs = (
        P("section", "tm", None),
        P("section", "tm", None),
        P("section", None, None, None),
        P("section", None, None),
    )
    return jax.shard_map(local, mesh=mesh, in_specs=in_specs, out_specs=out_specs, check_vma=False)
```

```python
import functools

import jax
import jax.numpy as jnp
import ml_dtypes
import numpy as np
from jax import lax
from jax.experimental import pallas as pl
from jax.experimental.pallas import tpu as pltpu
from jax.sharding import PartitionSpec as P

epsilon = 1e-05
BLOCK = 512
LANES = 128
F32 = jnp.float32
BF16 = jnp.bfloat16


def split(matrix):
    high = matrix.astype(ml_dtypes.bfloat16)
    low = (matrix - high.astype(np.float64)).astype(ml_dtypes.bfloat16)
    return high, low


def angles(size, times):
    return 2.0 * np.pi / size * np.outer(np.arange(size // 2) + 0.5, np.asarray(times, np.float64))


def to_freq(size, times):
    phase = angles(size, times)
    return np.concatenate([np.cos(phase), -np.sin(phase)], axis=0)


def from_freq(size, times):
    phase = angles(size, times).T
    return 2.0 / size * np.concatenate([np.cos(phase), -np.sin(phase)], axis=1)


def stacked(matrix):
    return np.concatenate(split(matrix), axis=0)


def beside(matrix):
    return np.concatenate(split(matrix), axis=1)


def tap_freq(size, taps):
    phase = angles(size, np.arange(taps) - (taps - 1) // 2)
    table = np.concatenate([np.cos(phase), np.sin(phase)], axis=0)
    return beside(np.concatenate([table, np.zeros((size, 1))], axis=1))


def dot(a, b):
    return jnp.dot(a, b, preferred_element_type=F32)


def transform(table, values):
    return sum(halves(dot(table[...], values.astype(BF16))))


def halves(values):
    half = values.shape[0] // 2
    return values[:half], values[half:]


def product(a, b):
    ar, ai = halves(a)
    br, bi = halves(b)
    return jnp.concatenate([ar * br - ai * bi, ar * bi + ai * br], axis=0)


def product_conj(a, b):
    ar, ai = halves(a)
    br, bi = halves(b)
    return jnp.concatenate([ar * br + ai * bi, ai * br - ar * bi], axis=0)


def sigmoid(values):
    return 0.5 * jnp.tanh(0.5 * values) + 0.5


def wide(stat, count):
    return jnp.concatenate([stat] * (count // LANES), axis=1)


def norm_rows(ref, start, count, at, gain, first, length, masked_ref, mean_ref, inverse_ref):
    width = masked_ref.shape[1]
    rows = pl.ds(start, count)
    tiles = [pl.ds(i * LANES, LANES) for i in range(width // LANES)]

    def values(tile):
        return ref[rows, tile].astype(F32)

    total = values(tiles[0])
    for tile in tiles[1:]:
        total = total + values(tile)
    mean = jnp.sum(total, axis=1, keepdims=True) * (1.0 / width)
    mean = jnp.broadcast_to(mean, (count, LANES))
    square = jnp.zeros((count, LANES), F32)
    for tile in tiles:
        center = values(tile) - mean
        square = square + center * center
    var = jnp.sum(square, axis=1, keepdims=True) * (1.0 / width)
    inverse = jnp.broadcast_to(lax.rsqrt(var + epsilon), (count, LANES))
    frame = first + at + lax.broadcasted_iota(jnp.int32, (count, LANES), 0)
    mask = ((frame >= 0) & (frame < length)).astype(F32)
    scale = mask * inverse
    out = pl.ds(at, count)
    for tile in tiles:
        masked_ref[out, tile] = ((values(tile) - mean) * scale * gain(tile)).astype(BF16)
    if mean_ref is not None:
        mean_ref[out, :] = mean
        inverse_ref[out, :] = inverse


def norm_pieces(pieces, gain, first, length, masked_ref, mean_ref=None, inverse_ref=None, chunk=128):
    at = 0
    for ref, start, count in pieces:
        for begin in range(0, count, chunk):
            norm_rows(
                ref, start + begin, min(chunk, count - begin), at + begin,
                gain, first, length, masked_ref, mean_ref, inverse_ref,
            )
        at += count


def window(pieces, columns):
    parts = [ref[pl.ds(start, count), columns] for ref, start, count in pieces]
    return parts[0] if len(parts) == 1 else jnp.concatenate(parts, axis=0)


def each_block(width, body):
    for begin in range(0, width, BLOCK):
        body(pl.ds(begin, BLOCK))


def tap_spectrum(table, weights):
    return dot(table, jnp.concatenate([weights, weights], axis=0))


def gate_factor(conv):
    gate = sigmoid(conv)
    return gate * (1.0 + conv * (1.0 - gate))


FIRST, BACK0, BACK1, AHEAD0 = range(0, 8, 2)


def looked_up(notes, layer):
    return notes[layer], notes[layer + 1], notes[FIRST]


def sorted_halos(near, far, at, halos):
    even = lax.rem(lax.axis_index("tm") + 1, 2)
    rows = pl.ds(at, halos.shape[1])
    halos[even] = near[rows, :]
    halos[1 - even] = far[rows, :]
    return halos.at[0], halos.at[1]


def lane_sum(values):
    total = values[:, :LANES]
    for lane in range(LANES, values.shape[1], LANES):
        total = total + values[:, lane : lane + LANES]
    return total


def first_pass(pieces, mean, inverse, gain, mask, tables, mixed, q, columns, scaled, sum_a, sum_b):
    g_table, x_table = tables
    grad_masked = wide(mask, BLOCK) * transform(x_table, product_conj(transform(g_table, mixed), q))
    centered = window(pieces, columns).astype(F32) - wide(mean[...], BLOCK)
    weighted = grad_masked * (centered * wide(inverse[...], BLOCK))
    gain = gain(columns)
    by_gain = grad_masked * gain
    scaled[:, columns] = by_gain
    sum_a[...] += lane_sum(by_gain)
    sum_b[...] += lane_sum(weighted * gain)
    return weighted


def last_pass(grad_pieces, pieces, mean, inverse, scaled, sum_a, sum_b, grad_x, chunk=128):
    width = scaled.shape[1]
    at = 0
    for (ref, start, count), (saved, base, _) in zip(grad_pieces, pieces):
        for begin in range(0, count, chunk):
            here = min(chunk, count - begin)
            rows = pl.ds(at + begin, here)
            inv = inverse[rows, :]
            mean_a = jnp.sum(sum_a[rows, :], axis=1, keepdims=True) * (1.0 / width)
            mean_b = jnp.sum(sum_b[rows, :], axis=1, keepdims=True) * (1.0 / width)
            slope = inv * jnp.broadcast_to(mean_b, (here, LANES)) * inv
            fixed = inv * jnp.broadcast_to(mean_a, (here, LANES)) - slope * mean[rows, :]
            for lane in range(0, width, LANES):
                tile = pl.ds(lane, LANES)
                x = saved[pl.ds(base + begin, here), tile].astype(F32)
                change = inv * scaled[rows, tile] - fixed - slope * x
                grad_x[rows, tile] = (ref[pl.ds(start + begin, here), tile].astype(F32) + change).astype(BF16)
        at += count


def frame_mask(rows, first, length):
    frame = first + lax.broadcasted_iota(jnp.int32, (rows, LANES), 0)
    return ((frame >= 0) & (frame < length)).astype(F32)


def slot_row(weights, slot):
    last = weights.shape[1] - 1
    return lambda columns: weights[slot, last : last + 1, columns].astype(F32)


def prepare_kernel(
    reach, back_lengths, ahead_lengths, back_slots, ahead_slots, kernels, gains, saved, act, ready, q_table,
    weights, later, near, far, notes, masked, mean, inverse, q,
):
    own, width = act.shape
    section, sections = lax.axis_index("section"), lax.axis_size("section")
    for even in range(2):

        @pl.when(lax.rem(lax.axis_index("tm") + 1, 2) == even)
        def _():
            for x, at in ((saved.at[1], 0), (act, reach)):
                tail, head = (near, far) if even else (far, near)
                tail[pl.ds(at, reach), :] = x[pl.ds(own - reach, reach), :]
                head[pl.ds(at, reach), :] = x[pl.ds(0, reach), :]

    count = kernels.shape[0]
    for slot in range(kernels.shape[1]):
        weights[slot, :count, :] = kernels[:, slot, :]
        weights[slot, count:, :] = gains[slot : slot + 1, :]
    later[...] = weights[ahead_slots[1, section]]
    slot, length, first = back_slots[0, section], back_lengths[section], lax.axis_index("tm") * own
    notes[FIRST] = first
    notes[BACK0] = slot
    notes[BACK0 + 1] = length
    notes[BACK1] = back_slots[1, section]
    notes[BACK1 + 1] = back_lengths[lax.rem(section + 1, sections)]
    notes[AHEAD0] = ahead_slots[0, section]
    notes[AHEAD0 + 1] = ahead_lengths[section]
    norm_pieces([(saved.at[0], 0, own)], slot_row(weights, slot), first, length, masked, mean, inverse)

    def block(columns):
        q[:, columns] = tap_spectrum(q_table[...], weights[slot, :, columns])

    each_block(width, block)


def prepare_later_kernel(notes, saved, act, weights, ready, q_table, *outs):
    own, width = act.shape
    layers = ((saved.at[1], BACK1, outs[:4]), (act, AHEAD0, outs[4:]))
    for x, layer, (masked, mean, inverse, _) in layers:
        slot, length, first = looked_up(notes, layer)
        norm_pieces([(x, 0, own)], slot_row(weights, slot), first, length, masked, mean, inverse)
    for _, layer, (_, _, _, q) in layers:
        slot = notes[layer]

        def block(columns, slot=slot, q=q):
            q[:, columns] = tap_spectrum(q_table[...], weights[slot, :, columns])

        each_block(width, block)


def norm_halo(left, right, own, gain, first, length, halo):
    reach = left.shape[0]
    norm_pieces([(left, 0, reach)], gain, first - reach, length, halo)
    norm_pieces([(right, 0, reach)], gain, first + own, length, halo.at[pl.ds(reach, reach)])


def joined(halo, own, columns):
    reach = halo.shape[0] // 2
    return jnp.concatenate([halo[:reach, columns], own[:, columns], halo[reach:, columns]], axis=0)


def first_backward_kernel(
    reaches, notes, saved, near, far, grads, weights, own_masked, own_mean, own_inverse, q,
    m_table, c_table, g_table, x_table,
    grad_x, halo, inner, gain_sum, halos, grad_halos, all_mean, all_inverse, scaled, sum_a, sum_b,
):
    own, width = grads.shape
    reach, grad_reach, out_reach = reaches
    slot, length, first = looked_up(notes, BACK0)
    gain = slot_row(weights, slot)
    left, right = sorted_halos(near, far, 0, halos)
    grad_left, grad_right = sorted_halos(near, far, reach, grad_halos)
    edge = reach - out_reach
    low, middle, high = pl.ds(0, out_reach), pl.ds(out_reach, own), pl.ds(out_reach + own, out_reach)
    bounds = ((left, first - reach, 0, edge, low), (right, first + own, reach, 0, high))
    for x, begin, at, skip, rows in bounds:
        norm_rows(x, 0, reach, 0, gain, begin, length, halo.at[pl.ds(at, reach)], sum_a, sum_b)
        all_mean[rows, :] = sum_a[pl.ds(skip, out_reach), :]
        all_inverse[rows, :] = sum_b[pl.ds(skip, out_reach), :]
    all_mean[middle, :] = own_mean[...]
    all_inverse[middle, :] = own_inverse[...]
    grad_pieces = [(grad_left, 0, grad_reach), (grads, 0, own), (grad_right, 0, grad_reach)]
    pieces = [(left, edge, out_reach), (saved.at[0], 0, own), (right, 0, out_reach)]
    out_pieces = [(grad_left, grad_reach - out_reach, out_reach), (grads, 0, own), (grad_right, 0, out_reach)]
    mask = frame_mask(own + 2 * out_reach, first - out_reach, length)
    sum_a[...] = jnp.zeros_like(sum_a)
    sum_b[...] = jnp.zeros_like(sum_b)

    def block(columns):
        m = transform(m_table, joined(halo, own_masked, columns))
        conv = transform(c_table, product(m, q[:, columns]))
        mixed = (window(grad_pieces, columns).astype(F32) * gate_factor(conv)).astype(BF16)
        inner[:, columns] = mixed[grad_reach : grad_reach + own]
        weighted = first_pass(
            pieces, all_mean, all_inverse, gain, mask, (g_table, x_table), mixed, q[:, columns], columns,
            scaled, sum_a, sum_b,
        )
        gain_sum[:, columns] = jnp.sum(weighted[out_reach : out_reach + own], axis=0, keepdims=True)

    each_block(width, block)
    last_pass(out_pieces, pieces, all_mean, all_inverse, scaled, sum_a, sum_b, grad_x)


def tap_term(go_table, t_table, m, mixed):
    g_own = dot(go_table[...], jnp.concatenate([mixed, mixed], axis=0))
    return transform(t_table, product_conj(m, g_own))


def put_taps(taps, tap, gain_sum, columns):
    row = lax.broadcasted_iota(jnp.int32, tap.shape, 0)
    taps[:, columns] = jnp.where(row == tap.shape[0] - 1, gain_sum, tap).astype(taps.dtype)


def first_taps_kernel(reach, halo, masked, inner, gain_sum, m_table, go_table, t_table, taps):
    wide_reach = halo.shape[0] // 2
    own, width = masked.shape
    pieces = [(halo, wide_reach - reach, reach), (masked, 0, own), (halo, wide_reach, reach)]

    def block(columns):
        m = transform(m_table, window(pieces, columns))
        put_taps(taps, tap_term(go_table, t_table, m, inner[:, columns]), gain_sum[:, columns], columns)

    each_block(width, block)


def add_kernel(mine, other, out):
    out[...] = (mine[...].astype(F32) + other[...].astype(F32)).astype(out.dtype)


def second_ready_kernel(
    reach, notes, near, far, weights, masked, q, m_table, c_table, m_out, factor, conv_out, halo, halos
):
    own, width = masked.shape
    slot, length, first = looked_up(notes, BACK1)
    left, right = sorted_halos(near, far, 0, halos)
    norm_halo(left, right, own, slot_row(weights, slot), first, length, halo)

    def block(columns):
        m = transform(m_table, joined(halo, masked, columns))
        conv = transform(c_table, product(m, q[:, columns]))
        m_out[:, columns] = m
        factor[:, columns] = gate_factor(conv)
        edge = (conv.shape[0] - own) // 2
        conv_out[:, columns] = conv[edge : edge + own]

    each_block(width, block)


def second_taps_kernel(notes, received, weights, m, factor, conv, taps0, go_table, t_table, mixed_out, taps):
    own, width = conv.shape
    rows = factor.shape[0]
    count = taps0.shape[0]
    taps[pl.ds(0, count), :] = taps0[...]
    taps1 = taps.at[pl.ds(count, count)]
    edge = (rows - own) // 2
    gain = slot_row(weights, notes[BACK1])

    def block(columns):
        mixed = (received[:rows, columns].astype(F32) * factor[:, columns]).astype(BF16)
        mixed_out[:, columns] = mixed
        inner = mixed[edge : edge + own]
        gain_sum = jnp.sum(inner.astype(F32) * conv[:, columns], axis=0, keepdims=True) / gain(columns)
        put_taps(taps1, tap_term(go_table, t_table, m[:, columns], inner), gain_sum, columns)

    each_block(width, block)


def second_backward_kernel(
    notes, saved, received, weights, mixed, q, mean, inverse, g_table, x_table, grad_x, scaled, sum_a, sum_b
):
    own, width = grad_x.shape
    slot, length, first = looked_up(notes, BACK1)
    pieces = [(saved.at[1], 0, own)]
    edge = (mixed.shape[0] - own) // 2
    mask = frame_mask(own, first, length)
    sum_a[...] = jnp.zeros_like(sum_a)
    sum_b[...] = jnp.zeros_like(sum_b)

    def block(columns):
        first_pass(
            pieces, mean, inverse, slot_row(weights, slot), mask, (g_table, x_table), mixed[:, columns], q[:, columns],
            columns, scaled, sum_a, sum_b,
        )

    each_block(width, block)
    last_pass([(received, edge, own)], pieces, mean, inverse, scaled, sum_a, sum_b, grad_x)


def first_forward_kernel(reach, notes, act, near, far, weights, masked, q, m_table, c_table, out, halo, halos):
    own, width = act.shape
    middle = reach // 2
    slot, length, first = looked_up(notes, AHEAD0)
    left, right = sorted_halos(near, far, reach, halos)
    inner = [(left, middle, middle), (act, 0, own), (right, 0, middle)]
    norm_halo(left, right, own, slot_row(weights, slot), first, length, halo)

    def block(columns):
        conv = transform(c_table, product(transform(m_table, joined(halo, masked, columns)), q[:, columns]))
        out[:, columns] = (window(inner, columns).astype(F32) + conv * sigmoid(conv)).astype(BF16)

    each_block(width, block)


def second_forward_kernel(notes, between, later, m_table, q_table, c_table, out, masked):
    own, width = out.shape
    rows = between.shape[0]
    edge = (rows - own) // 2
    slot, length, first = looked_up(notes, AHEAD0)
    last = later.shape[0] - 1

    def gain(columns):
        return later[last : last + 1, columns].astype(F32)

    norm_pieces([(between, 0, rows)], gain, first - edge, length, masked, chunk=rows // 2)

    def block(columns):
        q = tap_spectrum(q_table[...], later[:, columns])
        conv = transform(c_table, product(transform(m_table, masked[:, columns]), q))
        out[:, columns] = (between[edge : edge + own, columns].astype(F32) + conv * sigmoid(conv)).astype(BF16)

    each_block(width, block)


def pack_kernel(reaches, saved, grad, near, far, ready, sems):
    own = grad.shape[1]
    even = lax.rem(lax.axis_index("tm") + 1, 2)
    copies = []
    at = 0
    for x, reach in zip((saved, grad), reaches):
        for out, tail in ((near, even), (far, 1 - even)):
            start = pl.multiple_of(tail * (own - reach), 16)
            copies.append(
                pltpu.make_async_copy(
                    x.at[0, pl.ds(start, reach)], out.at[pl.ds(at, reach)], sems.at[len(copies)]
                )
            )
        at += reach
    ready[...] = jnp.zeros_like(ready)
    for copy in copies:
        copy.start()
    for copy in copies:
        copy.wait()


def final_kernel(slots, mine, other, act, act_out, taps, gains, sem):
    copy = pltpu.make_async_copy(act, act_out, sem)
    copy.start()
    section = lax.axis_index("section")
    count = taps.shape[0]
    total = mine[...].astype(F32) + other[...].astype(F32)
    ticks = total[: count + 1], total[count + 1 :]
    for slot in range(taps.shape[1]):
        use = [(slots[tick, section] == slot).astype(F32) for tick in range(2)]
        both = use[0] * ticks[0] + use[1] * ticks[1]
        taps[:, slot, :] = both[:count]
        gains[slot : slot + 1, :] = both[count:]
    copy.wait()


def span(reach, own):
    return np.arange(-reach, own + reach)


VMEM = pl.BlockSpec(memory_space=pltpu.VMEM)
SMEM = pl.BlockSpec(memory_space=pltpu.SMEM)
ANY = pl.BlockSpec(memory_space=pl.ANY)
HBM = pl.BlockSpec(memory_space=pltpu.HBM)
LIMIT = 24 * 1024 * 1024
FULL = 127 * 512 * 1024


def call(kernel, outs, scratch, operands, micros, specs=None, out_specs=None, limit=LIMIT):
    if specs is None:
        specs = [SMEM if x.dtype == jnp.int32 else VMEM for x in operands]
    return pl.pallas_call(
        kernel,
        out_shape=outs,
        in_specs=specs,
        out_specs=jax.tree.map(lambda _: VMEM, outs) if out_specs is None else out_specs,
        scratch_shapes=scratch,
        compiler_params=pltpu.CompilerParams(vmem_limit_bytes=limit),
        cost_estimate=pl.CostEstimate(flops=int(micros * 1e9), bytes_accessed=0, transcendentals=0),
    )(*operands)


def like(rows, width, dtype):
    return jax.ShapeDtypeStruct((rows, width), dtype)


def up16(count):
    return -(-count // 16) * 16


def local(
    act_in, grad_in, saved_inputs, kernels, norm_gains,
    forward_lengths, backward_lengths, forward_slots, backward_slots,
):
    sections = lax.axis_size("section")
    shards = lax.axis_size("tm")
    act, grad, saved = act_in[0], grad_in[0], saved_inputs[0]
    own, width = act.shape
    tap_count = kernels.shape[2]
    half = (tap_count - 1) // 2
    one, two, three = up16(half), up16(2 * half), up16(3 * half)
    large, size, small = own + 2 * three, own + 2 * two, own + 2 * one

    def shifted(x, by):
        return lax.ppermute(x, "section", [(i, (i + by) % sections) for i in range(sections)])

    def swapped(near, far):
        results = []
        for x, begin in ((near, 0), (far, 1)):
            pairs = [(i, i + 1) for i in range(begin, shards - 1, 2)]
            results.append(lax.ppermute(x, "tm", pairs + [(b, a) for a, b in pairs]))
        return results

    near0, far0, ready = call(
        functools.partial(pack_kernel, (three, two)),
        (like(three + two, width, BF16), like(three + two, width, BF16), like(8, LANES, F32)),
        [pltpu.SemaphoreType.DMA((4,))],
        (saved, grad_in),
        0, [HBM] * 2, None, FULL,
    )
    near0, far0 = swapped(near0, far0)
    tap_back = np.concatenate([from_freq(size, np.arange(tap_count) - half), np.zeros((1, size))], axis=0)
    m_table = stacked(to_freq(size, span(two, own)))
    q_table = tap_freq(size, tap_count)
    c_table = stacked(from_freq(size, span(one, own)))
    go_table = beside(to_freq(size, np.arange(own)))
    t_table = stacked(tap_back)

    def run(kernel, outs, scratch, operands, micros=0):
        return call(kernel, outs, scratch, [jnp.asarray(x) for x in operands], micros)

    rows = [pltpu.VMEM((own, width), F32)] + [pltpu.VMEM((own, LANES), F32)] * 2
    forward_slots, backward_slots = forward_slots.T, backward_slots.T

    def layer(size):
        return like(own, width, BF16), like(own, LANES, F32), like(own, LANES, F32), like(size, width, F32)

    weights, later, near1, far1, notes, *layer0 = call(
        functools.partial(prepare_kernel, two),
        (
            jax.ShapeDtypeStruct((kernels.shape[1], tap_count + 1, width), BF16), like(tap_count + 1, width, BF16),
            like(2 * two, width, BF16), like(2 * two, width, BF16), jax.ShapeDtypeStruct((8,), jnp.int32), *layer(large),
        ),
        [],
        [
            backward_lengths, forward_lengths, backward_slots, forward_slots,
            kernels[0].transpose(1, 0, 2), norm_gains[0], saved, act, ready, jnp.asarray(tap_freq(large, tap_count)),
        ],
        0,
        None, (VMEM,) * 4 + (SMEM,) + (VMEM,) * 4,
    )
    later = shifted(later, -1)
    near1, far1 = swapped(near1, far1)
    grad_mid, halo0, inner0, gain0 = run(
        functools.partial(first_backward_kernel, (three, two, one)),
        (
            like(small, width, BF16),
            like(2 * three, width, BF16), like(own, width, BF16), like(1, width, F32),
        ),
        [
            pltpu.VMEM((2, three, width), BF16), pltpu.VMEM((2, two, width), BF16),
            pltpu.VMEM((small, LANES), F32), pltpu.VMEM((small, LANES), F32),
            pltpu.VMEM((small, width), F32), pltpu.VMEM((small, LANES), F32), pltpu.VMEM((small, LANES), F32),
        ],
        [
            notes, saved, near0, far0, grad, weights, *layer0,
            stacked(to_freq(large, span(three, own))), stacked(from_freq(large, span(two, own))),
            stacked(to_freq(large, span(two, own))), stacked(from_freq(large, span(one, own))),
        ],
        4,
    )
    grad_mid = shifted(grad_mid, -1)
    layers = run(
        prepare_later_kernel, (*layer(size), *layer(size)), [], [notes, saved, act, weights, gain0, q_table], 0
    )
    masked1, mean1, inverse1, q1, masked2, _, _, q2 = layers
    taps0 = run(
        functools.partial(first_taps_kernel, two), like(tap_count + 1, width, BF16), [],
        [halo0, layer0[0], inner0, gain0, m_table, go_table, t_table],
        0,
    )
    halo_scratch = [pltpu.VMEM((2 * two, width), BF16), pltpu.VMEM((2, two, width), BF16)]
    between = run(
        functools.partial(first_forward_kernel, two),
        like(small, width, BF16),
        halo_scratch,
        [notes, act, near1, far1, weights, masked2, q2, m_table, c_table],
        3,
    )
    m1, factor1, conv1 = run(
        functools.partial(second_ready_kernel, two),
        (like(size, width, F32), like(small, width, F32), like(own, width, F32)),
        halo_scratch,
        [notes, near1, far1, weights, masked1, q1, m_table, c_table],
        3,
    )
    act_out = run(
        second_forward_kernel,
        like(own, width, BF16),
        [pltpu.VMEM((small, width), BF16)],
        [
            notes, between, later,
            stacked(to_freq(small, span(one, own))), tap_freq(small, tap_count), stacked(from_freq(small, span(0, own))),
        ],
        3,
    )
    act_out = shifted(act_out, 2)

    def summed(x, micros):
        step = 1
        while True:
            other = lax.ppermute(x, "tm", [(i, i ^ step) for i in range(shards)])
            step *= 2
            if step >= shards:
                return x, other
            x = call(add_kernel, like(*x.shape, BF16), [], (x, other), micros)

    mixed1, sums = run(
        second_taps_kernel,
        (like(small, width, BF16), like(2 * (tap_count + 1), width, BF16)),
        [],
        [notes, grad_mid, weights, m1, factor1, conv1, taps0, go_table, t_table],
        2,
    )
    grad_out = run(
        second_backward_kernel,
        like(own, width, BF16),
        rows,
        [
            notes, saved, grad_mid, weights, mixed1, q1, mean1, inverse1,
            stacked(to_freq(size, span(one, own))), stacked(from_freq(size, span(0, own))),
        ],
        6,
    )
    grad_out = shifted(grad_out, -1)
    sums = summed(sums, 6)
    slots = kernels.shape[1]
    act_out, taps, gains = call(
        final_kernel,
        (
            like(own, width, BF16),
            jax.ShapeDtypeStruct((tap_count, slots, width), F32), like(slots, width, F32),
        ),
        [pltpu.SemaphoreType.DMA],
        (backward_slots, *sums, act_out),
        0, [SMEM] + [VMEM] * 2 + [ANY], (ANY, VMEM, VMEM),
    )
    return act_out[None], grad_out[None], taps.transpose(1, 0, 2)[None], gains[None]


def solution(mesh):
    in_specs = (
        P("section", "tm", None),
        P("section", "tm", None),
        P("section", None, "tm", None),
        P("section", None, None, None),
        P("section", None, None),
        P(),
        P(),
        P(),
        P(),
    )
    out_specs = (
        P("section", "tm", None),
        P("section", "tm", None),
        P("section", None, None, None),
        P("section", None, None),
    )
    return jax.shard_map(local, mesh=mesh, in_specs=in_specs, out_specs=out_specs, check_vma=False)
```

```python
import functools

import jax
import jax.numpy as jnp
import ml_dtypes
import numpy as np
from jax import lax
from jax.experimental import pallas as pl
from jax.experimental.pallas import tpu as pltpu
from jax.sharding import PartitionSpec as P

epsilon = 1e-05
BLOCK = 256
LANES = 128
F32 = jnp.float32
BF16 = jnp.bfloat16


def split(matrix):
    high = matrix.astype(ml_dtypes.bfloat16)
    low = (matrix - high.astype(np.float64)).astype(ml_dtypes.bfloat16)
    return high, low


def angles(size, times):
    return 2.0 * np.pi / size * np.outer(np.arange(size // 2) + 0.5, np.asarray(times, np.float64))


def to_freq(size, times):
    phase = angles(size, times)
    return np.concatenate([np.cos(phase), -np.sin(phase)], axis=0)


def from_freq(size, times):
    phase = angles(size, times).T
    return 2.0 / size * np.concatenate([np.cos(phase), -np.sin(phase)], axis=1)


def stacked(matrix):
    return np.concatenate(split(matrix), axis=0)


def beside(matrix):
    return np.concatenate(split(matrix), axis=1)


def tap_freq(size, taps):
    phase = angles(size, np.arange(taps) - (taps - 1) // 2)
    table = np.concatenate([np.cos(phase), np.sin(phase)], axis=0)
    return beside(np.concatenate([table, np.zeros((size, 1))], axis=1))


def dot(a, b):
    return jnp.dot(a, b, preferred_element_type=F32)


def transform(table, values):
    return sum(halves(dot(table[...], values.astype(BF16))))


def halves(values):
    half = values.shape[0] // 2
    return values[:half], values[half:]


def product(a, b):
    ar, ai = halves(a)
    br, bi = halves(b)
    return jnp.concatenate([ar * br - ai * bi, ar * bi + ai * br], axis=0)


def product_conj(a, b):
    ar, ai = halves(a)
    br, bi = halves(b)
    return jnp.concatenate([ar * br + ai * bi, ai * br - ar * bi], axis=0)


def sigmoid(values):
    return 0.5 * jnp.tanh(0.5 * values) + 0.5


def wide(stat, count):
    return jnp.concatenate([stat] * (count // LANES), axis=1)


def norm_rows(ref, start, count, at, gain, first, length, masked_ref, mean_ref, inverse_ref):
    width = masked_ref.shape[1]
    rows = pl.ds(start, count)
    tiles = [pl.ds(i * LANES, LANES) for i in range(width // LANES)]

    def values(tile):
        return ref[rows, tile].astype(F32)

    total = values(tiles[0])
    for tile in tiles[1:]:
        total = total + values(tile)
    mean = jnp.sum(total, axis=1, keepdims=True) * (1.0 / width)
    mean = jnp.broadcast_to(mean, (count, LANES))
    square = jnp.zeros((count, LANES), F32)
    for tile in tiles:
        center = values(tile) - mean
        square = square + center * center
    var = jnp.sum(square, axis=1, keepdims=True) * (1.0 / width)
    inverse = jnp.broadcast_to(lax.rsqrt(var + epsilon), (count, LANES))
    frame = first + at + lax.broadcasted_iota(jnp.int32, (count, LANES), 0)
    mask = ((frame >= 0) & (frame < length)).astype(F32)
    scale = mask * inverse
    out = pl.ds(at, count)
    for tile in tiles:
        masked_ref[out, tile] = ((values(tile) - mean) * scale * gain(tile)).astype(BF16)
    if mean_ref is not None:
        mean_ref[out, :] = mean
        inverse_ref[out, :] = inverse


def norm_pieces(pieces, gain, first, length, masked_ref, mean_ref=None, inverse_ref=None, chunk=128):
    at = 0
    for ref, start, count in pieces:
        for begin in range(0, count, chunk):
            norm_rows(
                ref, start + begin, min(chunk, count - begin), at + begin,
                gain, first, length, masked_ref, mean_ref, inverse_ref,
            )
        at += count


def window(pieces, columns):
    parts = [ref[pl.ds(start, count), columns] for ref, start, count in pieces]
    return parts[0] if len(parts) == 1 else jnp.concatenate(parts, axis=0)


def each_block(width, body):
    for begin in range(0, width, BLOCK):
        body(pl.ds(begin, BLOCK))


def tap_spectrum(table, weights):
    return dot(table, jnp.concatenate([weights, weights], axis=0))


def gate_factor(conv):
    gate = sigmoid(conv)
    return gate * (1.0 + conv * (1.0 - gate))


FIRST, BACK0, BACK1, AHEAD0 = range(0, 8, 2)


def looked_up(notes, layer):
    return notes[layer], notes[layer + 1], notes[FIRST]


def sorted_halos(near, far, at, halos):
    even = lax.rem(lax.axis_index("tm") + 1, 2)
    rows = pl.ds(at, halos.shape[1])
    halos[even] = near[rows, :]
    halos[1 - even] = far[rows, :]
    return halos.at[0], halos.at[1]


def lane_sum(values):
    total = values[:, :LANES]
    for lane in range(LANES, values.shape[1], LANES):
        total = total + values[:, lane : lane + LANES]
    return total


def first_pass(pieces, mean, inverse, gain, mask, tables, mixed, q, columns, scaled, sum_a, sum_b):
    g_table, x_table = tables
    grad_masked = wide(mask, BLOCK) * transform(x_table, product_conj(transform(g_table, mixed), q))
    centered = window(pieces, columns).astype(F32) - wide(mean[...], BLOCK)
    weighted = grad_masked * (centered * wide(inverse[...], BLOCK))
    gain = gain(columns)
    by_gain = grad_masked * gain
    scaled[:, columns] = by_gain
    sum_a[...] += lane_sum(by_gain)
    sum_b[...] += lane_sum(weighted * gain)
    return weighted


def last_pass(grad_pieces, pieces, mean, inverse, scaled, sum_a, sum_b, grad_x, chunk=128):
    width = scaled.shape[1]
    at = 0
    for (ref, start, count), (saved, base, _) in zip(grad_pieces, pieces):
        for begin in range(0, count, chunk):
            here = min(chunk, count - begin)
            rows = pl.ds(at + begin, here)
            inv = inverse[rows, :]
            mean_a = jnp.sum(sum_a[rows, :], axis=1, keepdims=True) * (1.0 / width)
            mean_b = jnp.sum(sum_b[rows, :], axis=1, keepdims=True) * (1.0 / width)
            slope = inv * jnp.broadcast_to(mean_b, (here, LANES)) * inv
            fixed = inv * jnp.broadcast_to(mean_a, (here, LANES)) - slope * mean[rows, :]
            for lane in range(0, width, LANES):
                tile = pl.ds(lane, LANES)
                x = saved[pl.ds(base + begin, here), tile].astype(F32)
                change = inv * scaled[rows, tile] - fixed - slope * x
                grad_x[rows, tile] = (ref[pl.ds(start + begin, here), tile].astype(F32) + change).astype(BF16)
        at += count


def frame_mask(rows, first, length):
    frame = first + lax.broadcasted_iota(jnp.int32, (rows, LANES), 0)
    return ((frame >= 0) & (frame < length)).astype(F32)


def slot_row(weights, slot):
    last = weights.shape[1] - 1
    return lambda columns: weights[slot, last : last + 1, columns].astype(F32)


def prepare_kernel(
    reach, back_lengths, ahead_lengths, back_slots, ahead_slots, kernels, gains, saved, act, ready, q_table,
    weights, later, near, far, notes, masked, mean, inverse, q,
):
    own, width = act.shape
    section, sections = lax.axis_index("section"), lax.axis_size("section")
    for even in range(2):

        @pl.when(lax.rem(lax.axis_index("tm") + 1, 2) == even)
        def _():
            for x, at in ((saved.at[1], 0), (act, reach)):
                tail, head = (near, far) if even else (far, near)
                tail[pl.ds(at, reach), :] = x[pl.ds(own - reach, reach), :]
                head[pl.ds(at, reach), :] = x[pl.ds(0, reach), :]

    count = kernels.shape[0]
    for slot in range(kernels.shape[1]):
        weights[slot, :count, :] = kernels[:, slot, :]
        weights[slot, count:, :] = gains[slot : slot + 1, :]
    later[...] = weights[ahead_slots[1, section]]
    slot, length, first = back_slots[0, section], back_lengths[section], lax.axis_index("tm") * own
    notes[FIRST] = first
    notes[BACK0] = slot
    notes[BACK0 + 1] = length
    notes[BACK1] = back_slots[1, section]
    notes[BACK1 + 1] = back_lengths[lax.rem(section + 1, sections)]
    notes[AHEAD0] = ahead_slots[0, section]
    notes[AHEAD0 + 1] = ahead_lengths[section]
    norm_pieces([(saved.at[0], 0, own)], slot_row(weights, slot), first, length, masked, mean, inverse)

    def block(columns):
        q[:, columns] = tap_spectrum(q_table[...], weights[slot, :, columns])

    each_block(width, block)


def prepare_later_kernel(notes, saved, act, weights, ready, q_table, *outs):
    own, width = act.shape
    layers = ((saved.at[1], BACK1, outs[:4]), (act, AHEAD0, outs[4:]))
    for x, layer, (masked, mean, inverse, _) in layers:
        slot, length, first = looked_up(notes, layer)
        norm_pieces([(x, 0, own)], slot_row(weights, slot), first, length, masked, mean, inverse)
    for _, layer, (_, _, _, q) in layers:
        slot = notes[layer]

        def block(columns, slot=slot, q=q):
            q[:, columns] = tap_spectrum(q_table[...], weights[slot, :, columns])

        each_block(width, block)


def norm_halo(left, right, own, gain, first, length, halo):
    reach = left.shape[0]
    norm_pieces([(left, 0, reach)], gain, first - reach, length, halo)
    norm_pieces([(right, 0, reach)], gain, first + own, length, halo.at[pl.ds(reach, reach)])


def joined(halo, own, columns):
    reach = halo.shape[0] // 2
    return jnp.concatenate([halo[:reach, columns], own[:, columns], halo[reach:, columns]], axis=0)


def first_backward_kernel(
    reaches, notes, saved, near, far, grads, weights, own_masked, own_mean, own_inverse, q,
    m_table, c_table, g_table, x_table,
    grad_x, halo, inner, gain_sum, halos, grad_halos, all_mean, all_inverse, scaled, sum_a, sum_b,
):
    own, width = grads.shape
    reach, grad_reach, out_reach = reaches
    slot, length, first = looked_up(notes, BACK0)
    gain = slot_row(weights, slot)
    left, right = sorted_halos(near, far, 0, halos)
    grad_left, grad_right = sorted_halos(near, far, reach, grad_halos)
    edge = reach - out_reach
    low, middle, high = pl.ds(0, out_reach), pl.ds(out_reach, own), pl.ds(out_reach + own, out_reach)
    bounds = ((left, first - reach, 0, edge, low), (right, first + own, reach, 0, high))
    for x, begin, at, skip, rows in bounds:
        norm_rows(x, 0, reach, 0, gain, begin, length, halo.at[pl.ds(at, reach)], sum_a, sum_b)
        all_mean[rows, :] = sum_a[pl.ds(skip, out_reach), :]
        all_inverse[rows, :] = sum_b[pl.ds(skip, out_reach), :]
    all_mean[middle, :] = own_mean[...]
    all_inverse[middle, :] = own_inverse[...]
    grad_pieces = [(grad_left, 0, grad_reach), (grads, 0, own), (grad_right, 0, grad_reach)]
    pieces = [(left, edge, out_reach), (saved.at[0], 0, own), (right, 0, out_reach)]
    out_pieces = [(grad_left, grad_reach - out_reach, out_reach), (grads, 0, own), (grad_right, 0, out_reach)]
    mask = frame_mask(own + 2 * out_reach, first - out_reach, length)
    sum_a[...] = jnp.zeros_like(sum_a)
    sum_b[...] = jnp.zeros_like(sum_b)

    def block(columns):
        m = transform(m_table, joined(halo, own_masked, columns))
        conv = transform(c_table, product(m, q[:, columns]))
        mixed = (window(grad_pieces, columns).astype(F32) * gate_factor(conv)).astype(BF16)
        inner[:, columns] = mixed[grad_reach : grad_reach + own]
        weighted = first_pass(
            pieces, all_mean, all_inverse, gain, mask, (g_table, x_table), mixed, q[:, columns], columns,
            scaled, sum_a, sum_b,
        )
        gain_sum[:, columns] = jnp.sum(weighted[out_reach : out_reach + own], axis=0, keepdims=True)

    each_block(width, block)
    last_pass(out_pieces, pieces, all_mean, all_inverse, scaled, sum_a, sum_b, grad_x)


def tap_term(go_table, t_table, m, mixed):
    g_own = dot(go_table[...], jnp.concatenate([mixed, mixed], axis=0))
    return transform(t_table, product_conj(m, g_own))


def put_taps(taps, tap, gain_sum, columns):
    row = lax.broadcasted_iota(jnp.int32, tap.shape, 0)
    taps[:, columns] = jnp.where(row == tap.shape[0] - 1, gain_sum, tap).astype(taps.dtype)


def first_taps_kernel(reach, halo, masked, inner, gain_sum, m_table, go_table, t_table, taps):
    wide_reach = halo.shape[0] // 2
    own, width = masked.shape
    pieces = [(halo, wide_reach - reach, reach), (masked, 0, own), (halo, wide_reach, reach)]

    def block(columns):
        m = transform(m_table, window(pieces, columns))
        put_taps(taps, tap_term(go_table, t_table, m, inner[:, columns]), gain_sum[:, columns], columns)

    each_block(width, block)


def add_kernel(mine, other, out):
    out[...] = (mine[...].astype(F32) + other[...].astype(F32)).astype(out.dtype)


def second_ready_kernel(
    reach, notes, near, far, weights, masked, q, m_table, c_table, m_out, factor, conv_out, halo, halos
):
    own, width = masked.shape
    slot, length, first = looked_up(notes, BACK1)
    left, right = sorted_halos(near, far, 0, halos)
    norm_halo(left, right, own, slot_row(weights, slot), first, length, halo)

    def block(columns):
        m = transform(m_table, joined(halo, masked, columns))
        conv = transform(c_table, product(m, q[:, columns]))
        m_out[:, columns] = m
        factor[:, columns] = gate_factor(conv)
        edge = (conv.shape[0] - own) // 2
        conv_out[:, columns] = conv[edge : edge + own]

    each_block(width, block)


def second_taps_kernel(notes, received, weights, m, factor, conv, taps0, go_table, t_table, mixed_out, taps):
    own, width = conv.shape
    rows = factor.shape[0]
    count = taps0.shape[0]
    taps[pl.ds(0, count), :] = taps0[...]
    taps1 = taps.at[pl.ds(count, count)]
    edge = (rows - own) // 2
    gain = slot_row(weights, notes[BACK1])

    def block(columns):
        mixed = (received[:rows, columns].astype(F32) * factor[:, columns]).astype(BF16)
        mixed_out[:, columns] = mixed
        inner = mixed[edge : edge + own]
        gain_sum = jnp.sum(inner.astype(F32) * conv[:, columns], axis=0, keepdims=True) / gain(columns)
        put_taps(taps1, tap_term(go_table, t_table, m[:, columns], inner), gain_sum, columns)

    each_block(width, block)


def second_backward_kernel(
    notes, saved, received, weights, mixed, q, mean, inverse, g_table, x_table, grad_x, scaled, sum_a, sum_b
):
    own, width = grad_x.shape
    slot, length, first = looked_up(notes, BACK1)
    pieces = [(saved.at[1], 0, own)]
    edge = (mixed.shape[0] - own) // 2
    mask = frame_mask(own, first, length)
    sum_a[...] = jnp.zeros_like(sum_a)
    sum_b[...] = jnp.zeros_like(sum_b)

    def block(columns):
        first_pass(
            pieces, mean, inverse, slot_row(weights, slot), mask, (g_table, x_table), mixed[:, columns], q[:, columns],
            columns, scaled, sum_a, sum_b,
        )

    each_block(width, block)
    last_pass([(received, edge, own)], pieces, mean, inverse, scaled, sum_a, sum_b, grad_x)


def first_forward_kernel(reach, notes, act, near, far, weights, masked, q, m_table, c_table, out, halo, halos):
    own, width = act.shape
    middle = reach // 2
    slot, length, first = looked_up(notes, AHEAD0)
    left, right = sorted_halos(near, far, reach, halos)
    inner = [(left, middle, middle), (act, 0, own), (right, 0, middle)]
    norm_halo(left, right, own, slot_row(weights, slot), first, length, halo)

    def block(columns):
        conv = transform(c_table, product(transform(m_table, joined(halo, masked, columns)), q[:, columns]))
        out[:, columns] = (window(inner, columns).astype(F32) + conv * sigmoid(conv)).astype(BF16)

    each_block(width, block)


def second_forward_kernel(notes, between, later, m_table, q_table, c_table, out, masked):
    own, width = out.shape
    rows = between.shape[0]
    edge = (rows - own) // 2
    slot, length, first = looked_up(notes, AHEAD0)
    last = later.shape[0] - 1

    def gain(columns):
        return later[last : last + 1, columns].astype(F32)

    norm_pieces([(between, 0, rows)], gain, first - edge, length, masked, chunk=rows // 2)

    def block(columns):
        q = tap_spectrum(q_table[...], later[:, columns])
        conv = transform(c_table, product(transform(m_table, masked[:, columns]), q))
        out[:, columns] = (between[edge : edge + own, columns].astype(F32) + conv * sigmoid(conv)).astype(BF16)

    each_block(width, block)


def pack_kernel(reaches, saved, grad, near, far, ready, sems):
    own = grad.shape[1]
    even = lax.rem(lax.axis_index("tm") + 1, 2)
    copies = []
    at = 0
    for x, reach in zip((saved, grad), reaches):
        for out, tail in ((near, even), (far, 1 - even)):
            start = pl.multiple_of(tail * (own - reach), 16)
            copies.append(
                pltpu.make_async_copy(
                    x.at[0, pl.ds(start, reach)], out.at[pl.ds(at, reach)], sems.at[len(copies)]
                )
            )
        at += reach
    ready[...] = jnp.zeros_like(ready)
    for copy in copies:
        copy.start()
    for copy in copies:
        copy.wait()


def final_kernel(slots, mine, other, act, grad, act_out, grad_out, taps, gains, sems):
    copies = [
        pltpu.make_async_copy(act, act_out, sems.at[0]),
        pltpu.make_async_copy(grad, grad_out, sems.at[1]),
    ]
    for copy in copies:
        copy.start()
    section = lax.axis_index("section")
    count = taps.shape[0]
    total = mine[...].astype(F32) + other[...].astype(F32)
    ticks = total[: count + 1], total[count + 1 :]
    for slot in range(taps.shape[1]):
        use = [(slots[tick, section] == slot).astype(F32) for tick in range(2)]
        both = use[0] * ticks[0] + use[1] * ticks[1]
        taps[:, slot, :] = both[:count]
        gains[slot : slot + 1, :] = both[count:]
    for copy in copies:
        copy.wait()


def span(reach, own):
    return np.arange(-reach, own + reach)


VMEM = pl.BlockSpec(memory_space=pltpu.VMEM)
SMEM = pl.BlockSpec(memory_space=pltpu.SMEM)
ANY = pl.BlockSpec(memory_space=pl.ANY)
HBM = pl.BlockSpec(memory_space=pltpu.HBM)
LIMIT = 24 * 1024 * 1024
FULL = 127 * 512 * 1024


def call(kernel, outs, scratch, operands, micros, specs=None, out_specs=None, limit=LIMIT):
    if specs is None:
        specs = [SMEM if x.dtype == jnp.int32 else VMEM for x in operands]
    return pl.pallas_call(
        kernel,
        out_shape=outs,
        in_specs=specs,
        out_specs=jax.tree.map(lambda _: VMEM, outs) if out_specs is None else out_specs,
        scratch_shapes=scratch,
        compiler_params=pltpu.CompilerParams(vmem_limit_bytes=limit),
        cost_estimate=pl.CostEstimate(flops=int(micros * 1e9), bytes_accessed=0, transcendentals=0),
    )(*operands)


def like(rows, width, dtype):
    return jax.ShapeDtypeStruct((rows, width), dtype)


def up16(count):
    return -(-count // 16) * 16


def local(
    act_in, grad_in, saved_inputs, kernels, norm_gains,
    forward_lengths, backward_lengths, forward_slots, backward_slots,
):
    sections = lax.axis_size("section")
    shards = lax.axis_size("tm")
    act, grad, saved = act_in[0], grad_in[0], saved_inputs[0]
    own, width = act.shape
    tap_count = kernels.shape[2]
    half = (tap_count - 1) // 2
    one, two, three = up16(half), up16(2 * half), up16(3 * half)
    large, size, small = own + 2 * three, own + 2 * two, own + 2 * one

    def shifted(x, by):
        return lax.ppermute(x, "section", [(i, (i + by) % sections) for i in range(sections)])

    def swapped(near, far):
        results = []
        for x, begin in ((near, 0), (far, 1)):
            pairs = [(i, i + 1) for i in range(begin, shards - 1, 2)]
            results.append(lax.ppermute(x, "tm", pairs + [(b, a) for a, b in pairs]))
        return results

    near0, far0, ready = call(
        functools.partial(pack_kernel, (three, two)),
        (like(three + two, width, BF16), like(three + two, width, BF16), like(8, LANES, F32)),
        [pltpu.SemaphoreType.DMA((4,))],
        (saved, grad_in),
        0, [HBM] * 2, None, FULL,
    )
    near0, far0 = swapped(near0, far0)
    tap_back = np.concatenate([from_freq(size, np.arange(tap_count) - half), np.zeros((1, size))], axis=0)
    m_table = stacked(to_freq(size, span(two, own)))
    q_table = tap_freq(size, tap_count)
    c_table = stacked(from_freq(size, span(one, own)))
    go_table = beside(to_freq(size, np.arange(own)))
    t_table = stacked(tap_back)

    def run(kernel, outs, scratch, operands, micros=0):
        return call(kernel, outs, scratch, [jnp.asarray(x) for x in operands], micros)

    rows = [pltpu.VMEM((own, width), F32)] + [pltpu.VMEM((own, LANES), F32)] * 2
    forward_slots, backward_slots = forward_slots.T, backward_slots.T

    def layer(size):
        return like(own, width, BF16), like(own, LANES, F32), like(own, LANES, F32), like(size, width, F32)

    weights, later, near1, far1, notes, *layer0 = call(
        functools.partial(prepare_kernel, two),
        (
            jax.ShapeDtypeStruct((kernels.shape[1], tap_count + 1, width), BF16), like(tap_count + 1, width, BF16),
            like(2 * two, width, BF16), like(2 * two, width, BF16), jax.ShapeDtypeStruct((8,), jnp.int32), *layer(large),
        ),
        [],
        [
            backward_lengths, forward_lengths, backward_slots, forward_slots,
            kernels[0].transpose(1, 0, 2), norm_gains[0], saved, act, ready, jnp.asarray(tap_freq(large, tap_count)),
        ],
        0,
        None, (VMEM,) * 4 + (SMEM,) + (VMEM,) * 4,
    )
    later = shifted(later, -1)
    near1, far1 = swapped(near1, far1)
    grad_mid, halo0, inner0, gain0 = run(
        functools.partial(first_backward_kernel, (three, two, one)),
        (
            like(small, width, BF16),
            like(2 * three, width, BF16), like(own, width, BF16), like(1, width, F32),
        ),
        [
            pltpu.VMEM((2, three, width), BF16), pltpu.VMEM((2, two, width), BF16),
            pltpu.VMEM((small, LANES), F32), pltpu.VMEM((small, LANES), F32),
            pltpu.VMEM((small, width), F32), pltpu.VMEM((small, LANES), F32), pltpu.VMEM((small, LANES), F32),
        ],
        [
            notes, saved, near0, far0, grad, weights, *layer0,
            stacked(to_freq(large, span(three, own))), stacked(from_freq(large, span(two, own))),
            stacked(to_freq(large, span(two, own))), stacked(from_freq(large, span(one, own))),
        ],
        4,
    )
    grad_mid = shifted(grad_mid, -1)
    layers = run(
        prepare_later_kernel, (*layer(size), *layer(size)), [], [notes, saved, act, weights, gain0, q_table], 0
    )
    masked1, mean1, inverse1, q1, masked2, _, _, q2 = layers
    taps0 = run(
        functools.partial(first_taps_kernel, two), like(tap_count + 1, width, BF16), [],
        [halo0, layer0[0], inner0, gain0, m_table, go_table, t_table],
        0,
    )
    halo_scratch = [pltpu.VMEM((2 * two, width), BF16), pltpu.VMEM((2, two, width), BF16)]
    between = run(
        functools.partial(first_forward_kernel, two),
        like(small, width, BF16),
        halo_scratch,
        [notes, act, near1, far1, weights, masked2, q2, m_table, c_table],
        3,
    )
    m1, factor1, conv1 = run(
        functools.partial(second_ready_kernel, two),
        (like(size, width, F32), like(small, width, F32), like(own, width, F32)),
        halo_scratch,
        [notes, near1, far1, weights, masked1, q1, m_table, c_table],
        3,
    )
    act_out = run(
        second_forward_kernel,
        like(own, width, BF16),
        [pltpu.VMEM((small, width), BF16)],
        [
            notes, between, later,
            stacked(to_freq(small, span(one, own))), tap_freq(small, tap_count), stacked(from_freq(small, span(0, own))),
        ],
        3,
    )
    act_out = shifted(act_out, 2)

    def summed(x, micros):
        step = 1
        while True:
            other = lax.ppermute(x, "tm", [(i, i ^ step) for i in range(shards)])
            step *= 2
            if step >= shards:
                return x, other
            x = call(add_kernel, like(*x.shape, BF16), [], (x, other), micros)

    mixed1, sums = run(
        second_taps_kernel,
        (like(small, width, BF16), like(2 * (tap_count + 1), width, BF16)),
        [],
        [notes, grad_mid, weights, m1, factor1, conv1, taps0, go_table, t_table],
        2,
    )
    grad_out = run(
        second_backward_kernel,
        like(own, width, BF16),
        rows,
        [
            notes, saved, grad_mid, weights, mixed1, q1, mean1, inverse1,
            stacked(to_freq(size, span(one, own))), stacked(from_freq(size, span(0, own))),
        ],
        6,
    )
    grad_out = shifted(grad_out, -1)
    sums = summed(sums, 6)
    slots = kernels.shape[1]
    act_out, grad_out, taps, gains = call(
        final_kernel,
        (
            like(own, width, BF16), like(own, width, BF16),
            jax.ShapeDtypeStruct((tap_count, slots, width), F32), like(slots, width, F32),
        ),
        [pltpu.SemaphoreType.DMA((2,))],
        (backward_slots, *sums, act_out, grad_out),
        0, [SMEM] + [VMEM] * 2 + [ANY] * 2, (ANY, ANY, VMEM, VMEM),
    )
    return act_out[None], grad_out[None], taps.transpose(1, 0, 2)[None], gains[None]


def solution(mesh):
    in_specs = (
        P("section", "tm", None),
        P("section", "tm", None),
        P("section", None, "tm", None),
        P("section", None, None, None),
        P("section", None, None),
        P(),
        P(),
        P(),
        P(),
    )
    out_specs = (
        P("section", "tm", None),
        P("section", "tm", None),
        P("section", None, None, None),
        P("section", None, None),
    )
    return jax.shard_map(local, mesh=mesh, in_specs=in_specs, out_specs=out_specs, check_vma=False)
```

```python
import functools

import jax
import jax.numpy as jnp
import ml_dtypes
import numpy as np
from jax import lax
from jax.experimental import pallas as pl
from jax.experimental.pallas import tpu as pltpu
from jax.sharding import PartitionSpec as P

epsilon = 1e-05
BLOCK = 1024
LANES = 128
F32 = jnp.float32
BF16 = jnp.bfloat16


def split(matrix):
    high = matrix.astype(ml_dtypes.bfloat16)
    low = (matrix - high.astype(np.float64)).astype(ml_dtypes.bfloat16)
    return high, low


def angles(size, times):
    return 2.0 * np.pi / size * np.outer(np.arange(size // 2) + 0.5, np.asarray(times, np.float64))


def to_freq(size, times):
    phase = angles(size, times)
    return np.concatenate([np.cos(phase), -np.sin(phase)], axis=0)


def from_freq(size, times):
    phase = angles(size, times).T
    return 2.0 / size * np.concatenate([np.cos(phase), -np.sin(phase)], axis=1)


def stacked(matrix):
    return np.concatenate(split(matrix), axis=0)


def beside(matrix):
    return np.concatenate(split(matrix), axis=1)


def tap_freq(size, taps):
    phase = angles(size, np.arange(taps) - (taps - 1) // 2)
    table = np.concatenate([np.cos(phase), np.sin(phase)], axis=0)
    return beside(np.concatenate([table, np.zeros((size, 1))], axis=1))


def dot(a, b):
    return jnp.dot(a, b, preferred_element_type=F32)


def transform(table, values):
    return sum(halves(dot(table[...], values.astype(BF16))))


def halves(values):
    half = values.shape[0] // 2
    return values[:half], values[half:]


def product(a, b):
    ar, ai = halves(a)
    br, bi = halves(b)
    return jnp.concatenate([ar * br - ai * bi, ar * bi + ai * br], axis=0)


def product_conj(a, b):
    ar, ai = halves(a)
    br, bi = halves(b)
    return jnp.concatenate([ar * br + ai * bi, ai * br - ar * bi], axis=0)


def sigmoid(values):
    return 0.5 * jnp.tanh(0.5 * values) + 0.5


def wide(stat, count):
    return jnp.concatenate([stat] * (count // LANES), axis=1)


def norm_rows(ref, start, count, at, gain, first, length, masked_ref, mean_ref, inverse_ref):
    width = masked_ref.shape[1]
    rows = pl.ds(start, count)
    tiles = [pl.ds(i * LANES, LANES) for i in range(width // LANES)]

    def values(tile):
        return ref[rows, tile].astype(F32)

    total = values(tiles[0])
    for tile in tiles[1:]:
        total = total + values(tile)
    mean = jnp.sum(total, axis=1, keepdims=True) * (1.0 / width)
    mean = jnp.broadcast_to(mean, (count, LANES))
    square = jnp.zeros((count, LANES), F32)
    for tile in tiles:
        center = values(tile) - mean
        square = square + center * center
    var = jnp.sum(square, axis=1, keepdims=True) * (1.0 / width)
    inverse = jnp.broadcast_to(lax.rsqrt(var + epsilon), (count, LANES))
    frame = first + at + lax.broadcasted_iota(jnp.int32, (count, LANES), 0)
    mask = ((frame >= 0) & (frame < length)).astype(F32)
    scale = mask * inverse
    out = pl.ds(at, count)
    for tile in tiles:
        masked_ref[out, tile] = ((values(tile) - mean) * scale * gain(tile)).astype(BF16)
    if mean_ref is not None:
        mean_ref[out, :] = mean
        inverse_ref[out, :] = inverse


def norm_pieces(pieces, gain, first, length, masked_ref, mean_ref=None, inverse_ref=None, chunk=128):
    at = 0
    for ref, start, count in pieces:
        for begin in range(0, count, chunk):
            norm_rows(
                ref, start + begin, min(chunk, count - begin), at + begin,
                gain, first, length, masked_ref, mean_ref, inverse_ref,
            )
        at += count


def window(pieces, columns):
    parts = [ref[pl.ds(start, count), columns] for ref, start, count in pieces]
    return parts[0] if len(parts) == 1 else jnp.concatenate(parts, axis=0)


def each_block(width, body):
    for begin in range(0, width, BLOCK):
        body(pl.ds(begin, BLOCK))


def tap_spectrum(table, weights):
    return dot(table, jnp.concatenate([weights, weights], axis=0))


def gate_factor(conv):
    gate = sigmoid(conv)
    return gate * (1.0 + conv * (1.0 - gate))


FIRST, BACK0, BACK1, AHEAD0 = range(0, 8, 2)


def looked_up(notes, layer):
    return notes[layer], notes[layer + 1], notes[FIRST]


def sorted_halos(near, far, at, halos):
    even = lax.rem(lax.axis_index("tm") + 1, 2)
    rows = pl.ds(at, halos.shape[1])
    halos[even] = near[rows, :]
    halos[1 - even] = far[rows, :]
    return halos.at[0], halos.at[1]


def lane_sum(values):
    total = values[:, :LANES]
    for lane in range(LANES, values.shape[1], LANES):
        total = total + values[:, lane : lane + LANES]
    return total


def first_pass(pieces, mean, inverse, gain, mask, tables, mixed, q, columns, scaled, sum_a, sum_b):
    g_table, x_table = tables
    grad_masked = wide(mask, BLOCK) * transform(x_table, product_conj(transform(g_table, mixed), q))
    centered = window(pieces, columns).astype(F32) - wide(mean[...], BLOCK)
    weighted = grad_masked * (centered * wide(inverse[...], BLOCK))
    gain = gain(columns)
    by_gain = grad_masked * gain
    scaled[:, columns] = by_gain
    sum_a[...] += lane_sum(by_gain)
    sum_b[...] += lane_sum(weighted * gain)
    return weighted


def last_pass(grad_pieces, pieces, mean, inverse, scaled, sum_a, sum_b, grad_x, chunk=128):
    width = scaled.shape[1]
    at = 0
    for (ref, start, count), (saved, base, _) in zip(grad_pieces, pieces):
        for begin in range(0, count, chunk):
            here = min(chunk, count - begin)
            rows = pl.ds(at + begin, here)
            inv = inverse[rows, :]
            mean_a = jnp.sum(sum_a[rows, :], axis=1, keepdims=True) * (1.0 / width)
            mean_b = jnp.sum(sum_b[rows, :], axis=1, keepdims=True) * (1.0 / width)
            slope = inv * jnp.broadcast_to(mean_b, (here, LANES)) * inv
            fixed = inv * jnp.broadcast_to(mean_a, (here, LANES)) - slope * mean[rows, :]
            for lane in range(0, width, LANES):
                tile = pl.ds(lane, LANES)
                x = saved[pl.ds(base + begin, here), tile].astype(F32)
                change = inv * scaled[rows, tile] - fixed - slope * x
                grad_x[rows, tile] = (ref[pl.ds(start + begin, here), tile].astype(F32) + change).astype(BF16)
        at += count


def frame_mask(rows, first, length):
    frame = first + lax.broadcasted_iota(jnp.int32, (rows, LANES), 0)
    return ((frame >= 0) & (frame < length)).astype(F32)


def slot_row(weights, slot):
    last = weights.shape[1] - 1
    return lambda columns: weights[slot, last : last + 1, columns].astype(F32)


def prepare_kernel(
    reach, back_lengths, ahead_lengths, back_slots, ahead_slots, kernels, gains, saved, act, ready, q_table,
    weights, later, near, far, notes, masked, mean, inverse, q,
):
    own, width = act.shape
    section, sections = lax.axis_index("section"), lax.axis_size("section")
    for even in range(2):

        @pl.when(lax.rem(lax.axis_index("tm") + 1, 2) == even)
        def _():
            for x, at in ((saved.at[1], 0), (act, reach)):
                tail, head = (near, far) if even else (far, near)
                tail[pl.ds(at, reach), :] = x[pl.ds(own - reach, reach), :]
                head[pl.ds(at, reach), :] = x[pl.ds(0, reach), :]

    count = kernels.shape[0]
    for slot in range(kernels.shape[1]):
        weights[slot, :count, :] = kernels[:, slot, :]
        weights[slot, count:, :] = gains[slot : slot + 1, :]
    later[...] = weights[ahead_slots[1, section]]
    slot, length, first = back_slots[0, section], back_lengths[section], lax.axis_index("tm") * own
    notes[FIRST] = first
    notes[BACK0] = slot
    notes[BACK0 + 1] = length
    notes[BACK1] = back_slots[1, section]
    notes[BACK1 + 1] = back_lengths[lax.rem(section + 1, sections)]
    notes[AHEAD0] = ahead_slots[0, section]
    notes[AHEAD0 + 1] = ahead_lengths[section]
    norm_pieces([(saved.at[0], 0, own)], slot_row(weights, slot), first, length, masked, mean, inverse)

    def block(columns):
        q[:, columns] = tap_spectrum(q_table[...], weights[slot, :, columns])

    each_block(width, block)


def prepare_later_kernel(notes, saved, act, weights, ready, q_table, *outs):
    own, width = act.shape
    layers = ((saved.at[1], BACK1, outs[:4]), (act, AHEAD0, outs[4:]))
    for x, layer, (masked, mean, inverse, _) in layers:
        slot, length, first = looked_up(notes, layer)
        norm_pieces([(x, 0, own)], slot_row(weights, slot), first, length, masked, mean, inverse)
    for _, layer, (_, _, _, q) in layers:
        slot = notes[layer]

        def block(columns, slot=slot, q=q):
            q[:, columns] = tap_spectrum(q_table[...], weights[slot, :, columns])

        each_block(width, block)


def norm_halo(left, right, own, gain, first, length, halo):
    reach = left.shape[0]
    norm_pieces([(left, 0, reach)], gain, first - reach, length, halo)
    norm_pieces([(right, 0, reach)], gain, first + own, length, halo.at[pl.ds(reach, reach)])


def joined(halo, own, columns):
    reach = halo.shape[0] // 2
    return jnp.concatenate([halo[:reach, columns], own[:, columns], halo[reach:, columns]], axis=0)


def first_backward_kernel(
    reach, notes, saved, near, far, grads, weights, later, masked, mean, inverse, q,
    m_table, c_table, g_table, x_table,
    grad_x, near_edge, far_edge, halo, inner, gain_sum, halos, grad_halos, scaled, sum_a, sum_b,
):
    own, width = grads.shape
    edge = near_edge.shape[0]
    slot, length, first = looked_up(notes, BACK0)
    gain = slot_row(weights, slot)
    left, right = sorted_halos(near, far, 0, halos)
    grad_left, grad_right = sorted_halos(near, far, reach, grad_halos)
    norm_halo(left, right, own, gain, first, length, halo)
    grad_pieces = [(grad_left, 0, edge), (grads, 0, own), (grad_right, 0, edge)]
    pieces = [(saved.at[0], 0, own)]
    mask = frame_mask(own, first, length)
    sum_a[...] = jnp.zeros_like(sum_a)
    sum_b[...] = jnp.zeros_like(sum_b)
    grad_x[pl.ds(own, later.shape[0]), :] = later[...]

    def block(columns):
        m = transform(m_table, joined(halo, masked, columns))
        conv = transform(c_table, product(m, q[:, columns]))
        mixed = (window(grad_pieces, columns).astype(F32) * gate_factor(conv)).astype(BF16)
        inner[:, columns] = mixed[edge : edge + own]
        weighted = first_pass(
            pieces, mean, inverse, gain, mask, (g_table, x_table), mixed, q[:, columns], columns,
            scaled, sum_a, sum_b,
        )
        gain_sum[:, columns] = jnp.sum(weighted, axis=0, keepdims=True)

    each_block(width, block)
    last_pass([(grads, 0, own)], pieces, mean, inverse, scaled, sum_a, sum_b, grad_x)
    for even in range(2):

        @pl.when(lax.rem(lax.axis_index("tm") + 1, 2) == even)
        def _():
            top, bottom = (far_edge, near_edge) if even else (near_edge, far_edge)
            top[...] = grad_x[pl.ds(0, edge), :]
            bottom[...] = grad_x[pl.ds(own - edge, edge), :]


def tap_term(go_table, t_table, m, mixed):
    g_own = dot(go_table[...], jnp.concatenate([mixed, mixed], axis=0))
    return transform(t_table, product_conj(m, g_own))


def put_taps(taps, tap, gain_sum, columns):
    row = lax.broadcasted_iota(jnp.int32, tap.shape, 0)
    taps[:, columns] = jnp.where(row == tap.shape[0] - 1, gain_sum, tap).astype(taps.dtype)


def first_taps_kernel(halo, masked, inner, gain_sum, m_table, go_table, t_table, taps):
    def block(columns):
        m = transform(m_table, joined(halo, masked, columns))
        put_taps(taps, tap_term(go_table, t_table, m, inner[:, columns]), gain_sum[:, columns], columns)

    each_block(masked.shape[1], block)


def add_kernel(mine, other, out):
    out[...] = (mine[...].astype(F32) + other[...].astype(F32)).astype(out.dtype)


def second_ready_kernel(
    reach, notes, near, far, weights, masked, q, m_table, c_table, m_out, factor, conv_out, halo, halos
):
    own, width = masked.shape
    slot, length, first = looked_up(notes, BACK1)
    left, right = sorted_halos(near, far, 0, halos)
    norm_halo(left, right, own, slot_row(weights, slot), first, length, halo)

    def block(columns):
        m = transform(m_table, joined(halo, masked, columns))
        conv = transform(c_table, product(m, q[:, columns]))
        m_out[:, columns] = m
        factor[:, columns] = gate_factor(conv)
        edge = (conv.shape[0] - own) // 2
        conv_out[:, columns] = conv[edge : edge + own]

    each_block(width, block)


def second_taps_kernel(
    notes, received, near, far, weights, m, factor, conv, taps0, go_table, t_table, mixed_out, taps, halos
):
    own, width = conv.shape
    rows = factor.shape[0]
    count = taps0.shape[0]
    taps[pl.ds(0, count), :] = taps0[...]
    taps1 = taps.at[pl.ds(count, count)]
    edge = (rows - own) // 2
    gain = slot_row(weights, notes[BACK1])
    left, right = sorted_halos(near, far, 0, halos)
    pieces = [(left, 0, edge), (received, 0, own), (right, 0, edge)]

    def block(columns):
        mixed = (window(pieces, columns).astype(F32) * factor[:, columns]).astype(BF16)
        mixed_out[:, columns] = mixed
        inner = mixed[edge : edge + own]
        gain_sum = jnp.sum(inner.astype(F32) * conv[:, columns], axis=0, keepdims=True) / gain(columns)
        put_taps(taps1, tap_term(go_table, t_table, m[:, columns], inner), gain_sum, columns)

    each_block(width, block)


def second_backward_kernel(
    notes, saved, received, weights, mixed, q, mean, inverse, g_table, x_table, grad_x, scaled, sum_a, sum_b
):
    own, width = grad_x.shape
    slot, length, first = looked_up(notes, BACK1)
    pieces = [(saved.at[1], 0, own)]
    mask = frame_mask(own, first, length)
    sum_a[...] = jnp.zeros_like(sum_a)
    sum_b[...] = jnp.zeros_like(sum_b)

    def block(columns):
        first_pass(
            pieces, mean, inverse, slot_row(weights, slot), mask, (g_table, x_table), mixed[:, columns], q[:, columns],
            columns, scaled, sum_a, sum_b,
        )

    each_block(width, block)
    last_pass([(received, 0, own)], pieces, mean, inverse, scaled, sum_a, sum_b, grad_x)


def first_forward_kernel(reach, notes, act, near, far, weights, masked, q, m_table, c_table, out, halo, halos):
    own, width = act.shape
    middle = reach // 2
    slot, length, first = looked_up(notes, AHEAD0)
    left, right = sorted_halos(near, far, reach, halos)
    inner = [(left, middle, middle), (act, 0, own), (right, 0, middle)]
    norm_halo(left, right, own, slot_row(weights, slot), first, length, halo)

    def block(columns):
        conv = transform(c_table, product(transform(m_table, joined(halo, masked, columns)), q[:, columns]))
        out[:, columns] = (window(inner, columns).astype(F32) + conv * sigmoid(conv)).astype(BF16)

    each_block(width, block)


def second_forward_kernel(notes, between, received, m_table, q_table, c_table, out, masked):
    own, width = out.shape
    rows = between.shape[0]
    edge = (rows - own) // 2
    slot, length, first = looked_up(notes, AHEAD0)
    last = received.shape[0] - 1

    def gain(columns):
        return received[last : last + 1, columns].astype(F32)

    norm_pieces([(between, 0, rows)], gain, first - edge, length, masked, chunk=rows // 2)

    def block(columns):
        q = tap_spectrum(q_table[...], received[own:, columns])
        conv = transform(c_table, product(transform(m_table, masked[:, columns]), q))
        out[:, columns] = (between[edge : edge + own, columns].astype(F32) + conv * sigmoid(conv)).astype(BF16)

    each_block(width, block)


def pack_kernel(reaches, saved, grad, near, far, ready, sems):
    own = grad.shape[1]
    even = lax.rem(lax.axis_index("tm") + 1, 2)
    copies = []
    at = 0
    for x, reach in zip((saved, grad), reaches):
        for out, tail in ((near, even), (far, 1 - even)):
            start = pl.multiple_of(tail * (own - reach), 16)
            copies.append(
                pltpu.make_async_copy(
                    x.at[0, pl.ds(start, reach)], out.at[pl.ds(at, reach)], sems.at[len(copies)]
                )
            )
        at += reach
    ready[...] = jnp.zeros_like(ready)
    for copy in copies:
        copy.start()
    for copy in copies:
        copy.wait()


def final_kernel(slots, mine, other, act, grad, act_out, grad_out, taps, gains, sems):
    copies = [
        pltpu.make_async_copy(act, act_out, sems.at[0]),
        pltpu.make_async_copy(grad, grad_out, sems.at[1]),
    ]
    for copy in copies:
        copy.start()
    section = lax.axis_index("section")
    count = taps.shape[0]
    total = mine[...].astype(F32) + other[...].astype(F32)
    ticks = total[: count + 1], total[count + 1 :]
    for slot in range(taps.shape[1]):
        use = [(slots[tick, section] == slot).astype(F32) for tick in range(2)]
        both = use[0] * ticks[0] + use[1] * ticks[1]
        taps[:, slot, :] = both[:count]
        gains[slot : slot + 1, :] = both[count:]
    for copy in copies:
        copy.wait()


def span(reach, own):
    return np.arange(-reach, own + reach)


VMEM = pl.BlockSpec(memory_space=pltpu.VMEM)
SMEM = pl.BlockSpec(memory_space=pltpu.SMEM)
ANY = pl.BlockSpec(memory_space=pl.ANY)
HBM = pl.BlockSpec(memory_space=pltpu.HBM)
LIMIT = 24 * 1024 * 1024
FULL = 127 * 512 * 1024


def call(kernel, outs, scratch, operands, micros, specs=None, out_specs=None, limit=LIMIT):
    if specs is None:
        specs = [SMEM if x.dtype == jnp.int32 else VMEM for x in operands]
    return pl.pallas_call(
        kernel,
        out_shape=outs,
        in_specs=specs,
        out_specs=jax.tree.map(lambda _: VMEM, outs) if out_specs is None else out_specs,
        scratch_shapes=scratch,
        compiler_params=pltpu.CompilerParams(vmem_limit_bytes=limit),
        cost_estimate=pl.CostEstimate(flops=int(micros * 1e9), bytes_accessed=0, transcendentals=0),
    )(*operands)


def like(rows, width, dtype):
    return jax.ShapeDtypeStruct((rows, width), dtype)


def up16(count):
    return -(-count // 16) * 16


def local(
    act_in, grad_in, saved_inputs, kernels, norm_gains,
    forward_lengths, backward_lengths, forward_slots, backward_slots,
):
    sections = lax.axis_size("section")
    shards = lax.axis_size("tm")
    act, grad, saved = act_in[0], grad_in[0], saved_inputs[0]
    own, width = act.shape
    tap_count = kernels.shape[2]
    half = (tap_count - 1) // 2
    one, two = up16(half), up16(2 * half)
    size, small = own + 2 * two, own + 2 * one

    def shifted(x, by):
        return lax.ppermute(x, "section", [(i, (i + by) % sections) for i in range(sections)])

    def swapped(near, far, by=0):
        results = []
        for x, begin in ((near, 0), (far, 1)):
            pairs = [(i, i + 1) for i in range(begin, shards - 1, 2)]
            pairs = [
                (s * shards + i, (s + by) % sections * shards + j)
                for s in range(sections)
                for a, b in pairs
                for i, j in ((a, b), (b, a))
            ]
            results.append(lax.ppermute(x, ("section", "tm"), pairs))
        return results

    near0, far0, ready = call(
        functools.partial(pack_kernel, (two, one)),
        (like(two + one, width, BF16), like(two + one, width, BF16), like(8, LANES, F32)),
        [pltpu.SemaphoreType.DMA((4,))],
        (saved, grad_in),
        0, [HBM] * 2, None, FULL,
    )
    near0, far0 = swapped(near0, far0)
    tap_back = np.concatenate([from_freq(size, np.arange(tap_count) - half), np.zeros((1, size))], axis=0)
    m_table = stacked(to_freq(size, span(two, own)))
    q_table = tap_freq(size, tap_count)
    c_table = stacked(from_freq(size, span(one, own)))
    go_table = beside(to_freq(size, np.arange(own)))
    t_table = stacked(tap_back)

    def run(kernel, outs, scratch, operands, micros=0):
        return call(kernel, outs, scratch, [jnp.asarray(x) for x in operands], micros)

    rows = [pltpu.VMEM((own, width), F32)] + [pltpu.VMEM((own, LANES), F32)] * 2
    forward_slots, backward_slots = forward_slots.T, backward_slots.T

    def layer(size):
        return like(own, width, BF16), like(own, LANES, F32), like(own, LANES, F32), like(size, width, F32)

    weights, later, near1, far1, notes, *layer0 = call(
        functools.partial(prepare_kernel, two),
        (
            jax.ShapeDtypeStruct((kernels.shape[1], tap_count + 1, width), BF16), like(tap_count + 1, width, BF16),
            like(2 * two, width, BF16), like(2 * two, width, BF16), jax.ShapeDtypeStruct((8,), jnp.int32), *layer(size),
        ),
        [],
        [
            backward_lengths, forward_lengths, backward_slots, forward_slots,
            kernels[0].transpose(1, 0, 2), norm_gains[0], saved, act, ready, jnp.asarray(q_table),
        ],
        0,
        None, (VMEM,) * 4 + (SMEM,) + (VMEM,) * 4,
    )
    near1, far1 = swapped(near1, far1)
    g_table, x_table = stacked(to_freq(size, span(one, own))), stacked(from_freq(size, span(0, own)))
    grad_mid, near2, far2, halo0, inner0, gain0 = run(
        functools.partial(first_backward_kernel, two),
        (
            like(own + tap_count + 1, width, BF16), like(one, width, BF16), like(one, width, BF16),
            like(2 * two, width, BF16), like(own, width, BF16), like(1, width, F32),
        ),
        [pltpu.VMEM((2, two, width), BF16), pltpu.VMEM((2, one, width), BF16), *rows],
        [
            notes, saved, near0, far0, grad, weights, later, *layer0,
            m_table, c_table, g_table, x_table,
        ],
        4,
    )
    grad_mid = shifted(grad_mid, -1)
    near2, far2 = swapped(near2, far2, -1)
    layers = run(
        prepare_later_kernel, (*layer(size), *layer(size)), [], [notes, saved, act, weights, gain0, q_table], 0
    )
    masked1, mean1, inverse1, q1, masked2, _, _, q2 = layers
    taps0 = run(
        first_taps_kernel, like(tap_count + 1, width, BF16), [],
        [halo0, layer0[0], inner0, gain0, m_table, go_table, t_table],
        0,
    )
    halo_scratch = [pltpu.VMEM((2 * two, width), BF16), pltpu.VMEM((2, two, width), BF16)]
    between = run(
        functools.partial(first_forward_kernel, two),
        like(small, width, BF16),
        halo_scratch,
        [notes, act, near1, far1, weights, masked2, q2, m_table, c_table],
        3,
    )
    m1, factor1, conv1 = run(
        functools.partial(second_ready_kernel, two),
        (like(size, width, F32), like(small, width, F32), like(own, width, F32)),
        halo_scratch,
        [notes, near1, far1, weights, masked1, q1, m_table, c_table],
        3,
    )
    act_out = run(
        second_forward_kernel,
        like(own, width, BF16),
        [pltpu.VMEM((small, width), BF16)],
        [
            notes, between, grad_mid,
            stacked(to_freq(small, span(one, own))), tap_freq(small, tap_count), stacked(from_freq(small, span(0, own))),
        ],
        3,
    )
    act_out = shifted(act_out, 2)

    def summed(x, micros):
        step = 1
        while True:
            other = lax.ppermute(x, "tm", [(i, i ^ step) for i in range(shards)])
            step *= 2
            if step >= shards:
                return x, other
            x = call(add_kernel, like(*x.shape, BF16), [], (x, other), micros)

    mixed1, sums = run(
        second_taps_kernel,
        (like(small, width, BF16), like(2 * (tap_count + 1), width, BF16)),
        [pltpu.VMEM((2, one, width), BF16)],
        [notes, grad_mid, near2, far2, weights, m1, factor1, conv1, taps0, go_table, t_table],
        2,
    )
    grad_out = run(
        second_backward_kernel,
        like(own, width, BF16),
        rows,
        [
            notes, saved, grad_mid, weights, mixed1, q1, mean1, inverse1,
            g_table, x_table,
        ],
        6,
    )
    grad_out = shifted(grad_out, -1)
    sums = summed(sums, 6)
    slots = kernels.shape[1]
    act_out, grad_out, taps, gains = call(
        final_kernel,
        (
            like(own, width, BF16), like(own, width, BF16),
            jax.ShapeDtypeStruct((tap_count, slots, width), F32), like(slots, width, F32),
        ),
        [pltpu.SemaphoreType.DMA((2,))],
        (backward_slots, *sums, act_out, grad_out),
        0, [SMEM] + [VMEM] * 2 + [ANY] * 2, (ANY, ANY, VMEM, VMEM),
    )
    return act_out[None], grad_out[None], taps.transpose(1, 0, 2)[None], gains[None]


def solution(mesh):
    in_specs = (
        P("section", "tm", None),
        P("section", "tm", None),
        P("section", None, "tm", None),
        P("section", None, None, None),
        P("section", None, None),
        P(),
        P(),
        P(),
        P(),
    )
    out_specs = (
        P("section", "tm", None),
        P("section", "tm", None),
        P("section", None, None, None),
        P("section", None, None),
    )
    return jax.shard_map(local, mesh=mesh, in_specs=in_specs, out_specs=out_specs, check_vma=False)
```

```python
import functools

import jax
import jax.numpy as jnp
import ml_dtypes
import numpy as np
from jax import lax
from jax.experimental import pallas as pl
from jax.experimental.pallas import tpu as pltpu
from jax.sharding import PartitionSpec as P

epsilon = 1e-05
BLOCK = 1024
LANES = 128
F32 = jnp.float32
BF16 = jnp.bfloat16


def split(matrix):
    high = matrix.astype(ml_dtypes.bfloat16)
    low = (matrix - high.astype(np.float64)).astype(ml_dtypes.bfloat16)
    return high, low


def angles(size, times):
    return 2.0 * np.pi / size * np.outer(np.arange(size // 2) + 0.5, np.asarray(times, np.float64))


def to_freq(size, times):
    phase = angles(size, times)
    return np.concatenate([np.cos(phase), -np.sin(phase)], axis=0)


def from_freq(size, times):
    phase = angles(size, times).T
    return 2.0 / size * np.concatenate([np.cos(phase), -np.sin(phase)], axis=1)


def stacked(matrix):
    return np.concatenate(split(matrix), axis=0)


def beside(matrix):
    return np.concatenate(split(matrix), axis=1)


def tap_freq(size, taps):
    phase = angles(size, np.arange(taps) - (taps - 1) // 2)
    table = np.concatenate([np.cos(phase), np.sin(phase)], axis=0)
    return beside(np.concatenate([table, np.zeros((size, 1))], axis=1))


def dot(a, b):
    return jnp.dot(a, b, preferred_element_type=F32)


def transform(table, values):
    return sum(halves(dot(table[...], values.astype(BF16))))


def halves(values):
    half = values.shape[0] // 2
    return values[:half], values[half:]


def product(a, b):
    ar, ai = halves(a)
    br, bi = halves(b)
    return jnp.concatenate([ar * br - ai * bi, ar * bi + ai * br], axis=0)


def product_conj(a, b):
    ar, ai = halves(a)
    br, bi = halves(b)
    return jnp.concatenate([ar * br + ai * bi, ai * br - ar * bi], axis=0)


def sigmoid(values):
    return 0.5 * jnp.tanh(0.5 * values) + 0.5


def wide(stat, count):
    return jnp.concatenate([stat] * (count // LANES), axis=1)


def norm_rows(ref, start, count, at, gain, first, length, masked_ref, mean_ref, inverse_ref):
    width = masked_ref.shape[1]
    rows = pl.ds(start, count)
    tiles = [pl.ds(i * LANES, LANES) for i in range(width // LANES)]

    def values(tile):
        return ref[rows, tile].astype(F32)

    total = values(tiles[0])
    for tile in tiles[1:]:
        total = total + values(tile)
    mean = jnp.sum(total, axis=1, keepdims=True) * (1.0 / width)
    mean = jnp.broadcast_to(mean, (count, LANES))
    square = jnp.zeros((count, LANES), F32)
    for tile in tiles:
        center = values(tile) - mean
        square = square + center * center
    var = jnp.sum(square, axis=1, keepdims=True) * (1.0 / width)
    inverse = jnp.broadcast_to(lax.rsqrt(var + epsilon), (count, LANES))
    frame = first + at + lax.broadcasted_iota(jnp.int32, (count, LANES), 0)
    mask = ((frame >= 0) & (frame < length)).astype(F32)
    scale = mask * inverse
    out = pl.ds(at, count)
    for tile in tiles:
        masked_ref[out, tile] = ((values(tile) - mean) * scale * gain(tile)).astype(BF16)
    if mean_ref is not None:
        mean_ref[out, :] = mean
        inverse_ref[out, :] = inverse


def norm_pieces(pieces, gain, first, length, masked_ref, mean_ref=None, inverse_ref=None, chunk=128):
    at = 0
    for ref, start, count in pieces:
        for begin in range(0, count, chunk):
            norm_rows(
                ref, start + begin, min(chunk, count - begin), at + begin,
                gain, first, length, masked_ref, mean_ref, inverse_ref,
            )
        at += count


def window(pieces, columns):
    parts = [ref[pl.ds(start, count), columns] for ref, start, count in pieces]
    return parts[0] if len(parts) == 1 else jnp.concatenate(parts, axis=0)


def each_block(width, body):
    for begin in range(0, width, BLOCK):
        body(pl.ds(begin, BLOCK))


def tap_spectrum(table, weights):
    return dot(table, jnp.concatenate([weights, weights], axis=0))


def gate_factor(conv):
    gate = sigmoid(conv)
    return gate * (1.0 + conv * (1.0 - gate))


FIRST, BACK0, BACK1, AHEAD0 = range(0, 8, 2)


def looked_up(notes, layer):
    return notes[layer], notes[layer + 1], notes[FIRST]


def sorted_halos(near, far, at, halos):
    even = lax.rem(lax.axis_index("tm") + 1, 2)
    rows = pl.ds(at, halos.shape[1])
    halos[even] = near[rows, :]
    halos[1 - even] = far[rows, :]
    return halos.at[0], halos.at[1]


def lane_sum(values):
    total = values[:, :LANES]
    for lane in range(LANES, values.shape[1], LANES):
        total = total + values[:, lane : lane + LANES]
    return total


def first_pass(pieces, mean, inverse, gain, mask, tables, mixed, q, columns, scaled, sum_a, sum_b):
    g_table, x_table = tables
    grad_masked = wide(mask, BLOCK) * transform(x_table, product_conj(transform(g_table, mixed), q))
    centered = window(pieces, columns).astype(F32) - wide(mean[...], BLOCK)
    weighted = grad_masked * (centered * wide(inverse[...], BLOCK))
    gain = gain(columns)
    by_gain = grad_masked * gain
    scaled[:, columns] = by_gain
    sum_a[...] += lane_sum(by_gain)
    sum_b[...] += lane_sum(weighted * gain)
    return weighted


def last_pass(grad_pieces, pieces, mean, inverse, scaled, sum_a, sum_b, grad_x, chunk=128):
    width = scaled.shape[1]
    at = 0
    for (ref, start, count), (saved, base, _) in zip(grad_pieces, pieces):
        for begin in range(0, count, chunk):
            here = min(chunk, count - begin)
            rows = pl.ds(at + begin, here)
            inv = inverse[rows, :]
            mean_a = jnp.sum(sum_a[rows, :], axis=1, keepdims=True) * (1.0 / width)
            mean_b = jnp.sum(sum_b[rows, :], axis=1, keepdims=True) * (1.0 / width)
            slope = inv * jnp.broadcast_to(mean_b, (here, LANES)) * inv
            fixed = inv * jnp.broadcast_to(mean_a, (here, LANES)) - slope * mean[rows, :]
            for lane in range(0, width, LANES):
                tile = pl.ds(lane, LANES)
                x = saved[pl.ds(base + begin, here), tile].astype(F32)
                change = inv * scaled[rows, tile] - fixed - slope * x
                grad_x[rows, tile] = (ref[pl.ds(start + begin, here), tile].astype(F32) + change).astype(BF16)
        at += count


def frame_mask(rows, first, length):
    frame = first + lax.broadcasted_iota(jnp.int32, (rows, LANES), 0)
    return ((frame >= 0) & (frame < length)).astype(F32)


def slot_row(weights, slot):
    last = weights.shape[1] - 1
    return lambda columns: weights[slot, last : last + 1, columns].astype(F32)


def prepare_kernel(
    reach, notes, kernels, gains, saved, act, q_table, weights, later, near, far, masked, mean, inverse, q
):
    own, width = act.shape
    for even in range(2):

        @pl.when(lax.rem(lax.axis_index("tm") + 1, 2) == even)
        def _():
            for x, at in ((saved.at[1], 0), (act, reach)):
                tail, head = (near, far) if even else (far, near)
                tail[pl.ds(at, reach), :] = x[pl.ds(own - reach, reach), :]
                head[pl.ds(at, reach), :] = x[pl.ds(0, reach), :]

    count = kernels.shape[0]
    for slot in range(kernels.shape[1]):
        weights[slot, :count, :] = kernels[:, slot, :]
        weights[slot, count:, :] = gains[slot : slot + 1, :]
    later[...] = weights[notes[FIRST + 1]]
    slot, length, first = looked_up(notes, BACK0)
    norm_pieces([(saved.at[0], 0, own)], slot_row(weights, slot), first, length, masked, mean, inverse)

    def block(columns):
        q[:, columns] = tap_spectrum(q_table[...], weights[slot, :, columns])

    each_block(width, block)


def norm_halo(left, right, own, gain, first, length, halo):
    reach = left.shape[0]
    norm_pieces([(left, 0, reach)], gain, first - reach, length, halo)
    norm_pieces([(right, 0, reach)], gain, first + own, length, halo.at[pl.ds(reach, reach)])


def joined(halo, own, columns):
    reach = halo.shape[0] // 2
    return jnp.concatenate([halo[:reach, columns], own[:, columns], halo[reach:, columns]], axis=0)


def first_backward_kernel(
    reach, notes, saved, near, far, grads, weights, later, masked, mean, inverse, q,
    m_table, c_table, g_table, x_table,
    grad_x, near_edge, far_edge, halo, inner, gain_sum, halos, grad_halos, scaled, sum_a, sum_b,
):
    own, width = grads.shape
    edge = near_edge.shape[0]
    slot, length, first = looked_up(notes, BACK0)
    gain = slot_row(weights, slot)
    left, right = sorted_halos(near, far, 0, halos)
    grad_left, grad_right = sorted_halos(near, far, reach, grad_halos)
    norm_halo(left, right, own, gain, first, length, halo)
    grad_pieces = [(grad_left, 0, edge), (grads, 0, own), (grad_right, 0, edge)]
    pieces = [(saved.at[0], 0, own)]
    mask = frame_mask(own, first, length)
    sum_a[...] = jnp.zeros_like(sum_a)
    sum_b[...] = jnp.zeros_like(sum_b)
    grad_x[pl.ds(own, later.shape[0]), :] = later[...]

    def block(columns):
        m = transform(m_table, joined(halo, masked, columns))
        conv = transform(c_table, product(m, q[:, columns]))
        mixed = (window(grad_pieces, columns).astype(F32) * gate_factor(conv)).astype(BF16)
        inner[:, columns] = mixed[edge : edge + own]
        weighted = first_pass(
            pieces, mean, inverse, gain, mask, (g_table, x_table), mixed, q[:, columns], columns,
            scaled, sum_a, sum_b,
        )
        gain_sum[:, columns] = jnp.sum(weighted, axis=0, keepdims=True)

    each_block(width, block)
    last_pass([(grads, 0, own)], pieces, mean, inverse, scaled, sum_a, sum_b, grad_x)
    for even in range(2):

        @pl.when(lax.rem(lax.axis_index("tm") + 1, 2) == even)
        def _():
            top, bottom = (far_edge, near_edge) if even else (near_edge, far_edge)
            top[...] = grad_x[pl.ds(0, edge), :]
            bottom[...] = grad_x[pl.ds(own - edge, edge), :]


def tap_term(go_table, t_table, m, mixed):
    g_own = dot(go_table[...], jnp.concatenate([mixed, mixed], axis=0))
    return transform(t_table, product_conj(m, g_own))


def put_taps(taps, tap, gain_sum, columns):
    row = lax.broadcasted_iota(jnp.int32, tap.shape, 0)
    taps[:, columns] = jnp.where(row == tap.shape[0] - 1, gain_sum, tap).astype(taps.dtype)


def first_taps_kernel(halo, masked, inner, gain_sum, m_table, go_table, t_table, taps):
    def block(columns):
        m = transform(m_table, joined(halo, masked, columns))
        put_taps(taps, tap_term(go_table, t_table, m, inner[:, columns]), gain_sum[:, columns], columns)

    each_block(masked.shape[1], block)


def added(mine, other):
    return (mine[...].astype(F32) + other[...].astype(F32)).astype(BF16)


def add_kernel(mine, other, out):
    out[...] = added(mine, other)


def below_kernel(mine0, other0, mine1, other1, out):
    count = mine0.shape[0]
    out[pl.ds(0, count), :] = added(mine0, other0)
    out[pl.ds(count, count), :] = added(mine1, other1)


def second_ready_kernel(
    reach, notes, saved, near, far, weights, m_table, q_table, c_table,
    m_out, q_out, factor, conv_out, mean, inverse, halo, halos, masked,
):
    own, width = masked.shape
    slot, length, first = looked_up(notes, BACK1)
    gain = slot_row(weights, slot)
    left, right = sorted_halos(near, far, 0, halos)
    norm_pieces([(saved.at[1], 0, own)], gain, first, length, masked, mean, inverse)
    norm_halo(left, right, own, gain, first, length, halo)

    def block(columns):
        m = transform(m_table, joined(halo, masked, columns))
        q = tap_spectrum(q_table[...], weights[slot, :, columns])
        conv = transform(c_table, product(m, q))
        m_out[:, columns] = m
        q_out[:, columns] = q
        factor[:, columns] = gate_factor(conv)
        edge = (conv.shape[0] - own) // 2
        conv_out[:, columns] = conv[edge : edge + own]

    each_block(width, block)


def second_taps_kernel(
    notes, received, near, far, weights, m, factor, conv, go_table, t_table, mixed_out, taps, halos
):
    own, width = conv.shape
    rows = factor.shape[0]
    edge = (rows - own) // 2
    gain = slot_row(weights, notes[BACK1])
    left, right = sorted_halos(near, far, 0, halos)
    pieces = [(left, 0, edge), (received, 0, own), (right, 0, edge)]

    def block(columns):
        mixed = (window(pieces, columns).astype(F32) * factor[:, columns]).astype(BF16)
        mixed_out[:, columns] = mixed
        inner = mixed[edge : edge + own]
        gain_sum = jnp.sum(inner.astype(F32) * conv[:, columns], axis=0, keepdims=True) / gain(columns)
        put_taps(taps, tap_term(go_table, t_table, m[:, columns], inner), gain_sum, columns)

    each_block(width, block)


def second_backward_kernel(
    notes, saved, received, weights, mixed, q, mean, inverse, g_table, x_table, grad_x, scaled, sum_a, sum_b
):
    own, width = grad_x.shape
    slot, length, first = looked_up(notes, BACK1)
    pieces = [(saved.at[1], 0, own)]
    mask = frame_mask(own, first, length)
    sum_a[...] = jnp.zeros_like(sum_a)
    sum_b[...] = jnp.zeros_like(sum_b)

    def block(columns):
        first_pass(
            pieces, mean, inverse, slot_row(weights, slot), mask, (g_table, x_table), mixed[:, columns], q[:, columns],
            columns, scaled, sum_a, sum_b,
        )

    each_block(width, block)
    last_pass([(received, 0, own)], pieces, mean, inverse, scaled, sum_a, sum_b, grad_x)


def first_forward_kernel(reach, notes, act, near, far, weights, m_table, q_table, c_table, out, halo, halos, masked):
    own, width = act.shape
    middle = reach // 2
    slot, length, first = looked_up(notes, AHEAD0)
    gain = slot_row(weights, slot)
    left, right = sorted_halos(near, far, reach, halos)
    inner = [(left, middle, middle), (act, 0, own), (right, 0, middle)]
    norm_pieces([(act, 0, own)], gain, first, length, masked)
    norm_halo(left, right, own, gain, first, length, halo)

    def block(columns):
        q = tap_spectrum(q_table[...], weights[slot, :, columns])
        conv = transform(c_table, product(transform(m_table, joined(halo, masked, columns)), q))
        out[:, columns] = (window(inner, columns).astype(F32) + conv * sigmoid(conv)).astype(BF16)

    each_block(width, block)


def second_forward_kernel(notes, between, received, m_table, q_table, c_table, out, masked):
    own, width = out.shape
    rows = between.shape[0]
    edge = (rows - own) // 2
    slot, length, first = looked_up(notes, AHEAD0)
    last = received.shape[0] - 1

    def gain(columns):
        return received[last : last + 1, columns].astype(F32)

    norm_pieces([(between, 0, rows)], gain, first - edge, length, masked, chunk=rows // 2)

    def block(columns):
        q = tap_spectrum(q_table[...], received[own:, columns])
        conv = transform(c_table, product(transform(m_table, masked[:, columns]), q))
        out[:, columns] = (between[edge : edge + own, columns].astype(F32) + conv * sigmoid(conv)).astype(BF16)

    each_block(width, block)


def pack_kernel(
    reaches, saved, grad, back_lengths, ahead_lengths, back_slots, ahead_slots,
    near, far, notes, back_len, ahead_len, back_slot, ahead_slot, sems,
):
    own = grad.shape[1]
    even = lax.rem(lax.axis_index("tm") + 1, 2)
    copies = []
    at = 0
    for x, reach in zip((saved, grad), reaches):
        for out, tail in ((near, even), (far, 1 - even)):
            start = pl.multiple_of(tail * (own - reach), 16)
            copies.append((x.at[0, pl.ds(start, reach)], out.at[pl.ds(at, reach)]))
        at += reach
    small = [(back_lengths, back_len), (ahead_lengths, ahead_len), (back_slots, back_slot), (ahead_slots, ahead_slot)]
    copies = [pltpu.make_async_copy(a, b, sems.at[k]) for k, (a, b) in enumerate(small + copies)]
    for copy in copies:
        copy.start()
    for copy in copies:
        copy.wait()
    section, sections = lax.axis_index("section"), lax.axis_size("section")
    notes[FIRST] = lax.axis_index("tm") * own
    notes[FIRST + 1] = ahead_slot[1, section]
    notes[BACK0] = back_slot[0, section]
    notes[BACK0 + 1] = back_len[section]
    notes[BACK1] = back_slot[1, section]
    notes[BACK1 + 1] = back_len[lax.rem(section + 1, sections)]
    notes[AHEAD0] = ahead_slot[0, section]
    notes[AHEAD0 + 1] = ahead_len[section]


def final_kernel(notes, mine, other, act, grad, act_out, grad_out, taps, gains, sems):
    copies = [
        pltpu.make_async_copy(act, act_out, sems.at[0]),
        pltpu.make_async_copy(grad, grad_out, sems.at[1]),
    ]
    for copy in copies:
        copy.start()
    count = taps.shape[0]
    total = mine[...].astype(F32) + other[...].astype(F32)
    ticks = total[: count + 1], total[count + 1 :]
    for slot in range(taps.shape[1]):
        use = [(notes[layer] == slot).astype(F32) for layer in (BACK0, BACK1)]
        both = use[0] * ticks[0] + use[1] * ticks[1]
        taps[:, slot, :] = both[:count]
        gains[slot : slot + 1, :] = both[count:]
    for copy in copies:
        copy.wait()


def span(reach, own):
    return np.arange(-reach, own + reach)


VMEM = pl.BlockSpec(memory_space=pltpu.VMEM)
SMEM = pl.BlockSpec(memory_space=pltpu.SMEM)
ANY = pl.BlockSpec(memory_space=pl.ANY)
HBM = pl.BlockSpec(memory_space=pltpu.HBM)
LIMIT = 24 * 1024 * 1024
FULL = 127 * 512 * 1024


def call(kernel, outs, scratch, operands, micros, specs=None, out_specs=None, limit=LIMIT, after=None):
    if specs is None:
        specs = [SMEM if x.dtype == jnp.int32 else VMEM for x in operands]
    if after is not None:
        operands, specs = [*operands, after], [*specs, ANY]
        inner, place = kernel, len(operands) - 1

        def kernel(*refs):
            return inner(*refs[:place], *refs[place + 1 :])

    return pl.pallas_call(
        kernel,
        out_shape=outs,
        in_specs=specs,
        out_specs=jax.tree.map(lambda _: VMEM, outs) if out_specs is None else out_specs,
        scratch_shapes=scratch,
        compiler_params=pltpu.CompilerParams(vmem_limit_bytes=limit),
        cost_estimate=pl.CostEstimate(flops=int(micros * 1e9), bytes_accessed=0, transcendentals=0),
    )(*operands)


def like(rows, width, dtype):
    return jax.ShapeDtypeStruct((rows, width), dtype)


def up16(count):
    return -(-count // 16) * 16


def local(
    act_in, grad_in, saved_inputs, kernels, norm_gains,
    forward_lengths, backward_lengths, forward_slots, backward_slots,
):
    sections = lax.axis_size("section")
    shards = lax.axis_size("tm")
    act, grad, saved = act_in[0], grad_in[0], saved_inputs[0]
    own, width = act.shape
    tap_count = kernels.shape[2]
    half = (tap_count - 1) // 2
    one, two = up16(half), up16(2 * half)
    size, small = own + 2 * two, own + 2 * one

    def shifted(x, by):
        return lax.ppermute(x, "section", [(i, (i + by) % sections) for i in range(sections)])

    def swapped(near, far, by=0):
        results = []
        for x, begin in ((far, 1), (near, 0)):
            pairs = [(i, i + 1) for i in range(begin, shards - 1, 2)]
            pairs = [
                (s * shards + i, (s + by) % sections * shards + j)
                for s in range(sections)
                for a, b in pairs
                for i, j in ((a, b), (b, a))
            ]
            results.append(lax.ppermute(x, ("section", "tm"), pairs))
        return results[::-1]

    lengths = pltpu.SMEM(backward_lengths.shape, jnp.int32)
    forward_slots, backward_slots = forward_slots.T, backward_slots.T
    slots = pltpu.SMEM(backward_slots.shape, jnp.int32)
    near0, far0, notes = call(
        functools.partial(pack_kernel, (two, one)),
        (like(two + one, width, BF16), like(two + one, width, BF16), jax.ShapeDtypeStruct((8,), jnp.int32)),
        [lengths, lengths, slots, slots, pltpu.SemaphoreType.DMA((8,))],
        (saved, grad_in, backward_lengths, forward_lengths, backward_slots, forward_slots),
        0, [HBM] * 6, (VMEM, VMEM, SMEM), FULL,
    )
    near0, far0 = swapped(near0, far0)
    tap_back = np.concatenate([from_freq(size, np.arange(tap_count) - half), np.zeros((1, size))], axis=0)
    m_table = stacked(to_freq(size, span(two, own)))
    q_table = tap_freq(size, tap_count)
    c_table = stacked(from_freq(size, span(one, own)))
    go_table = beside(to_freq(size, np.arange(own)))
    t_table = stacked(tap_back)

    def run(kernel, outs, scratch, operands, micros=0, after=None):
        return call(kernel, outs, scratch, [jnp.asarray(x) for x in operands], micros, after=after)

    rows = [pltpu.VMEM((own, width), F32)] + [pltpu.VMEM((own, LANES), F32)] * 2
    layer = like(own, width, BF16), like(own, LANES, F32), like(own, LANES, F32), like(size, width, F32)
    weights, later, near1, far1, *layer0 = run(
        functools.partial(prepare_kernel, two),
        (
            jax.ShapeDtypeStruct((kernels.shape[1], tap_count + 1, width), BF16), like(tap_count + 1, width, BF16),
            like(2 * two, width, BF16), like(2 * two, width, BF16), *layer,
        ),
        [],
        [notes, kernels[0].transpose(1, 0, 2), norm_gains[0], saved, act, q_table],
        0,
    )
    near1, far1 = swapped(near1, far1)
    g_table, x_table = stacked(to_freq(size, span(one, own))), stacked(from_freq(size, span(0, own)))
    grad_mid, near2, far2, halo0, inner0, gain0 = run(
        functools.partial(first_backward_kernel, two),
        (
            like(own + tap_count + 1, width, BF16), like(one, width, BF16), like(one, width, BF16),
            like(2 * two, width, BF16), like(own, width, BF16), like(1, width, F32),
        ),
        [pltpu.VMEM((2, two, width), BF16), pltpu.VMEM((2, one, width), BF16), *rows],
        [
            notes, saved, near0, far0, grad, weights, later, *layer0,
            m_table, c_table, g_table, x_table,
        ],
        4,
    )
    grad_mid = shifted(grad_mid, -1)
    near2, far2 = swapped(near2, far2, -1)
    halo_scratch = [
        pltpu.VMEM((2 * two, width), BF16), pltpu.VMEM((2, two, width), BF16), pltpu.VMEM((own, width), BF16)
    ]
    between = run(
        functools.partial(first_forward_kernel, two),
        like(small, width, BF16),
        halo_scratch,
        [notes, act, near1, far1, weights, m_table, q_table, c_table],
        20,
    )
    act_ahead = run(
        second_forward_kernel,
        like(own, width, BF16),
        [pltpu.VMEM((small, width), BF16)],
        [
            notes, between, grad_mid,
            stacked(to_freq(small, span(one, own))), tap_freq(small, tap_count), stacked(from_freq(small, span(0, own))),
        ],
        3,
    )
    act_out = shifted(act_ahead, 2)
    taps0 = run(
        first_taps_kernel, like(tap_count + 1, width, BF16), [],
        [halo0, layer0[0], inner0, gain0, m_table, go_table, t_table],
        0,
        act_ahead,
    )
    m1, q1, factor1, conv1, mean1, inverse1 = run(
        functools.partial(second_ready_kernel, two),
        (
            like(size, width, F32), like(size, width, F32), like(small, width, F32), like(own, width, F32),
            like(own, LANES, F32), like(own, LANES, F32),
        ),
        halo_scratch,
        [notes, saved, near1, far1, weights, m_table, q_table, c_table],
        3,
        act_ahead,
    )

    def partner(x, step):
        return lax.ppermute(x, "tm", [(i, i ^ step) for i in range(shards)])

    other0 = partner(taps0, 1)
    mixed1, taps1 = run(
        second_taps_kernel,
        (like(small, width, BF16), like(tap_count + 1, width, BF16)),
        [pltpu.VMEM((2, one, width), BF16)],
        [notes, grad_mid, near2, far2, weights, m1, factor1, conv1, go_table, t_table],
        2,
    )
    grad_out = run(
        second_backward_kernel,
        like(own, width, BF16),
        rows,
        [
            notes, saved, grad_mid, weights, mixed1, q1, mean1, inverse1,
            g_table, x_table,
        ],
        6,
    )
    grad_out = shifted(grad_out, -1)
    other1 = partner(taps1, 1)
    mine = call(below_kernel, like(2 * (tap_count + 1), width, BF16), [], (taps0, other0, taps1, other1), 6)
    step = 2
    while True:
        other = partner(mine, step)
        step *= 2
        if step >= shards:
            break
        mine = call(add_kernel, like(*mine.shape, BF16), [], (mine, other), 0)
    slots = kernels.shape[1]
    act_out, grad_out, taps, gains = call(
        final_kernel,
        (
            like(own, width, BF16), like(own, width, BF16),
            jax.ShapeDtypeStruct((tap_count, slots, width), F32), like(slots, width, F32),
        ),
        [pltpu.SemaphoreType.DMA((2,))],
        (notes, mine, other, act_out, grad_out),
        0, [SMEM] + [VMEM] * 2 + [ANY] * 2, (ANY, ANY, VMEM, VMEM),
    )
    return act_out[None], grad_out[None], taps.transpose(1, 0, 2)[None], gains[None]


def solution(mesh):
    in_specs = (
        P("section", "tm", None),
        P("section", "tm", None),
        P("section", None, "tm", None),
        P("section", None, None, None),
        P("section", None, None),
        P(),
        P(),
        P(),
        P(),
    )
    out_specs = (
        P("section", "tm", None),
        P("section", "tm", None),
        P("section", None, None, None),
        P("section", None, None),
    )
    return jax.shard_map(local, mesh=mesh, in_specs=in_specs, out_specs=out_specs, check_vma=False)
```

```python
import functools

import jax
import jax.numpy as jnp
import ml_dtypes
import numpy as np
from jax import lax
from jax.experimental import pallas as pl
from jax.experimental.pallas import tpu as pltpu
from jax.sharding import PartitionSpec as P

epsilon = 1e-05
BLOCK = 1024
LANES = 128
F32 = jnp.float32
BF16 = jnp.bfloat16


def split(matrix):
    high = matrix.astype(ml_dtypes.bfloat16)
    low = (matrix - high.astype(np.float64)).astype(ml_dtypes.bfloat16)
    return high, low


def angles(size, times):
    return 2.0 * np.pi / size * np.outer(np.arange(size // 2) + 0.5, np.asarray(times, np.float64))


def to_freq(size, times):
    phase = angles(size, times)
    return np.concatenate([np.cos(phase), -np.sin(phase)], axis=0)


def from_freq(size, times):
    phase = angles(size, times).T
    return 2.0 / size * np.concatenate([np.cos(phase), -np.sin(phase)], axis=1)


def stacked(matrix):
    return np.concatenate(split(matrix), axis=0)


def beside(matrix):
    return np.concatenate(split(matrix), axis=1)


def tap_freq(size, taps):
    phase = angles(size, np.arange(taps) - (taps - 1) // 2)
    table = np.concatenate([np.cos(phase), np.sin(phase)], axis=0)
    return beside(np.concatenate([table, np.zeros((size, 1))], axis=1))


def dot(a, b):
    return jnp.dot(a, b, preferred_element_type=F32)


def transform(table, values):
    return sum(halves(dot(table[...], values.astype(BF16))))


def halves(values):
    half = values.shape[0] // 2
    return values[:half], values[half:]


def product(a, b):
    ar, ai = halves(a)
    br, bi = halves(b)
    return jnp.concatenate([ar * br - ai * bi, ar * bi + ai * br], axis=0)


def product_conj(a, b):
    ar, ai = halves(a)
    br, bi = halves(b)
    return jnp.concatenate([ar * br + ai * bi, ai * br - ar * bi], axis=0)


def sigmoid(values):
    return 0.5 * jnp.tanh(0.5 * values) + 0.5


def wide(stat, count):
    return jnp.concatenate([stat] * (count // LANES), axis=1)


def norm_rows(ref, start, count, at, gain, first, length, masked_ref, mean_ref, inverse_ref):
    width = masked_ref.shape[1]
    rows = pl.ds(start, count)
    tiles = [pl.ds(i * LANES, LANES) for i in range(width // LANES)]

    def values(tile):
        return ref[rows, tile].astype(F32)

    total = values(tiles[0])
    for tile in tiles[1:]:
        total = total + values(tile)
    mean = jnp.sum(total, axis=1, keepdims=True) * (1.0 / width)
    mean = jnp.broadcast_to(mean, (count, LANES))
    square = jnp.zeros((count, LANES), F32)
    for tile in tiles:
        center = values(tile) - mean
        square = square + center * center
    var = jnp.sum(square, axis=1, keepdims=True) * (1.0 / width)
    inverse = jnp.broadcast_to(lax.rsqrt(var + epsilon), (count, LANES))
    frame = first + at + lax.broadcasted_iota(jnp.int32, (count, LANES), 0)
    mask = ((frame >= 0) & (frame < length)).astype(F32)
    scale = mask * inverse
    out = pl.ds(at, count)
    for tile in tiles:
        masked_ref[out, tile] = ((values(tile) - mean) * scale * gain(tile)).astype(BF16)
    if mean_ref is not None:
        mean_ref[out, :] = mean
        inverse_ref[out, :] = inverse


def norm_pieces(pieces, gain, first, length, masked_ref, mean_ref=None, inverse_ref=None, chunk=128):
    at = 0
    for ref, start, count in pieces:
        for begin in range(0, count, chunk):
            norm_rows(
                ref, start + begin, min(chunk, count - begin), at + begin,
                gain, first, length, masked_ref, mean_ref, inverse_ref,
            )
        at += count


def window(pieces, columns):
    parts = [ref[pl.ds(start, count), columns] for ref, start, count in pieces]
    return parts[0] if len(parts) == 1 else jnp.concatenate(parts, axis=0)


def each_block(width, body):
    for begin in range(0, width, BLOCK):
        body(pl.ds(begin, BLOCK))


def tap_spectrum(table, weights):
    return dot(table, jnp.concatenate([weights, weights], axis=0))


def gate_factor(conv):
    gate = sigmoid(conv)
    return gate * (1.0 + conv * (1.0 - gate))


FIRST, BACK0, BACK1, AHEAD0 = range(0, 8, 2)


def looked_up(notes, layer):
    return notes[layer], notes[layer + 1], notes[FIRST]


def sorted_halos(near, far, at, halos):
    even = lax.rem(lax.axis_index("tm") + 1, 2)
    rows = pl.ds(at, halos.shape[1])
    halos[even] = near[rows, :]
    halos[1 - even] = far[rows, :]
    return halos.at[0], halos.at[1]


def lane_sum(values):
    total = values[:, :LANES]
    for lane in range(LANES, values.shape[1], LANES):
        total = total + values[:, lane : lane + LANES]
    return total


def first_pass(pieces, mean, inverse, gain, mask, tables, mixed, q, columns, scaled, sum_a, sum_b):
    g_table, x_table = tables
    grad_masked = wide(mask, BLOCK) * transform(x_table, product_conj(transform(g_table, mixed), q))
    centered = window(pieces, columns).astype(F32) - wide(mean[...], BLOCK)
    weighted = grad_masked * (centered * wide(inverse[...], BLOCK))
    gain = gain(columns)
    by_gain = grad_masked * gain
    scaled[:, columns] = by_gain
    sum_a[...] += lane_sum(by_gain)
    sum_b[...] += lane_sum(weighted * gain)
    return weighted


def last_pass(grad_pieces, pieces, mean, inverse, scaled, sum_a, sum_b, grad_x, chunk=128):
    width = scaled.shape[1]
    at = 0
    for (ref, start, count), (saved, base, _) in zip(grad_pieces, pieces):
        for begin in range(0, count, chunk):
            here = min(chunk, count - begin)
            rows = pl.ds(at + begin, here)
            inv = inverse[rows, :]
            mean_a = jnp.sum(sum_a[rows, :], axis=1, keepdims=True) * (1.0 / width)
            mean_b = jnp.sum(sum_b[rows, :], axis=1, keepdims=True) * (1.0 / width)
            slope = inv * jnp.broadcast_to(mean_b, (here, LANES)) * inv
            fixed = inv * jnp.broadcast_to(mean_a, (here, LANES)) - slope * mean[rows, :]
            for lane in range(0, width, LANES):
                tile = pl.ds(lane, LANES)
                x = saved[pl.ds(base + begin, here), tile].astype(F32)
                change = inv * scaled[rows, tile] - fixed - slope * x
                grad_x[rows, tile] = (ref[pl.ds(start + begin, here), tile].astype(F32) + change).astype(BF16)
        at += count


def frame_mask(rows, first, length):
    frame = first + lax.broadcasted_iota(jnp.int32, (rows, LANES), 0)
    return ((frame >= 0) & (frame < length)).astype(F32)


def slot_row(weights, slot):
    last = weights.shape[1] - 1
    return lambda columns: weights[slot, last : last + 1, columns].astype(F32)


def prepare_kernel(
    reach, notes, kernels, gains, saved, act, weights, later, near, far, masked, mean, inverse
):
    own, width = act.shape
    for even in range(2):

        @pl.when(lax.rem(lax.axis_index("tm") + 1, 2) == even)
        def _():
            for x, at in ((saved.at[1], 0), (act, reach)):
                tail, head = (near, far) if even else (far, near)
                tail[pl.ds(at, reach), :] = x[pl.ds(own - reach, reach), :]
                head[pl.ds(at, reach), :] = x[pl.ds(0, reach), :]

    count = kernels.shape[0]
    for slot in range(kernels.shape[1]):
        weights[slot, :count, :] = kernels[:, slot, :]
        weights[slot, count:, :] = gains[slot : slot + 1, :]
    later[...] = weights[notes[FIRST + 1]]
    slot, length, first = looked_up(notes, BACK0)
    norm_pieces([(saved.at[0], 0, own)], slot_row(weights, slot), first, length, masked, mean, inverse)


def norm_halo(left, right, own, gain, first, length, halo):
    reach = left.shape[0]
    norm_pieces([(left, 0, reach)], gain, first - reach, length, halo)
    norm_pieces([(right, 0, reach)], gain, first + own, length, halo.at[pl.ds(reach, reach)])


def joined(halo, own, columns):
    reach = halo.shape[0] // 2
    return jnp.concatenate([halo[:reach, columns], own[:, columns], halo[reach:, columns]], axis=0)


def first_backward_kernel(
    reach, notes, saved, far, near, grads, weights, later, masked, mean, inverse,
    m_table, q_table, c_table, g_table, x_table,
    grad_x, near_edge, far_edge, halo, inner, gain_sum, halos, grad_halos, scaled, sum_a, sum_b,
):
    own, width = grads.shape
    edge = near_edge.shape[0]
    slot, length, first = looked_up(notes, BACK0)
    gain = slot_row(weights, slot)
    left, right = sorted_halos(near, far, 0, halos)
    grad_left, grad_right = sorted_halos(near, far, reach, grad_halos)
    norm_halo(left, right, own, gain, first, length, halo)
    grad_pieces = [(grad_left, 0, edge), (grads, 0, own), (grad_right, 0, edge)]
    pieces = [(saved.at[0], 0, own)]
    mask = frame_mask(own, first, length)
    sum_a[...] = jnp.zeros_like(sum_a)
    sum_b[...] = jnp.zeros_like(sum_b)
    grad_x[pl.ds(own, later.shape[0]), :] = later[...]

    def block(columns):
        m = transform(m_table, joined(halo, masked, columns))
        q = tap_spectrum(q_table[...], weights[slot, :, columns])
        conv = transform(c_table, product(m, q))
        mixed = (window(grad_pieces, columns).astype(F32) * gate_factor(conv)).astype(BF16)
        inner[:, columns] = mixed[edge : edge + own]
        weighted = first_pass(
            pieces, mean, inverse, gain, mask, (g_table, x_table), mixed, q, columns, scaled, sum_a, sum_b
        )
        gain_sum[:, columns] = jnp.sum(weighted, axis=0, keepdims=True)

    each_block(width, block)
    last_pass([(grads, 0, own)], pieces, mean, inverse, scaled, sum_a, sum_b, grad_x)
    for even in range(2):

        @pl.when(lax.rem(lax.axis_index("tm") + 1, 2) == even)
        def _():
            top, bottom = (far_edge, near_edge) if even else (near_edge, far_edge)
            top[...] = grad_x[pl.ds(0, edge), :]
            bottom[...] = grad_x[pl.ds(own - edge, edge), :]


def tap_term(go_table, t_table, m, mixed):
    g_own = dot(go_table[...], jnp.concatenate([mixed, mixed], axis=0))
    return transform(t_table, product_conj(m, g_own))


def put_taps(taps, tap, gain_sum, columns):
    row = lax.broadcasted_iota(jnp.int32, tap.shape, 0)
    taps[:, columns] = jnp.where(row == tap.shape[0] - 1, gain_sum, tap).astype(taps.dtype)


def first_taps_kernel(halo, masked, inner, gain_sum, m_table, go_table, t_table, taps):
    def block(columns):
        m = transform(m_table, joined(halo, masked, columns))
        put_taps(taps, tap_term(go_table, t_table, m, inner[:, columns]), gain_sum[:, columns], columns)

    each_block(masked.shape[1], block)


def added(mine, other):
    return (mine[...].astype(F32) + other[...].astype(F32)).astype(BF16)


def add_kernel(mine, other, out):
    out[...] = added(mine, other)


def below_kernel(mine0, other0, mine1, other1, out):
    count = mine0.shape[0]
    out[pl.ds(0, count), :] = added(mine0, other0)
    out[pl.ds(count, count), :] = added(mine1, other1)


def second_ready_kernel(
    reach, notes, saved, far, near, weights, m_table, q_table, c_table,
    m_out, q_out, factor, conv_out, mean, inverse, halo, halos, masked,
):
    own, width = masked.shape
    slot, length, first = looked_up(notes, BACK1)
    gain = slot_row(weights, slot)
    left, right = sorted_halos(near, far, 0, halos)
    norm_pieces([(saved.at[1], 0, own)], gain, first, length, masked, mean, inverse)
    norm_halo(left, right, own, gain, first, length, halo)

    def block(columns):
        m = transform(m_table, joined(halo, masked, columns))
        q = tap_spectrum(q_table[...], weights[slot, :, columns])
        conv = transform(c_table, product(m, q))
        m_out[:, columns] = m
        q_out[:, columns] = q
        factor[:, columns] = gate_factor(conv)
        edge = (conv.shape[0] - own) // 2
        conv_out[:, columns] = conv[edge : edge + own]

    each_block(width, block)


def second_taps_kernel(
    notes, received, far, near, weights, m, factor, conv, go_table, t_table, mixed_out, taps, halos
):
    own, width = conv.shape
    rows = factor.shape[0]
    edge = (rows - own) // 2
    gain = slot_row(weights, notes[BACK1])
    left, right = sorted_halos(near, far, 0, halos)
    pieces = [(left, 0, edge), (received, 0, own), (right, 0, edge)]

    def block(columns):
        mixed = (window(pieces, columns).astype(F32) * factor[:, columns]).astype(BF16)
        mixed_out[:, columns] = mixed
        inner = mixed[edge : edge + own]
        gain_sum = jnp.sum(inner.astype(F32) * conv[:, columns], axis=0, keepdims=True) / gain(columns)
        put_taps(taps, tap_term(go_table, t_table, m[:, columns], inner), gain_sum, columns)

    each_block(width, block)


def second_backward_kernel(
    notes, saved, received, weights, mixed, q, mean, inverse, g_table, x_table, grad_x, scaled, sum_a, sum_b
):
    own, width = grad_x.shape
    slot, length, first = looked_up(notes, BACK1)
    pieces = [(saved.at[1], 0, own)]
    mask = frame_mask(own, first, length)
    sum_a[...] = jnp.zeros_like(sum_a)
    sum_b[...] = jnp.zeros_like(sum_b)

    def block(columns):
        first_pass(
            pieces, mean, inverse, slot_row(weights, slot), mask, (g_table, x_table), mixed[:, columns], q[:, columns],
            columns, scaled, sum_a, sum_b,
        )

    each_block(width, block)
    last_pass([(received, 0, own)], pieces, mean, inverse, scaled, sum_a, sum_b, grad_x)


def first_forward_kernel(reach, notes, act, far, near, weights, m_table, q_table, c_table, out, halo, halos, masked):
    own, width = act.shape
    middle = reach // 2
    slot, length, first = looked_up(notes, AHEAD0)
    gain = slot_row(weights, slot)
    left, right = sorted_halos(near, far, reach, halos)
    inner = [(left, middle, middle), (act, 0, own), (right, 0, middle)]
    norm_pieces([(act, 0, own)], gain, first, length, masked)
    norm_halo(left, right, own, gain, first, length, halo)

    def block(columns):
        q = tap_spectrum(q_table[...], weights[slot, :, columns])
        conv = transform(c_table, product(transform(m_table, joined(halo, masked, columns)), q))
        out[:, columns] = (window(inner, columns).astype(F32) + conv * sigmoid(conv)).astype(BF16)

    each_block(width, block)


def second_forward_kernel(notes, between, received, m_table, q_table, c_table, out, masked):
    own, width = out.shape
    rows = between.shape[0]
    edge = (rows - own) // 2
    slot, length, first = looked_up(notes, AHEAD0)
    last = received.shape[0] - 1

    def gain(columns):
        return received[last : last + 1, columns].astype(F32)

    norm_pieces([(between, 0, rows)], gain, first - edge, length, masked, chunk=rows // 2)

    def block(columns):
        q = tap_spectrum(q_table[...], received[own:, columns])
        conv = transform(c_table, product(transform(m_table, masked[:, columns]), q))
        out[:, columns] = (between[edge : edge + own, columns].astype(F32) + conv * sigmoid(conv)).astype(BF16)

    each_block(width, block)


def pack_kernel(
    reaches, saved, grad, back_lengths, ahead_lengths, back_slots, ahead_slots,
    near, far, notes, back_len, ahead_len, back_slot, ahead_slot, sems,
):
    own = grad.shape[1]
    even = lax.rem(lax.axis_index("tm") + 1, 2)
    copies = []
    at = 0
    for x, reach in zip((saved, grad), reaches):
        for out, tail in ((near, even), (far, 1 - even)):
            start = pl.multiple_of(tail * (own - reach), 16)
            copies.append((x.at[0, pl.ds(start, reach)], out.at[pl.ds(at, reach)]))
        at += reach
    small = [(back_lengths, back_len), (ahead_lengths, ahead_len), (back_slots, back_slot), (ahead_slots, ahead_slot)]
    copies = [pltpu.make_async_copy(a, b, sems.at[k]) for k, (a, b) in enumerate(small + copies)]
    for copy in copies:
        copy.start()
    for copy in copies:
        copy.wait()
    section, sections = lax.axis_index("section"), lax.axis_size("section")
    notes[FIRST] = lax.axis_index("tm") * own
    notes[FIRST + 1] = ahead_slot[1, section]
    notes[BACK0] = back_slot[0, section]
    notes[BACK0 + 1] = back_len[section]
    notes[BACK1] = back_slot[1, section]
    notes[BACK1 + 1] = back_len[lax.rem(section + 1, sections)]
    notes[AHEAD0] = ahead_slot[0, section]
    notes[AHEAD0 + 1] = ahead_len[section]


def final_kernel(notes, mine, other, act, grad, act_out, grad_out, taps, gains, sems):
    copies = [
        pltpu.make_async_copy(act, act_out, sems.at[0]),
        pltpu.make_async_copy(grad, grad_out, sems.at[1]),
    ]
    for copy in copies:
        copy.start()
    count = taps.shape[0]
    total = mine[...].astype(F32) + other[...].astype(F32)
    ticks = total[: count + 1], total[count + 1 :]
    for slot in range(taps.shape[1]):
        use = [(notes[layer] == slot).astype(F32) for layer in (BACK0, BACK1)]
        both = use[0] * ticks[0] + use[1] * ticks[1]
        taps[:, slot, :] = both[:count]
        gains[slot : slot + 1, :] = both[count:]
    for copy in copies:
        copy.wait()


def span(reach, own):
    return np.arange(-reach, own + reach)


VMEM = pl.BlockSpec(memory_space=pltpu.VMEM)
SMEM = pl.BlockSpec(memory_space=pltpu.SMEM)
ANY = pl.BlockSpec(memory_space=pl.ANY)
HBM = pl.BlockSpec(memory_space=pltpu.HBM)
LIMIT = 24 * 1024 * 1024
FULL = 127 * 512 * 1024


def call(kernel, outs, scratch, operands, micros, specs=None, out_specs=None, limit=LIMIT, after=None):
    if specs is None:
        specs = [SMEM if x.dtype == jnp.int32 else VMEM for x in operands]
    if after is not None:
        operands, specs = [*operands, after], [*specs, ANY]
        inner, place = kernel, len(operands) - 1

        def kernel(*refs):
            return inner(*refs[:place], *refs[place + 1 :])

    return pl.pallas_call(
        kernel,
        out_shape=outs,
        in_specs=specs,
        out_specs=jax.tree.map(lambda _: VMEM, outs) if out_specs is None else out_specs,
        scratch_shapes=scratch,
        compiler_params=pltpu.CompilerParams(vmem_limit_bytes=limit),
        cost_estimate=pl.CostEstimate(flops=int(micros * 1e9), bytes_accessed=0, transcendentals=0),
    )(*operands)


def like(rows, width, dtype):
    return jax.ShapeDtypeStruct((rows, width), dtype)


def up16(count):
    return -(-count // 16) * 16


def local(
    act_in, grad_in, saved_inputs, kernels, norm_gains,
    forward_lengths, backward_lengths, forward_slots, backward_slots,
):
    sections = lax.axis_size("section")
    shards = lax.axis_size("tm")
    act, grad, saved = act_in[0], grad_in[0], saved_inputs[0]
    own, width = act.shape
    tap_count = kernels.shape[2]
    half = (tap_count - 1) // 2
    one, two = up16(half), up16(2 * half)
    size, small = own + 2 * two, own + 2 * one

    def shifted(x, by):
        return lax.ppermute(x, "section", [(i, (i + by) % sections) for i in range(sections)])

    def swapped(near, far, by=0):
        results = []
        for x, begin in ((far, 1), (near, 0)):
            pairs = [(i, i + 1) for i in range(begin, shards - 1, 2)]
            pairs = [
                (s * shards + i, (s + by) % sections * shards + j)
                for s in range(sections)
                for a, b in pairs
                for i, j in ((a, b), (b, a))
            ]
            results.append(lax.ppermute(x, ("section", "tm"), pairs))
        return results[::-1]

    lengths = pltpu.SMEM(backward_lengths.shape, jnp.int32)
    forward_slots, backward_slots = forward_slots.T, backward_slots.T
    slots = pltpu.SMEM(backward_slots.shape, jnp.int32)
    near0, far0, notes = call(
        functools.partial(pack_kernel, (two, one)),
        (like(two + one, width, BF16), like(two + one, width, BF16), jax.ShapeDtypeStruct((8,), jnp.int32)),
        [lengths, lengths, slots, slots, pltpu.SemaphoreType.DMA((8,))],
        (saved, grad_in, backward_lengths, forward_lengths, backward_slots, forward_slots),
        0, [HBM] * 6, (VMEM, VMEM, SMEM), FULL,
    )
    near0, far0 = swapped(near0, far0)
    tap_back = np.concatenate([from_freq(size, np.arange(tap_count) - half), np.zeros((1, size))], axis=0)
    m_table = stacked(to_freq(size, span(two, own)))
    q_table = tap_freq(size, tap_count)
    c_table = stacked(from_freq(size, span(one, own)))
    go_table = beside(to_freq(size, np.arange(own)))
    t_table = stacked(tap_back)

    def run(kernel, outs, scratch, operands, micros=0, after=None):
        return call(kernel, outs, scratch, [jnp.asarray(x) for x in operands], micros, after=after)

    rows = [pltpu.VMEM((own, width), F32)] + [pltpu.VMEM((own, LANES), F32)] * 2
    layer = like(own, width, BF16), like(own, LANES, F32), like(own, LANES, F32)
    weights, later, near1, far1, *layer0 = run(
        functools.partial(prepare_kernel, two),
        (
            jax.ShapeDtypeStruct((kernels.shape[1], tap_count + 1, width), BF16), like(tap_count + 1, width, BF16),
            like(2 * two, width, BF16), like(2 * two, width, BF16), *layer,
        ),
        [],
        [notes, kernels[0].transpose(1, 0, 2), norm_gains[0], saved, act],
        0,
    )
    near1, far1 = swapped(near1, far1)
    g_table, x_table = stacked(to_freq(size, span(one, own))), stacked(from_freq(size, span(0, own)))
    grad_mid, near2, far2, halo0, inner0, gain0 = run(
        functools.partial(first_backward_kernel, two),
        (
            like(own + tap_count + 1, width, BF16), like(one, width, BF16), like(one, width, BF16),
            like(2 * two, width, BF16), like(own, width, BF16), like(1, width, F32),
        ),
        [pltpu.VMEM((2, two, width), BF16), pltpu.VMEM((2, one, width), BF16), *rows],
        [
            notes, saved, far0, near0, grad, weights, later, *layer0,
            m_table, q_table, c_table, g_table, x_table,
        ],
        4,
    )
    grad_mid = shifted(grad_mid, -1)
    near2, far2 = swapped(near2, far2, -1)
    taps0 = run(
        first_taps_kernel, like(tap_count + 1, width, BF16), [],
        [halo0, layer0[0], inner0, gain0, m_table, go_table, t_table],
        0,
    )
    halo_scratch = [
        pltpu.VMEM((2 * two, width), BF16), pltpu.VMEM((2, two, width), BF16), pltpu.VMEM((own, width), BF16)
    ]
    between = run(
        functools.partial(first_forward_kernel, two),
        like(small, width, BF16),
        halo_scratch,
        [notes, act, far1, near1, weights, m_table, q_table, c_table],
        20,
        taps0,
    )
    act_ahead = run(
        second_forward_kernel,
        like(own, width, BF16),
        [pltpu.VMEM((small, width), BF16)],
        [
            notes, between, grad_mid,
            stacked(to_freq(small, span(one, own))), tap_freq(small, tap_count), stacked(from_freq(small, span(0, own))),
        ],
        3,
    )
    act_out = shifted(act_ahead, 2)
    m1, q1, factor1, conv1, mean1, inverse1 = run(
        functools.partial(second_ready_kernel, two),
        (
            like(size, width, F32), like(size, width, F32), like(small, width, F32), like(own, width, F32),
            like(own, LANES, F32), like(own, LANES, F32),
        ),
        halo_scratch,
        [notes, saved, far1, near1, weights, m_table, q_table, c_table],
        3,
        act_ahead,
    )

    def partner(x, step):
        return lax.ppermute(x, "tm", [(i, i ^ step) for i in range(shards)])

    other0 = partner(taps0, 1)
    mixed1, taps1 = run(
        second_taps_kernel,
        (like(small, width, BF16), like(tap_count + 1, width, BF16)),
        [pltpu.VMEM((2, one, width), BF16)],
        [notes, grad_mid, far2, near2, weights, m1, factor1, conv1, go_table, t_table],
        2,
    )
    grad_out = run(
        second_backward_kernel,
        like(own, width, BF16),
        rows,
        [
            notes, saved, grad_mid, weights, mixed1, q1, mean1, inverse1,
            g_table, x_table,
        ],
        6,
    )
    grad_out = shifted(grad_out, -1)
    other1 = partner(taps1, 1)
    mine = call(below_kernel, like(2 * (tap_count + 1), width, BF16), [], (taps0, other0, taps1, other1), 6)
    step = 2
    while True:
        other = partner(mine, step)
        step *= 2
        if step >= shards:
            break
        mine = call(add_kernel, like(*mine.shape, BF16), [], (mine, other), 0)
    slots = kernels.shape[1]
    act_out, grad_out, taps, gains = call(
        final_kernel,
        (
            like(own, width, BF16), like(own, width, BF16),
            jax.ShapeDtypeStruct((tap_count, slots, width), F32), like(slots, width, F32),
        ),
        [pltpu.SemaphoreType.DMA((2,))],
        (notes, mine, other, act_out, grad_out),
        0, [SMEM] + [VMEM] * 2 + [ANY] * 2, (ANY, ANY, VMEM, VMEM),
    )
    return act_out[None], grad_out[None], taps.transpose(1, 0, 2)[None], gains[None]


def solution(mesh):
    in_specs = (
        P("section", "tm", None),
        P("section", "tm", None),
        P("section", None, "tm", None),
        P("section", None, None, None),
        P("section", None, None),
        P(),
        P(),
        P(),
        P(),
    )
    out_specs = (
        P("section", "tm", None),
        P("section", "tm", None),
        P("section", None, None, None),
        P("section", None, None),
    )
    return jax.shard_map(local, mesh=mesh, in_specs=in_specs, out_specs=out_specs, check_vma=False)
```

```python
import functools

import jax
import jax.numpy as jnp
import ml_dtypes
import numpy as np
from jax import lax
from jax.experimental import pallas as pl
from jax.experimental.pallas import tpu as pltpu
from jax.sharding import PartitionSpec as P

epsilon = 1e-05
BLOCK = 2048
LANES = 128
F32 = jnp.float32
BF16 = jnp.bfloat16


def split(matrix):
    high = matrix.astype(ml_dtypes.bfloat16)
    low = (matrix - high.astype(np.float64)).astype(ml_dtypes.bfloat16)
    return high, low


def angles(size, times):
    return 2.0 * np.pi / size * np.outer(np.arange(size // 2) + 0.5, np.asarray(times, np.float64))


def to_freq(size, times):
    phase = angles(size, times)
    return np.concatenate([np.cos(phase), -np.sin(phase)], axis=0)


def from_freq(size, times):
    phase = angles(size, times).T
    return 2.0 / size * np.concatenate([np.cos(phase), -np.sin(phase)], axis=1)


def stacked(matrix):
    return np.concatenate(split(matrix), axis=0)


def beside(matrix):
    return np.concatenate(split(matrix), axis=1)


def tap_freq(size, taps):
    phase = angles(size, np.arange(taps) - (taps - 1) // 2)
    table = np.concatenate([np.cos(phase), np.sin(phase)], axis=0)
    return beside(np.concatenate([table, np.zeros((size, 1))], axis=1))


def dot(a, b):
    return jnp.dot(a, b, preferred_element_type=F32)


def transform(table, values):
    return sum(halves(dot(table[...], values.astype(BF16))))


def halves(values):
    half = values.shape[0] // 2
    return values[:half], values[half:]


def product(a, b):
    ar, ai = halves(a)
    br, bi = halves(b)
    return jnp.concatenate([ar * br - ai * bi, ar * bi + ai * br], axis=0)


def product_conj(a, b):
    ar, ai = halves(a)
    br, bi = halves(b)
    return jnp.concatenate([ar * br + ai * bi, ai * br - ar * bi], axis=0)


def sigmoid(values):
    return 0.5 * jnp.tanh(0.5 * values) + 0.5


def wide(stat, count):
    return jnp.concatenate([stat] * (count // LANES), axis=1)


def norm_rows(ref, start, count, at, gain, first, length, masked_ref, mean_ref, inverse_ref):
    width = masked_ref.shape[1]
    rows = pl.ds(start, count)
    tiles = [pl.ds(i * LANES, LANES) for i in range(width // LANES)]

    def values(tile):
        return ref[rows, tile].astype(F32)

    total = values(tiles[0])
    for tile in tiles[1:]:
        total = total + values(tile)
    mean = jnp.sum(total, axis=1, keepdims=True) * (1.0 / width)
    mean = jnp.broadcast_to(mean, (count, LANES))
    square = jnp.zeros((count, LANES), F32)
    for tile in tiles:
        center = values(tile) - mean
        square = square + center * center
    var = jnp.sum(square, axis=1, keepdims=True) * (1.0 / width)
    inverse = jnp.broadcast_to(lax.rsqrt(var + epsilon), (count, LANES))
    frame = first + at + lax.broadcasted_iota(jnp.int32, (count, LANES), 0)
    mask = ((frame >= 0) & (frame < length)).astype(F32)
    scale = mask * inverse
    out = pl.ds(at, count)
    for tile in tiles:
        masked_ref[out, tile] = ((values(tile) - mean) * scale * gain(tile)).astype(BF16)
    if mean_ref is not None:
        mean_ref[out, :] = mean
        inverse_ref[out, :] = inverse


def norm_pieces(pieces, gain, first, length, masked_ref, mean_ref=None, inverse_ref=None, chunk=128):
    at = 0
    for ref, start, count in pieces:
        for begin in range(0, count, chunk):
            norm_rows(
                ref, start + begin, min(chunk, count - begin), at + begin,
                gain, first, length, masked_ref, mean_ref, inverse_ref,
            )
        at += count


def window(pieces, columns):
    parts = [ref[pl.ds(start, count), columns] for ref, start, count in pieces]
    return parts[0] if len(parts) == 1 else jnp.concatenate(parts, axis=0)


def each_block(width, body):
    for begin in range(0, width, BLOCK):
        body(pl.ds(begin, BLOCK))


def tap_spectrum(table, weights):
    return dot(table, jnp.concatenate([weights, weights], axis=0))


def gate_factor(conv):
    gate = sigmoid(conv)
    return gate * (1.0 + conv * (1.0 - gate))


FIRST, BACK0, BACK1, AHEAD0 = range(0, 8, 2)


def looked_up(notes, layer):
    return notes[layer], notes[layer + 1], notes[FIRST]


def sorted_halos(near, far, at, halos):
    even = lax.rem(lax.axis_index("tm") + 1, 2)
    rows = pl.ds(at, halos.shape[1])
    halos[even] = near[rows, :]
    halos[1 - even] = far[rows, :]
    return halos.at[0], halos.at[1]


def lane_sum(values):
    total = values[:, :LANES]
    for lane in range(LANES, values.shape[1], LANES):
        total = total + values[:, lane : lane + LANES]
    return total


def first_pass(pieces, mean, inverse, gain, mask, tables, mixed, q, columns, scaled, sum_a, sum_b):
    g_table, x_table = tables
    grad_masked = wide(mask, BLOCK) * transform(x_table, product_conj(transform(g_table, mixed), q))
    centered = window(pieces, columns).astype(F32) - wide(mean[...], BLOCK)
    weighted = grad_masked * (centered * wide(inverse[...], BLOCK))
    gain = gain(columns)
    by_gain = grad_masked * gain
    scaled[:, columns] = by_gain
    sum_a[...] += lane_sum(by_gain)
    sum_b[...] += lane_sum(weighted * gain)
    return weighted


def last_pass(grad_pieces, pieces, mean, inverse, scaled, sum_a, sum_b, grad_x, chunk=128):
    width = scaled.shape[1]
    at = 0
    for (ref, start, count), (saved, base, _) in zip(grad_pieces, pieces):
        for begin in range(0, count, chunk):
            here = min(chunk, count - begin)
            rows = pl.ds(at + begin, here)
            inv = inverse[rows, :]
            mean_a = jnp.sum(sum_a[rows, :], axis=1, keepdims=True) * (1.0 / width)
            mean_b = jnp.sum(sum_b[rows, :], axis=1, keepdims=True) * (1.0 / width)
            slope = inv * jnp.broadcast_to(mean_b, (here, LANES)) * inv
            fixed = inv * jnp.broadcast_to(mean_a, (here, LANES)) - slope * mean[rows, :]
            for lane in range(0, width, LANES):
                tile = pl.ds(lane, LANES)
                x = saved[pl.ds(base + begin, here), tile].astype(F32)
                change = inv * scaled[rows, tile] - fixed - slope * x
                grad_x[rows, tile] = (ref[pl.ds(start + begin, here), tile].astype(F32) + change).astype(BF16)
        at += count


def frame_mask(rows, first, length):
    frame = first + lax.broadcasted_iota(jnp.int32, (rows, LANES), 0)
    return ((frame >= 0) & (frame < length)).astype(F32)


def slot_row(weights, slot):
    last = weights.shape[1] - 1
    return lambda columns: weights[slot, last : last + 1, columns].astype(F32)


def prepare_kernel(
    reach, notes, kernels, gains, saved, act, weights, later, near, far, masked, mean, inverse
):
    own, width = act.shape
    for even in range(2):

        @pl.when(lax.rem(lax.axis_index("tm") + 1, 2) == even)
        def _():
            for x, at in ((saved.at[1], 0), (act, reach)):
                tail, head = (near, far) if even else (far, near)
                tail[pl.ds(at, reach), :] = x[pl.ds(own - reach, reach), :]
                head[pl.ds(at, reach), :] = x[pl.ds(0, reach), :]

    count = kernels.shape[0]
    for slot in range(kernels.shape[1]):
        weights[slot, :count, :] = kernels[:, slot, :]
        weights[slot, count:, :] = gains[slot : slot + 1, :]
    later[...] = weights[notes[FIRST + 1]]
    slot, length, first = looked_up(notes, BACK0)
    norm_pieces([(saved.at[0], 0, own)], slot_row(weights, slot), first, length, masked, mean, inverse)


def prepare_later_kernel(notes, saved, act, weights, q_table, *outs):
    own, width = act.shape
    layers = ((saved.at[1], BACK1, outs[:4]), (act, AHEAD0, outs[4:]))
    for x, layer, (masked, mean, inverse, _) in layers:
        slot, length, first = looked_up(notes, layer)
        norm_pieces([(x, 0, own)], slot_row(weights, slot), first, length, masked, mean, inverse)
    for _, layer, (_, _, _, q) in layers:
        slot = notes[layer]

        def block(columns, slot=slot, q=q):
            q[:, columns] = tap_spectrum(q_table[...], weights[slot, :, columns])

        each_block(width, block)


def norm_halo(left, right, own, gain, first, length, halo):
    reach = left.shape[0]
    norm_pieces([(left, 0, reach)], gain, first - reach, length, halo)
    norm_pieces([(right, 0, reach)], gain, first + own, length, halo.at[pl.ds(reach, reach)])


def joined(halo, own, columns):
    reach = halo.shape[0] // 2
    return jnp.concatenate([halo[:reach, columns], own[:, columns], halo[reach:, columns]], axis=0)


def first_backward_kernel(
    reach, notes, saved, far, near, grads, weights, later, masked, mean, inverse,
    m_table, q_table, c_table, g_table, x_table,
    grad_x, near_edge, far_edge, halo, inner, gain_sum, halos, grad_halos, scaled, sum_a, sum_b,
):
    own, width = grads.shape
    edge = near_edge.shape[0]
    slot, length, first = looked_up(notes, BACK0)
    gain = slot_row(weights, slot)
    left, right = sorted_halos(near, far, 0, halos)
    grad_left, grad_right = sorted_halos(near, far, reach, grad_halos)
    norm_halo(left, right, own, gain, first, length, halo)
    grad_pieces = [(grad_left, 0, edge), (grads, 0, own), (grad_right, 0, edge)]
    pieces = [(saved.at[0], 0, own)]
    mask = frame_mask(own, first, length)
    sum_a[...] = jnp.zeros_like(sum_a)
    sum_b[...] = jnp.zeros_like(sum_b)
    grad_x[pl.ds(own, later.shape[0]), :] = later[...]

    def block(columns):
        m = transform(m_table, joined(halo, masked, columns))
        q = tap_spectrum(q_table[...], weights[slot, :, columns])
        conv = transform(c_table, product(m, q))
        mixed = (window(grad_pieces, columns).astype(F32) * gate_factor(conv)).astype(BF16)
        inner[:, columns] = mixed[edge : edge + own]
        weighted = first_pass(
            pieces, mean, inverse, gain, mask, (g_table, x_table), mixed, q, columns, scaled, sum_a, sum_b
        )
        gain_sum[:, columns] = jnp.sum(weighted, axis=0, keepdims=True)

    each_block(width, block)
    last_pass([(grads, 0, own)], pieces, mean, inverse, scaled, sum_a, sum_b, grad_x)
    for even in range(2):

        @pl.when(lax.rem(lax.axis_index("tm") + 1, 2) == even)
        def _():
            top, bottom = (far_edge, near_edge) if even else (near_edge, far_edge)
            top[...] = grad_x[pl.ds(0, edge), :]
            bottom[...] = grad_x[pl.ds(own - edge, edge), :]


def tap_term(go_table, t_table, m, mixed):
    g_own = dot(go_table[...], jnp.concatenate([mixed, mixed], axis=0))
    return transform(t_table, product_conj(m, g_own))


def put_taps(taps, tap, gain_sum, columns):
    row = lax.broadcasted_iota(jnp.int32, tap.shape, 0)
    taps[:, columns] = jnp.where(row == tap.shape[0] - 1, gain_sum, tap).astype(taps.dtype)


def first_taps_kernel(halo, masked, inner, gain_sum, m_table, go_table, t_table, taps):
    def block(columns):
        m = transform(m_table, joined(halo, masked, columns))
        put_taps(taps, tap_term(go_table, t_table, m, inner[:, columns]), gain_sum[:, columns], columns)

    each_block(masked.shape[1], block)


def added(mine, other):
    return (mine[...].astype(F32) + other[...].astype(F32)).astype(BF16)


def add_kernel(mine, other, out):
    out[...] = added(mine, other)


def below_kernel(mine0, other0, mine1, other1, out):
    count = mine0.shape[0]
    out[pl.ds(0, count), :] = added(mine0, other0)
    out[pl.ds(count, count), :] = added(mine1, other1)


def second_ready_kernel(
    reach, notes, far, near, weights, masked, q, m_table, c_table, m_out, factor, conv_out, halo, halos
):
    own, width = masked.shape
    slot, length, first = looked_up(notes, BACK1)
    left, right = sorted_halos(near, far, 0, halos)
    norm_halo(left, right, own, slot_row(weights, slot), first, length, halo)

    def block(columns):
        m = transform(m_table, joined(halo, masked, columns))
        conv = transform(c_table, product(m, q[:, columns]))
        m_out[:, columns] = m
        factor[:, columns] = gate_factor(conv)
        edge = (conv.shape[0] - own) // 2
        conv_out[:, columns] = conv[edge : edge + own]

    each_block(width, block)


def second_taps_kernel(
    notes, received, far, near, weights, m, factor, conv, go_table, t_table, mixed_out, taps, halos
):
    own, width = conv.shape
    rows = factor.shape[0]
    edge = (rows - own) // 2
    gain = slot_row(weights, notes[BACK1])
    left, right = sorted_halos(near, far, 0, halos)
    pieces = [(left, 0, edge), (received, 0, own), (right, 0, edge)]

    def block(columns):
        mixed = (window(pieces, columns).astype(F32) * factor[:, columns]).astype(BF16)
        mixed_out[:, columns] = mixed
        inner = mixed[edge : edge + own]
        gain_sum = jnp.sum(inner.astype(F32) * conv[:, columns], axis=0, keepdims=True) / gain(columns)
        put_taps(taps, tap_term(go_table, t_table, m[:, columns], inner), gain_sum, columns)

    each_block(width, block)


def second_backward_kernel(
    notes, saved, received, weights, mixed, q, mean, inverse, g_table, x_table, grad_x, scaled, sum_a, sum_b
):
    own, width = grad_x.shape
    slot, length, first = looked_up(notes, BACK1)
    pieces = [(saved.at[1], 0, own)]
    mask = frame_mask(own, first, length)
    sum_a[...] = jnp.zeros_like(sum_a)
    sum_b[...] = jnp.zeros_like(sum_b)

    def block(columns):
        first_pass(
            pieces, mean, inverse, slot_row(weights, slot), mask, (g_table, x_table), mixed[:, columns], q[:, columns],
            columns, scaled, sum_a, sum_b,
        )

    each_block(width, block)
    last_pass([(received, 0, own)], pieces, mean, inverse, scaled, sum_a, sum_b, grad_x)


def first_forward_kernel(reach, notes, act, far, near, weights, masked, q, m_table, c_table, out, halo, halos):
    own, width = act.shape
    middle = reach // 2
    slot, length, first = looked_up(notes, AHEAD0)
    left, right = sorted_halos(near, far, reach, halos)
    inner = [(left, middle, middle), (act, 0, own), (right, 0, middle)]
    norm_halo(left, right, own, slot_row(weights, slot), first, length, halo)

    def block(columns):
        conv = transform(c_table, product(transform(m_table, joined(halo, masked, columns)), q[:, columns]))
        out[:, columns] = (window(inner, columns).astype(F32) + conv * sigmoid(conv)).astype(BF16)

    each_block(width, block)


def second_forward_kernel(notes, between, received, m_table, q_table, c_table, out, masked):
    own, width = out.shape
    rows = between.shape[0]
    edge = (rows - own) // 2
    slot, length, first = looked_up(notes, AHEAD0)
    last = received.shape[0] - 1

    def gain(columns):
        return received[last : last + 1, columns].astype(F32)

    norm_pieces([(between, 0, rows)], gain, first - edge, length, masked, chunk=rows // 2)

    def block(columns):
        q = tap_spectrum(q_table[...], received[own:, columns])
        conv = transform(c_table, product(transform(m_table, masked[:, columns]), q))
        out[:, columns] = (between[edge : edge + own, columns].astype(F32) + conv * sigmoid(conv)).astype(BF16)

    each_block(width, block)


def pack_kernel(
    reaches, saved, grad, back_lengths, ahead_lengths, back_slots, ahead_slots,
    near, far, notes, back_len, ahead_len, back_slot, ahead_slot, sems,
):
    own = grad.shape[1]
    even = lax.rem(lax.axis_index("tm") + 1, 2)
    copies = []
    at = 0
    for x, reach in zip((saved, grad), reaches):
        for out, tail in ((near, even), (far, 1 - even)):
            start = pl.multiple_of(tail * (own - reach), 16)
            copies.append((x.at[0, pl.ds(start, reach)], out.at[pl.ds(at, reach)]))
        at += reach
    small = [(back_lengths, back_len), (ahead_lengths, ahead_len), (back_slots, back_slot), (ahead_slots, ahead_slot)]
    copies = [pltpu.make_async_copy(a, b, sems.at[k]) for k, (a, b) in enumerate(small + copies)]
    for copy in copies:
        copy.start()
    for copy in copies:
        copy.wait()
    section, sections = lax.axis_index("section"), lax.axis_size("section")
    notes[FIRST] = lax.axis_index("tm") * own
    notes[FIRST + 1] = ahead_slot[1, section]
    notes[BACK0] = back_slot[0, section]
    notes[BACK0 + 1] = back_len[section]
    notes[BACK1] = back_slot[1, section]
    notes[BACK1 + 1] = back_len[lax.rem(section + 1, sections)]
    notes[AHEAD0] = ahead_slot[0, section]
    notes[AHEAD0 + 1] = ahead_len[section]


def final_kernel(notes, mine, other, act, grad, act_out, grad_out, taps, gains, sems):
    copies = [
        pltpu.make_async_copy(act, act_out, sems.at[0]),
        pltpu.make_async_copy(grad, grad_out, sems.at[1]),
    ]
    for copy in copies:
        copy.start()
    count = taps.shape[0]
    total = mine[...].astype(F32) + other[...].astype(F32)
    ticks = total[: count + 1], total[count + 1 :]
    for slot in range(taps.shape[1]):
        use = [(notes[layer] == slot).astype(F32) for layer in (BACK0, BACK1)]
        both = use[0] * ticks[0] + use[1] * ticks[1]
        taps[:, slot, :] = both[:count]
        gains[slot : slot + 1, :] = both[count:]
    for copy in copies:
        copy.wait()


def span(reach, own):
    return np.arange(-reach, own + reach)


VMEM = pl.BlockSpec(memory_space=pltpu.VMEM)
SMEM = pl.BlockSpec(memory_space=pltpu.SMEM)
ANY = pl.BlockSpec(memory_space=pl.ANY)
HBM = pl.BlockSpec(memory_space=pltpu.HBM)
LIMIT = 24 * 1024 * 1024
FULL = 127 * 512 * 1024


def call(kernel, outs, scratch, operands, micros, specs=None, out_specs=None, limit=LIMIT, after=None):
    if specs is None:
        specs = [SMEM if x.dtype == jnp.int32 else VMEM for x in operands]
    if after is not None:
        operands, specs = [*operands, after], [*specs, ANY]
        inner, place = kernel, len(operands) - 1

        def kernel(*refs):
            return inner(*refs[:place], *refs[place + 1 :])

    return pl.pallas_call(
        kernel,
        out_shape=outs,
        in_specs=specs,
        out_specs=jax.tree.map(lambda _: VMEM, outs) if out_specs is None else out_specs,
        scratch_shapes=scratch,
        compiler_params=pltpu.CompilerParams(vmem_limit_bytes=limit),
        cost_estimate=pl.CostEstimate(flops=int(micros * 1e9), bytes_accessed=0, transcendentals=0),
    )(*operands)


def like(rows, width, dtype):
    return jax.ShapeDtypeStruct((rows, width), dtype)


def up16(count):
    return -(-count // 16) * 16


def local(
    act_in, grad_in, saved_inputs, kernels, norm_gains,
    forward_lengths, backward_lengths, forward_slots, backward_slots,
):
    sections = lax.axis_size("section")
    shards = lax.axis_size("tm")
    act, grad, saved = act_in[0], grad_in[0], saved_inputs[0]
    own, width = act.shape
    tap_count = kernels.shape[2]
    half = (tap_count - 1) // 2
    one, two = up16(half), up16(2 * half)
    size, small = own + 2 * two, own + 2 * one

    def shifted(x, by):
        return lax.ppermute(x, "section", [(i, (i + by) % sections) for i in range(sections)])

    def swapped(near, far, by=0):
        results = []
        for x, begin in ((far, 1), (near, 0)):
            pairs = [(i, i + 1) for i in range(begin, shards - 1, 2)]
            pairs = [
                (s * shards + i, (s + by) % sections * shards + j)
                for s in range(sections)
                for a, b in pairs
                for i, j in ((a, b), (b, a))
            ]
            results.append(lax.ppermute(x, ("section", "tm"), pairs))
        return results[::-1]

    lengths = pltpu.SMEM(backward_lengths.shape, jnp.int32)
    forward_slots, backward_slots = forward_slots.T, backward_slots.T
    slots = pltpu.SMEM(backward_slots.shape, jnp.int32)
    near0, far0, notes = call(
        functools.partial(pack_kernel, (two, one)),
        (like(two + one, width, BF16), like(two + one, width, BF16), jax.ShapeDtypeStruct((8,), jnp.int32)),
        [lengths, lengths, slots, slots, pltpu.SemaphoreType.DMA((8,))],
        (saved, grad_in, backward_lengths, forward_lengths, backward_slots, forward_slots),
        0, [HBM] * 6, (VMEM, VMEM, SMEM), FULL,
    )
    near0, far0 = swapped(near0, far0)
    tap_back = np.concatenate([from_freq(size, np.arange(tap_count) - half), np.zeros((1, size))], axis=0)
    m_table = stacked(to_freq(size, span(two, own)))
    q_table = tap_freq(size, tap_count)
    c_table = stacked(from_freq(size, span(one, own)))
    go_table = beside(to_freq(size, np.arange(own)))
    t_table = stacked(tap_back)

    def run(kernel, outs, scratch, operands, micros=0, after=None):
        return call(kernel, outs, scratch, [jnp.asarray(x) for x in operands], micros, after=after)

    rows = [pltpu.VMEM((own, width), F32)] + [pltpu.VMEM((own, LANES), F32)] * 2
    layer = like(own, width, BF16), like(own, LANES, F32), like(own, LANES, F32)
    weights, later, near1, far1, *layer0 = run(
        functools.partial(prepare_kernel, two),
        (
            jax.ShapeDtypeStruct((kernels.shape[1], tap_count + 1, width), BF16), like(tap_count + 1, width, BF16),
            like(2 * two, width, BF16), like(2 * two, width, BF16), *layer,
        ),
        [],
        [notes, kernels[0].transpose(1, 0, 2), norm_gains[0], saved, act],
        0,
    )
    near1, far1 = swapped(near1, far1)
    g_table, x_table = stacked(to_freq(size, span(one, own))), stacked(from_freq(size, span(0, own)))
    grad_mid, near2, far2, halo0, inner0, gain0 = run(
        functools.partial(first_backward_kernel, two),
        (
            like(own + tap_count + 1, width, BF16), like(one, width, BF16), like(one, width, BF16),
            like(2 * two, width, BF16), like(own, width, BF16), like(1, width, F32),
        ),
        [pltpu.VMEM((2, two, width), BF16), pltpu.VMEM((2, one, width), BF16), *rows],
        [
            notes, saved, far0, near0, grad, weights, later, *layer0,
            m_table, q_table, c_table, g_table, x_table,
        ],
        4,
    )
    grad_mid = shifted(grad_mid, -1)
    near2, far2 = swapped(near2, far2, -1)
    layer = (*layer, like(size, width, F32))
    masked1, mean1, inverse1, q1, masked2, _, _, q2 = run(
        prepare_later_kernel, (*layer, *layer), [], [notes, saved, act, weights, q_table], 0, gain0
    )
    halo_scratch = [pltpu.VMEM((2 * two, width), BF16), pltpu.VMEM((2, two, width), BF16)]
    between = run(
        functools.partial(first_forward_kernel, two),
        like(small, width, BF16),
        halo_scratch,
        [notes, act, far1, near1, weights, masked2, q2, m_table, c_table],
        20,
    )
    act_ahead = run(
        second_forward_kernel,
        like(own, width, BF16),
        [pltpu.VMEM((small, width), BF16)],
        [
            notes, between, grad_mid,
            stacked(to_freq(small, span(one, own))), tap_freq(small, tap_count), stacked(from_freq(small, span(0, own))),
        ],
        3,
    )
    act_out = shifted(act_ahead, 2)
    taps0 = run(
        first_taps_kernel, like(tap_count + 1, width, BF16), [],
        [halo0, layer0[0], inner0, gain0, m_table, go_table, t_table],
        0,
        act_ahead,
    )
    m1, factor1, conv1 = run(
        functools.partial(second_ready_kernel, two),
        (like(size, width, F32), like(small, width, F32), like(own, width, F32)),
        halo_scratch,
        [notes, far1, near1, weights, masked1, q1, m_table, c_table],
        3,
        act_ahead,
    )

    def partner(x, step):
        return lax.ppermute(x, "tm", [(i, i ^ step) for i in range(shards)])

    other0 = partner(taps0, 1)
    mixed1, taps1 = run(
        second_taps_kernel,
        (like(small, width, BF16), like(tap_count + 1, width, BF16)),
        [pltpu.VMEM((2, one, width), BF16)],
        [notes, grad_mid, far2, near2, weights, m1, factor1, conv1, go_table, t_table],
        2,
    )
    grad_out = run(
        second_backward_kernel,
        like(own, width, BF16),
        rows,
        [
            notes, saved, grad_mid, weights, mixed1, q1, mean1, inverse1,
            g_table, x_table,
        ],
        6,
    )
    grad_out = shifted(grad_out, -1)
    other1 = partner(taps1, 1)
    mine = call(below_kernel, like(2 * (tap_count + 1), width, BF16), [], (taps0, other0, taps1, other1), 6)
    step = 2
    while True:
        other = partner(mine, step)
        step *= 2
        if step >= shards:
            break
        mine = call(add_kernel, like(*mine.shape, BF16), [], (mine, other), 0)
    slots = kernels.shape[1]
    act_out, grad_out, taps, gains = call(
        final_kernel,
        (
            like(own, width, BF16), like(own, width, BF16),
            jax.ShapeDtypeStruct((tap_count, slots, width), F32), like(slots, width, F32),
        ),
        [pltpu.SemaphoreType.DMA((2,))],
        (notes, mine, other, act_out, grad_out),
        0, [SMEM] + [VMEM] * 2 + [ANY] * 2, (ANY, ANY, VMEM, VMEM),
    )
    return act_out[None], grad_out[None], taps.transpose(1, 0, 2)[None], gains[None]


def solution(mesh):
    in_specs = (
        P("section", "tm", None),
        P("section", "tm", None),
        P("section", None, "tm", None),
        P("section", None, None, None),
        P("section", None, None),
        P(),
        P(),
        P(),
        P(),
    )
    out_specs = (
        P("section", "tm", None),
        P("section", "tm", None),
        P("section", None, None, None),
        P("section", None, None),
    )
    return jax.shard_map(local, mesh=mesh, in_specs=in_specs, out_specs=out_specs, check_vma=False)
```

```python
import functools

import jax
import jax.numpy as jnp
import ml_dtypes
import numpy as np
from jax import lax
from jax.experimental import pallas as pl
from jax.experimental.pallas import tpu as pltpu
from jax.sharding import PartitionSpec as P

epsilon = 1e-05
BLOCK = 2048
LANES = 128
F32 = jnp.float32
BF16 = jnp.bfloat16


def split(matrix):
    high = matrix.astype(ml_dtypes.bfloat16)
    low = (matrix - high.astype(np.float64)).astype(ml_dtypes.bfloat16)
    return high, low


def angles(size, times):
    return 2.0 * np.pi / size * np.outer(np.arange(size // 2) + 0.5, np.asarray(times, np.float64))


def to_freq(size, times):
    phase = angles(size, times)
    return np.concatenate([np.cos(phase), -np.sin(phase)], axis=0)


def from_freq(size, times):
    phase = angles(size, times).T
    return 2.0 / size * np.concatenate([np.cos(phase), -np.sin(phase)], axis=1)


def stacked(matrix):
    return np.concatenate(split(matrix), axis=0)


def beside(matrix):
    return np.concatenate(split(matrix), axis=1)


def tap_freq(size, taps):
    phase = angles(size, np.arange(taps) - (taps - 1) // 2)
    table = np.concatenate([np.cos(phase), np.sin(phase)], axis=0)
    return beside(np.concatenate([table, np.zeros((size, 1))], axis=1))


def dot(a, b):
    return jnp.dot(a, b, preferred_element_type=F32)


def transform(table, values):
    return sum(halves(dot(table[...], values.astype(BF16))))


def halves(values):
    half = values.shape[0] // 2
    return values[:half], values[half:]


def product(a, b):
    ar, ai = halves(a)
    br, bi = halves(b)
    return jnp.concatenate([ar * br - ai * bi, ar * bi + ai * br], axis=0)


def product_conj(a, b):
    ar, ai = halves(a)
    br, bi = halves(b)
    return jnp.concatenate([ar * br + ai * bi, ai * br - ar * bi], axis=0)


def sigmoid(values):
    return 0.5 * jnp.tanh(0.5 * values) + 0.5


def wide(stat, count):
    return jnp.concatenate([stat] * (count // LANES), axis=1)


def norm_rows(ref, start, count, at, gain, first, length, masked_ref, mean_ref, inverse_ref):
    width = masked_ref.shape[1]
    rows = pl.ds(start, count)
    tiles = [pl.ds(i * LANES, LANES) for i in range(width // LANES)]

    def values(tile):
        return ref[rows, tile].astype(F32)

    total = values(tiles[0])
    for tile in tiles[1:]:
        total = total + values(tile)
    mean = jnp.sum(total, axis=1, keepdims=True) * (1.0 / width)
    mean = jnp.broadcast_to(mean, (count, LANES))
    square = jnp.zeros((count, LANES), F32)
    for tile in tiles:
        center = values(tile) - mean
        square = square + center * center
    var = jnp.sum(square, axis=1, keepdims=True) * (1.0 / width)
    inverse = jnp.broadcast_to(lax.rsqrt(var + epsilon), (count, LANES))
    frame = first + at + lax.broadcasted_iota(jnp.int32, (count, LANES), 0)
    mask = ((frame >= 0) & (frame < length)).astype(F32)
    scale = mask * inverse
    out = pl.ds(at, count)
    for tile in tiles:
        masked_ref[out, tile] = ((values(tile) - mean) * scale * gain(tile)).astype(BF16)
    if mean_ref is not None:
        mean_ref[out, :] = mean
        inverse_ref[out, :] = inverse


def norm_pieces(pieces, gain, first, length, masked_ref, mean_ref=None, inverse_ref=None, chunk=128):
    at = 0
    for ref, start, count in pieces:
        for begin in range(0, count, chunk):
            norm_rows(
                ref, start + begin, min(chunk, count - begin), at + begin,
                gain, first, length, masked_ref, mean_ref, inverse_ref,
            )
        at += count


def window(pieces, columns):
    parts = [ref[pl.ds(start, count), columns] for ref, start, count in pieces]
    return parts[0] if len(parts) == 1 else jnp.concatenate(parts, axis=0)


def each_block(width, body):
    for begin in range(0, width, BLOCK):
        body(pl.ds(begin, BLOCK))


def tap_spectrum(table, weights):
    return dot(table, jnp.concatenate([weights, weights], axis=0))


def gate_factor(conv):
    gate = sigmoid(conv)
    return gate * (1.0 + conv * (1.0 - gate))


FIRST, BACK0, BACK1, AHEAD0 = range(0, 8, 2)


def looked_up(notes, layer):
    return notes[layer], notes[layer + 1], notes[FIRST]


def sorted_halos(near, far, at, halos):
    even = lax.rem(lax.axis_index("tm") + 1, 2)
    rows = pl.ds(at, halos.shape[1])
    halos[even] = near[rows, :]
    halos[1 - even] = far[rows, :]
    return halos.at[0], halos.at[1]


def lane_sum(values):
    total = values[:, :LANES]
    for lane in range(LANES, values.shape[1], LANES):
        total = total + values[:, lane : lane + LANES]
    return total


def first_pass(pieces, mean, inverse, gain, mask, tables, mixed, q, columns, scaled, sum_a, sum_b):
    g_table, x_table = tables
    grad_masked = wide(mask, BLOCK) * transform(x_table, product_conj(transform(g_table, mixed), q))
    centered = window(pieces, columns).astype(F32) - wide(mean[...], BLOCK)
    weighted = grad_masked * (centered * wide(inverse[...], BLOCK))
    gain = gain(columns)
    by_gain = grad_masked * gain
    scaled[:, columns] = by_gain
    sum_a[...] += lane_sum(by_gain)
    sum_b[...] += lane_sum(weighted * gain)
    return weighted


def last_pass(grad_pieces, pieces, mean, inverse, scaled, sum_a, sum_b, grad_x, chunk=128):
    width = scaled.shape[1]
    at = 0
    for (ref, start, count), (saved, base, _) in zip(grad_pieces, pieces):
        for begin in range(0, count, chunk):
            here = min(chunk, count - begin)
            rows = pl.ds(at + begin, here)
            inv = inverse[rows, :]
            mean_a = jnp.sum(sum_a[rows, :], axis=1, keepdims=True) * (1.0 / width)
            mean_b = jnp.sum(sum_b[rows, :], axis=1, keepdims=True) * (1.0 / width)
            slope = inv * jnp.broadcast_to(mean_b, (here, LANES)) * inv
            fixed = inv * jnp.broadcast_to(mean_a, (here, LANES)) - slope * mean[rows, :]
            for lane in range(0, width, LANES):
                tile = pl.ds(lane, LANES)
                x = saved[pl.ds(base + begin, here), tile].astype(F32)
                change = inv * scaled[rows, tile] - fixed - slope * x
                grad_x[rows, tile] = (ref[pl.ds(start + begin, here), tile].astype(F32) + change).astype(BF16)
        at += count


def frame_mask(rows, first, length):
    frame = first + lax.broadcasted_iota(jnp.int32, (rows, LANES), 0)
    return ((frame >= 0) & (frame < length)).astype(F32)


def slot_row(weights, slot):
    last = weights.shape[1] - 1
    return lambda columns: weights[slot, last : last + 1, columns].astype(F32)


def prepare_kernel(notes, kernels, gains, saved, weights, ahead0, ahead1, masked, mean, inverse):
    own = saved.shape[1]
    count = kernels.shape[0]
    for slot in range(kernels.shape[1]):
        weights[slot, :count, :] = kernels[:, slot, :]
        weights[slot, count:, :] = gains[slot : slot + 1, :]
    ahead0[...] = weights[notes[AHEAD0]]
    ahead1[...] = weights[notes[FIRST + 1]]
    slot, length, first = looked_up(notes, BACK0)
    norm_pieces([(saved.at[0], 0, own)], slot_row(weights, slot), first, length, masked, mean, inverse)


def second_pack_kernel(reach, saved, act, near, far):
    own = act.shape[0]
    for even in range(2):

        @pl.when(lax.rem(lax.axis_index("tm") + 1, 2) == even)
        def _():
            for x, at in ((saved.at[1], 0), (act, reach)):
                tail, head = (near, far) if even else (far, near)
                tail[pl.ds(at, reach), :] = x[pl.ds(own - reach, reach), :]
                head[pl.ds(at, reach), :] = x[pl.ds(0, reach), :]


def norm_halo(left, right, own, gain, first, length, halo):
    reach = left.shape[0]
    norm_pieces([(left, 0, reach)], gain, first - reach, length, halo)
    norm_pieces([(right, 0, reach)], gain, first + own, length, halo.at[pl.ds(reach, reach)])


def joined(halo, own, columns):
    reach = halo.shape[0] // 2
    return jnp.concatenate([halo[:reach, columns], own[:, columns], halo[reach:, columns]], axis=0)


def first_backward_kernel(
    reach, notes, saved, far, near, grads, weights, masked, mean, inverse,
    m_table, q_table, c_table, g_table, x_table,
    grad_x, near_edge, far_edge, halo, inner, gain_sum, halos, grad_halos, scaled, sum_a, sum_b,
):
    own, width = grads.shape
    edge = near_edge.shape[0]
    slot, length, first = looked_up(notes, BACK0)
    gain = slot_row(weights, slot)
    left, right = sorted_halos(near, far, 0, halos)
    grad_left, grad_right = sorted_halos(near, far, reach, grad_halos)
    norm_halo(left, right, own, gain, first, length, halo)
    grad_pieces = [(grad_left, 0, edge), (grads, 0, own), (grad_right, 0, edge)]
    pieces = [(saved.at[0], 0, own)]
    mask = frame_mask(own, first, length)
    sum_a[...] = jnp.zeros_like(sum_a)
    sum_b[...] = jnp.zeros_like(sum_b)

    def block(columns):
        m = transform(m_table, joined(halo, masked, columns))
        q = tap_spectrum(q_table[...], weights[slot, :, columns])
        conv = transform(c_table, product(m, q))
        mixed = (window(grad_pieces, columns).astype(F32) * gate_factor(conv)).astype(BF16)
        inner[:, columns] = mixed[edge : edge + own]
        weighted = first_pass(
            pieces, mean, inverse, gain, mask, (g_table, x_table), mixed, q, columns, scaled, sum_a, sum_b
        )
        gain_sum[:, columns] = jnp.sum(weighted, axis=0, keepdims=True)

    each_block(width, block)
    last_pass([(grads, 0, own)], pieces, mean, inverse, scaled, sum_a, sum_b, grad_x)
    for even in range(2):

        @pl.when(lax.rem(lax.axis_index("tm") + 1, 2) == even)
        def _():
            top, bottom = (far_edge, near_edge) if even else (near_edge, far_edge)
            top[...] = grad_x[pl.ds(0, edge), :]
            bottom[...] = grad_x[pl.ds(own - edge, edge), :]


def tap_term(go_table, t_table, m, mixed):
    g_own = dot(go_table[...], jnp.concatenate([mixed, mixed], axis=0))
    return transform(t_table, product_conj(m, g_own))


def put_taps(taps, tap, gain_sum, columns):
    row = lax.broadcasted_iota(jnp.int32, tap.shape, 0)
    taps[:, columns] = jnp.where(row == tap.shape[0] - 1, gain_sum, tap).astype(taps.dtype)


def first_taps_kernel(halo, masked, inner, gain_sum, m_table, go_table, t_table, taps):
    def block(columns):
        m = transform(m_table, joined(halo, masked, columns))
        put_taps(taps, tap_term(go_table, t_table, m, inner[:, columns]), gain_sum[:, columns], columns)

    each_block(masked.shape[1], block)


def added(mine, other):
    return (mine[...].astype(F32) + other[...].astype(F32)).astype(BF16)


def add_kernel(mine, other, out):
    out[...] = added(mine, other)


def below_kernel(mine0, other0, mine1, other1, out):
    count = mine0.shape[0]
    out[pl.ds(0, count), :] = added(mine0, other0)
    out[pl.ds(count, count), :] = added(mine1, other1)


def second_ready_kernel(
    reach, notes, saved, near, far, weights, m_table, q_table, c_table,
    m_out, q_out, factor, conv_out, mean, inverse, halo, halos, masked,
):
    own, width = masked.shape
    slot, length, first = looked_up(notes, BACK1)
    gain = slot_row(weights, slot)
    left, right = sorted_halos(near, far, 0, halos)
    norm_pieces([(saved.at[1], 0, own)], gain, first, length, masked, mean, inverse)
    norm_halo(left, right, own, gain, first, length, halo)

    def block(columns):
        m = transform(m_table, joined(halo, masked, columns))
        q = tap_spectrum(q_table[...], weights[slot, :, columns])
        conv = transform(c_table, product(m, q))
        m_out[:, columns] = m
        q_out[:, columns] = q
        factor[:, columns] = gate_factor(conv)
        edge = (conv.shape[0] - own) // 2
        conv_out[:, columns] = conv[edge : edge + own]

    each_block(width, block)


def second_taps_kernel(
    notes, received, far, near, weights, m, factor, conv, go_table, t_table, mixed_out, taps, halos
):
    own, width = conv.shape
    rows = factor.shape[0]
    edge = (rows - own) // 2
    gain = slot_row(weights, notes[BACK1])
    left, right = sorted_halos(near, far, 0, halos)
    pieces = [(left, 0, edge), (received, 0, own), (right, 0, edge)]

    def block(columns):
        mixed = (window(pieces, columns).astype(F32) * factor[:, columns]).astype(BF16)
        mixed_out[:, columns] = mixed
        inner = mixed[edge : edge + own]
        gain_sum = jnp.sum(inner.astype(F32) * conv[:, columns], axis=0, keepdims=True) / gain(columns)
        put_taps(taps, tap_term(go_table, t_table, m[:, columns], inner), gain_sum, columns)

    each_block(width, block)


def second_backward_kernel(
    notes, saved, received, weights, mixed, q, mean, inverse, g_table, x_table, grad_x, scaled, sum_a, sum_b
):
    own, width = grad_x.shape
    slot, length, first = looked_up(notes, BACK1)
    pieces = [(saved.at[1], 0, own)]
    mask = frame_mask(own, first, length)
    sum_a[...] = jnp.zeros_like(sum_a)
    sum_b[...] = jnp.zeros_like(sum_b)

    def block(columns):
        first_pass(
            pieces, mean, inverse, slot_row(weights, slot), mask, (g_table, x_table), mixed[:, columns], q[:, columns],
            columns, scaled, sum_a, sum_b,
        )

    each_block(width, block)
    last_pass([(received, 0, own)], pieces, mean, inverse, scaled, sum_a, sum_b, grad_x)


def row_gain(layer):
    last = layer.shape[0] - 1
    return lambda columns: layer[last : last + 1, columns].astype(F32)


def first_forward_kernel(reach, notes, act, far, near, layer, m_table, q_table, c_table, out, halo, halos, masked):
    own, width = act.shape
    middle = reach // 2
    _, length, first = looked_up(notes, AHEAD0)
    left, right = sorted_halos(near, far, reach, halos)
    inner = [(left, middle, middle), (act, 0, own), (right, 0, middle)]
    norm_pieces([(act, 0, own)], row_gain(layer), first, length, masked)
    norm_halo(left, right, own, row_gain(layer), first, length, halo)

    def block(columns):
        q = tap_spectrum(q_table[...], layer[:, columns])
        conv = transform(c_table, product(transform(m_table, joined(halo, masked, columns)), q))
        out[:, columns] = (window(inner, columns).astype(F32) + conv * sigmoid(conv)).astype(BF16)

    each_block(width, block)


def second_forward_kernel(notes, between, layer, m_table, q_table, c_table, out, masked):
    own, width = out.shape
    rows = between.shape[0]
    edge = (rows - own) // 2
    _, length, first = looked_up(notes, AHEAD0)
    norm_pieces([(between, 0, rows)], row_gain(layer), first - edge, length, masked, chunk=rows // 2)

    def block(columns):
        q = tap_spectrum(q_table[...], layer[:, columns])
        conv = transform(c_table, product(transform(m_table, masked[:, columns]), q))
        out[:, columns] = (between[edge : edge + own, columns].astype(F32) + conv * sigmoid(conv)).astype(BF16)

    each_block(width, block)


def pack_kernel(
    reaches, saved, grad, back_lengths, ahead_lengths, back_slots, ahead_slots,
    near, far, notes, back_len, ahead_len, back_slot, ahead_slot, sems,
):
    own = grad.shape[1]
    even = lax.rem(lax.axis_index("tm") + 1, 2)
    copies = []
    at = 0
    for x, reach in zip((saved, grad), reaches):
        for out, tail in ((near, even), (far, 1 - even)):
            start = pl.multiple_of(tail * (own - reach), 16)
            copies.append((x.at[0, pl.ds(start, reach)], out.at[pl.ds(at, reach)]))
        at += reach
    small = [(back_lengths, back_len), (ahead_lengths, ahead_len), (back_slots, back_slot), (ahead_slots, ahead_slot)]
    copies = [pltpu.make_async_copy(a, b, sems.at[k]) for k, (a, b) in enumerate(small + copies)]
    for copy in copies:
        copy.start()
    for copy in copies:
        copy.wait()
    section, sections = lax.axis_index("section"), lax.axis_size("section")
    notes[FIRST] = lax.axis_index("tm") * own
    notes[FIRST + 1] = ahead_slot[1, section]
    notes[BACK0] = back_slot[0, section]
    notes[BACK0 + 1] = back_len[section]
    notes[BACK1] = back_slot[1, section]
    notes[BACK1 + 1] = back_len[lax.rem(section + 1, sections)]
    notes[AHEAD0] = ahead_slot[0, section]
    notes[AHEAD0 + 1] = ahead_len[lax.rem(section + sections - 2, sections)]


def final_kernel(notes, mine, other, act, grad, act_out, grad_out, taps, gains, sems):
    copies = [
        pltpu.make_async_copy(act, act_out, sems.at[0]),
        pltpu.make_async_copy(grad, grad_out, sems.at[1]),
    ]
    for copy in copies:
        copy.start()
    count = taps.shape[0]
    total = mine[...].astype(F32) + other[...].astype(F32)
    ticks = total[: count + 1], total[count + 1 :]
    for slot in range(taps.shape[1]):
        use = [(notes[layer] == slot).astype(F32) for layer in (BACK0, BACK1)]
        both = use[0] * ticks[0] + use[1] * ticks[1]
        taps[:, slot, :] = both[:count]
        gains[slot : slot + 1, :] = both[count:]
    for copy in copies:
        copy.wait()


def span(reach, own):
    return np.arange(-reach, own + reach)


VMEM = pl.BlockSpec(memory_space=pltpu.VMEM)
SMEM = pl.BlockSpec(memory_space=pltpu.SMEM)
ANY = pl.BlockSpec(memory_space=pl.ANY)
HBM = pl.BlockSpec(memory_space=pltpu.HBM)
LIMIT = 24 * 1024 * 1024
FULL = 127 * 512 * 1024


def call(kernel, outs, scratch, operands, micros, specs=None, out_specs=None, limit=LIMIT, after=()):
    if specs is None:
        specs = [SMEM if x.dtype == jnp.int32 else VMEM for x in operands]
    if after:
        inner, place = kernel, len(operands)
        operands, specs = [*operands, *after], [*specs, *[ANY] * len(after)]

        def kernel(*refs):
            return inner(*refs[:place], *refs[place + len(after) :])

    return pl.pallas_call(
        kernel,
        out_shape=outs,
        in_specs=specs,
        out_specs=jax.tree.map(lambda _: VMEM, outs) if out_specs is None else out_specs,
        scratch_shapes=scratch,
        compiler_params=pltpu.CompilerParams(vmem_limit_bytes=limit),
        cost_estimate=pl.CostEstimate(flops=int(micros * 1e9), bytes_accessed=0, transcendentals=0),
    )(*operands)


def like(rows, width, dtype):
    return jax.ShapeDtypeStruct((rows, width), dtype)


def up16(count):
    return -(-count // 16) * 16


def local(
    act_in, grad_in, saved_inputs, kernels, norm_gains,
    forward_lengths, backward_lengths, forward_slots, backward_slots,
):
    sections = lax.axis_size("section")
    shards = lax.axis_size("tm")
    act, grad, saved = act_in[0], grad_in[0], saved_inputs[0]
    own, width = act.shape
    tap_count = kernels.shape[2]
    half = (tap_count - 1) // 2
    one, two = up16(half), up16(2 * half)
    size, small = own + 2 * two, own + 2 * one

    def shifted(x, by):
        return lax.ppermute(x, "section", [(i, (i + by) % sections) for i in range(sections)])

    def swapped(near, far, by=0):
        results = []
        for x, begin in ((far, 1), (near, 0)):
            pairs = [(i, i + 1) for i in range(begin, shards - 1, 2)]
            pairs = [
                (s * shards + i, (s + by) % sections * shards + j)
                for s in range(sections)
                for a, b in pairs
                for i, j in ((a, b), (b, a))
            ]
            results.append(lax.ppermute(x, ("section", "tm"), pairs))
        return results[::-1]

    act = shifted(act, 2)
    lengths = pltpu.SMEM(backward_lengths.shape, jnp.int32)
    forward_slots, backward_slots = forward_slots.T, backward_slots.T
    slots = pltpu.SMEM(backward_slots.shape, jnp.int32)
    near0, far0, notes = call(
        functools.partial(pack_kernel, (two, one)),
        (like(two + one, width, BF16), like(two + one, width, BF16), jax.ShapeDtypeStruct((8,), jnp.int32)),
        [lengths, lengths, slots, slots, pltpu.SemaphoreType.DMA((8,))],
        (saved, grad_in, backward_lengths, forward_lengths, backward_slots, forward_slots),
        0, [HBM] * 6, (VMEM, VMEM, SMEM), FULL,
    )
    near0, far0 = swapped(near0, far0)
    tap_back = np.concatenate([from_freq(size, np.arange(tap_count) - half), np.zeros((1, size))], axis=0)
    m_table = stacked(to_freq(size, span(two, own)))
    q_table = tap_freq(size, tap_count)
    c_table = stacked(from_freq(size, span(one, own)))
    go_table = beside(to_freq(size, np.arange(own)))
    t_table = stacked(tap_back)

    def run(kernel, outs, scratch, operands, micros=0, *after):
        return call(kernel, outs, scratch, [jnp.asarray(x) for x in operands], micros, after=after)

    rows = [pltpu.VMEM((own, width), F32)] + [pltpu.VMEM((own, LANES), F32)] * 2
    layer = like(own, width, BF16), like(own, LANES, F32), like(own, LANES, F32)
    weights, ahead0, ahead1, *layer0 = run(
        prepare_kernel,
        (
            jax.ShapeDtypeStruct((kernels.shape[1], tap_count + 1, width), BF16), like(tap_count + 1, width, BF16),
            like(tap_count + 1, width, BF16), *layer,
        ),
        [],
        [notes, kernels[0].transpose(1, 0, 2), norm_gains[0], saved],
        0,
    )
    packed1 = run(
        functools.partial(second_pack_kernel, two), (like(2 * two, width, BF16),) * 2, [], [saved, act], 0, weights
    )
    near1, far1 = swapped(*packed1)
    ahead0, ahead1 = shifted(ahead0, 2), shifted(ahead1, 1)
    g_table, x_table = stacked(to_freq(size, span(one, own))), stacked(from_freq(size, span(0, own)))
    grad_mid, near2, far2, halo0, inner0, gain0 = run(
        functools.partial(first_backward_kernel, two),
        (
            like(own, width, BF16), like(one, width, BF16), like(one, width, BF16),
            like(2 * two, width, BF16), like(own, width, BF16), like(1, width, F32),
        ),
        [pltpu.VMEM((2, two, width), BF16), pltpu.VMEM((2, one, width), BF16), *rows],
        [
            notes, saved, far0, near0, grad, weights, *layer0,
            m_table, q_table, c_table, g_table, x_table,
        ],
        4,
        packed1[0], ahead0, ahead1,
    )
    grad_mid = shifted(grad_mid, -1)
    near2, far2 = swapped(near2, far2, -1)
    taps0 = run(
        first_taps_kernel, like(tap_count + 1, width, BF16), [],
        [halo0, layer0[0], inner0, gain0, m_table, go_table, t_table],
        0,
    )
    halo_scratch = [
        pltpu.VMEM((2 * two, width), BF16), pltpu.VMEM((2, two, width), BF16), pltpu.VMEM((own, width), BF16)
    ]
    m1, q1, factor1, conv1, mean1, inverse1 = run(
        functools.partial(second_ready_kernel, two),
        (
            like(size, width, F32), like(size, width, F32), like(small, width, F32), like(own, width, F32),
            like(own, LANES, F32), like(own, LANES, F32),
        ),
        halo_scratch,
        [notes, saved, near1, far1, weights, m_table, q_table, c_table],
        20,
        taps0,
    )
    def partner(x, step):
        return lax.ppermute(x, "tm", [(i, i ^ step) for i in range(shards)])

    other0 = partner(taps0, 1)
    mixed1, taps1 = run(
        second_taps_kernel,
        (like(small, width, BF16), like(tap_count + 1, width, BF16)),
        [pltpu.VMEM((2, one, width), BF16)],
        [notes, grad_mid, far2, near2, weights, m1, factor1, conv1, go_table, t_table],
        2,
    )
    grad_out = run(
        second_backward_kernel,
        like(own, width, BF16),
        rows,
        [
            notes, saved, grad_mid, weights, mixed1, q1, mean1, inverse1,
            g_table, x_table,
        ],
        6,
    )
    grad_out = shifted(grad_out, -1)
    other1 = partner(taps1, 1)
    mine = call(below_kernel, like(2 * (tap_count + 1), width, BF16), [], (taps0, other0, taps1, other1), 6)
    between = run(
        functools.partial(first_forward_kernel, two),
        like(small, width, BF16),
        halo_scratch,
        [notes, act, far1, near1, ahead0, m_table, q_table, c_table],
        10,
        mine,
    )
    act_out = run(
        second_forward_kernel,
        like(own, width, BF16),
        [pltpu.VMEM((small, width), BF16)],
        [
            notes, between, ahead1,
            stacked(to_freq(small, span(one, own))), tap_freq(small, tap_count), stacked(from_freq(small, span(0, own))),
        ],
        10,
    )
    step = 2
    while True:
        other = partner(mine, step)
        step *= 2
        if step >= shards:
            break
        mine = call(add_kernel, like(*mine.shape, BF16), [], (mine, other), 0)
    slots = kernels.shape[1]
    act_out, grad_out, taps, gains = call(
        final_kernel,
        (
            like(own, width, BF16), like(own, width, BF16),
            jax.ShapeDtypeStruct((tap_count, slots, width), F32), like(slots, width, F32),
        ),
        [pltpu.SemaphoreType.DMA((2,))],
        (notes, mine, other, act_out, grad_out),
        0, [SMEM] + [VMEM] * 2 + [ANY] * 2, (ANY, ANY, VMEM, VMEM),
    )
    return act_out[None], grad_out[None], taps.transpose(1, 0, 2)[None], gains[None]


def solution(mesh):
    in_specs = (
        P("section", "tm", None),
        P("section", "tm", None),
        P("section", None, "tm", None),
        P("section", None, None, None),
        P("section", None, None),
        P(),
        P(),
        P(),
        P(),
    )
    out_specs = (
        P("section", "tm", None),
        P("section", "tm", None),
        P("section", None, None, None),
        P("section", None, None),
    )
    return jax.shard_map(local, mesh=mesh, in_specs=in_specs, out_specs=out_specs, check_vma=False)
```

```python
import functools

import jax
import jax.numpy as jnp
import ml_dtypes
import numpy as np
from jax import lax
from jax.experimental import pallas as pl
from jax.experimental.pallas import tpu as pltpu
from jax.sharding import PartitionSpec as P

epsilon = 1e-05
BLOCK = 2048
LANES = 128
F32 = jnp.float32
BF16 = jnp.bfloat16


def split(matrix):
    high = matrix.astype(ml_dtypes.bfloat16)
    low = (matrix - high.astype(np.float64)).astype(ml_dtypes.bfloat16)
    return high, low


def angles(size, times):
    return 2.0 * np.pi / size * np.outer(np.arange(size // 2) + 0.5, np.asarray(times, np.float64))


def to_freq(size, times):
    phase = angles(size, times)
    return np.concatenate([np.cos(phase), -np.sin(phase)], axis=0)


def from_freq(size, times):
    phase = angles(size, times).T
    return 2.0 / size * np.concatenate([np.cos(phase), -np.sin(phase)], axis=1)


def stacked(matrix):
    return np.concatenate(split(matrix), axis=0)


def beside(matrix):
    return np.concatenate(split(matrix), axis=1)


def tap_freq(size, taps):
    phase = angles(size, np.arange(taps) - (taps - 1) // 2)
    table = np.concatenate([np.cos(phase), np.sin(phase)], axis=0)
    return beside(np.concatenate([table, np.zeros((size, 1))], axis=1))


def dot(a, b):
    return jnp.dot(a, b, preferred_element_type=F32)


def transform(table, values):
    return sum(halves(dot(table[...], values.astype(BF16))))


def halves(values):
    half = values.shape[0] // 2
    return values[:half], values[half:]


def product(a, b):
    ar, ai = halves(a)
    br, bi = halves(b)
    return jnp.concatenate([ar * br - ai * bi, ar * bi + ai * br], axis=0)


def product_conj(a, b):
    ar, ai = halves(a)
    br, bi = halves(b)
    return jnp.concatenate([ar * br + ai * bi, ai * br - ar * bi], axis=0)


def sigmoid(values):
    return 0.5 * jnp.tanh(0.5 * values) + 0.5


def wide(stat, count):
    return jnp.concatenate([stat] * (count // LANES), axis=1)


def norm_rows(ref, start, count, at, gain, first, length, masked_ref, mean_ref, inverse_ref):
    width = masked_ref.shape[1]
    rows = pl.ds(start, count)
    tiles = [pl.ds(i * LANES, LANES) for i in range(width // LANES)]

    def values(tile):
        return ref[rows, tile].astype(F32)

    total = values(tiles[0])
    for tile in tiles[1:]:
        total = total + values(tile)
    mean = jnp.sum(total, axis=1, keepdims=True) * (1.0 / width)
    mean = jnp.broadcast_to(mean, (count, LANES))
    square = jnp.zeros((count, LANES), F32)
    for tile in tiles:
        center = values(tile) - mean
        square = square + center * center
    var = jnp.sum(square, axis=1, keepdims=True) * (1.0 / width)
    inverse = jnp.broadcast_to(lax.rsqrt(var + epsilon), (count, LANES))
    frame = first + at + lax.broadcasted_iota(jnp.int32, (count, LANES), 0)
    mask = ((frame >= 0) & (frame < length)).astype(F32)
    scale = mask * inverse
    out = pl.ds(at, count)
    for tile in tiles:
        masked_ref[out, tile] = ((values(tile) - mean) * scale * gain(tile)).astype(BF16)
    if mean_ref is not None:
        mean_ref[out, :] = mean
        inverse_ref[out, :] = inverse


def norm_pieces(pieces, gain, first, length, masked_ref, mean_ref=None, inverse_ref=None, chunk=128):
    at = 0
    for ref, start, count in pieces:
        for begin in range(0, count, chunk):
            norm_rows(
                ref, start + begin, min(chunk, count - begin), at + begin,
                gain, first, length, masked_ref, mean_ref, inverse_ref,
            )
        at += count


def window(pieces, columns):
    parts = [ref[pl.ds(start, count), columns] for ref, start, count in pieces]
    return parts[0] if len(parts) == 1 else jnp.concatenate(parts, axis=0)


def each_block(width, body):
    for begin in range(0, width, BLOCK):
        body(pl.ds(begin, BLOCK))


def tap_spectrum(table, weights):
    return dot(table, jnp.concatenate([weights, weights], axis=0))


def gate_factor(conv):
    gate = sigmoid(conv)
    return gate * (1.0 + conv * (1.0 - gate))


FIRST, BACK0, BACK1, AHEAD0 = range(0, 8, 2)


def looked_up(notes, layer):
    return notes[layer], notes[layer + 1], notes[FIRST]


def sorted_halos(near, far, at, halos):
    even = lax.rem(lax.axis_index("tm") + 1, 2)
    rows = pl.ds(at, halos.shape[1])
    halos[even] = near[rows, :]
    halos[1 - even] = far[rows, :]
    return halos.at[0], halos.at[1]


def lane_sum(values):
    total = values[:, :LANES]
    for lane in range(LANES, values.shape[1], LANES):
        total = total + values[:, lane : lane + LANES]
    return total


def first_pass(pieces, mean, inverse, gain, mask, tables, mixed, q, columns, scaled, sum_a, sum_b):
    g_table, x_table = tables
    grad_masked = wide(mask, BLOCK) * transform(x_table, product_conj(transform(g_table, mixed), q))
    centered = window(pieces, columns).astype(F32) - wide(mean[...], BLOCK)
    weighted = grad_masked * (centered * wide(inverse[...], BLOCK))
    gain = gain(columns)
    by_gain = grad_masked * gain
    scaled[:, columns] = by_gain
    sum_a[...] += lane_sum(by_gain)
    sum_b[...] += lane_sum(weighted * gain)
    return weighted


def last_pass(grad_pieces, pieces, mean, inverse, scaled, sum_a, sum_b, grad_x, chunk=128):
    width = scaled.shape[1]
    at = 0
    for (ref, start, count), (saved, base, _) in zip(grad_pieces, pieces):
        for begin in range(0, count, chunk):
            here = min(chunk, count - begin)
            rows = pl.ds(at + begin, here)
            inv = inverse[rows, :]
            mean_a = jnp.sum(sum_a[rows, :], axis=1, keepdims=True) * (1.0 / width)
            mean_b = jnp.sum(sum_b[rows, :], axis=1, keepdims=True) * (1.0 / width)
            slope = inv * jnp.broadcast_to(mean_b, (here, LANES)) * inv
            fixed = inv * jnp.broadcast_to(mean_a, (here, LANES)) - slope * mean[rows, :]
            for lane in range(0, width, LANES):
                tile = pl.ds(lane, LANES)
                x = saved[pl.ds(base + begin, here), tile].astype(F32)
                change = inv * scaled[rows, tile] - fixed - slope * x
                grad_x[rows, tile] = (ref[pl.ds(start + begin, here), tile].astype(F32) + change).astype(BF16)
        at += count


def frame_mask(rows, first, length):
    frame = first + lax.broadcasted_iota(jnp.int32, (rows, LANES), 0)
    return ((frame >= 0) & (frame < length)).astype(F32)


def slot_row(weights, slot):
    last = weights.shape[1] - 1
    return lambda columns: weights[slot, last : last + 1, columns].astype(F32)


def prepare_kernel(
    reach, notes, kernels, gains, saved, act, weights, ahead0, ahead1, near, far, masked, mean, inverse
):
    own = act.shape[0]
    for even in range(2):

        @pl.when(lax.rem(lax.axis_index("tm") + 1, 2) == even)
        def _():
            for x, at in ((saved.at[1], 0), (act, reach)):
                tail, head = (near, far) if even else (far, near)
                tail[pl.ds(at, reach), :] = x[pl.ds(own - reach, reach), :]
                head[pl.ds(at, reach), :] = x[pl.ds(0, reach), :]

    count = kernels.shape[0]
    for slot in range(kernels.shape[1]):
        weights[slot, :count, :] = kernels[:, slot, :]
        weights[slot, count:, :] = gains[slot : slot + 1, :]
    ahead0[...] = weights[notes[AHEAD0]]
    ahead1[...] = weights[notes[FIRST + 1]]
    slot, length, first = looked_up(notes, BACK0)
    norm_pieces([(saved.at[0], 0, own)], slot_row(weights, slot), first, length, masked, mean, inverse)


def norm_halo(left, right, own, gain, first, length, halo):
    reach = left.shape[0]
    norm_pieces([(left, 0, reach)], gain, first - reach, length, halo)
    norm_pieces([(right, 0, reach)], gain, first + own, length, halo.at[pl.ds(reach, reach)])


def joined(halo, own, columns):
    reach = halo.shape[0] // 2
    return jnp.concatenate([halo[:reach, columns], own[:, columns], halo[reach:, columns]], axis=0)


def first_backward_kernel(
    reach, notes, saved, far, near, grads, weights, masked, mean, inverse,
    m_table, q_table, c_table, g_table, x_table,
    grad_x, near_edge, far_edge, halo, inner, gain_sum, halos, grad_halos, scaled, sum_a, sum_b,
):
    own, width = grads.shape
    edge = near_edge.shape[0]
    slot, length, first = looked_up(notes, BACK0)
    gain = slot_row(weights, slot)
    left, right = sorted_halos(near, far, 0, halos)
    grad_left, grad_right = sorted_halos(near, far, reach, grad_halos)
    norm_halo(left, right, own, gain, first, length, halo)
    grad_pieces = [(grad_left, 0, edge), (grads, 0, own), (grad_right, 0, edge)]
    pieces = [(saved.at[0], 0, own)]
    mask = frame_mask(own, first, length)
    sum_a[...] = jnp.zeros_like(sum_a)
    sum_b[...] = jnp.zeros_like(sum_b)

    def block(columns):
        m = transform(m_table, joined(halo, masked, columns))
        q = tap_spectrum(q_table[...], weights[slot, :, columns])
        conv = transform(c_table, product(m, q))
        mixed = (window(grad_pieces, columns).astype(F32) * gate_factor(conv)).astype(BF16)
        inner[:, columns] = mixed[edge : edge + own]
        weighted = first_pass(
            pieces, mean, inverse, gain, mask, (g_table, x_table), mixed, q, columns, scaled, sum_a, sum_b
        )
        gain_sum[:, columns] = jnp.sum(weighted, axis=0, keepdims=True)

    each_block(width, block)
    last_pass([(grads, 0, own)], pieces, mean, inverse, scaled, sum_a, sum_b, grad_x)
    for even in range(2):

        @pl.when(lax.rem(lax.axis_index("tm") + 1, 2) == even)
        def _():
            top, bottom = (far_edge, near_edge) if even else (near_edge, far_edge)
            top[...] = grad_x[pl.ds(0, edge), :]
            bottom[...] = grad_x[pl.ds(own - edge, edge), :]


def tap_term(go_table, t_table, m, mixed):
    g_own = dot(go_table[...], jnp.concatenate([mixed, mixed], axis=0))
    return transform(t_table, product_conj(m, g_own))


def put_taps(taps, tap, gain_sum, columns):
    row = lax.broadcasted_iota(jnp.int32, tap.shape, 0)
    taps[:, columns] = jnp.where(row == tap.shape[0] - 1, gain_sum, tap).astype(taps.dtype)


def first_taps_kernel(halo, masked, inner, gain_sum, m_table, go_table, t_table, taps):
    def block(columns):
        m = transform(m_table, joined(halo, masked, columns))
        put_taps(taps, tap_term(go_table, t_table, m, inner[:, columns]), gain_sum[:, columns], columns)

    each_block(masked.shape[1], block)


def added(mine, other):
    return (mine[...].astype(F32) + other[...].astype(F32)).astype(BF16)


def add_kernel(mine, other, out):
    out[...] = added(mine, other)


def below_kernel(mine0, other0, mine1, other1, out):
    count = mine0.shape[0]
    out[pl.ds(0, count), :] = added(mine0, other0)
    out[pl.ds(count, count), :] = added(mine1, other1)


def second_ready_kernel(
    reach, notes, saved, far, near, weights, ahead0, m_table, q_table, c_table,
    m_out, q_out, factor, conv_out, mean, inverse, ahead, halo, halos, masked,
):
    left, right = sorted_halos(near, far, reach, halos)
    ahead[pl.ds(0, reach), :] = left[...]
    ahead[pl.ds(reach, reach), :] = right[...]
    ahead[pl.ds(2 * reach, ahead0.shape[0]), :] = ahead0[...]
    own, width = masked.shape
    slot, length, first = looked_up(notes, BACK1)
    gain = slot_row(weights, slot)
    left, right = sorted_halos(near, far, 0, halos)
    norm_pieces([(saved.at[1], 0, own)], gain, first, length, masked, mean, inverse)
    norm_halo(left, right, own, gain, first, length, halo)

    def block(columns):
        m = transform(m_table, joined(halo, masked, columns))
        q = tap_spectrum(q_table[...], weights[slot, :, columns])
        conv = transform(c_table, product(m, q))
        m_out[:, columns] = m
        q_out[:, columns] = q
        factor[:, columns] = gate_factor(conv)
        edge = (conv.shape[0] - own) // 2
        conv_out[:, columns] = conv[edge : edge + own]

    each_block(width, block)


def second_taps_kernel(
    notes, received, far, near, weights, m, factor, conv, go_table, t_table, mixed_out, taps, halos
):
    own, width = conv.shape
    rows = factor.shape[0]
    edge = (rows - own) // 2
    gain = slot_row(weights, notes[BACK1])
    left, right = sorted_halos(near, far, 0, halos)
    pieces = [(left, 0, edge), (received, 0, own), (right, 0, edge)]

    def block(columns):
        mixed = (window(pieces, columns).astype(F32) * factor[:, columns]).astype(BF16)
        mixed_out[:, columns] = mixed
        inner = mixed[edge : edge + own]
        gain_sum = jnp.sum(inner.astype(F32) * conv[:, columns], axis=0, keepdims=True) / gain(columns)
        put_taps(taps, tap_term(go_table, t_table, m[:, columns], inner), gain_sum, columns)

    each_block(width, block)


def second_backward_kernel(
    notes, saved, received, weights, mixed, q, mean, inverse, g_table, x_table, grad_x, scaled, sum_a, sum_b
):
    own, width = grad_x.shape
    slot, length, first = looked_up(notes, BACK1)
    pieces = [(saved.at[1], 0, own)]
    mask = frame_mask(own, first, length)
    sum_a[...] = jnp.zeros_like(sum_a)
    sum_b[...] = jnp.zeros_like(sum_b)

    def block(columns):
        first_pass(
            pieces, mean, inverse, slot_row(weights, slot), mask, (g_table, x_table), mixed[:, columns], q[:, columns],
            columns, scaled, sum_a, sum_b,
        )

    each_block(width, block)
    last_pass([(received, 0, own)], pieces, mean, inverse, scaled, sum_a, sum_b, grad_x)


def row_gain(layer):
    last = layer.shape[0] - 1
    return lambda columns: layer[last : last + 1, columns].astype(F32)


def first_forward_kernel(reach, notes, act, ahead, m_table, q_table, c_table, out, halo, masked):
    own, width = act.shape
    middle = reach // 2
    _, length, first = looked_up(notes, AHEAD0)
    left, right = ahead.at[pl.ds(0, reach)], ahead.at[pl.ds(reach, reach)]
    layer = ahead.at[pl.ds(2 * reach, ahead.shape[0] - 2 * reach)]
    inner = [(left, middle, middle), (act, 0, own), (right, 0, middle)]
    norm_pieces([(act, 0, own)], row_gain(layer), first, length, masked)
    norm_halo(left, right, own, row_gain(layer), first, length, halo)

    def block(columns):
        q = tap_spectrum(q_table[...], layer[:, columns])
        conv = transform(c_table, product(transform(m_table, joined(halo, masked, columns)), q))
        out[:, columns] = (window(inner, columns).astype(F32) + conv * sigmoid(conv)).astype(BF16)

    each_block(width, block)


def second_forward_kernel(notes, between, layer, m_table, q_table, c_table, out, masked):
    own, width = out.shape
    rows = between.shape[0]
    edge = (rows - own) // 2
    _, length, first = looked_up(notes, AHEAD0)
    norm_pieces([(between, 0, rows)], row_gain(layer), first - edge, length, masked, chunk=rows // 2)

    def block(columns):
        q = tap_spectrum(q_table[...], layer[:, columns])
        conv = transform(c_table, product(transform(m_table, masked[:, columns]), q))
        out[:, columns] = (between[edge : edge + own, columns].astype(F32) + conv * sigmoid(conv)).astype(BF16)

    each_block(width, block)


def pack_kernel(
    reaches, saved, grad, back_lengths, ahead_lengths, back_slots, ahead_slots,
    near, far, notes, back_len, ahead_len, back_slot, ahead_slot, sems,
):
    own = grad.shape[1]
    even = lax.rem(lax.axis_index("tm") + 1, 2)
    copies = []
    at = 0
    for x, reach in zip((saved, grad), reaches):
        for out, tail in ((near, even), (far, 1 - even)):
            start = pl.multiple_of(tail * (own - reach), 16)
            copies.append((x.at[0, pl.ds(start, reach)], out.at[pl.ds(at, reach)]))
        at += reach
    small = [(back_lengths, back_len), (ahead_lengths, ahead_len), (back_slots, back_slot), (ahead_slots, ahead_slot)]
    copies = [pltpu.make_async_copy(a, b, sems.at[k]) for k, (a, b) in enumerate(small + copies)]
    for copy in copies:
        copy.start()
    for copy in copies:
        copy.wait()
    section, sections = lax.axis_index("section"), lax.axis_size("section")
    notes[FIRST] = lax.axis_index("tm") * own
    notes[FIRST + 1] = ahead_slot[1, section]
    notes[BACK0] = back_slot[0, section]
    notes[BACK0 + 1] = back_len[section]
    notes[BACK1] = back_slot[1, section]
    notes[BACK1 + 1] = back_len[lax.rem(section + 1, sections)]
    notes[AHEAD0] = ahead_slot[0, section]
    notes[AHEAD0 + 1] = ahead_len[lax.rem(section + sections - 2, sections)]


def final_kernel(notes, mine, other, act, grad, act_out, grad_out, taps, gains, sems):
    copies = [
        pltpu.make_async_copy(act, act_out, sems.at[0]),
        pltpu.make_async_copy(grad, grad_out, sems.at[1]),
    ]
    for copy in copies:
        copy.start()
    count = taps.shape[0]
    total = mine[...].astype(F32) + other[...].astype(F32)
    ticks = total[: count + 1], total[count + 1 :]
    for slot in range(taps.shape[1]):
        use = [(notes[layer] == slot).astype(F32) for layer in (BACK0, BACK1)]
        both = use[0] * ticks[0] + use[1] * ticks[1]
        taps[:, slot, :] = both[:count]
        gains[slot : slot + 1, :] = both[count:]
    for copy in copies:
        copy.wait()


def span(reach, own):
    return np.arange(-reach, own + reach)


VMEM = pl.BlockSpec(memory_space=pltpu.VMEM)
SMEM = pl.BlockSpec(memory_space=pltpu.SMEM)
ANY = pl.BlockSpec(memory_space=pl.ANY)
HBM = pl.BlockSpec(memory_space=pltpu.HBM)
LIMIT = 24 * 1024 * 1024
FULL = 127 * 512 * 1024


def call(kernel, outs, scratch, operands, micros, specs=None, out_specs=None, limit=LIMIT, after=()):
    if specs is None:
        specs = [SMEM if x.dtype == jnp.int32 else VMEM for x in operands]
    if after:
        inner, place = kernel, len(operands)
        operands, specs = [*operands, *after], [*specs, *[ANY] * len(after)]

        def kernel(*refs):
            return inner(*refs[:place], *refs[place + len(after) :])

    return pl.pallas_call(
        kernel,
        out_shape=outs,
        in_specs=specs,
        out_specs=jax.tree.map(lambda _: VMEM, outs) if out_specs is None else out_specs,
        scratch_shapes=scratch,
        compiler_params=pltpu.CompilerParams(vmem_limit_bytes=limit),
        cost_estimate=pl.CostEstimate(flops=int(micros * 1e9), bytes_accessed=0, transcendentals=0),
    )(*operands)


def like(rows, width, dtype):
    return jax.ShapeDtypeStruct((rows, width), dtype)


def up16(count):
    return -(-count // 16) * 16


def local(
    act_in, grad_in, saved_inputs, kernels, norm_gains,
    forward_lengths, backward_lengths, forward_slots, backward_slots,
):
    sections = lax.axis_size("section")
    shards = lax.axis_size("tm")
    act, grad, saved = act_in[0], grad_in[0], saved_inputs[0]
    own, width = act.shape
    tap_count = kernels.shape[2]
    half = (tap_count - 1) // 2
    one, two = up16(half), up16(2 * half)
    size, small = own + 2 * two, own + 2 * one

    def shifted(x, by):
        return lax.ppermute(x, "section", [(i, (i + by) % sections) for i in range(sections)])

    def swapped(near, far, by=0):
        results = []
        for x, begin in ((far, 1), (near, 0)):
            pairs = [(i, i + 1) for i in range(begin, shards - 1, 2)]
            pairs = [
                (s * shards + i, (s + by) % sections * shards + j)
                for s in range(sections)
                for a, b in pairs
                for i, j in ((a, b), (b, a))
            ]
            results.append(lax.ppermute(x, ("section", "tm"), pairs))
        return results[::-1]

    act_ahead = shifted(act, 2)
    lengths = pltpu.SMEM(backward_lengths.shape, jnp.int32)
    forward_slots, backward_slots = forward_slots.T, backward_slots.T
    slots = pltpu.SMEM(backward_slots.shape, jnp.int32)
    near0, far0, notes = call(
        functools.partial(pack_kernel, (two, one)),
        (like(two + one, width, BF16), like(two + one, width, BF16), jax.ShapeDtypeStruct((8,), jnp.int32)),
        [lengths, lengths, slots, slots, pltpu.SemaphoreType.DMA((8,))],
        (saved, grad_in, backward_lengths, forward_lengths, backward_slots, forward_slots),
        0, [HBM] * 6, (VMEM, VMEM, SMEM), FULL,
    )
    near0, far0 = swapped(near0, far0)
    tap_back = np.concatenate([from_freq(size, np.arange(tap_count) - half), np.zeros((1, size))], axis=0)
    m_table = stacked(to_freq(size, span(two, own)))
    q_table = tap_freq(size, tap_count)
    c_table = stacked(from_freq(size, span(one, own)))
    go_table = beside(to_freq(size, np.arange(own)))
    t_table = stacked(tap_back)

    def run(kernel, outs, scratch, operands, micros=0, *after):
        return call(kernel, outs, scratch, [jnp.asarray(x) for x in operands], micros, after=after)

    rows = [pltpu.VMEM((own, width), F32)] + [pltpu.VMEM((own, LANES), F32)] * 2
    layer = like(own, width, BF16), like(own, LANES, F32), like(own, LANES, F32)
    weights, ahead0, ahead1, near1, far1, *layer0 = run(
        functools.partial(prepare_kernel, two),
        (
            jax.ShapeDtypeStruct((kernels.shape[1], tap_count + 1, width), BF16), like(tap_count + 1, width, BF16),
            like(tap_count + 1, width, BF16), like(2 * two, width, BF16), like(2 * two, width, BF16), *layer,
        ),
        [],
        [notes, kernels[0].transpose(1, 0, 2), norm_gains[0], saved, act],
        0,
    )
    near1, far1 = swapped(near1, far1)
    ahead1 = shifted(ahead1, 1)
    g_table, x_table = stacked(to_freq(size, span(one, own))), stacked(from_freq(size, span(0, own)))
    grad_mid, near2, far2, halo0, inner0, gain0 = run(
        functools.partial(first_backward_kernel, two),
        (
            like(own, width, BF16), like(one, width, BF16), like(one, width, BF16),
            like(2 * two, width, BF16), like(own, width, BF16), like(1, width, F32),
        ),
        [pltpu.VMEM((2, two, width), BF16), pltpu.VMEM((2, one, width), BF16), *rows],
        [
            notes, saved, far0, near0, grad, weights, *layer0,
            m_table, q_table, c_table, g_table, x_table,
        ],
        4,
        act_ahead,
    )
    grad_mid = shifted(grad_mid, -1)
    near2, far2 = swapped(near2, far2, -1)
    taps0 = run(
        first_taps_kernel, like(tap_count + 1, width, BF16), [],
        [halo0, layer0[0], inner0, gain0, m_table, go_table, t_table],
        0,
    )
    halo_scratch = [
        pltpu.VMEM((2 * two, width), BF16), pltpu.VMEM((2, two, width), BF16), pltpu.VMEM((own, width), BF16)
    ]
    m1, q1, factor1, conv1, mean1, inverse1, ahead0 = run(
        functools.partial(second_ready_kernel, two),
        (
            like(size, width, F32), like(size, width, F32), like(small, width, F32), like(own, width, F32),
            like(own, LANES, F32), like(own, LANES, F32), like(2 * two + tap_count + 1, width, BF16),
        ),
        halo_scratch,
        [notes, saved, far1, near1, weights, ahead0, m_table, q_table, c_table],
        5,
        taps0, near2, far2,
    )
    ahead0 = shifted(ahead0, 2)
    def partner(x, step):
        return lax.ppermute(x, "tm", [(i, i ^ step) for i in range(shards)])

    other0 = partner(taps0, 1)
    mixed1, taps1 = run(
        second_taps_kernel,
        (like(small, width, BF16), like(tap_count + 1, width, BF16)),
        [pltpu.VMEM((2, one, width), BF16)],
        [notes, grad_mid, far2, near2, weights, m1, factor1, conv1, go_table, t_table],
        2,
    )
    grad_out = run(
        second_backward_kernel,
        like(own, width, BF16),
        rows,
        [
            notes, saved, grad_mid, weights, mixed1, q1, mean1, inverse1,
            g_table, x_table,
        ],
        6,
    )
    grad_out = shifted(grad_out, -1)
    other1 = partner(taps1, 1)
    mine = call(below_kernel, like(2 * (tap_count + 1), width, BF16), [], (taps0, other0, taps1, other1), 6)
    between = run(
        functools.partial(first_forward_kernel, two),
        like(small, width, BF16),
        [pltpu.VMEM((2 * two, width), BF16), pltpu.VMEM((own, width), BF16)],
        [notes, act_ahead, ahead0, m_table, q_table, c_table],
        10,
        mine,
    )
    act_out = run(
        second_forward_kernel,
        like(own, width, BF16),
        [pltpu.VMEM((small, width), BF16)],
        [
            notes, between, ahead1,
            stacked(to_freq(small, span(one, own))), tap_freq(small, tap_count), stacked(from_freq(small, span(0, own))),
        ],
        10,
    )
    step = 2
    while True:
        other = partner(mine, step)
        step *= 2
        if step >= shards:
            break
        mine = call(add_kernel, like(*mine.shape, BF16), [], (mine, other), 0)
    slots = kernels.shape[1]
    act_out, grad_out, taps, gains = call(
        final_kernel,
        (
            like(own, width, BF16), like(own, width, BF16),
            jax.ShapeDtypeStruct((tap_count, slots, width), F32), like(slots, width, F32),
        ),
        [pltpu.SemaphoreType.DMA((2,))],
        (notes, mine, other, act_out, grad_out),
        0, [SMEM] + [VMEM] * 2 + [ANY] * 2, (ANY, ANY, VMEM, VMEM),
    )
    return act_out[None], grad_out[None], taps.transpose(1, 0, 2)[None], gains[None]


def solution(mesh):
    in_specs = (
        P("section", "tm", None),
        P("section", "tm", None),
        P("section", None, "tm", None),
        P("section", None, None, None),
        P("section", None, None),
        P(),
        P(),
        P(),
        P(),
    )
    out_specs = (
        P("section", "tm", None),
        P("section", "tm", None),
        P("section", None, None, None),
        P("section", None, None),
    )
    return jax.shard_map(local, mesh=mesh, in_specs=in_specs, out_specs=out_specs, check_vma=False)
```

```python
import functools

import jax
import jax.numpy as jnp
import ml_dtypes
import numpy as np
from jax import lax
from jax.experimental import pallas as pl
from jax.experimental.pallas import tpu as pltpu
from jax.sharding import PartitionSpec as P

epsilon = 1e-05
BLOCK = 2048
LANES = 128
F32 = jnp.float32
BF16 = jnp.bfloat16


def split(matrix):
    high = matrix.astype(ml_dtypes.bfloat16)
    low = (matrix - high.astype(np.float64)).astype(ml_dtypes.bfloat16)
    return high, low


def angles(size, times):
    return 2.0 * np.pi / size * np.outer(np.arange(size // 2) + 0.5, np.asarray(times, np.float64))


def to_freq(size, times):
    phase = angles(size, times)
    return np.concatenate([np.cos(phase), -np.sin(phase)], axis=0)


def from_freq(size, times):
    phase = angles(size, times).T
    return 2.0 / size * np.concatenate([np.cos(phase), -np.sin(phase)], axis=1)


def stacked(matrix):
    return np.concatenate(split(matrix), axis=0)


def beside(matrix):
    return np.concatenate(split(matrix), axis=1)


def tap_freq(size, taps):
    phase = angles(size, np.arange(taps) - (taps - 1) // 2)
    table = np.concatenate([np.cos(phase), np.sin(phase)], axis=0)
    return beside(np.concatenate([table, np.zeros((size, 1))], axis=1))


def dot(a, b):
    return jnp.dot(a, b, preferred_element_type=F32)


def transform(table, values):
    return sum(halves(dot(table[...], values.astype(BF16))))


def halves(values):
    half = values.shape[0] // 2
    return values[:half], values[half:]


def product(a, b):
    ar, ai = halves(a)
    br, bi = halves(b)
    return jnp.concatenate([ar * br - ai * bi, ar * bi + ai * br], axis=0)


def product_conj(a, b):
    ar, ai = halves(a)
    br, bi = halves(b)
    return jnp.concatenate([ar * br + ai * bi, ai * br - ar * bi], axis=0)


def sigmoid(values):
    return 0.5 * jnp.tanh(0.5 * values) + 0.5


def wide(stat, count):
    return jnp.concatenate([stat] * (count // LANES), axis=1)


def norm_rows(ref, start, count, at, gain, first, length, masked_ref, mean_ref, inverse_ref):
    width = masked_ref.shape[1]
    rows = pl.ds(start, count)
    tiles = [pl.ds(i * LANES, LANES) for i in range(width // LANES)]

    def values(tile):
        return ref[rows, tile].astype(F32)

    total = values(tiles[0])
    for tile in tiles[1:]:
        total = total + values(tile)
    mean = jnp.sum(total, axis=1, keepdims=True) * (1.0 / width)
    mean = jnp.broadcast_to(mean, (count, LANES))
    square = jnp.zeros((count, LANES), F32)
    for tile in tiles:
        center = values(tile) - mean
        square = square + center * center
    var = jnp.sum(square, axis=1, keepdims=True) * (1.0 / width)
    inverse = jnp.broadcast_to(lax.rsqrt(var + epsilon), (count, LANES))
    frame = first + at + lax.broadcasted_iota(jnp.int32, (count, LANES), 0)
    mask = ((frame >= 0) & (frame < length)).astype(F32)
    scale = mask * inverse
    out = pl.ds(at, count)
    for tile in tiles:
        masked_ref[out, tile] = ((values(tile) - mean) * scale * gain(tile)).astype(BF16)
    if mean_ref is not None:
        mean_ref[out, :] = mean
        inverse_ref[out, :] = inverse


def norm_pieces(pieces, gain, first, length, masked_ref, mean_ref=None, inverse_ref=None, chunk=128):
    at = 0
    for ref, start, count in pieces:
        for begin in range(0, count, chunk):
            norm_rows(
                ref, start + begin, min(chunk, count - begin), at + begin,
                gain, first, length, masked_ref, mean_ref, inverse_ref,
            )
        at += count


def window(pieces, columns):
    parts = [ref[pl.ds(start, count), columns] for ref, start, count in pieces]
    return parts[0] if len(parts) == 1 else jnp.concatenate(parts, axis=0)


def each_block(width, body):
    for begin in range(0, width, BLOCK):
        body(pl.ds(begin, BLOCK))


def tap_spectrum(table, weights):
    return dot(table, jnp.concatenate([weights, weights], axis=0))


def gate_factor(conv):
    gate = sigmoid(conv)
    return gate * (1.0 + conv * (1.0 - gate))


FIRST, BACK0, BACK1, AHEAD0 = range(0, 8, 2)


def looked_up(notes, layer):
    return notes[layer], notes[layer + 1], notes[FIRST]


def sorted_halos(near, far, at, halos):
    even = lax.rem(lax.axis_index("tm") + 1, 2)
    rows = pl.ds(at, halos.shape[1])
    halos[even] = near[rows, :]
    halos[1 - even] = far[rows, :]
    return halos.at[0], halos.at[1]


def lane_sum(values):
    total = values[:, :LANES]
    for lane in range(LANES, values.shape[1], LANES):
        total = total + values[:, lane : lane + LANES]
    return total


def first_pass(pieces, mean, inverse, gain, mask, tables, mixed, q, columns, scaled, sum_a, sum_b):
    g_table, x_table = tables
    grad_masked = wide(mask, BLOCK) * transform(x_table, product_conj(transform(g_table, mixed), q))
    centered = window(pieces, columns).astype(F32) - wide(mean[...], BLOCK)
    weighted = grad_masked * (centered * wide(inverse[...], BLOCK))
    gain = gain(columns)
    by_gain = grad_masked * gain
    scaled[:, columns] = by_gain
    sum_a[...] += lane_sum(by_gain)
    sum_b[...] += lane_sum(weighted * gain)
    return weighted


def last_pass(grad_pieces, pieces, mean, inverse, scaled, sum_a, sum_b, grad_x, chunk=128):
    width = scaled.shape[1]
    at = 0
    for (ref, start, count), (saved, base, _) in zip(grad_pieces, pieces):
        for begin in range(0, count, chunk):
            here = min(chunk, count - begin)
            rows = pl.ds(at + begin, here)
            inv = inverse[rows, :]
            mean_a = jnp.sum(sum_a[rows, :], axis=1, keepdims=True) * (1.0 / width)
            mean_b = jnp.sum(sum_b[rows, :], axis=1, keepdims=True) * (1.0 / width)
            slope = inv * jnp.broadcast_to(mean_b, (here, LANES)) * inv
            fixed = inv * jnp.broadcast_to(mean_a, (here, LANES)) - slope * mean[rows, :]
            for lane in range(0, width, LANES):
                tile = pl.ds(lane, LANES)
                x = saved[pl.ds(base + begin, here), tile].astype(F32)
                change = inv * scaled[rows, tile] - fixed - slope * x
                grad_x[rows, tile] = (ref[pl.ds(start + begin, here), tile].astype(F32) + change).astype(BF16)
        at += count


def frame_mask(rows, first, length):
    frame = first + lax.broadcasted_iota(jnp.int32, (rows, LANES), 0)
    return ((frame >= 0) & (frame < length)).astype(F32)


def slot_row(weights, slot):
    last = weights.shape[1] - 1
    return lambda columns: weights[slot, last : last + 1, columns].astype(F32)


def prepare_kernel(
    reach, notes, kernels, gains, saved, act, weights, ahead0, ahead1, near, far, masked, mean, inverse
):
    own = act.shape[0]
    for even in range(2):

        @pl.when(lax.rem(lax.axis_index("tm") + 1, 2) == even)
        def _():
            for x, at in ((saved.at[1], 0), (act, reach)):
                tail, head = (near, far) if even else (far, near)
                tail[pl.ds(at, reach), :] = x[pl.ds(own - reach, reach), :]
                head[pl.ds(at, reach), :] = x[pl.ds(0, reach), :]

    count = kernels.shape[0]
    for slot in range(kernels.shape[1]):
        weights[slot, :count, :] = kernels[:, slot, :]
        weights[slot, count:, :] = gains[slot : slot + 1, :]
    ahead0[...] = weights[notes[AHEAD0]]
    ahead1[...] = weights[notes[FIRST + 1]]
    slot, length, first = looked_up(notes, BACK0)
    norm_pieces([(saved.at[0], 0, own)], slot_row(weights, slot), first, length, masked, mean, inverse)


def norm_halo(left, right, own, gain, first, length, halo):
    reach = left.shape[0]
    norm_pieces([(left, 0, reach)], gain, first - reach, length, halo)
    norm_pieces([(right, 0, reach)], gain, first + own, length, halo.at[pl.ds(reach, reach)])


def joined(halo, own, columns):
    reach = halo.shape[0] // 2
    return jnp.concatenate([halo[:reach, columns], own[:, columns], halo[reach:, columns]], axis=0)


def first_backward_kernel(
    reach, notes, saved, far, near, grads, weights, masked, mean, inverse,
    m_table, q_table, c_table, g_table, x_table,
    grad_x, near_edge, far_edge, halo, inner, gain_sum, halos, grad_halos, scaled, sum_a, sum_b,
):
    own, width = grads.shape
    edge = near_edge.shape[0]
    slot, length, first = looked_up(notes, BACK0)
    gain = slot_row(weights, slot)
    left, right = sorted_halos(near, far, 0, halos)
    grad_left, grad_right = sorted_halos(near, far, reach, grad_halos)
    norm_halo(left, right, own, gain, first, length, halo)
    grad_pieces = [(grad_left, 0, edge), (grads, 0, own), (grad_right, 0, edge)]
    pieces = [(saved.at[0], 0, own)]
    mask = frame_mask(own, first, length)
    sum_a[...] = jnp.zeros_like(sum_a)
    sum_b[...] = jnp.zeros_like(sum_b)

    def block(columns):
        m = transform(m_table, joined(halo, masked, columns))
        q = tap_spectrum(q_table[...], weights[slot, :, columns])
        conv = transform(c_table, product(m, q))
        mixed = (window(grad_pieces, columns).astype(F32) * gate_factor(conv)).astype(BF16)
        inner[:, columns] = mixed[edge : edge + own]
        weighted = first_pass(
            pieces, mean, inverse, gain, mask, (g_table, x_table), mixed, q, columns, scaled, sum_a, sum_b
        )
        gain_sum[:, columns] = jnp.sum(weighted, axis=0, keepdims=True)

    each_block(width, block)
    last_pass([(grads, 0, own)], pieces, mean, inverse, scaled, sum_a, sum_b, grad_x)
    for even in range(2):

        @pl.when(lax.rem(lax.axis_index("tm") + 1, 2) == even)
        def _():
            top, bottom = (far_edge, near_edge) if even else (near_edge, far_edge)
            top[...] = grad_x[pl.ds(0, edge), :]
            bottom[...] = grad_x[pl.ds(own - edge, edge), :]


def tap_term(go_table, t_table, m, mixed):
    g_own = dot(go_table[...], jnp.concatenate([mixed, mixed], axis=0))
    return transform(t_table, product_conj(m, g_own))


def put_taps(taps, tap, gain_sum, columns):
    row = lax.broadcasted_iota(jnp.int32, tap.shape, 0)
    taps[:, columns] = jnp.where(row == tap.shape[0] - 1, gain_sum, tap).astype(taps.dtype)


def first_taps_kernel(halo, masked, inner, gain_sum, m_table, go_table, t_table, taps):
    def block(columns):
        m = transform(m_table, joined(halo, masked, columns))
        put_taps(taps, tap_term(go_table, t_table, m, inner[:, columns]), gain_sum[:, columns], columns)

    each_block(masked.shape[1], block)


def added(mine, other):
    return (mine[...].astype(F32) + other[...].astype(F32)).astype(BF16)


def add_kernel(mine, other, out):
    out[...] = added(mine, other)


def below_kernel(mine0, other0, mine1, other1, out):
    count = mine0.shape[0]
    out[pl.ds(0, count), :] = added(mine0, other0)
    out[pl.ds(count, count), :] = added(mine1, other1)


def second_ready_kernel(
    reach, notes, saved, far, near, weights, ahead0, ahead1, m_table, q_table, c_table,
    m_out, q_out, factor, conv_out, mean, inverse, ahead, next_layer, halo, halos, masked,
):
    left, right = sorted_halos(near, far, reach, halos)
    ahead[pl.ds(0, reach), :] = left[...]
    ahead[pl.ds(reach, reach), :] = right[...]
    ahead[pl.ds(2 * reach, ahead0.shape[0]), :] = ahead0[...]
    next_layer[...] = ahead1[...]
    own, width = masked.shape
    slot, length, first = looked_up(notes, BACK1)
    gain = slot_row(weights, slot)
    left, right = sorted_halos(near, far, 0, halos)
    norm_pieces([(saved.at[1], 0, own)], gain, first, length, masked, mean, inverse)
    norm_halo(left, right, own, gain, first, length, halo)

    def block(columns):
        m = transform(m_table, joined(halo, masked, columns))
        q = tap_spectrum(q_table[...], weights[slot, :, columns])
        conv = transform(c_table, product(m, q))
        m_out[:, columns] = m
        q_out[:, columns] = q
        factor[:, columns] = gate_factor(conv)
        edge = (conv.shape[0] - own) // 2
        conv_out[:, columns] = conv[edge : edge + own]

    each_block(width, block)


def second_taps_kernel(
    notes, received, far, near, weights, m, factor, conv, go_table, t_table, mixed_out, taps, halos
):
    own, width = conv.shape
    rows = factor.shape[0]
    edge = (rows - own) // 2
    gain = slot_row(weights, notes[BACK1])
    left, right = sorted_halos(near, far, 0, halos)
    pieces = [(left, 0, edge), (received, 0, own), (right, 0, edge)]

    def block(columns):
        mixed = (window(pieces, columns).astype(F32) * factor[:, columns]).astype(BF16)
        mixed_out[:, columns] = mixed
        inner = mixed[edge : edge + own]
        gain_sum = jnp.sum(inner.astype(F32) * conv[:, columns], axis=0, keepdims=True) / gain(columns)
        put_taps(taps, tap_term(go_table, t_table, m[:, columns], inner), gain_sum, columns)

    each_block(width, block)


def second_backward_kernel(
    notes, saved, received, weights, mixed, q, mean, inverse, g_table, x_table, grad_x, scaled, sum_a, sum_b
):
    own, width = grad_x.shape
    slot, length, first = looked_up(notes, BACK1)
    pieces = [(saved.at[1], 0, own)]
    mask = frame_mask(own, first, length)
    sum_a[...] = jnp.zeros_like(sum_a)
    sum_b[...] = jnp.zeros_like(sum_b)

    def block(columns):
        first_pass(
            pieces, mean, inverse, slot_row(weights, slot), mask, (g_table, x_table), mixed[:, columns], q[:, columns],
            columns, scaled, sum_a, sum_b,
        )

    each_block(width, block)
    last_pass([(received, 0, own)], pieces, mean, inverse, scaled, sum_a, sum_b, grad_x)


def row_gain(layer):
    last = layer.shape[0] - 1
    return lambda columns: layer[last : last + 1, columns].astype(F32)


def first_forward_kernel(reach, notes, act, ahead, m_table, q_table, c_table, out, halo, masked):
    own, width = act.shape
    middle = reach // 2
    _, length, first = looked_up(notes, AHEAD0)
    left, right = ahead.at[pl.ds(0, reach)], ahead.at[pl.ds(reach, reach)]
    layer = ahead.at[pl.ds(2 * reach, ahead.shape[0] - 2 * reach)]
    inner = [(left, middle, middle), (act, 0, own), (right, 0, middle)]
    norm_pieces([(act, 0, own)], row_gain(layer), first, length, masked)
    norm_halo(left, right, own, row_gain(layer), first, length, halo)

    def block(columns):
        q = tap_spectrum(q_table[...], layer[:, columns])
        conv = transform(c_table, product(transform(m_table, joined(halo, masked, columns)), q))
        out[:, columns] = (window(inner, columns).astype(F32) + conv * sigmoid(conv)).astype(BF16)

    each_block(width, block)


def second_forward_kernel(notes, between, layer, m_table, q_table, c_table, out, masked):
    own, width = out.shape
    rows = between.shape[0]
    edge = (rows - own) // 2
    _, length, first = looked_up(notes, AHEAD0)
    norm_pieces([(between, 0, rows)], row_gain(layer), first - edge, length, masked, chunk=rows // 2)

    def block(columns):
        q = tap_spectrum(q_table[...], layer[:, columns])
        conv = transform(c_table, product(transform(m_table, masked[:, columns]), q))
        out[:, columns] = (between[edge : edge + own, columns].astype(F32) + conv * sigmoid(conv)).astype(BF16)

    each_block(width, block)


def pack_kernel(
    reaches, saved, grad, back_lengths, ahead_lengths, back_slots, ahead_slots,
    near, far, notes, back_len, ahead_len, back_slot, ahead_slot, sems,
):
    own = grad.shape[1]
    even = lax.rem(lax.axis_index("tm") + 1, 2)
    copies = []
    at = 0
    for x, reach in zip((saved, grad), reaches):
        for out, tail in ((near, even), (far, 1 - even)):
            start = pl.multiple_of(tail * (own - reach), 16)
            copies.append((x.at[0, pl.ds(start, reach)], out.at[pl.ds(at, reach)]))
        at += reach
    small = [(back_lengths, back_len), (ahead_lengths, ahead_len), (back_slots, back_slot), (ahead_slots, ahead_slot)]
    copies = [pltpu.make_async_copy(a, b, sems.at[k]) for k, (a, b) in enumerate(small + copies)]
    for copy in copies:
        copy.start()
    for copy in copies:
        copy.wait()
    section, sections = lax.axis_index("section"), lax.axis_size("section")
    notes[FIRST] = lax.axis_index("tm") * own
    notes[FIRST + 1] = ahead_slot[1, section]
    notes[BACK0] = back_slot[0, section]
    notes[BACK0 + 1] = back_len[section]
    notes[BACK1] = back_slot[1, section]
    notes[BACK1 + 1] = back_len[lax.rem(section + 1, sections)]
    notes[AHEAD0] = ahead_slot[0, section]
    notes[AHEAD0 + 1] = ahead_len[lax.rem(section + sections - 2, sections)]


def final_kernel(notes, mine, other, act, grad, act_out, grad_out, taps_out, gains_out, taps, gains, sems):
    copies = [
        pltpu.make_async_copy(act, act_out, sems.at[0]),
        pltpu.make_async_copy(grad, grad_out, sems.at[1]),
    ]
    for copy in copies:
        copy.start()
    count, slots, width = taps.shape
    step = width // 4
    for begin in range(0, width, step):
        columns = pl.ds(begin, step)
        total = mine[:, columns].astype(F32) + other[:, columns].astype(F32)
        ticks = total[: count + 1], total[count + 1 :]
        for slot in range(slots):
            use = [(notes[layer] == slot).astype(F32) for layer in (BACK0, BACK1)]
            both = use[0] * ticks[0] + use[1] * ticks[1]
            taps[:, slot, columns] = both[:count]
            gains[slot : slot + 1, columns] = both[count:]
        for source, target in ((taps.at[:, :, columns], taps_out.at[:, :, columns]),):
            copies.append(pltpu.make_async_copy(source, target, sems.at[len(copies)]))
            copies[-1].start()
    copies.append(pltpu.make_async_copy(gains, gains_out, sems.at[len(copies)]))
    copies[-1].start()
    for copy in copies:
        copy.wait()


def span(reach, own):
    return np.arange(-reach, own + reach)


VMEM = pl.BlockSpec(memory_space=pltpu.VMEM)
SMEM = pl.BlockSpec(memory_space=pltpu.SMEM)
ANY = pl.BlockSpec(memory_space=pl.ANY)
HBM = pl.BlockSpec(memory_space=pltpu.HBM)
LIMIT = 24 * 1024 * 1024
FULL = 127 * 512 * 1024


def call(kernel, outs, scratch, operands, micros, specs=None, out_specs=None, limit=LIMIT, after=()):
    if specs is None:
        specs = [SMEM if x.dtype == jnp.int32 else VMEM for x in operands]
    if after:
        inner, place = kernel, len(operands)
        operands, specs = [*operands, *after], [*specs, *[ANY] * len(after)]

        def kernel(*refs):
            return inner(*refs[:place], *refs[place + len(after) :])

    return pl.pallas_call(
        kernel,
        out_shape=outs,
        in_specs=specs,
        out_specs=jax.tree.map(lambda _: VMEM, outs) if out_specs is None else out_specs,
        scratch_shapes=scratch,
        compiler_params=pltpu.CompilerParams(vmem_limit_bytes=limit),
        cost_estimate=pl.CostEstimate(flops=int(micros * 1e9), bytes_accessed=0, transcendentals=0),
    )(*operands)


def like(rows, width, dtype):
    return jax.ShapeDtypeStruct((rows, width), dtype)


def up16(count):
    return -(-count // 16) * 16


def local(
    act_in, grad_in, saved_inputs, kernels, norm_gains,
    forward_lengths, backward_lengths, forward_slots, backward_slots,
):
    sections = lax.axis_size("section")
    shards = lax.axis_size("tm")
    act, grad, saved = act_in[0], grad_in[0], saved_inputs[0]
    own, width = act.shape
    tap_count = kernels.shape[2]
    half = (tap_count - 1) // 2
    one, two = up16(half), up16(2 * half)
    size, small = own + 2 * two, own + 2 * one

    def shifted(x, by):
        return lax.ppermute(x, "section", [(i, (i + by) % sections) for i in range(sections)])

    def swapped(near, far, by=0):
        results = []
        for x, begin in ((far, 1), (near, 0)):
            pairs = [(i, i + 1) for i in range(begin, shards - 1, 2)]
            pairs = [
                (s * shards + i, (s + by) % sections * shards + j)
                for s in range(sections)
                for a, b in pairs
                for i, j in ((a, b), (b, a))
            ]
            results.append(lax.ppermute(x, ("section", "tm"), pairs))
        return results[::-1]

    act_ahead = shifted(act, 2)
    lengths = pltpu.SMEM(backward_lengths.shape, jnp.int32)
    forward_slots, backward_slots = forward_slots.T, backward_slots.T
    slots = pltpu.SMEM(backward_slots.shape, jnp.int32)
    near0, far0, notes = call(
        functools.partial(pack_kernel, (two, one)),
        (like(two + one, width, BF16), like(two + one, width, BF16), jax.ShapeDtypeStruct((8,), jnp.int32)),
        [lengths, lengths, slots, slots, pltpu.SemaphoreType.DMA((8,))],
        (saved, grad_in, backward_lengths, forward_lengths, backward_slots, forward_slots),
        0, [HBM] * 6, (VMEM, VMEM, SMEM), FULL,
    )
    near0, far0 = swapped(near0, far0)
    tap_back = np.concatenate([from_freq(size, np.arange(tap_count) - half), np.zeros((1, size))], axis=0)
    m_table = stacked(to_freq(size, span(two, own)))
    q_table = tap_freq(size, tap_count)
    c_table = stacked(from_freq(size, span(one, own)))
    go_table = beside(to_freq(size, np.arange(own)))
    t_table = stacked(tap_back)

    def run(kernel, outs, scratch, operands, micros=0, *after):
        return call(kernel, outs, scratch, [jnp.asarray(x) for x in operands], micros, after=after)

    rows = [pltpu.VMEM((own, width), F32)] + [pltpu.VMEM((own, LANES), F32)] * 2
    layer = like(own, width, BF16), like(own, LANES, F32), like(own, LANES, F32)
    weights, ahead0, ahead1, near1, far1, *layer0 = run(
        functools.partial(prepare_kernel, two),
        (
            jax.ShapeDtypeStruct((kernels.shape[1], tap_count + 1, width), BF16), like(tap_count + 1, width, BF16),
            like(tap_count + 1, width, BF16), like(2 * two, width, BF16), like(2 * two, width, BF16), *layer,
        ),
        [],
        [notes, kernels[0].transpose(1, 0, 2), norm_gains[0], saved, act],
        0,
    )
    near1, far1 = swapped(near1, far1)
    g_table, x_table = stacked(to_freq(size, span(one, own))), stacked(from_freq(size, span(0, own)))
    grad_mid, near2, far2, halo0, inner0, gain0 = run(
        functools.partial(first_backward_kernel, two),
        (
            like(own, width, BF16), like(one, width, BF16), like(one, width, BF16),
            like(2 * two, width, BF16), like(own, width, BF16), like(1, width, F32),
        ),
        [pltpu.VMEM((2, two, width), BF16), pltpu.VMEM((2, one, width), BF16), *rows],
        [
            notes, saved, far0, near0, grad, weights, *layer0,
            m_table, q_table, c_table, g_table, x_table,
        ],
        4,
        act_ahead,
    )
    grad_mid = shifted(grad_mid, -1)
    near2, far2 = swapped(near2, far2, -1)
    taps0 = run(
        first_taps_kernel, like(tap_count + 1, width, BF16), [],
        [halo0, layer0[0], inner0, gain0, m_table, go_table, t_table],
        0,
    )
    halo_scratch = [
        pltpu.VMEM((2 * two, width), BF16), pltpu.VMEM((2, two, width), BF16), pltpu.VMEM((own, width), BF16)
    ]
    m1, q1, factor1, conv1, mean1, inverse1, ahead0, ahead1 = run(
        functools.partial(second_ready_kernel, two),
        (
            like(size, width, F32), like(size, width, F32), like(small, width, F32), like(own, width, F32),
            like(own, LANES, F32), like(own, LANES, F32), like(2 * two + tap_count + 1, width, BF16),
            like(tap_count + 1, width, BF16),
        ),
        halo_scratch,
        [notes, saved, far1, near1, weights, ahead0, ahead1, m_table, q_table, c_table],
        5,
        taps0, near2, far2,
    )
    ahead0, ahead1 = shifted(ahead0, 2), shifted(ahead1, 1)
    def partner(x, step):
        return lax.ppermute(x, "tm", [(i, i ^ step) for i in range(shards)])

    other0 = partner(taps0, 1)
    mixed1, taps1 = run(
        second_taps_kernel,
        (like(small, width, BF16), like(tap_count + 1, width, BF16)),
        [pltpu.VMEM((2, one, width), BF16)],
        [notes, grad_mid, far2, near2, weights, m1, factor1, conv1, go_table, t_table],
        2,
    )
    grad_out = run(
        second_backward_kernel,
        like(own, width, BF16),
        rows,
        [
            notes, saved, grad_mid, weights, mixed1, q1, mean1, inverse1,
            g_table, x_table,
        ],
        6,
    )
    grad_out = shifted(grad_out, -1)
    other1 = partner(taps1, 1)
    mine = call(below_kernel, like(2 * (tap_count + 1), width, BF16), [], (taps0, other0, taps1, other1), 6)
    between = run(
        functools.partial(first_forward_kernel, two),
        like(small, width, BF16),
        [pltpu.VMEM((2 * two, width), BF16), pltpu.VMEM((own, width), BF16)],
        [notes, act_ahead, ahead0, m_table, q_table, c_table],
        10,
        mine,
    )
    act_out = run(
        second_forward_kernel,
        like(own, width, BF16),
        [pltpu.VMEM((small, width), BF16)],
        [
            notes, between, ahead1,
            stacked(to_freq(small, span(one, own))), tap_freq(small, tap_count), stacked(from_freq(small, span(0, own))),
        ],
        10,
    )
    step = 2
    while True:
        other = partner(mine, step)
        step *= 2
        if step >= shards:
            break
        mine = call(add_kernel, like(*mine.shape, BF16), [], (mine, other), 0)
    slots = kernels.shape[1]
    act_out, grad_out, taps, gains = call(
        final_kernel,
        (
            like(own, width, BF16), like(own, width, BF16),
            jax.ShapeDtypeStruct((tap_count, slots, width), F32), like(slots, width, F32),
        ),
        [
            pltpu.VMEM((tap_count, slots, width), F32), pltpu.VMEM((slots, width), F32),
            pltpu.SemaphoreType.DMA((7,)),
        ],
        (notes, mine, other, act_out, grad_out),
        0, [SMEM] + [VMEM] * 2 + [ANY] * 2, (ANY,) * 4,
    )
    return act_out[None], grad_out[None], taps.transpose(1, 0, 2)[None], gains[None]


def solution(mesh):
    in_specs = (
        P("section", "tm", None),
        P("section", "tm", None),
        P("section", None, "tm", None),
        P("section", None, None, None),
        P("section", None, None),
        P(),
        P(),
        P(),
        P(),
    )
    out_specs = (
        P("section", "tm", None),
        P("section", "tm", None),
        P("section", None, None, None),
        P("section", None, None),
    )
    return jax.shard_map(local, mesh=mesh, in_specs=in_specs, out_specs=out_specs, check_vma=False)
```

```python
import functools

import jax
import jax.numpy as jnp
import ml_dtypes
import numpy as np
from jax import lax
from jax.experimental import pallas as pl
from jax.experimental.pallas import tpu as pltpu
from jax.sharding import PartitionSpec as P

epsilon = 1e-05
BLOCK = 2048
LANES = 128
F32 = jnp.float32
BF16 = jnp.bfloat16


def split(matrix):
    high = matrix.astype(ml_dtypes.bfloat16)
    low = (matrix - high.astype(np.float64)).astype(ml_dtypes.bfloat16)
    return high, low


def angles(size, times):
    return 2.0 * np.pi / size * np.outer(np.arange(size // 2) + 0.5, np.asarray(times, np.float64))


def to_freq(size, times):
    phase = angles(size, times)
    return np.concatenate([np.cos(phase), -np.sin(phase)], axis=0)


def from_freq(size, times):
    phase = angles(size, times).T
    return 2.0 / size * np.concatenate([np.cos(phase), -np.sin(phase)], axis=1)


def stacked(matrix):
    return np.concatenate(split(matrix), axis=0)


def beside(matrix):
    return np.concatenate(split(matrix), axis=1)


def tap_freq(size, taps):
    phase = angles(size, np.arange(taps) - (taps - 1) // 2)
    table = np.concatenate([np.cos(phase), np.sin(phase)], axis=0)
    return beside(np.concatenate([table, np.zeros((size, 1))], axis=1))


def dot(a, b):
    return jnp.dot(a, b, preferred_element_type=F32)


def transform(table, values):
    return sum(halves(dot(table[...], values.astype(BF16))))


def halves(values):
    half = values.shape[0] // 2
    return values[:half], values[half:]


def product(a, b):
    ar, ai = halves(a)
    br, bi = halves(b)
    return jnp.concatenate([ar * br - ai * bi, ar * bi + ai * br], axis=0)


def product_conj(a, b):
    ar, ai = halves(a)
    br, bi = halves(b)
    return jnp.concatenate([ar * br + ai * bi, ai * br - ar * bi], axis=0)


def sigmoid(values):
    return 0.5 * jnp.tanh(0.5 * values) + 0.5


def wide(stat, count):
    return jnp.concatenate([stat] * (count // LANES), axis=1)


def norm_rows(ref, start, count, at, gain, first, length, masked_ref, mean_ref, inverse_ref):
    width = masked_ref.shape[1]
    rows = pl.ds(start, count)
    tiles = [pl.ds(i * LANES, LANES) for i in range(width // LANES)]

    def values(tile):
        return ref[rows, tile].astype(F32)

    total = values(tiles[0])
    for tile in tiles[1:]:
        total = total + values(tile)
    mean = jnp.sum(total, axis=1, keepdims=True) * (1.0 / width)
    mean = jnp.broadcast_to(mean, (count, LANES))
    square = jnp.zeros((count, LANES), F32)
    for tile in tiles:
        center = values(tile) - mean
        square = square + center * center
    var = jnp.sum(square, axis=1, keepdims=True) * (1.0 / width)
    inverse = jnp.broadcast_to(lax.rsqrt(var + epsilon), (count, LANES))
    frame = first + at + lax.broadcasted_iota(jnp.int32, (count, LANES), 0)
    mask = ((frame >= 0) & (frame < length)).astype(F32)
    scale = mask * inverse
    out = pl.ds(at, count)
    for tile in tiles:
        masked_ref[out, tile] = ((values(tile) - mean) * scale * gain(tile)).astype(BF16)
    if mean_ref is not None:
        mean_ref[out, :] = mean
        inverse_ref[out, :] = inverse


def norm_pieces(pieces, gain, first, length, masked_ref, mean_ref=None, inverse_ref=None, chunk=128):
    at = 0
    for ref, start, count in pieces:
        for begin in range(0, count, chunk):
            norm_rows(
                ref, start + begin, min(chunk, count - begin), at + begin,
                gain, first, length, masked_ref, mean_ref, inverse_ref,
            )
        at += count


def window(pieces, columns):
    parts = [ref[pl.ds(start, count), columns] for ref, start, count in pieces]
    return parts[0] if len(parts) == 1 else jnp.concatenate(parts, axis=0)


def each_block(width, body):
    for begin in range(0, width, BLOCK):
        body(pl.ds(begin, BLOCK))


def tap_spectrum(table, weights):
    return dot(table, jnp.concatenate([weights, weights], axis=0))


def gate_factor(conv):
    gate = sigmoid(conv)
    return gate * (1.0 + conv * (1.0 - gate))


FIRST, BACK0, BACK1, AHEAD0 = range(0, 8, 2)


def looked_up(notes, layer):
    return notes[layer], notes[layer + 1], notes[FIRST]


def sorted_halos(near, far, at, halos):
    even = lax.rem(lax.axis_index("tm") + 1, 2)
    rows = pl.ds(at, halos.shape[1])
    halos[even] = near[rows, :]
    halos[1 - even] = far[rows, :]
    return halos.at[0], halos.at[1]


def lane_sum(values):
    total = values[:, :LANES]
    for lane in range(LANES, values.shape[1], LANES):
        total = total + values[:, lane : lane + LANES]
    return total


def first_pass(pieces, mean, inverse, gain, mask, tables, mixed, q, columns, scaled, sum_a, sum_b):
    g_table, x_table = tables
    grad_masked = wide(mask, BLOCK) * transform(x_table, product_conj(transform(g_table, mixed), q))
    centered = window(pieces, columns).astype(F32) - wide(mean[...], BLOCK)
    weighted = grad_masked * (centered * wide(inverse[...], BLOCK))
    gain = gain(columns)
    by_gain = grad_masked * gain
    scaled[:, columns] = by_gain
    sum_a[...] += lane_sum(by_gain)
    sum_b[...] += lane_sum(weighted * gain)
    return weighted


def last_pass(grad_pieces, pieces, mean, inverse, scaled, sum_a, sum_b, grad_x, chunk=128):
    width = scaled.shape[1]
    at = 0
    for (ref, start, count), (saved, base, _) in zip(grad_pieces, pieces):
        for begin in range(0, count, chunk):
            here = min(chunk, count - begin)
            rows = pl.ds(at + begin, here)
            inv = inverse[rows, :]
            mean_a = jnp.sum(sum_a[rows, :], axis=1, keepdims=True) * (1.0 / width)
            mean_b = jnp.sum(sum_b[rows, :], axis=1, keepdims=True) * (1.0 / width)
            slope = inv * jnp.broadcast_to(mean_b, (here, LANES)) * inv
            fixed = inv * jnp.broadcast_to(mean_a, (here, LANES)) - slope * mean[rows, :]
            for lane in range(0, width, LANES):
                tile = pl.ds(lane, LANES)
                x = saved[pl.ds(base + begin, here), tile].astype(F32)
                change = inv * scaled[rows, tile] - fixed - slope * x
                grad_x[rows, tile] = (ref[pl.ds(start + begin, here), tile].astype(F32) + change).astype(BF16)
        at += count


def frame_mask(rows, first, length):
    frame = first + lax.broadcasted_iota(jnp.int32, (rows, LANES), 0)
    return ((frame >= 0) & (frame < length)).astype(F32)


def slot_row(weights, slot):
    last = weights.shape[1] - 1
    return lambda columns: weights[slot, last : last + 1, columns].astype(F32)


def prepare_kernel(
    reach, notes, kernels, gains, saved, act, weights, ahead0, ahead1, near, far, masked, mean, inverse
):
    own = act.shape[0]
    for even in range(2):

        @pl.when(lax.rem(lax.axis_index("tm") + 1, 2) == even)
        def _():
            for x, at in ((saved.at[1], 0), (act, reach)):
                tail, head = (near, far) if even else (far, near)
                tail[pl.ds(at, reach), :] = x[pl.ds(own - reach, reach), :]
                head[pl.ds(at, reach), :] = x[pl.ds(0, reach), :]

    count = kernels.shape[0]
    for slot in range(kernels.shape[1]):
        weights[slot, :count, :] = kernels[:, slot, :]
        weights[slot, count:, :] = gains[slot : slot + 1, :]
    ahead0[...] = weights[notes[AHEAD0]]
    ahead1[...] = weights[notes[FIRST + 1]]
    slot, length, first = looked_up(notes, BACK0)
    norm_pieces([(saved.at[0], 0, own)], slot_row(weights, slot), first, length, masked, mean, inverse)


def norm_halo(left, right, own, gain, first, length, halo):
    reach = left.shape[0]
    norm_pieces([(left, 0, reach)], gain, first - reach, length, halo)
    norm_pieces([(right, 0, reach)], gain, first + own, length, halo.at[pl.ds(reach, reach)])


def joined(halo, own, columns):
    reach = halo.shape[0] // 2
    return jnp.concatenate([halo[:reach, columns], own[:, columns], halo[reach:, columns]], axis=0)


def first_backward_kernel(
    reach, notes, saved, far, near, grads, weights, masked, mean, inverse,
    m_table, q_table, c_table, g_table, x_table,
    grad_x, near_edge, far_edge, halo, inner, gain_sum, halos, grad_halos, scaled, sum_a, sum_b,
):
    own, width = grads.shape
    edge = near_edge.shape[0]
    slot, length, first = looked_up(notes, BACK0)
    gain = slot_row(weights, slot)
    left, right = sorted_halos(near, far, 0, halos)
    grad_left, grad_right = sorted_halos(near, far, reach, grad_halos)
    norm_halo(left, right, own, gain, first, length, halo)
    grad_pieces = [(grad_left, 0, edge), (grads, 0, own), (grad_right, 0, edge)]
    pieces = [(saved.at[0], 0, own)]
    mask = frame_mask(own, first, length)
    sum_a[...] = jnp.zeros_like(sum_a)
    sum_b[...] = jnp.zeros_like(sum_b)

    def block(columns):
        m = transform(m_table, joined(halo, masked, columns))
        q = tap_spectrum(q_table[...], weights[slot, :, columns])
        conv = transform(c_table, product(m, q))
        mixed = (window(grad_pieces, columns).astype(F32) * gate_factor(conv)).astype(BF16)
        inner[:, columns] = mixed[edge : edge + own]
        weighted = first_pass(
            pieces, mean, inverse, gain, mask, (g_table, x_table), mixed, q, columns, scaled, sum_a, sum_b
        )
        gain_sum[:, columns] = jnp.sum(weighted, axis=0, keepdims=True)

    each_block(width, block)
    last_pass([(grads, 0, own)], pieces, mean, inverse, scaled, sum_a, sum_b, grad_x)
    for even in range(2):

        @pl.when(lax.rem(lax.axis_index("tm") + 1, 2) == even)
        def _():
            top, bottom = (far_edge, near_edge) if even else (near_edge, far_edge)
            top[...] = grad_x[pl.ds(0, edge), :]
            bottom[...] = grad_x[pl.ds(own - edge, edge), :]


def tap_term(go_table, t_table, m, mixed):
    g_own = dot(go_table[...], jnp.concatenate([mixed, mixed], axis=0))
    return transform(t_table, product_conj(m, g_own))


def put_taps(taps, tap, gain_sum, columns):
    row = lax.broadcasted_iota(jnp.int32, tap.shape, 0)
    taps[:, columns] = jnp.where(row == tap.shape[0] - 1, gain_sum, tap).astype(taps.dtype)


def first_taps_kernel(halo, masked, inner, gain_sum, m_table, go_table, t_table, taps):
    def block(columns):
        m = transform(m_table, joined(halo, masked, columns))
        put_taps(taps, tap_term(go_table, t_table, m, inner[:, columns]), gain_sum[:, columns], columns)

    each_block(masked.shape[1], block)


def added(mine, other):
    return (mine[...].astype(F32) + other[...].astype(F32)).astype(BF16)


def add_kernel(mine, other, out):
    out[...] = added(mine, other)


def second_ready_kernel(
    reach, notes, saved, far, near, weights, m_table, q_table, c_table,
    m_out, q_out, factor, conv_out, mean, inverse, ahead, halo, halos, masked,
):
    left, right = sorted_halos(near, far, reach, halos)
    ahead[pl.ds(0, reach), :] = left[...]
    ahead[pl.ds(reach, reach), :] = right[...]
    own, width = masked.shape
    slot, length, first = looked_up(notes, BACK1)
    gain = slot_row(weights, slot)
    left, right = sorted_halos(near, far, 0, halos)
    norm_pieces([(saved.at[1], 0, own)], gain, first, length, masked, mean, inverse)
    norm_halo(left, right, own, gain, first, length, halo)

    def block(columns):
        m = transform(m_table, joined(halo, masked, columns))
        q = tap_spectrum(q_table[...], weights[slot, :, columns])
        conv = transform(c_table, product(m, q))
        m_out[:, columns] = m
        q_out[:, columns] = q
        factor[:, columns] = gate_factor(conv)
        edge = (conv.shape[0] - own) // 2
        conv_out[:, columns] = conv[edge : edge + own]

    each_block(width, block)


def second_taps_kernel(
    notes, received, far, near, weights, m, factor, conv, taps0, go_table, t_table, mixed_out, taps, halos
):
    own, width = conv.shape
    rows = factor.shape[0]
    count = taps0.shape[0]
    taps[pl.ds(0, count), :] = taps0[...]
    taps1 = taps.at[pl.ds(count, count)]
    edge = (rows - own) // 2
    gain = slot_row(weights, notes[BACK1])
    left, right = sorted_halos(near, far, 0, halos)
    pieces = [(left, 0, edge), (received, 0, own), (right, 0, edge)]

    def block(columns):
        mixed = (window(pieces, columns).astype(F32) * factor[:, columns]).astype(BF16)
        mixed_out[:, columns] = mixed
        inner = mixed[edge : edge + own]
        gain_sum = jnp.sum(inner.astype(F32) * conv[:, columns], axis=0, keepdims=True) / gain(columns)
        put_taps(taps1, tap_term(go_table, t_table, m[:, columns], inner), gain_sum, columns)

    each_block(width, block)


def second_backward_kernel(
    notes, saved, received, weights, mixed, q, mean, inverse, g_table, x_table, grad_x, scaled, sum_a, sum_b
):
    own, width = grad_x.shape
    slot, length, first = looked_up(notes, BACK1)
    pieces = [(saved.at[1], 0, own)]
    mask = frame_mask(own, first, length)
    sum_a[...] = jnp.zeros_like(sum_a)
    sum_b[...] = jnp.zeros_like(sum_b)

    def block(columns):
        first_pass(
            pieces, mean, inverse, slot_row(weights, slot), mask, (g_table, x_table), mixed[:, columns], q[:, columns],
            columns, scaled, sum_a, sum_b,
        )

    each_block(width, block)
    last_pass([(received, 0, own)], pieces, mean, inverse, scaled, sum_a, sum_b, grad_x)


def row_gain(layer):
    last = layer.shape[0] - 1
    return lambda columns: layer[last : last + 1, columns].astype(F32)


def first_forward_kernel(reach, notes, act, ahead, layer, m_table, q_table, c_table, out, halo, masked):
    own, width = act.shape
    middle = reach // 2
    _, length, first = looked_up(notes, AHEAD0)
    left, right = ahead.at[pl.ds(0, reach)], ahead.at[pl.ds(reach, reach)]
    inner = [(left, middle, middle), (act, 0, own), (right, 0, middle)]
    norm_pieces([(act, 0, own)], row_gain(layer), first, length, masked)
    norm_halo(left, right, own, row_gain(layer), first, length, halo)

    def block(columns):
        q = tap_spectrum(q_table[...], layer[:, columns])
        conv = transform(c_table, product(transform(m_table, joined(halo, masked, columns)), q))
        out[:, columns] = (window(inner, columns).astype(F32) + conv * sigmoid(conv)).astype(BF16)

    each_block(width, block)


def second_forward_kernel(notes, between, layer, m_table, q_table, c_table, out, masked):
    own, width = out.shape
    rows = between.shape[0]
    edge = (rows - own) // 2
    _, length, first = looked_up(notes, AHEAD0)
    norm_pieces([(between, 0, rows)], row_gain(layer), first - edge, length, masked, chunk=rows // 2)

    def block(columns):
        q = tap_spectrum(q_table[...], layer[:, columns])
        conv = transform(c_table, product(transform(m_table, masked[:, columns]), q))
        out[:, columns] = (between[edge : edge + own, columns].astype(F32) + conv * sigmoid(conv)).astype(BF16)

    each_block(width, block)


def pack_kernel(
    reaches, saved, grad, back_lengths, ahead_lengths, back_slots, ahead_slots,
    near, far, notes, back_len, ahead_len, back_slot, ahead_slot, sems,
):
    own = grad.shape[1]
    even = lax.rem(lax.axis_index("tm") + 1, 2)
    copies = []
    at = 0
    for x, reach in zip((saved, grad), reaches):
        for out, tail in ((near, even), (far, 1 - even)):
            start = pl.multiple_of(tail * (own - reach), 16)
            copies.append((x.at[0, pl.ds(start, reach)], out.at[pl.ds(at, reach)]))
        at += reach
    small = [(back_lengths, back_len), (ahead_lengths, ahead_len), (back_slots, back_slot), (ahead_slots, ahead_slot)]
    copies = [pltpu.make_async_copy(a, b, sems.at[k]) for k, (a, b) in enumerate(small + copies)]
    for copy in copies:
        copy.start()
    for copy in copies:
        copy.wait()
    section, sections = lax.axis_index("section"), lax.axis_size("section")
    notes[FIRST] = lax.axis_index("tm") * own
    notes[FIRST + 1] = ahead_slot[1, section]
    notes[BACK0] = back_slot[0, section]
    notes[BACK0 + 1] = back_len[section]
    notes[BACK1] = back_slot[1, section]
    notes[BACK1 + 1] = back_len[lax.rem(section + 1, sections)]
    notes[AHEAD0] = ahead_slot[0, section]
    notes[AHEAD0 + 1] = ahead_len[lax.rem(section + sections - 2, sections)]


def final_kernel(notes, mine, other, act, grad, act_out, grad_out, taps_out, gains_out, taps, gains, sems):
    copies = [
        pltpu.make_async_copy(act, act_out, sems.at[0]),
        pltpu.make_async_copy(grad, grad_out, sems.at[1]),
    ]
    for copy in copies:
        copy.start()
    count, slots, width = taps.shape
    step = width // 4
    for begin in range(0, width, step):
        columns = pl.ds(begin, step)
        total = mine[:, columns].astype(F32) + other[:, columns].astype(F32)
        ticks = total[: count + 1], total[count + 1 :]
        for slot in range(slots):
            use = [(notes[layer] == slot).astype(F32) for layer in (BACK0, BACK1)]
            both = use[0] * ticks[0] + use[1] * ticks[1]
            taps[:, slot, columns] = both[:count]
            gains[slot : slot + 1, columns] = both[count:]
        for source, target in ((taps.at[:, :, columns], taps_out.at[:, :, columns]),):
            copies.append(pltpu.make_async_copy(source, target, sems.at[len(copies)]))
            copies[-1].start()
    copies.append(pltpu.make_async_copy(gains, gains_out, sems.at[len(copies)]))
    copies[-1].start()
    for copy in copies:
        copy.wait()


def span(reach, own):
    return np.arange(-reach, own + reach)


VMEM = pl.BlockSpec(memory_space=pltpu.VMEM)
SMEM = pl.BlockSpec(memory_space=pltpu.SMEM)
ANY = pl.BlockSpec(memory_space=pl.ANY)
HBM = pl.BlockSpec(memory_space=pltpu.HBM)
LIMIT = 24 * 1024 * 1024
FULL = 127 * 512 * 1024


def call(kernel, outs, scratch, operands, micros, specs=None, out_specs=None, limit=LIMIT, after=()):
    if specs is None:
        specs = [SMEM if x.dtype == jnp.int32 else VMEM for x in operands]
    if after:
        inner, place = kernel, len(operands)
        operands, specs = [*operands, *after], [*specs, *[ANY] * len(after)]

        def kernel(*refs):
            return inner(*refs[:place], *refs[place + len(after) :])

    return pl.pallas_call(
        kernel,
        out_shape=outs,
        in_specs=specs,
        out_specs=jax.tree.map(lambda _: VMEM, outs) if out_specs is None else out_specs,
        scratch_shapes=scratch,
        compiler_params=pltpu.CompilerParams(vmem_limit_bytes=limit),
        cost_estimate=pl.CostEstimate(flops=int(micros * 1e9), bytes_accessed=0, transcendentals=0),
    )(*operands)


def like(rows, width, dtype):
    return jax.ShapeDtypeStruct((rows, width), dtype)


def up16(count):
    return -(-count // 16) * 16


def local(
    act_in, grad_in, saved_inputs, kernels, norm_gains,
    forward_lengths, backward_lengths, forward_slots, backward_slots,
):
    sections = lax.axis_size("section")
    shards = lax.axis_size("tm")
    act, grad, saved = act_in[0], grad_in[0], saved_inputs[0]
    own, width = act.shape
    tap_count = kernels.shape[2]
    half = (tap_count - 1) // 2
    one, two = up16(half), up16(2 * half)
    size, small = own + 2 * two, own + 2 * one

    def shifted(x, by):
        return lax.ppermute(x, "section", [(i, (i + by) % sections) for i in range(sections)])

    def swapped(near, far, by=0):
        results = []
        for x, begin in ((far, 1), (near, 0)):
            pairs = [(i, i + 1) for i in range(begin, shards - 1, 2)]
            pairs = [
                (s * shards + i, (s + by) % sections * shards + j)
                for s in range(sections)
                for a, b in pairs
                for i, j in ((a, b), (b, a))
            ]
            results.append(lax.ppermute(x, ("section", "tm"), pairs))
        return results[::-1]

    act_ahead = shifted(act, 2)
    lengths = pltpu.SMEM(backward_lengths.shape, jnp.int32)
    forward_slots, backward_slots = forward_slots.T, backward_slots.T
    slots = pltpu.SMEM(backward_slots.shape, jnp.int32)
    near0, far0, notes = call(
        functools.partial(pack_kernel, (two, one)),
        (like(two + one, width, BF16), like(two + one, width, BF16), jax.ShapeDtypeStruct((8,), jnp.int32)),
        [lengths, lengths, slots, slots, pltpu.SemaphoreType.DMA((8,))],
        (saved, grad_in, backward_lengths, forward_lengths, backward_slots, forward_slots),
        0, [HBM] * 6, (VMEM, VMEM, SMEM), FULL,
    )
    near0, far0 = swapped(near0, far0)
    tap_back = np.concatenate([from_freq(size, np.arange(tap_count) - half), np.zeros((1, size))], axis=0)
    m_table = stacked(to_freq(size, span(two, own)))
    q_table = tap_freq(size, tap_count)
    c_table = stacked(from_freq(size, span(one, own)))
    go_table = beside(to_freq(size, np.arange(own)))
    t_table = stacked(tap_back)

    def run(kernel, outs, scratch, operands, micros=0, *after):
        return call(kernel, outs, scratch, [jnp.asarray(x) for x in operands], micros, after=after)

    rows = [pltpu.VMEM((own, width), F32)] + [pltpu.VMEM((own, LANES), F32)] * 2
    layer = like(own, width, BF16), like(own, LANES, F32), like(own, LANES, F32)
    weights, ahead0, ahead1, near1, far1, *layer0 = run(
        functools.partial(prepare_kernel, two),
        (
            jax.ShapeDtypeStruct((kernels.shape[1], tap_count + 1, width), BF16), like(tap_count + 1, width, BF16),
            like(tap_count + 1, width, BF16), like(2 * two, width, BF16), like(2 * two, width, BF16), *layer,
        ),
        [],
        [notes, kernels[0].transpose(1, 0, 2), norm_gains[0], saved, act],
        0,
    )
    near1, far1 = swapped(near1, far1)
    ahead0, ahead1 = shifted(ahead0, 2), shifted(ahead1, 1)
    g_table, x_table = stacked(to_freq(size, span(one, own))), stacked(from_freq(size, span(0, own)))
    grad_mid, near2, far2, halo0, inner0, gain0 = run(
        functools.partial(first_backward_kernel, two),
        (
            like(own, width, BF16), like(one, width, BF16), like(one, width, BF16),
            like(2 * two, width, BF16), like(own, width, BF16), like(1, width, F32),
        ),
        [pltpu.VMEM((2, two, width), BF16), pltpu.VMEM((2, one, width), BF16), *rows],
        [
            notes, saved, far0, near0, grad, weights, *layer0,
            m_table, q_table, c_table, g_table, x_table,
        ],
        4,
        act_ahead,
    )
    grad_mid = shifted(grad_mid, -1)
    near2, far2 = swapped(near2, far2, -1)
    taps0 = run(
        first_taps_kernel, like(tap_count + 1, width, BF16), [],
        [halo0, layer0[0], inner0, gain0, m_table, go_table, t_table],
        0,
        near2, far2,
    )
    halo_scratch = [
        pltpu.VMEM((2 * two, width), BF16), pltpu.VMEM((2, two, width), BF16), pltpu.VMEM((own, width), BF16)
    ]
    m1, q1, factor1, conv1, mean1, inverse1, ahead = run(
        functools.partial(second_ready_kernel, two),
        (
            like(size, width, F32), like(size, width, F32), like(small, width, F32), like(own, width, F32),
            like(own, LANES, F32), like(own, LANES, F32), like(2 * two, width, BF16),
        ),
        halo_scratch,
        [notes, saved, far1, near1, weights, m_table, q_table, c_table],
        5,
        taps0,
    )
    ahead = shifted(ahead, 2)
    def partner(x, step):
        return lax.ppermute(x, "tm", [(i, i ^ step) for i in range(shards)])

    mixed1, sums = run(
        second_taps_kernel,
        (like(small, width, BF16), like(2 * (tap_count + 1), width, BF16)),
        [pltpu.VMEM((2, one, width), BF16)],
        [notes, grad_mid, far2, near2, weights, m1, factor1, conv1, taps0, go_table, t_table],
        2,
        ahead0, ahead1,
    )
    grad_out = run(
        second_backward_kernel,
        like(own, width, BF16),
        rows,
        [
            notes, saved, grad_mid, weights, mixed1, q1, mean1, inverse1,
            g_table, x_table,
        ],
        6,
    )
    grad_out = shifted(grad_out, -1)
    mine = call(add_kernel, like(*sums.shape, BF16), [], (sums, partner(sums, 1)), 6)
    between = run(
        functools.partial(first_forward_kernel, two),
        like(small, width, BF16),
        [pltpu.VMEM((2 * two, width), BF16), pltpu.VMEM((own, width), BF16)],
        [notes, act_ahead, ahead, ahead0, m_table, q_table, c_table],
        10,
        mine,
    )
    act_out = run(
        second_forward_kernel,
        like(own, width, BF16),
        [pltpu.VMEM((small, width), BF16)],
        [
            notes, between, ahead1,
            stacked(to_freq(small, span(one, own))), tap_freq(small, tap_count), stacked(from_freq(small, span(0, own))),
        ],
        10,
    )
    step = 2
    while True:
        other = partner(mine, step)
        step *= 2
        if step >= shards:
            break
        mine = call(add_kernel, like(*mine.shape, BF16), [], (mine, other), 0)
    slots = kernels.shape[1]
    act_out, grad_out, taps, gains = call(
        final_kernel,
        (
            like(own, width, BF16), like(own, width, BF16),
            jax.ShapeDtypeStruct((tap_count, slots, width), F32), like(slots, width, F32),
        ),
        [
            pltpu.VMEM((tap_count, slots, width), F32), pltpu.VMEM((slots, width), F32),
            pltpu.SemaphoreType.DMA((7,)),
        ],
        (notes, mine, other, act_out, grad_out),
        0, [SMEM] + [VMEM] * 2 + [ANY] * 2, (ANY,) * 4,
    )
    return act_out[None], grad_out[None], taps.transpose(1, 0, 2)[None], gains[None]


def solution(mesh):
    in_specs = (
        P("section", "tm", None),
        P("section", "tm", None),
        P("section", None, "tm", None),
        P("section", None, None, None),
        P("section", None, None),
        P(),
        P(),
        P(),
        P(),
    )
    out_specs = (
        P("section", "tm", None),
        P("section", "tm", None),
        P("section", None, None, None),
        P("section", None, None),
    )
    return jax.shard_map(local, mesh=mesh, in_specs=in_specs, out_specs=out_specs, check_vma=False)
```

```python
import functools

import jax
import jax.numpy as jnp
import ml_dtypes
import numpy as np
from jax import lax
from jax.experimental import pallas as pl
from jax.experimental.pallas import tpu as pltpu
from jax.sharding import PartitionSpec as P

epsilon = 1e-05
BLOCK = 2048
LANES = 128
F32 = jnp.float32
BF16 = jnp.bfloat16


def split(matrix):
    high = matrix.astype(ml_dtypes.bfloat16)
    low = (matrix - high.astype(np.float64)).astype(ml_dtypes.bfloat16)
    return high, low


def angles(size, times):
    return 2.0 * np.pi / size * np.outer(np.arange(size // 2) + 0.5, np.asarray(times, np.float64))


def to_freq(size, times):
    phase = angles(size, times)
    return np.concatenate([np.cos(phase), -np.sin(phase)], axis=0)


def from_freq(size, times):
    phase = angles(size, times).T
    return 2.0 / size * np.concatenate([np.cos(phase), -np.sin(phase)], axis=1)


def stacked(matrix):
    return np.concatenate(split(matrix), axis=0)


def beside(matrix):
    return np.concatenate(split(matrix), axis=1)


def tap_freq(size, taps):
    phase = angles(size, np.arange(taps) - (taps - 1) // 2)
    table = np.concatenate([np.cos(phase), np.sin(phase)], axis=0)
    return beside(np.concatenate([table, np.zeros((size, 1))], axis=1))


def dot(a, b):
    return jnp.dot(a, b, preferred_element_type=F32)


def transform(table, values):
    return sum(halves(dot(table[...], values.astype(BF16))))


def halves(values):
    half = values.shape[0] // 2
    return values[:half], values[half:]


def product(a, b):
    ar, ai = halves(a)
    br, bi = halves(b)
    return jnp.concatenate([ar * br - ai * bi, ar * bi + ai * br], axis=0)


def product_conj(a, b):
    ar, ai = halves(a)
    br, bi = halves(b)
    return jnp.concatenate([ar * br + ai * bi, ai * br - ar * bi], axis=0)


def sigmoid(values):
    return 0.5 * jnp.tanh(0.5 * values) + 0.5


def wide(stat, count):
    return jnp.concatenate([stat] * (count // LANES), axis=1)


def norm_rows(ref, start, count, at, gain, first, length, masked_ref, mean_ref, inverse_ref):
    width = masked_ref.shape[1]
    rows = pl.ds(start, count)
    tiles = [pl.ds(i * LANES, LANES) for i in range(width // LANES)]

    def values(tile):
        return ref[rows, tile].astype(F32)

    total = values(tiles[0])
    for tile in tiles[1:]:
        total = total + values(tile)
    mean = jnp.sum(total, axis=1, keepdims=True) * (1.0 / width)
    mean = jnp.broadcast_to(mean, (count, LANES))
    square = jnp.zeros((count, LANES), F32)
    for tile in tiles:
        center = values(tile) - mean
        square = square + center * center
    var = jnp.sum(square, axis=1, keepdims=True) * (1.0 / width)
    inverse = jnp.broadcast_to(lax.rsqrt(var + epsilon), (count, LANES))
    frame = first + at + lax.broadcasted_iota(jnp.int32, (count, LANES), 0)
    mask = ((frame >= 0) & (frame < length)).astype(F32)
    scale = mask * inverse
    out = pl.ds(at, count)
    for tile in tiles:
        masked_ref[out, tile] = ((values(tile) - mean) * scale * gain(tile)).astype(BF16)
    if mean_ref is not None:
        mean_ref[out, :] = mean
        inverse_ref[out, :] = inverse


def norm_pieces(pieces, gain, first, length, masked_ref, mean_ref=None, inverse_ref=None, chunk=128):
    at = 0
    for ref, start, count in pieces:
        for begin in range(0, count, chunk):
            norm_rows(
                ref, start + begin, min(chunk, count - begin), at + begin,
                gain, first, length, masked_ref, mean_ref, inverse_ref,
            )
        at += count


def window(pieces, columns):
    parts = [ref[pl.ds(start, count), columns] for ref, start, count in pieces]
    return parts[0] if len(parts) == 1 else jnp.concatenate(parts, axis=0)


def each_block(width, body):
    for begin in range(0, width, BLOCK):
        body(pl.ds(begin, BLOCK))


def tap_spectrum(table, weights):
    return dot(table, jnp.concatenate([weights, weights], axis=0))


def gate_factor(conv):
    gate = sigmoid(conv)
    return gate * (1.0 + conv * (1.0 - gate))


FIRST, BACK0, BACK1, AHEAD0 = range(0, 8, 2)


def looked_up(notes, layer):
    return notes[layer], notes[layer + 1], notes[FIRST]


def sorted_halos(near, far, at, halos):
    even = lax.rem(lax.axis_index("tm") + 1, 2)
    rows = pl.ds(at, halos.shape[1])
    halos[even] = near[rows, :]
    halos[1 - even] = far[rows, :]
    return halos.at[0], halos.at[1]


def lane_sum(values):
    total = values[:, :LANES]
    for lane in range(LANES, values.shape[1], LANES):
        total = total + values[:, lane : lane + LANES]
    return total


def first_pass(pieces, mean, inverse, gain, mask, tables, mixed, q, columns, scaled, sum_a, sum_b):
    g_table, x_table = tables
    grad_masked = wide(mask, BLOCK) * transform(x_table, product_conj(transform(g_table, mixed), q))
    centered = window(pieces, columns).astype(F32) - wide(mean[...], BLOCK)
    weighted = grad_masked * (centered * wide(inverse[...], BLOCK))
    gain = gain(columns)
    by_gain = grad_masked * gain
    scaled[:, columns] = by_gain
    sum_a[...] += lane_sum(by_gain)
    sum_b[...] += lane_sum(weighted * gain)
    return weighted


def last_pass(grad_pieces, pieces, mean, inverse, scaled, sum_a, sum_b, grad_x, chunk=128):
    width = scaled.shape[1]
    at = 0
    for (ref, start, count), (saved, base, _) in zip(grad_pieces, pieces):
        for begin in range(0, count, chunk):
            here = min(chunk, count - begin)
            rows = pl.ds(at + begin, here)
            inv = inverse[rows, :]
            mean_a = jnp.sum(sum_a[rows, :], axis=1, keepdims=True) * (1.0 / width)
            mean_b = jnp.sum(sum_b[rows, :], axis=1, keepdims=True) * (1.0 / width)
            slope = inv * jnp.broadcast_to(mean_b, (here, LANES)) * inv
            fixed = inv * jnp.broadcast_to(mean_a, (here, LANES)) - slope * mean[rows, :]
            for lane in range(0, width, LANES):
                tile = pl.ds(lane, LANES)
                x = saved[pl.ds(base + begin, here), tile].astype(F32)
                change = inv * scaled[rows, tile] - fixed - slope * x
                grad_x[rows, tile] = (ref[pl.ds(start + begin, here), tile].astype(F32) + change).astype(BF16)
        at += count


def frame_mask(rows, first, length):
    frame = first + lax.broadcasted_iota(jnp.int32, (rows, LANES), 0)
    return ((frame >= 0) & (frame < length)).astype(F32)


def slot_row(weights, slot):
    last = weights.shape[1] - 1
    return lambda columns: weights[slot, last : last + 1, columns].astype(F32)


def prepare_kernel(
    reach, notes, kernels, gains, saved, act, weights, ahead0, ahead1, near, far, masked, mean, inverse
):
    own = act.shape[0]
    for even in range(2):

        @pl.when(lax.rem(lax.axis_index("tm") + 1, 2) == even)
        def _():
            for x, at in ((saved.at[1], 0), (act, reach)):
                tail, head = (near, far) if even else (far, near)
                tail[pl.ds(at, reach), :] = x[pl.ds(own - reach, reach), :]
                head[pl.ds(at, reach), :] = x[pl.ds(0, reach), :]

    count = kernels.shape[0]
    for slot in range(kernels.shape[1]):
        weights[slot, :count, :] = kernels[:, slot, :]
        weights[slot, count:, :] = gains[slot : slot + 1, :]
    ahead0[...] = weights[notes[AHEAD0]]
    ahead1[...] = weights[notes[FIRST + 1]]
    slot, length, first = looked_up(notes, BACK0)
    norm_pieces([(saved.at[0], 0, own)], slot_row(weights, slot), first, length, masked, mean, inverse)


def norm_halo(left, right, own, gain, first, length, halo):
    reach = left.shape[0]
    norm_pieces([(left, 0, reach)], gain, first - reach, length, halo)
    norm_pieces([(right, 0, reach)], gain, first + own, length, halo.at[pl.ds(reach, reach)])


def joined(halo, own, columns):
    reach = halo.shape[0] // 2
    return jnp.concatenate([halo[:reach, columns], own[:, columns], halo[reach:, columns]], axis=0)


def first_backward_kernel(
    reach, notes, saved, far, near, grads, weights, masked, mean, inverse,
    m_table, q_table, c_table, g_table, x_table,
    grad_x, near_edge, far_edge, halo, inner, gain_sum, halos, grad_halos, scaled, sum_a, sum_b,
):
    own, width = grads.shape
    edge = near_edge.shape[0]
    slot, length, first = looked_up(notes, BACK0)
    gain = slot_row(weights, slot)
    left, right = sorted_halos(near, far, 0, halos)
    grad_left, grad_right = sorted_halos(near, far, reach, grad_halos)
    norm_halo(left, right, own, gain, first, length, halo)
    grad_pieces = [(grad_left, 0, edge), (grads, 0, own), (grad_right, 0, edge)]
    pieces = [(saved.at[0], 0, own)]
    mask = frame_mask(own, first, length)
    sum_a[...] = jnp.zeros_like(sum_a)
    sum_b[...] = jnp.zeros_like(sum_b)

    def block(columns):
        m = transform(m_table, joined(halo, masked, columns))
        q = tap_spectrum(q_table[...], weights[slot, :, columns])
        conv = transform(c_table, product(m, q))
        mixed = (window(grad_pieces, columns).astype(F32) * gate_factor(conv)).astype(BF16)
        inner[:, columns] = mixed[edge : edge + own]
        weighted = first_pass(
            pieces, mean, inverse, gain, mask, (g_table, x_table), mixed, q, columns, scaled, sum_a, sum_b
        )
        gain_sum[:, columns] = jnp.sum(weighted, axis=0, keepdims=True)

    each_block(width, block)
    last_pass([(grads, 0, own)], pieces, mean, inverse, scaled, sum_a, sum_b, grad_x)
    for even in range(2):

        @pl.when(lax.rem(lax.axis_index("tm") + 1, 2) == even)
        def _():
            top, bottom = (far_edge, near_edge) if even else (near_edge, far_edge)
            top[...] = grad_x[pl.ds(0, edge), :]
            bottom[...] = grad_x[pl.ds(own - edge, edge), :]


def tap_term(go_table, t_table, m, mixed):
    g_own = dot(go_table[...], jnp.concatenate([mixed, mixed], axis=0))
    return transform(t_table, product_conj(m, g_own))


def put_taps(taps, tap, gain_sum, columns):
    row = lax.broadcasted_iota(jnp.int32, tap.shape, 0)
    taps[:, columns] = jnp.where(row == tap.shape[0] - 1, gain_sum, tap).astype(taps.dtype)


def first_taps_kernel(halo, masked, inner, gain_sum, m_table, go_table, t_table, taps):
    def block(columns):
        m = transform(m_table, joined(halo, masked, columns))
        put_taps(taps, tap_term(go_table, t_table, m, inner[:, columns]), gain_sum[:, columns], columns)

    each_block(masked.shape[1], block)


def added(mine, other):
    return (mine[...].astype(F32) + other[...].astype(F32)).astype(BF16)


def add_kernel(mine, other, out):
    out[...] = added(mine, other)


def second_early_kernel(notes, saved, weights, q_table, masked, mean, inverse, q):
    own = masked.shape[0]
    slot, length, first = looked_up(notes, BACK1)
    norm_pieces([(saved.at[1], 0, own)], slot_row(weights, slot), first, length, masked, mean, inverse)

    def block(columns):
        q[:, columns] = tap_spectrum(q_table[...], weights[slot, :, columns])

    each_block(masked.shape[1], block)


def second_ready_kernel(
    reach, notes, far, near, weights, ahead0, masked, q, m_table, c_table, m_out, factor, conv_out, ahead, halo, halos
):
    left, right = sorted_halos(near, far, reach, halos)
    ahead[pl.ds(0, reach), :] = left[...]
    ahead[pl.ds(reach, reach), :] = right[...]
    ahead[pl.ds(2 * reach, ahead0.shape[0]), :] = ahead0[...]
    own, width = masked.shape
    slot, length, first = looked_up(notes, BACK1)
    left, right = sorted_halos(near, far, 0, halos)
    norm_halo(left, right, own, slot_row(weights, slot), first, length, halo)

    def block(columns):
        m = transform(m_table, joined(halo, masked, columns))
        conv = transform(c_table, product(m, q[:, columns]))
        m_out[:, columns] = m
        factor[:, columns] = gate_factor(conv)
        edge = (conv.shape[0] - own) // 2
        conv_out[:, columns] = conv[edge : edge + own]

    each_block(width, block)


def second_taps_kernel(
    notes, received, far, near, weights, m, factor, conv, taps0, go_table, t_table, mixed_out, taps, halos
):
    own, width = conv.shape
    rows = factor.shape[0]
    count = taps0.shape[0]
    taps[pl.ds(0, count), :] = taps0[...]
    taps1 = taps.at[pl.ds(count, count)]
    edge = (rows - own) // 2
    gain = slot_row(weights, notes[BACK1])
    left, right = sorted_halos(near, far, 0, halos)
    pieces = [(left, 0, edge), (received, 0, own), (right, 0, edge)]

    def block(columns):
        mixed = (window(pieces, columns).astype(F32) * factor[:, columns]).astype(BF16)
        mixed_out[:, columns] = mixed
        inner = mixed[edge : edge + own]
        gain_sum = jnp.sum(inner.astype(F32) * conv[:, columns], axis=0, keepdims=True) / gain(columns)
        put_taps(taps1, tap_term(go_table, t_table, m[:, columns], inner), gain_sum, columns)

    each_block(width, block)


def second_backward_kernel(
    notes, saved, received, weights, mixed, q, mean, inverse, g_table, x_table, grad_x, scaled, sum_a, sum_b
):
    own, width = grad_x.shape
    slot, length, first = looked_up(notes, BACK1)
    pieces = [(saved.at[1], 0, own)]
    mask = frame_mask(own, first, length)
    sum_a[...] = jnp.zeros_like(sum_a)
    sum_b[...] = jnp.zeros_like(sum_b)

    def block(columns):
        first_pass(
            pieces, mean, inverse, slot_row(weights, slot), mask, (g_table, x_table), mixed[:, columns], q[:, columns],
            columns, scaled, sum_a, sum_b,
        )

    each_block(width, block)
    last_pass([(received, 0, own)], pieces, mean, inverse, scaled, sum_a, sum_b, grad_x)


def row_gain(layer):
    last = layer.shape[0] - 1
    return lambda columns: layer[last : last + 1, columns].astype(F32)


def first_forward_kernel(reach, notes, act, ahead, m_table, q_table, c_table, out, halo, masked):
    own, width = act.shape
    middle = reach // 2
    _, length, first = looked_up(notes, AHEAD0)
    left, right = ahead.at[pl.ds(0, reach)], ahead.at[pl.ds(reach, reach)]
    layer = ahead.at[pl.ds(2 * reach, ahead.shape[0] - 2 * reach)]
    inner = [(left, middle, middle), (act, 0, own), (right, 0, middle)]
    norm_pieces([(act, 0, own)], row_gain(layer), first, length, masked)
    norm_halo(left, right, own, row_gain(layer), first, length, halo)

    def block(columns):
        q = tap_spectrum(q_table[...], layer[:, columns])
        conv = transform(c_table, product(transform(m_table, joined(halo, masked, columns)), q))
        out[:, columns] = (window(inner, columns).astype(F32) + conv * sigmoid(conv)).astype(BF16)

    each_block(width, block)


def second_forward_kernel(notes, between, layer, m_table, q_table, c_table, out, masked):
    own, width = out.shape
    rows = between.shape[0]
    edge = (rows - own) // 2
    _, length, first = looked_up(notes, AHEAD0)
    norm_pieces([(between, 0, rows)], row_gain(layer), first - edge, length, masked, chunk=rows // 2)

    def block(columns):
        q = tap_spectrum(q_table[...], layer[:, columns])
        conv = transform(c_table, product(transform(m_table, masked[:, columns]), q))
        out[:, columns] = (between[edge : edge + own, columns].astype(F32) + conv * sigmoid(conv)).astype(BF16)

    each_block(width, block)


def pack_kernel(
    reaches, saved, grad, back_lengths, ahead_lengths, back_slots, ahead_slots,
    near, far, notes, back_len, ahead_len, back_slot, ahead_slot, sems,
):
    own = grad.shape[1]
    even = lax.rem(lax.axis_index("tm") + 1, 2)
    copies = []
    at = 0
    for x, reach in zip((saved, grad), reaches):
        for out, tail in ((near, even), (far, 1 - even)):
            start = pl.multiple_of(tail * (own - reach), 16)
            copies.append((x.at[0, pl.ds(start, reach)], out.at[pl.ds(at, reach)]))
        at += reach
    small = [(back_lengths, back_len), (ahead_lengths, ahead_len), (back_slots, back_slot), (ahead_slots, ahead_slot)]
    copies = [pltpu.make_async_copy(a, b, sems.at[k]) for k, (a, b) in enumerate(small + copies)]
    for copy in copies:
        copy.start()
    for copy in copies:
        copy.wait()
    section, sections = lax.axis_index("section"), lax.axis_size("section")
    notes[FIRST] = lax.axis_index("tm") * own
    notes[FIRST + 1] = ahead_slot[1, section]
    notes[BACK0] = back_slot[0, section]
    notes[BACK0 + 1] = back_len[section]
    notes[BACK1] = back_slot[1, section]
    notes[BACK1 + 1] = back_len[lax.rem(section + 1, sections)]
    notes[AHEAD0] = ahead_slot[0, section]
    notes[AHEAD0 + 1] = ahead_len[lax.rem(section + sections - 2, sections)]


def final_kernel(notes, mine, other, act, grad, act_out, grad_out, taps_out, gains_out, taps, gains, sems):
    copies = [
        pltpu.make_async_copy(act, act_out, sems.at[0]),
        pltpu.make_async_copy(grad, grad_out, sems.at[1]),
    ]
    for copy in copies:
        copy.start()
    count, slots, width = taps.shape
    step = width // 4
    for begin in range(0, width, step):
        columns = pl.ds(begin, step)
        total = mine[:, columns].astype(F32) + other[:, columns].astype(F32)
        ticks = total[: count + 1], total[count + 1 :]
        for slot in range(slots):
            use = [(notes[layer] == slot).astype(F32) for layer in (BACK0, BACK1)]
            both = use[0] * ticks[0] + use[1] * ticks[1]
            taps[:, slot, columns] = both[:count]
            gains[slot : slot + 1, columns] = both[count:]
        for source, target in ((taps.at[:, :, columns], taps_out.at[:, :, columns]),):
            copies.append(pltpu.make_async_copy(source, target, sems.at[len(copies)]))
            copies[-1].start()
    copies.append(pltpu.make_async_copy(gains, gains_out, sems.at[len(copies)]))
    copies[-1].start()
    for copy in copies:
        copy.wait()


def span(reach, own):
    return np.arange(-reach, own + reach)


VMEM = pl.BlockSpec(memory_space=pltpu.VMEM)
SMEM = pl.BlockSpec(memory_space=pltpu.SMEM)
ANY = pl.BlockSpec(memory_space=pl.ANY)
HBM = pl.BlockSpec(memory_space=pltpu.HBM)
LIMIT = 24 * 1024 * 1024
FULL = 127 * 512 * 1024


def call(kernel, outs, scratch, operands, micros, specs=None, out_specs=None, limit=LIMIT, after=()):
    if specs is None:
        specs = [SMEM if x.dtype == jnp.int32 else VMEM for x in operands]
    if after:
        inner, place = kernel, len(operands)
        operands, specs = [*operands, *after], [*specs, *[ANY] * len(after)]

        def kernel(*refs):
            return inner(*refs[:place], *refs[place + len(after) :])

    return pl.pallas_call(
        kernel,
        out_shape=outs,
        in_specs=specs,
        out_specs=jax.tree.map(lambda _: VMEM, outs) if out_specs is None else out_specs,
        scratch_shapes=scratch,
        compiler_params=pltpu.CompilerParams(vmem_limit_bytes=limit),
        cost_estimate=pl.CostEstimate(flops=int(micros * 1e9), bytes_accessed=0, transcendentals=0),
    )(*operands)


def like(rows, width, dtype):
    return jax.ShapeDtypeStruct((rows, width), dtype)


def up16(count):
    return -(-count // 16) * 16


def local(
    act_in, grad_in, saved_inputs, kernels, norm_gains,
    forward_lengths, backward_lengths, forward_slots, backward_slots,
):
    sections = lax.axis_size("section")
    shards = lax.axis_size("tm")
    act, grad, saved = act_in[0], grad_in[0], saved_inputs[0]
    own, width = act.shape
    tap_count = kernels.shape[2]
    half = (tap_count - 1) // 2
    one, two = up16(half), up16(2 * half)
    size, small = own + 2 * two, own + 2 * one

    def shifted(x, by):
        return lax.ppermute(x, "section", [(i, (i + by) % sections) for i in range(sections)])

    def swapped(near, far, by=0):
        results = []
        for x, begin in ((far, 1), (near, 0)):
            pairs = [(i, i + 1) for i in range(begin, shards - 1, 2)]
            pairs = [
                (s * shards + i, (s + by) % sections * shards + j)
                for s in range(sections)
                for a, b in pairs
                for i, j in ((a, b), (b, a))
            ]
            results.append(lax.ppermute(x, ("section", "tm"), pairs))
        return results[::-1]

    act_ahead = shifted(act, 2)
    lengths = pltpu.SMEM(backward_lengths.shape, jnp.int32)
    forward_slots, backward_slots = forward_slots.T, backward_slots.T
    slots = pltpu.SMEM(backward_slots.shape, jnp.int32)
    near0, far0, notes = call(
        functools.partial(pack_kernel, (two, one)),
        (like(two + one, width, BF16), like(two + one, width, BF16), jax.ShapeDtypeStruct((8,), jnp.int32)),
        [lengths, lengths, slots, slots, pltpu.SemaphoreType.DMA((8,))],
        (saved, grad_in, backward_lengths, forward_lengths, backward_slots, forward_slots),
        0, [HBM] * 6, (VMEM, VMEM, SMEM), FULL,
    )
    near0, far0 = swapped(near0, far0)
    tap_back = np.concatenate([from_freq(size, np.arange(tap_count) - half), np.zeros((1, size))], axis=0)
    m_table = stacked(to_freq(size, span(two, own)))
    q_table = tap_freq(size, tap_count)
    c_table = stacked(from_freq(size, span(one, own)))
    go_table = beside(to_freq(size, np.arange(own)))
    t_table = stacked(tap_back)

    def run(kernel, outs, scratch, operands, micros=0, *after):
        return call(kernel, outs, scratch, [jnp.asarray(x) for x in operands], micros, after=after)

    rows = [pltpu.VMEM((own, width), F32)] + [pltpu.VMEM((own, LANES), F32)] * 2
    layer = like(own, width, BF16), like(own, LANES, F32), like(own, LANES, F32)
    weights, ahead0, ahead1, near1, far1, *layer0 = run(
        functools.partial(prepare_kernel, two),
        (
            jax.ShapeDtypeStruct((kernels.shape[1], tap_count + 1, width), BF16), like(tap_count + 1, width, BF16),
            like(tap_count + 1, width, BF16), like(2 * two, width, BF16), like(2 * two, width, BF16), *layer,
        ),
        [],
        [notes, kernels[0].transpose(1, 0, 2), norm_gains[0], saved, act],
        0,
    )
    near1, far1 = swapped(near1, far1)
    ahead1 = shifted(ahead1, 1)
    g_table, x_table = stacked(to_freq(size, span(one, own))), stacked(from_freq(size, span(0, own)))
    grad_mid, near2, far2, halo0, inner0, gain0 = run(
        functools.partial(first_backward_kernel, two),
        (
            like(own, width, BF16), like(one, width, BF16), like(one, width, BF16),
            like(2 * two, width, BF16), like(own, width, BF16), like(1, width, F32),
        ),
        [pltpu.VMEM((2, two, width), BF16), pltpu.VMEM((2, one, width), BF16), *rows],
        [
            notes, saved, far0, near0, grad, weights, *layer0,
            m_table, q_table, c_table, g_table, x_table,
        ],
        4,
        act_ahead,
    )
    grad_mid = shifted(grad_mid, -1)
    near2, far2 = swapped(near2, far2, -1)
    taps0 = run(
        first_taps_kernel, like(tap_count + 1, width, BF16), [],
        [halo0, layer0[0], inner0, gain0, m_table, go_table, t_table],
        0,
    )
    masked1, mean1, inverse1, q1 = run(
        second_early_kernel, (*layer, like(size, width, F32)), [], [notes, saved, weights, q_table], 1, taps0
    )
    m1, factor1, conv1, ahead0 = run(
        functools.partial(second_ready_kernel, two),
        (
            like(size, width, F32), like(small, width, F32), like(own, width, F32),
            like(2 * two + tap_count + 1, width, BF16),
        ),
        [pltpu.VMEM((2 * two, width), BF16), pltpu.VMEM((2, two, width), BF16)],
        [notes, far1, near1, weights, ahead0, masked1, q1, m_table, c_table],
        5,
        near2, far2,
    )
    ahead0 = shifted(ahead0, 2)
    def partner(x, step):
        return lax.ppermute(x, "tm", [(i, i ^ step) for i in range(shards)])

    mixed1, sums = run(
        second_taps_kernel,
        (like(small, width, BF16), like(2 * (tap_count + 1), width, BF16)),
        [pltpu.VMEM((2, one, width), BF16)],
        [notes, grad_mid, far2, near2, weights, m1, factor1, conv1, taps0, go_table, t_table],
        2,
    )
    grad_out = run(
        second_backward_kernel,
        like(own, width, BF16),
        rows,
        [
            notes, saved, grad_mid, weights, mixed1, q1, mean1, inverse1,
            g_table, x_table,
        ],
        6,
    )
    grad_out = shifted(grad_out, -1)
    mine = call(add_kernel, like(*sums.shape, BF16), [], (sums, partner(sums, 1)), 6)
    between = run(
        functools.partial(first_forward_kernel, two),
        like(small, width, BF16),
        [pltpu.VMEM((2 * two, width), BF16), pltpu.VMEM((own, width), BF16)],
        [notes, act_ahead, ahead0, m_table, q_table, c_table],
        10,
        mine,
    )
    act_out = run(
        second_forward_kernel,
        like(own, width, BF16),
        [pltpu.VMEM((small, width), BF16)],
        [
            notes, between, ahead1,
            stacked(to_freq(small, span(one, own))), tap_freq(small, tap_count), stacked(from_freq(small, span(0, own))),
        ],
        10,
    )
    step = 2
    while True:
        other = partner(mine, step)
        step *= 2
        if step >= shards:
            break
        mine = call(add_kernel, like(*mine.shape, BF16), [], (mine, other), 0)
    slots = kernels.shape[1]
    act_out, grad_out, taps, gains = call(
        final_kernel,
        (
            like(own, width, BF16), like(own, width, BF16),
            jax.ShapeDtypeStruct((tap_count, slots, width), F32), like(slots, width, F32),
        ),
        [
            pltpu.VMEM((tap_count, slots, width), F32), pltpu.VMEM((slots, width), F32),
            pltpu.SemaphoreType.DMA((7,)),
        ],
        (notes, mine, other, act_out, grad_out),
        0, [SMEM] + [VMEM] * 2 + [ANY] * 2, (ANY,) * 4,
    )
    return act_out[None], grad_out[None], taps.transpose(1, 0, 2)[None], gains[None]


def solution(mesh):
    in_specs = (
        P("section", "tm", None),
        P("section", "tm", None),
        P("section", None, "tm", None),
        P("section", None, None, None),
        P("section", None, None),
        P(),
        P(),
        P(),
        P(),
    )
    out_specs = (
        P("section", "tm", None),
        P("section", "tm", None),
        P("section", None, None, None),
        P("section", None, None),
    )
    return jax.shard_map(local, mesh=mesh, in_specs=in_specs, out_specs=out_specs, check_vma=False)
```

```python
import functools

import jax
import jax.numpy as jnp
import ml_dtypes
import numpy as np
from jax import lax
from jax.experimental import pallas as pl
from jax.experimental.pallas import tpu as pltpu
from jax.sharding import PartitionSpec as P

epsilon = 1e-05
BLOCK = 2048
LANES = 128
F32 = jnp.float32
BF16 = jnp.bfloat16


def split(matrix):
    high = matrix.astype(ml_dtypes.bfloat16)
    low = (matrix - high.astype(np.float64)).astype(ml_dtypes.bfloat16)
    return high, low


def angles(size, times):
    return 2.0 * np.pi / size * np.outer(np.arange(size // 2) + 0.5, np.asarray(times, np.float64))


def to_freq(size, times):
    phase = angles(size, times)
    return np.concatenate([np.cos(phase), -np.sin(phase)], axis=0)


def from_freq(size, times):
    phase = angles(size, times).T
    return 2.0 / size * np.concatenate([np.cos(phase), -np.sin(phase)], axis=1)


def stacked(matrix):
    return np.concatenate(split(matrix), axis=0)


def beside(matrix):
    return np.concatenate(split(matrix), axis=1)


def tap_freq(size, taps):
    phase = angles(size, np.arange(taps) - (taps - 1) // 2)
    table = np.concatenate([np.cos(phase), np.sin(phase)], axis=0)
    return beside(np.concatenate([table, np.zeros((size, 1))], axis=1))


def dot(a, b):
    return jnp.dot(a, b, preferred_element_type=F32)


def transform(table, values):
    return sum(halves(dot(table[...], values.astype(BF16))))


def halves(values):
    half = values.shape[0] // 2
    return values[:half], values[half:]


def product(a, b):
    ar, ai = halves(a)
    br, bi = halves(b)
    return jnp.concatenate([ar * br - ai * bi, ar * bi + ai * br], axis=0)


def product_conj(a, b):
    ar, ai = halves(a)
    br, bi = halves(b)
    return jnp.concatenate([ar * br + ai * bi, ai * br - ar * bi], axis=0)


def sigmoid(values):
    return 0.5 * jnp.tanh(0.5 * values) + 0.5


def wide(stat, count):
    return jnp.concatenate([stat] * (count // LANES), axis=1)


def norm_rows(ref, start, count, at, gain, first, length, masked_ref, mean_ref, inverse_ref):
    width = masked_ref.shape[1]
    rows = pl.ds(start, count)
    tiles = [pl.ds(i * LANES, LANES) for i in range(width // LANES)]

    def values(tile):
        return ref[rows, tile].astype(F32)

    total = values(tiles[0])
    for tile in tiles[1:]:
        total = total + values(tile)
    mean = jnp.sum(total, axis=1, keepdims=True) * (1.0 / width)
    mean = jnp.broadcast_to(mean, (count, LANES))
    square = jnp.zeros((count, LANES), F32)
    for tile in tiles:
        center = values(tile) - mean
        square = square + center * center
    var = jnp.sum(square, axis=1, keepdims=True) * (1.0 / width)
    inverse = jnp.broadcast_to(lax.rsqrt(var + epsilon), (count, LANES))
    frame = first + at + lax.broadcasted_iota(jnp.int32, (count, LANES), 0)
    mask = ((frame >= 0) & (frame < length)).astype(F32)
    scale = mask * inverse
    out = pl.ds(at, count)
    for tile in tiles:
        masked_ref[out, tile] = ((values(tile) - mean) * scale * gain(tile)).astype(BF16)
    if mean_ref is not None:
        mean_ref[out, :] = mean
        inverse_ref[out, :] = inverse


def norm_pieces(pieces, gain, first, length, masked_ref, mean_ref=None, inverse_ref=None, chunk=128):
    at = 0
    for ref, start, count in pieces:
        for begin in range(0, count, chunk):
            norm_rows(
                ref, start + begin, min(chunk, count - begin), at + begin,
                gain, first, length, masked_ref, mean_ref, inverse_ref,
            )
        at += count


def window(pieces, columns):
    parts = [ref[pl.ds(start, count), columns] for ref, start, count in pieces]
    return parts[0] if len(parts) == 1 else jnp.concatenate(parts, axis=0)


def each_block(width, body):
    for begin in range(0, width, BLOCK):
        body(pl.ds(begin, BLOCK))


def tap_spectrum(table, weights):
    return dot(table, jnp.concatenate([weights, weights], axis=0))


def gate_factor(conv):
    gate = sigmoid(conv)
    return gate * (1.0 + conv * (1.0 - gate))


FIRST, BACK0, BACK1, AHEAD0 = range(0, 8, 2)


def looked_up(notes, layer):
    return notes[layer], notes[layer + 1], notes[FIRST]


def sorted_halos(near, far, at, halos):
    even = lax.rem(lax.axis_index("tm") + 1, 2)
    rows = pl.ds(at, halos.shape[1])
    halos[even] = near[rows, :]
    halos[1 - even] = far[rows, :]
    return halos.at[0], halos.at[1]


def lane_sum(values):
    total = values[:, :LANES]
    for lane in range(LANES, values.shape[1], LANES):
        total = total + values[:, lane : lane + LANES]
    return total


def first_pass(pieces, mean, inverse, gain, mask, tables, mixed, q, columns, scaled, sum_a, sum_b):
    g_table, x_table = tables
    grad_masked = wide(mask, BLOCK) * transform(x_table, product_conj(transform(g_table, mixed), q))
    centered = window(pieces, columns).astype(F32) - wide(mean[...], BLOCK)
    weighted = grad_masked * (centered * wide(inverse[...], BLOCK))
    gain = gain(columns)
    by_gain = grad_masked * gain
    scaled[:, columns] = by_gain
    sum_a[...] += lane_sum(by_gain)
    sum_b[...] += lane_sum(weighted * gain)
    return weighted


def last_pass(grad_pieces, pieces, mean, inverse, scaled, sum_a, sum_b, grad_x, chunk=128):
    width = scaled.shape[1]
    at = 0
    for (ref, start, count), (saved, base, _) in zip(grad_pieces, pieces):
        for begin in range(0, count, chunk):
            here = min(chunk, count - begin)
            rows = pl.ds(at + begin, here)
            inv = inverse[rows, :]
            mean_a = jnp.sum(sum_a[rows, :], axis=1, keepdims=True) * (1.0 / width)
            mean_b = jnp.sum(sum_b[rows, :], axis=1, keepdims=True) * (1.0 / width)
            slope = inv * jnp.broadcast_to(mean_b, (here, LANES)) * inv
            fixed = inv * jnp.broadcast_to(mean_a, (here, LANES)) - slope * mean[rows, :]
            for lane in range(0, width, LANES):
                tile = pl.ds(lane, LANES)
                x = saved[pl.ds(base + begin, here), tile].astype(F32)
                change = inv * scaled[rows, tile] - fixed - slope * x
                grad_x[rows, tile] = (ref[pl.ds(start + begin, here), tile].astype(F32) + change).astype(BF16)
        at += count


def frame_mask(rows, first, length):
    frame = first + lax.broadcasted_iota(jnp.int32, (rows, LANES), 0)
    return ((frame >= 0) & (frame < length)).astype(F32)


def slot_row(weights, slot):
    last = weights.shape[1] - 1
    return lambda columns: weights[slot, last : last + 1, columns].astype(F32)


def prepare_kernel(
    reach, notes, kernels, gains, saved, act, weights, ahead0, ahead1, near, far, masked, mean, inverse
):
    own = act.shape[0]
    for even in range(2):

        @pl.when(lax.rem(lax.axis_index("tm") + 1, 2) == even)
        def _():
            for x, at in ((saved.at[1], 0), (act, reach)):
                tail, head = (near, far) if even else (far, near)
                tail[pl.ds(at, reach), :] = x[pl.ds(own - reach, reach), :]
                head[pl.ds(at, reach), :] = x[pl.ds(0, reach), :]

    count = kernels.shape[0]
    for slot in range(kernels.shape[1]):
        weights[slot, :count, :] = kernels[:, slot, :]
        weights[slot, count:, :] = gains[slot : slot + 1, :]
    ahead0[...] = weights[notes[AHEAD0]]
    ahead1[...] = weights[notes[FIRST + 1]]
    slot, length, first = looked_up(notes, BACK0)
    norm_pieces([(saved.at[0], 0, own)], slot_row(weights, slot), first, length, masked, mean, inverse)


def norm_halo(left, right, own, gain, first, length, halo):
    reach = left.shape[0]
    norm_pieces([(left, 0, reach)], gain, first - reach, length, halo)
    norm_pieces([(right, 0, reach)], gain, first + own, length, halo.at[pl.ds(reach, reach)])


def joined(halo, own, columns):
    reach = halo.shape[0] // 2
    return jnp.concatenate([halo[:reach, columns], own[:, columns], halo[reach:, columns]], axis=0)


def first_backward_kernel(
    reach, notes, saved, far, near, grads, weights, masked, mean, inverse,
    m_table, q_table, c_table, g_table, x_table,
    grad_x, near_edge, far_edge, halo, inner, gain_sum, halos, grad_halos, scaled, sum_a, sum_b,
):
    own, width = grads.shape
    edge = near_edge.shape[0]
    slot, length, first = looked_up(notes, BACK0)
    gain = slot_row(weights, slot)
    left, right = sorted_halos(near, far, 0, halos)
    grad_left, grad_right = sorted_halos(near, far, reach, grad_halos)
    norm_halo(left, right, own, gain, first, length, halo)
    grad_pieces = [(grad_left, 0, edge), (grads, 0, own), (grad_right, 0, edge)]
    pieces = [(saved.at[0], 0, own)]
    mask = frame_mask(own, first, length)
    sum_a[...] = jnp.zeros_like(sum_a)
    sum_b[...] = jnp.zeros_like(sum_b)

    def block(columns):
        m = transform(m_table, joined(halo, masked, columns))
        q = tap_spectrum(q_table[...], weights[slot, :, columns])
        conv = transform(c_table, product(m, q))
        mixed = (window(grad_pieces, columns).astype(F32) * gate_factor(conv)).astype(BF16)
        inner[:, columns] = mixed[edge : edge + own]
        weighted = first_pass(
            pieces, mean, inverse, gain, mask, (g_table, x_table), mixed, q, columns, scaled, sum_a, sum_b
        )
        gain_sum[:, columns] = jnp.sum(weighted, axis=0, keepdims=True)

    each_block(width, block)
    last_pass([(grads, 0, own)], pieces, mean, inverse, scaled, sum_a, sum_b, grad_x)
    for even in range(2):

        @pl.when(lax.rem(lax.axis_index("tm") + 1, 2) == even)
        def _():
            top, bottom = (far_edge, near_edge) if even else (near_edge, far_edge)
            top[...] = grad_x[pl.ds(0, edge), :]
            bottom[...] = grad_x[pl.ds(own - edge, edge), :]


def tap_term(go_table, t_table, m, mixed):
    g_own = dot(go_table[...], jnp.concatenate([mixed, mixed], axis=0))
    return transform(t_table, product_conj(m, g_own))


def put_taps(taps, tap, gain_sum, columns):
    row = lax.broadcasted_iota(jnp.int32, tap.shape, 0)
    taps[:, columns] = jnp.where(row == tap.shape[0] - 1, gain_sum, tap).astype(taps.dtype)


def first_taps_kernel(halo, masked, inner, gain_sum, m_table, go_table, t_table, taps):
    def block(columns):
        m = transform(m_table, joined(halo, masked, columns))
        put_taps(taps, tap_term(go_table, t_table, m, inner[:, columns]), gain_sum[:, columns], columns)

    each_block(masked.shape[1], block)


def added(mine, other):
    return (mine[...].astype(F32) + other[...].astype(F32)).astype(BF16)


def add_kernel(mine, other, out):
    out[...] = added(mine, other)


def second_early_kernel(notes, saved, weights, q_table, masked, mean, inverse, q):
    own = masked.shape[0]
    slot, length, first = looked_up(notes, BACK1)
    norm_pieces([(saved.at[1], 0, own)], slot_row(weights, slot), first, length, masked, mean, inverse)

    def block(columns):
        q[:, columns] = tap_spectrum(q_table[...], weights[slot, :, columns])

    each_block(masked.shape[1], block)


def second_ready_kernel(
    reach, notes, far, near, weights, ahead0, masked, q, m_table, c_table, m_out, factor, conv_out, ahead, halo, halos
):
    left, right = sorted_halos(near, far, reach, halos)
    ahead[pl.ds(0, reach), :] = left[...]
    ahead[pl.ds(reach, reach), :] = right[...]
    ahead[pl.ds(2 * reach, ahead0.shape[0]), :] = ahead0[...]
    own, width = masked.shape
    slot, length, first = looked_up(notes, BACK1)
    left, right = sorted_halos(near, far, 0, halos)
    norm_halo(left, right, own, slot_row(weights, slot), first, length, halo)

    def block(columns):
        m = transform(m_table, joined(halo, masked, columns))
        conv = transform(c_table, product(m, q[:, columns]))
        m_out[:, columns] = m
        factor[:, columns] = gate_factor(conv)
        edge = (conv.shape[0] - own) // 2
        conv_out[:, columns] = conv[edge : edge + own]

    each_block(width, block)


def second_taps_kernel(
    notes, received, far, near, weights, m, factor, conv, taps0, go_table, t_table, mixed_out, taps, halos
):
    own, width = conv.shape
    rows = factor.shape[0]
    count = taps0.shape[0]
    taps[pl.ds(0, count), :] = taps0[...]
    taps1 = taps.at[pl.ds(count, count)]
    edge = (rows - own) // 2
    gain = slot_row(weights, notes[BACK1])
    left, right = sorted_halos(near, far, 0, halos)
    pieces = [(left, 0, edge), (received, 0, own), (right, 0, edge)]

    def block(columns):
        mixed = (window(pieces, columns).astype(F32) * factor[:, columns]).astype(BF16)
        mixed_out[:, columns] = mixed
        inner = mixed[edge : edge + own]
        gain_sum = jnp.sum(inner.astype(F32) * conv[:, columns], axis=0, keepdims=True) / gain(columns)
        put_taps(taps1, tap_term(go_table, t_table, m[:, columns], inner), gain_sum, columns)

    each_block(width, block)


def second_backward_kernel(
    notes, saved, received, weights, mixed, q, mean, inverse, g_table, x_table, grad_x, scaled, sum_a, sum_b
):
    own, width = grad_x.shape
    slot, length, first = looked_up(notes, BACK1)
    pieces = [(saved.at[1], 0, own)]
    mask = frame_mask(own, first, length)
    sum_a[...] = jnp.zeros_like(sum_a)
    sum_b[...] = jnp.zeros_like(sum_b)

    def block(columns):
        first_pass(
            pieces, mean, inverse, slot_row(weights, slot), mask, (g_table, x_table), mixed[:, columns], q[:, columns],
            columns, scaled, sum_a, sum_b,
        )

    each_block(width, block)
    last_pass([(received, 0, own)], pieces, mean, inverse, scaled, sum_a, sum_b, grad_x)


def row_gain(layer):
    last = layer.shape[0] - 1
    return lambda columns: layer[last : last + 1, columns].astype(F32)


def first_forward_kernel(reach, notes, act, ahead, m_table, q_table, c_table, out, halo, masked):
    own, width = act.shape
    middle = reach // 2
    _, length, first = looked_up(notes, AHEAD0)
    left, right = ahead.at[pl.ds(0, reach)], ahead.at[pl.ds(reach, reach)]
    layer = ahead.at[pl.ds(2 * reach, ahead.shape[0] - 2 * reach)]
    inner = [(left, middle, middle), (act, 0, own), (right, 0, middle)]
    norm_pieces([(act, 0, own)], row_gain(layer), first, length, masked)
    norm_halo(left, right, own, row_gain(layer), first, length, halo)

    def block(columns):
        q = tap_spectrum(q_table[...], layer[:, columns])
        conv = transform(c_table, product(transform(m_table, joined(halo, masked, columns)), q))
        out[:, columns] = (window(inner, columns).astype(F32) + conv * sigmoid(conv)).astype(BF16)

    each_block(width, block)


def second_forward_kernel(notes, between, layer, m_table, q_table, c_table, out, masked):
    own, width = out.shape
    rows = between.shape[0]
    edge = (rows - own) // 2
    _, length, first = looked_up(notes, AHEAD0)
    norm_pieces([(between, 0, rows)], row_gain(layer), first - edge, length, masked, chunk=rows // 2)

    def block(columns):
        q = tap_spectrum(q_table[...], layer[:, columns])
        conv = transform(c_table, product(transform(m_table, masked[:, columns]), q))
        out[:, columns] = (between[edge : edge + own, columns].astype(F32) + conv * sigmoid(conv)).astype(BF16)

    each_block(width, block)


def pack_kernel(
    reaches, saved, grad, back_lengths, ahead_lengths, back_slots, ahead_slots,
    near, far, notes, back_len, ahead_len, back_slot, ahead_slot, sems,
):
    own = grad.shape[1]
    even = lax.rem(lax.axis_index("tm") + 1, 2)
    copies = []
    at = 0
    for x, reach in zip((saved, grad), reaches):
        for out, tail in ((near, even), (far, 1 - even)):
            start = pl.multiple_of(tail * (own - reach), 16)
            copies.append((x.at[0, pl.ds(start, reach)], out.at[pl.ds(at, reach)]))
        at += reach
    small = [(back_lengths, back_len), (ahead_lengths, ahead_len), (back_slots, back_slot), (ahead_slots, ahead_slot)]
    copies = [pltpu.make_async_copy(a, b, sems.at[k]) for k, (a, b) in enumerate(small + copies)]
    for copy in copies:
        copy.start()
    for copy in copies:
        copy.wait()
    section, sections = lax.axis_index("section"), lax.axis_size("section")
    notes[FIRST] = lax.axis_index("tm") * own
    notes[FIRST + 1] = ahead_slot[1, section]
    notes[BACK0] = back_slot[0, section]
    notes[BACK0 + 1] = back_len[section]
    notes[BACK1] = back_slot[1, section]
    notes[BACK1 + 1] = back_len[lax.rem(section + 1, sections)]
    notes[AHEAD0] = ahead_slot[0, section]
    notes[AHEAD0 + 1] = ahead_len[lax.rem(section + sections - 2, sections)]


def final_kernel(notes, mine, other, act, grad, act_out, grad_out, taps_out, gains_out, taps, gains, sems):
    copies = [
        pltpu.make_async_copy(act, act_out, sems.at[0]),
        pltpu.make_async_copy(grad, grad_out, sems.at[1]),
    ]
    for copy in copies:
        copy.start()
    count, slots, width = taps.shape
    step = width // 4
    for begin in range(0, width, step):
        columns = pl.ds(begin, step)
        total = mine[:, columns].astype(F32) + other[:, columns].astype(F32)
        ticks = total[: count + 1], total[count + 1 :]
        for slot in range(slots):
            use = [(notes[layer] == slot).astype(F32) for layer in (BACK0, BACK1)]
            both = use[0] * ticks[0] + use[1] * ticks[1]
            taps[:, slot, columns] = both[:count]
            gains[slot : slot + 1, columns] = both[count:]
        for source, target in ((taps.at[:, :, columns], taps_out.at[:, :, columns]),):
            copies.append(pltpu.make_async_copy(source, target, sems.at[len(copies)]))
            copies[-1].start()
    copies.append(pltpu.make_async_copy(gains, gains_out, sems.at[len(copies)]))
    copies[-1].start()
    for copy in copies:
        copy.wait()


def span(reach, own):
    return np.arange(-reach, own + reach)


VMEM = pl.BlockSpec(memory_space=pltpu.VMEM)
SMEM = pl.BlockSpec(memory_space=pltpu.SMEM)
ANY = pl.BlockSpec(memory_space=pl.ANY)
HBM = pl.BlockSpec(memory_space=pltpu.HBM)
LIMIT = 24 * 1024 * 1024
FULL = 127 * 512 * 1024


def call(kernel, outs, scratch, operands, micros, specs=None, out_specs=None, limit=LIMIT, after=()):
    if specs is None:
        specs = [SMEM if x.dtype == jnp.int32 else VMEM for x in operands]
    if after:
        inner, place = kernel, len(operands)
        operands, specs = [*operands, *after], [*specs, *[ANY] * len(after)]

        def kernel(*refs):
            return inner(*refs[:place], *refs[place + len(after) :])

    return pl.pallas_call(
        kernel,
        out_shape=outs,
        in_specs=specs,
        out_specs=jax.tree.map(lambda _: VMEM, outs) if out_specs is None else out_specs,
        scratch_shapes=scratch,
        compiler_params=pltpu.CompilerParams(vmem_limit_bytes=limit),
        cost_estimate=pl.CostEstimate(flops=int(micros * 1e9), bytes_accessed=0, transcendentals=0),
    )(*operands)


def like(rows, width, dtype):
    return jax.ShapeDtypeStruct((rows, width), dtype)


def up16(count):
    return -(-count // 16) * 16


def local(
    act_in, grad_in, saved_inputs, kernels, norm_gains,
    forward_lengths, backward_lengths, forward_slots, backward_slots,
):
    sections = lax.axis_size("section")
    shards = lax.axis_size("tm")
    act, grad, saved = act_in[0], grad_in[0], saved_inputs[0]
    own, width = act.shape
    tap_count = kernels.shape[2]
    half = (tap_count - 1) // 2
    one, two = up16(half), up16(2 * half)
    size, small = own + 2 * two, own + 2 * one

    def shifted(x, by):
        return lax.ppermute(x, "section", [(i, (i + by) % sections) for i in range(sections)])

    def swapped(near, far, by=0):
        results = []
        for x, begin in ((far, 1), (near, 0)):
            pairs = [(i, i + 1) for i in range(begin, shards - 1, 2)]
            pairs = [
                (s * shards + i, (s + by) % sections * shards + j)
                for s in range(sections)
                for a, b in pairs
                for i, j in ((a, b), (b, a))
            ]
            results.append(lax.ppermute(x, ("section", "tm"), pairs))
        return results[::-1]

    act_ahead = shifted(act, 2)
    lengths = pltpu.SMEM(backward_lengths.shape, jnp.int32)
    forward_slots, backward_slots = forward_slots.T, backward_slots.T
    slots = pltpu.SMEM(backward_slots.shape, jnp.int32)
    near0, far0, notes = call(
        functools.partial(pack_kernel, (two, one)),
        (like(two + one, width, BF16), like(two + one, width, BF16), jax.ShapeDtypeStruct((8,), jnp.int32)),
        [lengths, lengths, slots, slots, pltpu.SemaphoreType.DMA((8,))],
        (saved, grad_in, backward_lengths, forward_lengths, backward_slots, forward_slots),
        0, [HBM] * 6, (VMEM, VMEM, SMEM), FULL,
    )
    near0, far0 = swapped(near0, far0)
    tap_back = np.concatenate([from_freq(size, np.arange(tap_count) - half), np.zeros((1, size))], axis=0)
    m_table = stacked(to_freq(size, span(two, own)))
    q_table = tap_freq(size, tap_count)
    c_table = stacked(from_freq(size, span(one, own)))
    go_table = beside(to_freq(size, np.arange(own)))
    t_table = stacked(tap_back)

    def run(kernel, outs, scratch, operands, micros=0, *after):
        return call(kernel, outs, scratch, [jnp.asarray(x) for x in operands], micros, after=after)

    rows = [pltpu.VMEM((own, width), F32)] + [pltpu.VMEM((own, LANES), F32)] * 2
    layer = like(own, width, BF16), like(own, LANES, F32), like(own, LANES, F32)
    weights, ahead0, ahead1, near1, far1, *layer0 = run(
        functools.partial(prepare_kernel, two),
        (
            jax.ShapeDtypeStruct((kernels.shape[1], tap_count + 1, width), BF16), like(tap_count + 1, width, BF16),
            like(tap_count + 1, width, BF16), like(2 * two, width, BF16), like(2 * two, width, BF16), *layer,
        ),
        [],
        [notes, kernels[0].transpose(1, 0, 2), norm_gains[0], saved, act],
        0,
    )
    near1, far1 = swapped(near1, far1)
    ahead1 = shifted(ahead1, 1)
    g_table, x_table = stacked(to_freq(size, span(one, own))), stacked(from_freq(size, span(0, own)))
    grad_mid, near2, far2, halo0, inner0, gain0 = run(
        functools.partial(first_backward_kernel, two),
        (
            like(own, width, BF16), like(one, width, BF16), like(one, width, BF16),
            like(2 * two, width, BF16), like(own, width, BF16), like(1, width, F32),
        ),
        [pltpu.VMEM((2, two, width), BF16), pltpu.VMEM((2, one, width), BF16), *rows],
        [
            notes, saved, far0, near0, grad, weights, *layer0,
            m_table, q_table, c_table, g_table, x_table,
        ],
        4,
        act_ahead,
    )
    grad_mid = shifted(grad_mid, -1)
    near2, far2 = swapped(near2, far2, -1)
    taps0 = run(
        first_taps_kernel, like(tap_count + 1, width, BF16), [],
        [halo0, layer0[0], inner0, gain0, m_table, go_table, t_table],
        0,
    )
    masked1, mean1, inverse1, q1 = run(
        second_early_kernel, (*layer, like(size, width, F32)), [], [notes, saved, weights, q_table], 1, taps0
    )
    m1, factor1, conv1, ahead0 = run(
        functools.partial(second_ready_kernel, two),
        (
            like(size, width, F32), like(small, width, F32), like(own, width, F32),
            like(2 * two + tap_count + 1, width, BF16),
        ),
        [pltpu.VMEM((2 * two, width), BF16), pltpu.VMEM((2, two, width), BF16)],
        [notes, far1, near1, weights, ahead0, masked1, q1, m_table, c_table],
        5,
    )
    ahead0 = shifted(ahead0, 2)
    def partner(x, step):
        return lax.ppermute(x, "tm", [(i, i ^ step) for i in range(shards)])

    mixed1, sums = run(
        second_taps_kernel,
        (like(small, width, BF16), like(2 * (tap_count + 1), width, BF16)),
        [pltpu.VMEM((2, one, width), BF16)],
        [notes, grad_mid, far2, near2, weights, m1, factor1, conv1, taps0, go_table, t_table],
        2,
    )
    grad_out = run(
        second_backward_kernel,
        like(own, width, BF16),
        rows,
        [
            notes, saved, grad_mid, weights, mixed1, q1, mean1, inverse1,
            g_table, x_table,
        ],
        6,
    )
    grad_out = shifted(grad_out, -1)
    mine = call(add_kernel, like(*sums.shape, BF16), [], (sums, partner(sums, 1)), 6)
    between = run(
        functools.partial(first_forward_kernel, two),
        like(small, width, BF16),
        [pltpu.VMEM((2 * two, width), BF16), pltpu.VMEM((own, width), BF16)],
        [notes, act_ahead, ahead0, m_table, q_table, c_table],
        10,
        mine,
    )
    act_out = run(
        second_forward_kernel,
        like(own, width, BF16),
        [pltpu.VMEM((small, width), BF16)],
        [
            notes, between, ahead1,
            stacked(to_freq(small, span(one, own))), tap_freq(small, tap_count), stacked(from_freq(small, span(0, own))),
        ],
        10,
    )
    step = 2
    while True:
        other = partner(mine, step)
        step *= 2
        if step >= shards:
            break
        mine = call(add_kernel, like(*mine.shape, BF16), [], (mine, other), 0)
    slots = kernels.shape[1]
    act_out, grad_out, taps, gains = call(
        final_kernel,
        (
            like(own, width, BF16), like(own, width, BF16),
            jax.ShapeDtypeStruct((tap_count, slots, width), F32), like(slots, width, F32),
        ),
        [
            pltpu.VMEM((tap_count, slots, width), F32), pltpu.VMEM((slots, width), F32),
            pltpu.SemaphoreType.DMA((7,)),
        ],
        (notes, mine, other, act_out, grad_out),
        0, [SMEM] + [VMEM] * 2 + [ANY] * 2, (ANY,) * 4,
    )
    return act_out[None], grad_out[None], taps.transpose(1, 0, 2)[None], gains[None]


def solution(mesh):
    in_specs = (
        P("section", "tm", None),
        P("section", "tm", None),
        P("section", None, "tm", None),
        P("section", None, None, None),
        P("section", None, None),
        P(),
        P(),
        P(),
        P(),
    )
    out_specs = (
        P("section", "tm", None),
        P("section", "tm", None),
        P("section", None, None, None),
        P("section", None, None),
    )
    return jax.shard_map(local, mesh=mesh, in_specs=in_specs, out_specs=out_specs, check_vma=False)
```

```python
import functools

import jax
import jax.numpy as jnp
import ml_dtypes
import numpy as np
from jax import lax
from jax.experimental import pallas as pl
from jax.experimental.pallas import tpu as pltpu
from jax.sharding import PartitionSpec as P

epsilon = 1e-05
BLOCK = 2048
LANES = 128
F32 = jnp.float32
BF16 = jnp.bfloat16


def split(matrix):
    high = matrix.astype(ml_dtypes.bfloat16)
    low = (matrix - high.astype(np.float64)).astype(ml_dtypes.bfloat16)
    return high, low


def angles(size, times):
    return 2.0 * np.pi / size * np.outer(np.arange(size // 2) + 0.5, np.asarray(times, np.float64))


def to_freq(size, times):
    phase = angles(size, times)
    return np.concatenate([np.cos(phase), -np.sin(phase)], axis=0)


def from_freq(size, times):
    phase = angles(size, times).T
    return 2.0 / size * np.concatenate([np.cos(phase), -np.sin(phase)], axis=1)


def stacked(matrix):
    return np.concatenate(split(matrix), axis=0)


def beside(matrix):
    return np.concatenate(split(matrix), axis=1)


def tap_freq(size, taps):
    phase = angles(size, np.arange(taps) - (taps - 1) // 2)
    table = np.concatenate([np.cos(phase), np.sin(phase)], axis=0)
    return beside(np.concatenate([table, np.zeros((size, 1))], axis=1))


def dot(a, b):
    return jnp.dot(a, b, preferred_element_type=F32)


def transform(table, values):
    return sum(halves(dot(table[...], values.astype(BF16))))


def halves(values):
    half = values.shape[0] // 2
    return values[:half], values[half:]


def product(a, b):
    ar, ai = halves(a)
    br, bi = halves(b)
    return jnp.concatenate([ar * br - ai * bi, ar * bi + ai * br], axis=0)


def product_conj(a, b):
    ar, ai = halves(a)
    br, bi = halves(b)
    return jnp.concatenate([ar * br + ai * bi, ai * br - ar * bi], axis=0)


def sigmoid(values):
    return 0.5 * jnp.tanh(0.5 * values) + 0.5


def wide(stat, count):
    return jnp.concatenate([stat] * (count // LANES), axis=1)


def norm_rows(ref, start, count, at, gain, first, length, masked_ref, mean_ref, inverse_ref):
    width = masked_ref.shape[1]
    rows = pl.ds(start, count)
    tiles = [pl.ds(i * LANES, LANES) for i in range(width // LANES)]

    def values(tile):
        return ref[rows, tile].astype(F32)

    total = values(tiles[0])
    for tile in tiles[1:]:
        total = total + values(tile)
    mean = jnp.sum(total, axis=1, keepdims=True) * (1.0 / width)
    mean = jnp.broadcast_to(mean, (count, LANES))
    square = jnp.zeros((count, LANES), F32)
    for tile in tiles:
        center = values(tile) - mean
        square = square + center * center
    var = jnp.sum(square, axis=1, keepdims=True) * (1.0 / width)
    inverse = jnp.broadcast_to(lax.rsqrt(var + epsilon), (count, LANES))
    frame = first + at + lax.broadcasted_iota(jnp.int32, (count, LANES), 0)
    mask = ((frame >= 0) & (frame < length)).astype(F32)
    scale = mask * inverse
    out = pl.ds(at, count)
    for tile in tiles:
        masked_ref[out, tile] = ((values(tile) - mean) * scale * gain(tile)).astype(BF16)
    if mean_ref is not None:
        mean_ref[out, :] = mean
        inverse_ref[out, :] = inverse


def norm_pieces(pieces, gain, first, length, masked_ref, mean_ref=None, inverse_ref=None, chunk=128):
    at = 0
    for ref, start, count in pieces:
        for begin in range(0, count, chunk):
            norm_rows(
                ref, start + begin, min(chunk, count - begin), at + begin,
                gain, first, length, masked_ref, mean_ref, inverse_ref,
            )
        at += count


def window(pieces, columns):
    parts = [ref[pl.ds(start, count), columns] for ref, start, count in pieces]
    return parts[0] if len(parts) == 1 else jnp.concatenate(parts, axis=0)


def each_block(width, body):
    for begin in range(0, width, BLOCK):
        body(pl.ds(begin, BLOCK))


def tap_spectrum(table, weights):
    return dot(table, jnp.concatenate([weights, weights], axis=0))


def gate_factor(conv):
    gate = sigmoid(conv)
    return gate * (1.0 + conv * (1.0 - gate))


FIRST, BACK0, BACK1, AHEAD0 = range(0, 8, 2)


def looked_up(notes, layer):
    return notes[layer], notes[layer + 1], notes[FIRST]


def sorted_halos(near, far, at, halos):
    even = lax.rem(lax.axis_index("tm") + 1, 2)
    rows = pl.ds(at, halos.shape[1])
    halos[even] = near[rows, :]
    halos[1 - even] = far[rows, :]
    return halos.at[0], halos.at[1]


def lane_sum(values):
    total = values[:, :LANES]
    for lane in range(LANES, values.shape[1], LANES):
        total = total + values[:, lane : lane + LANES]
    return total


def first_pass(pieces, mean, inverse, gain, mask, tables, mixed, q, columns, scaled, sum_a, sum_b):
    g_table, x_table = tables
    grad_masked = wide(mask, BLOCK) * transform(x_table, product_conj(transform(g_table, mixed), q))
    centered = window(pieces, columns).astype(F32) - wide(mean[...], BLOCK)
    weighted = grad_masked * (centered * wide(inverse[...], BLOCK))
    gain = gain(columns)
    by_gain = grad_masked * gain
    scaled[:, columns] = by_gain
    sum_a[...] += lane_sum(by_gain)
    sum_b[...] += lane_sum(weighted * gain)
    return weighted


def last_pass(grad_pieces, pieces, mean, inverse, scaled, sum_a, sum_b, grad_x, chunk=128):
    width = scaled.shape[1]
    at = 0
    for (ref, start, count), (saved, base, _) in zip(grad_pieces, pieces):
        for begin in range(0, count, chunk):
            here = min(chunk, count - begin)
            rows = pl.ds(at + begin, here)
            inv = inverse[rows, :]
            mean_a = jnp.sum(sum_a[rows, :], axis=1, keepdims=True) * (1.0 / width)
            mean_b = jnp.sum(sum_b[rows, :], axis=1, keepdims=True) * (1.0 / width)
            slope = inv * jnp.broadcast_to(mean_b, (here, LANES)) * inv
            fixed = inv * jnp.broadcast_to(mean_a, (here, LANES)) - slope * mean[rows, :]
            for lane in range(0, width, LANES):
                tile = pl.ds(lane, LANES)
                x = saved[pl.ds(base + begin, here), tile].astype(F32)
                change = inv * scaled[rows, tile] - fixed - slope * x
                grad_x[rows, tile] = (ref[pl.ds(start + begin, here), tile].astype(F32) + change).astype(BF16)
        at += count


def frame_mask(rows, first, length):
    frame = first + lax.broadcasted_iota(jnp.int32, (rows, LANES), 0)
    return ((frame >= 0) & (frame < length)).astype(F32)


def slot_row(weights, slot):
    last = weights.shape[1] - 1
    return lambda columns: weights[slot, last : last + 1, columns].astype(F32)


def prepare_kernel(
    reach, notes, kernels, gains, saved, act, weights, ahead0, ahead1, near, far, masked, mean, inverse
):
    own = act.shape[0]
    for even in range(2):

        @pl.when(lax.rem(lax.axis_index("tm") + 1, 2) == even)
        def _():
            for x, at in ((saved.at[1], 0), (act, reach)):
                tail, head = (near, far) if even else (far, near)
                tail[pl.ds(at, reach), :] = x[pl.ds(own - reach, reach), :]
                head[pl.ds(at, reach), :] = x[pl.ds(0, reach), :]

    count = kernels.shape[0]
    for slot in range(kernels.shape[1]):
        weights[slot, :count, :] = kernels[:, slot, :]
        weights[slot, count:, :] = gains[slot : slot + 1, :]
    ahead0[...] = weights[notes[AHEAD0]]
    ahead1[...] = weights[notes[FIRST + 1]]
    slot, length, first = looked_up(notes, BACK0)
    norm_pieces([(saved.at[0], 0, own)], slot_row(weights, slot), first, length, masked, mean, inverse)


def norm_halo(left, right, own, gain, first, length, halo):
    reach = left.shape[0]
    norm_pieces([(left, 0, reach)], gain, first - reach, length, halo)
    norm_pieces([(right, 0, reach)], gain, first + own, length, halo.at[pl.ds(reach, reach)])


def joined(halo, own, columns):
    reach = halo.shape[0] // 2
    return jnp.concatenate([halo[:reach, columns], own[:, columns], halo[reach:, columns]], axis=0)


def first_backward_kernel(
    reach, notes, saved, far, near, grads, weights, masked, mean, inverse,
    m_table, q_table, c_table, g_table, x_table,
    grad_x, near_edge, far_edge, halo, inner, gain_sum, halos, grad_halos, scaled, sum_a, sum_b,
):
    own, width = grads.shape
    edge = near_edge.shape[0]
    slot, length, first = looked_up(notes, BACK0)
    gain = slot_row(weights, slot)
    left, right = sorted_halos(near, far, 0, halos)
    grad_left, grad_right = sorted_halos(near, far, reach, grad_halos)
    norm_halo(left, right, own, gain, first, length, halo)
    grad_pieces = [(grad_left, 0, edge), (grads, 0, own), (grad_right, 0, edge)]
    pieces = [(saved.at[0], 0, own)]
    mask = frame_mask(own, first, length)
    sum_a[...] = jnp.zeros_like(sum_a)
    sum_b[...] = jnp.zeros_like(sum_b)

    def block(columns):
        m = transform(m_table, joined(halo, masked, columns))
        q = tap_spectrum(q_table[...], weights[slot, :, columns])
        conv = transform(c_table, product(m, q))
        mixed = (window(grad_pieces, columns).astype(F32) * gate_factor(conv)).astype(BF16)
        inner[:, columns] = mixed[edge : edge + own]
        weighted = first_pass(
            pieces, mean, inverse, gain, mask, (g_table, x_table), mixed, q, columns, scaled, sum_a, sum_b
        )
        gain_sum[:, columns] = jnp.sum(weighted, axis=0, keepdims=True)

    each_block(width, block)
    last_pass([(grads, 0, own)], pieces, mean, inverse, scaled, sum_a, sum_b, grad_x)
    for even in range(2):

        @pl.when(lax.rem(lax.axis_index("tm") + 1, 2) == even)
        def _():
            top, bottom = (far_edge, near_edge) if even else (near_edge, far_edge)
            top[...] = grad_x[pl.ds(0, edge), :]
            bottom[...] = grad_x[pl.ds(own - edge, edge), :]


def tap_term(go_table, t_table, m, mixed):
    g_own = dot(go_table[...], jnp.concatenate([mixed, mixed], axis=0))
    return transform(t_table, product_conj(m, g_own))


def put_taps(taps, tap, gain_sum, columns):
    row = lax.broadcasted_iota(jnp.int32, tap.shape, 0)
    taps[:, columns] = jnp.where(row == tap.shape[0] - 1, gain_sum, tap).astype(taps.dtype)


def first_taps_kernel(halo, masked, inner, gain_sum, m_table, go_table, t_table, taps):
    def block(columns):
        m = transform(m_table, joined(halo, masked, columns))
        put_taps(taps, tap_term(go_table, t_table, m, inner[:, columns]), gain_sum[:, columns], columns)

    each_block(masked.shape[1], block)


def added(mine, other):
    return (mine[...].astype(F32) + other[...].astype(F32)).astype(BF16)


def add_kernel(mine0, other0, mine1, other1, out0, out1):
    out0[...] = added(mine0, other0)
    out1[...] = added(mine1, other1)


def second_early_kernel(notes, saved, weights, q_table, masked, mean, inverse, q):
    own = masked.shape[0]
    slot, length, first = looked_up(notes, BACK1)
    norm_pieces([(saved.at[1], 0, own)], slot_row(weights, slot), first, length, masked, mean, inverse)

    def block(columns):
        q[:, columns] = tap_spectrum(q_table[...], weights[slot, :, columns])

    each_block(masked.shape[1], block)


def second_ready_kernel(
    reach, notes, far, near, weights, ahead0, masked, q, m_table, c_table, m_out, factor, conv_out, ahead, halo, halos
):
    left, right = sorted_halos(near, far, reach, halos)
    ahead[pl.ds(0, reach), :] = left[...]
    ahead[pl.ds(reach, reach), :] = right[...]
    ahead[pl.ds(2 * reach, ahead0.shape[0]), :] = ahead0[...]
    own, width = masked.shape
    slot, length, first = looked_up(notes, BACK1)
    left, right = sorted_halos(near, far, 0, halos)
    norm_halo(left, right, own, slot_row(weights, slot), first, length, halo)

    def block(columns):
        m = transform(m_table, joined(halo, masked, columns))
        conv = transform(c_table, product(m, q[:, columns]))
        m_out[:, columns] = m
        factor[:, columns] = gate_factor(conv)
        edge = (conv.shape[0] - own) // 2
        conv_out[:, columns] = conv[edge : edge + own]

    each_block(width, block)


def second_taps_kernel(
    notes, received, far, near, weights, m, factor, conv, taps0, go_table, t_table, mixed_out, taps, taps0_out, halos
):
    taps0_out[...] = taps0[...]
    own, width = conv.shape
    rows = factor.shape[0]
    edge = (rows - own) // 2
    gain = slot_row(weights, notes[BACK1])
    left, right = sorted_halos(near, far, 0, halos)
    pieces = [(left, 0, edge), (received, 0, own), (right, 0, edge)]

    def block(columns):
        mixed = (window(pieces, columns).astype(F32) * factor[:, columns]).astype(BF16)
        mixed_out[:, columns] = mixed
        inner = mixed[edge : edge + own]
        gain_sum = jnp.sum(inner.astype(F32) * conv[:, columns], axis=0, keepdims=True) / gain(columns)
        put_taps(taps, tap_term(go_table, t_table, m[:, columns], inner), gain_sum, columns)

    each_block(width, block)


def second_backward_kernel(
    notes, saved, received, weights, mixed, q, mean, inverse, g_table, x_table, grad_x, scaled, sum_a, sum_b
):
    own, width = grad_x.shape
    slot, length, first = looked_up(notes, BACK1)
    pieces = [(saved.at[1], 0, own)]
    mask = frame_mask(own, first, length)
    sum_a[...] = jnp.zeros_like(sum_a)
    sum_b[...] = jnp.zeros_like(sum_b)

    def block(columns):
        first_pass(
            pieces, mean, inverse, slot_row(weights, slot), mask, (g_table, x_table), mixed[:, columns], q[:, columns],
            columns, scaled, sum_a, sum_b,
        )

    each_block(width, block)
    last_pass([(received, 0, own)], pieces, mean, inverse, scaled, sum_a, sum_b, grad_x)


def row_gain(layer):
    last = layer.shape[0] - 1
    return lambda columns: layer[last : last + 1, columns].astype(F32)


def first_forward_kernel(reach, notes, act, ahead, m_table, q_table, c_table, out, halo, masked):
    own, width = act.shape
    middle = reach // 2
    _, length, first = looked_up(notes, AHEAD0)
    left, right = ahead.at[pl.ds(0, reach)], ahead.at[pl.ds(reach, reach)]
    layer = ahead.at[pl.ds(2 * reach, ahead.shape[0] - 2 * reach)]
    inner = [(left, middle, middle), (act, 0, own), (right, 0, middle)]
    norm_pieces([(act, 0, own)], row_gain(layer), first, length, masked)
    norm_halo(left, right, own, row_gain(layer), first, length, halo)

    def block(columns):
        q = tap_spectrum(q_table[...], layer[:, columns])
        conv = transform(c_table, product(transform(m_table, joined(halo, masked, columns)), q))
        out[:, columns] = (window(inner, columns).astype(F32) + conv * sigmoid(conv)).astype(BF16)

    each_block(width, block)


def second_forward_kernel(notes, between, layer, m_table, q_table, c_table, out, masked):
    own, width = out.shape
    rows = between.shape[0]
    edge = (rows - own) // 2
    _, length, first = looked_up(notes, AHEAD0)
    norm_pieces([(between, 0, rows)], row_gain(layer), first - edge, length, masked, chunk=rows // 2)

    def block(columns):
        q = tap_spectrum(q_table[...], layer[:, columns])
        conv = transform(c_table, product(transform(m_table, masked[:, columns]), q))
        out[:, columns] = (between[edge : edge + own, columns].astype(F32) + conv * sigmoid(conv)).astype(BF16)

    each_block(width, block)


def pack_kernel(
    reaches, saved, grad, back_lengths, ahead_lengths, back_slots, ahead_slots,
    near, far, notes, back_len, ahead_len, back_slot, ahead_slot, sems,
):
    own = grad.shape[1]
    even = lax.rem(lax.axis_index("tm") + 1, 2)
    copies = []
    at = 0
    for x, reach in zip((saved, grad), reaches):
        for out, tail in ((near, even), (far, 1 - even)):
            start = pl.multiple_of(tail * (own - reach), 16)
            copies.append((x.at[0, pl.ds(start, reach)], out.at[pl.ds(at, reach)]))
        at += reach
    small = [(back_lengths, back_len), (ahead_lengths, ahead_len), (back_slots, back_slot), (ahead_slots, ahead_slot)]
    copies = [pltpu.make_async_copy(a, b, sems.at[k]) for k, (a, b) in enumerate(small + copies)]
    for copy in copies:
        copy.start()
    for copy in copies:
        copy.wait()
    section, sections = lax.axis_index("section"), lax.axis_size("section")
    notes[FIRST] = lax.axis_index("tm") * own
    notes[FIRST + 1] = ahead_slot[1, section]
    notes[BACK0] = back_slot[0, section]
    notes[BACK0 + 1] = back_len[section]
    notes[BACK1] = back_slot[1, section]
    notes[BACK1 + 1] = back_len[lax.rem(section + 1, sections)]
    notes[AHEAD0] = ahead_slot[0, section]
    notes[AHEAD0 + 1] = ahead_len[lax.rem(section + sections - 2, sections)]


def final_kernel(notes, mine0, mine1, other0, other1, act, grad, act_out, grad_out, taps_out, gains_out, taps, gains, sems):
    copies = [
        pltpu.make_async_copy(act, act_out, sems.at[0]),
        pltpu.make_async_copy(grad, grad_out, sems.at[1]),
    ]
    for copy in copies:
        copy.start()
    count, slots, width = taps.shape
    step = width // 4
    for begin in range(0, width, step):
        columns = pl.ds(begin, step)
        pairs = (mine0, other0), (mine1, other1)
        ticks = [a[:, columns].astype(F32) + b[:, columns].astype(F32) for a, b in pairs]
        for slot in range(slots):
            use = [(notes[layer] == slot).astype(F32) for layer in (BACK0, BACK1)]
            both = use[0] * ticks[0] + use[1] * ticks[1]
            taps[:, slot, columns] = both[:count]
            gains[slot : slot + 1, columns] = both[count:]
        for source, target in ((taps.at[:, :, columns], taps_out.at[:, :, columns]),):
            copies.append(pltpu.make_async_copy(source, target, sems.at[len(copies)]))
            copies[-1].start()
    copies.append(pltpu.make_async_copy(gains, gains_out, sems.at[len(copies)]))
    copies[-1].start()
    for copy in copies:
        copy.wait()


def span(reach, own):
    return np.arange(-reach, own + reach)


VMEM = pl.BlockSpec(memory_space=pltpu.VMEM)
SMEM = pl.BlockSpec(memory_space=pltpu.SMEM)
ANY = pl.BlockSpec(memory_space=pl.ANY)
HBM = pl.BlockSpec(memory_space=pltpu.HBM)
LIMIT = 24 * 1024 * 1024
FULL = 127 * 512 * 1024


def call(kernel, outs, scratch, operands, micros, specs=None, out_specs=None, limit=LIMIT, after=()):
    if specs is None:
        specs = [SMEM if x.dtype == jnp.int32 else VMEM for x in operands]
    if after:
        inner, place = kernel, len(operands)
        operands, specs = [*operands, *after], [*specs, *[ANY] * len(after)]

        def kernel(*refs):
            return inner(*refs[:place], *refs[place + len(after) :])

    return pl.pallas_call(
        kernel,
        out_shape=outs,
        in_specs=specs,
        out_specs=jax.tree.map(lambda _: VMEM, outs) if out_specs is None else out_specs,
        scratch_shapes=scratch,
        compiler_params=pltpu.CompilerParams(vmem_limit_bytes=limit),
        cost_estimate=pl.CostEstimate(flops=int(micros * 1e9), bytes_accessed=0, transcendentals=0),
    )(*operands)


def like(rows, width, dtype):
    return jax.ShapeDtypeStruct((rows, width), dtype)


def up16(count):
    return -(-count // 16) * 16


def local(
    act_in, grad_in, saved_inputs, kernels, norm_gains,
    forward_lengths, backward_lengths, forward_slots, backward_slots,
):
    sections = lax.axis_size("section")
    shards = lax.axis_size("tm")
    act, grad, saved = act_in[0], grad_in[0], saved_inputs[0]
    own, width = act.shape
    tap_count = kernels.shape[2]
    half = (tap_count - 1) // 2
    one, two = up16(half), up16(2 * half)
    size, small = own + 2 * two, own + 2 * one

    def shifted(x, by):
        return lax.ppermute(x, "section", [(i, (i + by) % sections) for i in range(sections)])

    def swapped(near, far, by=0):
        results = []
        for x, begin in ((far, 1), (near, 0)):
            pairs = [(i, i + 1) for i in range(begin, shards - 1, 2)]
            pairs = [
                (s * shards + i, (s + by) % sections * shards + j)
                for s in range(sections)
                for a, b in pairs
                for i, j in ((a, b), (b, a))
            ]
            results.append(lax.ppermute(x, ("section", "tm"), pairs))
        return results[::-1]

    act_ahead = shifted(act, 2)
    lengths = pltpu.SMEM(backward_lengths.shape, jnp.int32)
    forward_slots, backward_slots = forward_slots.T, backward_slots.T
    slots = pltpu.SMEM(backward_slots.shape, jnp.int32)
    near0, far0, notes = call(
        functools.partial(pack_kernel, (two, one)),
        (like(two + one, width, BF16), like(two + one, width, BF16), jax.ShapeDtypeStruct((8,), jnp.int32)),
        [lengths, lengths, slots, slots, pltpu.SemaphoreType.DMA((8,))],
        (saved, grad_in, backward_lengths, forward_lengths, backward_slots, forward_slots),
        0, [HBM] * 6, (VMEM, VMEM, SMEM), FULL,
    )
    near0, far0 = swapped(near0, far0)
    tap_back = np.concatenate([from_freq(size, np.arange(tap_count) - half), np.zeros((1, size))], axis=0)
    m_table = stacked(to_freq(size, span(two, own)))
    q_table = tap_freq(size, tap_count)
    c_table = stacked(from_freq(size, span(one, own)))
    go_table = beside(to_freq(size, np.arange(own)))
    t_table = stacked(tap_back)

    def run(kernel, outs, scratch, operands, micros=0, *after):
        return call(kernel, outs, scratch, [jnp.asarray(x) for x in operands], micros, after=after)

    rows = [pltpu.VMEM((own, width), F32)] + [pltpu.VMEM((own, LANES), F32)] * 2
    layer = like(own, width, BF16), like(own, LANES, F32), like(own, LANES, F32)
    weights, ahead0, ahead1, near1, far1, *layer0 = run(
        functools.partial(prepare_kernel, two),
        (
            jax.ShapeDtypeStruct((kernels.shape[1], tap_count + 1, width), BF16), like(tap_count + 1, width, BF16),
            like(tap_count + 1, width, BF16), like(2 * two, width, BF16), like(2 * two, width, BF16), *layer,
        ),
        [],
        [notes, kernels[0].transpose(1, 0, 2), norm_gains[0], saved, act],
        0,
    )
    near1, far1 = swapped(near1, far1)
    ahead1 = shifted(ahead1, 1)
    g_table, x_table = stacked(to_freq(size, span(one, own))), stacked(from_freq(size, span(0, own)))
    grad_mid, near2, far2, halo0, inner0, gain0 = run(
        functools.partial(first_backward_kernel, two),
        (
            like(own, width, BF16), like(one, width, BF16), like(one, width, BF16),
            like(2 * two, width, BF16), like(own, width, BF16), like(1, width, F32),
        ),
        [pltpu.VMEM((2, two, width), BF16), pltpu.VMEM((2, one, width), BF16), *rows],
        [
            notes, saved, far0, near0, grad, weights, *layer0,
            m_table, q_table, c_table, g_table, x_table,
        ],
        4,
        act_ahead,
    )
    grad_mid = shifted(grad_mid, -1)
    near2, far2 = swapped(near2, far2, -1)
    taps0 = run(
        first_taps_kernel, like(tap_count + 1, width, BF16), [],
        [halo0, layer0[0], inner0, gain0, m_table, go_table, t_table],
        0,
    )
    masked1, mean1, inverse1, q1 = run(
        second_early_kernel, (*layer, like(size, width, F32)), [], [notes, saved, weights, q_table], 1, taps0
    )
    m1, factor1, conv1, ahead0 = run(
        functools.partial(second_ready_kernel, two),
        (
            like(size, width, F32), like(small, width, F32), like(own, width, F32),
            like(2 * two + tap_count + 1, width, BF16),
        ),
        [pltpu.VMEM((2 * two, width), BF16), pltpu.VMEM((2, two, width), BF16)],
        [notes, far1, near1, weights, ahead0, masked1, q1, m_table, c_table],
        5,
    )
    ahead0 = shifted(ahead0, 2)
    def partner(x, step):
        return lax.ppermute(x, "tm", [(i, i ^ step) for i in range(shards)])

    mixed1, taps1, taps0 = run(
        second_taps_kernel,
        (like(small, width, BF16), like(tap_count + 1, width, BF16), like(tap_count + 1, width, BF16)),
        [pltpu.VMEM((2, one, width), BF16)],
        [notes, grad_mid, far2, near2, weights, m1, factor1, conv1, taps0, go_table, t_table],
        2,
    )
    grad_out = run(
        second_backward_kernel,
        like(own, width, BF16),
        rows,
        [
            notes, saved, grad_mid, weights, mixed1, q1, mean1, inverse1,
            g_table, x_table,
        ],
        6,
    )
    grad_out = shifted(grad_out, -1)
    steps = [1 << i for i in range(shards.bit_length() - 1)]
    mine = taps0, taps1
    other = partner(taps0, steps[0]), partner(taps1, steps[-1])
    order = list(zip(steps, steps[::-1]))[1:]
    for count, pair in enumerate(order):
        operands = (mine[0], other[0], mine[1], other[1])
        mine = call(add_kernel, (like(*taps0.shape, BF16),) * 2, [], operands, 0 if count else 6)
        other = tuple(partner(x, step) for x, step in zip(mine, pair))
    between = run(
        functools.partial(first_forward_kernel, two),
        like(small, width, BF16),
        [pltpu.VMEM((2 * two, width), BF16), pltpu.VMEM((own, width), BF16)],
        [notes, act_ahead, ahead0, m_table, q_table, c_table],
        10,
        mine[0],
    )
    act_out = run(
        second_forward_kernel,
        like(own, width, BF16),
        [pltpu.VMEM((small, width), BF16)],
        [
            notes, between, ahead1,
            stacked(to_freq(small, span(one, own))), tap_freq(small, tap_count), stacked(from_freq(small, span(0, own))),
        ],
        10,
    )
    slots = kernels.shape[1]
    act_out, grad_out, taps, gains = call(
        final_kernel,
        (
            like(own, width, BF16), like(own, width, BF16),
            jax.ShapeDtypeStruct((tap_count, slots, width), F32), like(slots, width, F32),
        ),
        [
            pltpu.VMEM((tap_count, slots, width), F32), pltpu.VMEM((slots, width), F32),
            pltpu.SemaphoreType.DMA((7,)),
        ],
        (notes, *mine, *other, act_out, grad_out),
        0, [SMEM] + [VMEM] * 4 + [ANY] * 2, (ANY,) * 4,
    )
    return act_out[None], grad_out[None], taps.transpose(1, 0, 2)[None], gains[None]


def solution(mesh):
    in_specs = (
        P("section", "tm", None),
        P("section", "tm", None),
        P("section", None, "tm", None),
        P("section", None, None, None),
        P("section", None, None),
        P(),
        P(),
        P(),
        P(),
    )
    out_specs = (
        P("section", "tm", None),
        P("section", "tm", None),
        P("section", None, None, None),
        P("section", None, None),
    )
    return jax.shard_map(local, mesh=mesh, in_specs=in_specs, out_specs=out_specs, check_vma=False)
```

```python
import functools

import jax
import jax.numpy as jnp
import ml_dtypes
import numpy as np
from jax import lax
from jax.experimental import pallas as pl
from jax.experimental.pallas import tpu as pltpu
from jax.sharding import PartitionSpec as P

epsilon = 1e-05
BLOCK = 2048
LANES = 128
F32 = jnp.float32
BF16 = jnp.bfloat16


def split(matrix):
    high = matrix.astype(ml_dtypes.bfloat16)
    low = (matrix - high.astype(np.float64)).astype(ml_dtypes.bfloat16)
    return high, low


def angles(size, times):
    return 2.0 * np.pi / size * np.outer(np.arange(size // 2) + 0.5, np.asarray(times, np.float64))


def to_freq(size, times):
    phase = angles(size, times)
    return np.concatenate([np.cos(phase), -np.sin(phase)], axis=0)


def from_freq(size, times):
    phase = angles(size, times).T
    return 2.0 / size * np.concatenate([np.cos(phase), -np.sin(phase)], axis=1)


def stacked(matrix):
    return np.concatenate(split(matrix), axis=0)


def beside(matrix):
    return np.concatenate(split(matrix), axis=1)


def tap_freq(size, taps):
    phase = angles(size, np.arange(taps) - (taps - 1) // 2)
    table = np.concatenate([np.cos(phase), np.sin(phase)], axis=0)
    return beside(np.concatenate([table, np.zeros((size, 1))], axis=1))


def dot(a, b):
    return jnp.dot(a, b, preferred_element_type=F32)


def transform(table, values):
    return sum(halves(dot(table[...], values.astype(BF16))))


def rounded_transform(table, values):
    return dot(table[: table.shape[0] // 2], values.astype(BF16))


def halves(values):
    half = values.shape[0] // 2
    return values[:half], values[half:]


def product(a, b):
    ar, ai = halves(a)
    br, bi = halves(b)
    return jnp.concatenate([ar * br - ai * bi, ar * bi + ai * br], axis=0)


def product_conj(a, b):
    ar, ai = halves(a)
    br, bi = halves(b)
    return jnp.concatenate([ar * br + ai * bi, ai * br - ar * bi], axis=0)


def sigmoid(values):
    return 0.5 * jnp.tanh(0.5 * values) + 0.5


def wide(stat, count):
    return jnp.concatenate([stat] * (count // LANES), axis=1)


def norm_rows(ref, start, count, at, gain, first, length, masked_ref, mean_ref, inverse_ref):
    width = masked_ref.shape[1]
    rows = pl.ds(start, count)
    tiles = [pl.ds(i * LANES, LANES) for i in range(width // LANES)]

    def values(tile):
        return ref[rows, tile].astype(F32)

    total = values(tiles[0])
    for tile in tiles[1:]:
        total = total + values(tile)
    mean = jnp.sum(total, axis=1, keepdims=True) * (1.0 / width)
    mean = jnp.broadcast_to(mean, (count, LANES))
    square = jnp.zeros((count, LANES), F32)
    for tile in tiles:
        center = values(tile) - mean
        square = square + center * center
    var = jnp.sum(square, axis=1, keepdims=True) * (1.0 / width)
    inverse = jnp.broadcast_to(lax.rsqrt(var + epsilon), (count, LANES))
    frame = first + at + lax.broadcasted_iota(jnp.int32, (count, LANES), 0)
    mask = ((frame >= 0) & (frame < length)).astype(F32)
    scale = mask * inverse
    out = pl.ds(at, count)
    for tile in tiles:
        masked_ref[out, tile] = ((values(tile) - mean) * scale * gain(tile)).astype(BF16)
    if mean_ref is not None:
        mean_ref[out, :] = mean
        inverse_ref[out, :] = inverse


def norm_pieces(pieces, gain, first, length, masked_ref, mean_ref=None, inverse_ref=None, chunk=128):
    at = 0
    for ref, start, count in pieces:
        for begin in range(0, count, chunk):
            norm_rows(
                ref, start + begin, min(chunk, count - begin), at + begin,
                gain, first, length, masked_ref, mean_ref, inverse_ref,
            )
        at += count


def window(pieces, columns):
    parts = [ref[pl.ds(start, count), columns] for ref, start, count in pieces]
    return parts[0] if len(parts) == 1 else jnp.concatenate(parts, axis=0)


def each_block(width, body):
    for begin in range(0, width, BLOCK):
        body(pl.ds(begin, BLOCK))


def tap_spectrum(table, weights):
    return dot(table, jnp.concatenate([weights, weights], axis=0))


def gate_factor(conv):
    gate = sigmoid(conv)
    return gate * (1.0 + conv * (1.0 - gate))


FIRST, BACK0, BACK1, AHEAD0 = range(0, 8, 2)


def looked_up(notes, layer):
    return notes[layer], notes[layer + 1], notes[FIRST]


def sorted_halos(near, far, at, halos):
    even = lax.rem(lax.axis_index("tm") + 1, 2)
    rows = pl.ds(at, halos.shape[1])
    halos[even] = near[rows, :]
    halos[1 - even] = far[rows, :]
    return halos.at[0], halos.at[1]


def lane_sum(values):
    total = values[:, :LANES]
    for lane in range(LANES, values.shape[1], LANES):
        total = total + values[:, lane : lane + LANES]
    return total


def first_pass(pieces, mean, inverse, gain, mask, tables, mixed, q, columns, scaled, sum_a, sum_b):
    g_table, x_table = tables
    grad_masked = wide(mask, BLOCK) * transform(x_table, product_conj(transform(g_table, mixed), q))
    centered = window(pieces, columns).astype(F32) - wide(mean[...], BLOCK)
    weighted = grad_masked * (centered * wide(inverse[...], BLOCK))
    gain = gain(columns)
    by_gain = grad_masked * gain
    scaled[:, columns] = by_gain
    sum_a[...] += lane_sum(by_gain)
    sum_b[...] += lane_sum(weighted * gain)
    return weighted


def last_pass(grad_pieces, pieces, mean, inverse, scaled, sum_a, sum_b, grad_x, chunk=128):
    width = scaled.shape[1]
    at = 0
    for (ref, start, count), (saved, base, _) in zip(grad_pieces, pieces):
        for begin in range(0, count, chunk):
            here = min(chunk, count - begin)
            rows = pl.ds(at + begin, here)
            inv = inverse[rows, :]
            mean_a = jnp.sum(sum_a[rows, :], axis=1, keepdims=True) * (1.0 / width)
            mean_b = jnp.sum(sum_b[rows, :], axis=1, keepdims=True) * (1.0 / width)
            slope = inv * jnp.broadcast_to(mean_b, (here, LANES)) * inv
            fixed = inv * jnp.broadcast_to(mean_a, (here, LANES)) - slope * mean[rows, :]
            for lane in range(0, width, LANES):
                tile = pl.ds(lane, LANES)
                x = saved[pl.ds(base + begin, here), tile].astype(F32)
                change = inv * scaled[rows, tile] - fixed - slope * x
                grad_x[rows, tile] = (ref[pl.ds(start + begin, here), tile].astype(F32) + change).astype(BF16)
        at += count


def frame_mask(rows, first, length):
    frame = first + lax.broadcasted_iota(jnp.int32, (rows, LANES), 0)
    return ((frame >= 0) & (frame < length)).astype(F32)


def slot_row(weights, slot):
    last = weights.shape[1] - 1
    return lambda columns: weights[slot, last : last + 1, columns].astype(F32)


def prepare_kernel(
    reach, notes, kernels, gains, saved, act, weights, ahead0, ahead1, near, far, masked, mean, inverse
):
    own = act.shape[0]
    for even in range(2):

        @pl.when(lax.rem(lax.axis_index("tm") + 1, 2) == even)
        def _():
            for x, at in ((saved.at[1], 0), (act, reach)):
                tail, head = (near, far) if even else (far, near)
                tail[pl.ds(at, reach), :] = x[pl.ds(own - reach, reach), :]
                head[pl.ds(at, reach), :] = x[pl.ds(0, reach), :]

    count = kernels.shape[0]
    for slot in range(kernels.shape[1]):
        weights[slot, :count, :] = kernels[:, slot, :]
        weights[slot, count:, :] = gains[slot : slot + 1, :]
    ahead0[...] = weights[notes[AHEAD0]]
    ahead1[...] = weights[notes[FIRST + 1]]
    slot, length, first = looked_up(notes, BACK0)
    norm_pieces([(saved.at[0], 0, own)], slot_row(weights, slot), first, length, masked, mean, inverse)


def norm_halo(left, right, own, gain, first, length, halo):
    reach = left.shape[0]
    norm_pieces([(left, 0, reach)], gain, first - reach, length, halo)
    norm_pieces([(right, 0, reach)], gain, first + own, length, halo.at[pl.ds(reach, reach)])


def joined(halo, own, columns):
    reach = halo.shape[0] // 2
    return jnp.concatenate([halo[:reach, columns], own[:, columns], halo[reach:, columns]], axis=0)


def first_backward_kernel(
    reach, notes, saved, far, near, grads, weights, masked, mean, inverse,
    m_table, q_table, c_table, g_table, x_table,
    grad_x, near_edge, far_edge, halo, inner, gain_sum, halos, grad_halos, scaled, sum_a, sum_b,
):
    own, width = grads.shape
    edge = near_edge.shape[0]
    slot, length, first = looked_up(notes, BACK0)
    gain = slot_row(weights, slot)
    left, right = sorted_halos(near, far, 0, halos)
    grad_left, grad_right = sorted_halos(near, far, reach, grad_halos)
    norm_halo(left, right, own, gain, first, length, halo)
    grad_pieces = [(grad_left, 0, edge), (grads, 0, own), (grad_right, 0, edge)]
    pieces = [(saved.at[0], 0, own)]
    mask = frame_mask(own, first, length)
    sum_a[...] = jnp.zeros_like(sum_a)
    sum_b[...] = jnp.zeros_like(sum_b)

    def block(columns):
        m = transform(m_table, joined(halo, masked, columns))
        q = tap_spectrum(q_table[...], weights[slot, :, columns])
        conv = transform(c_table, product(m, q))
        mixed = (window(grad_pieces, columns).astype(F32) * gate_factor(conv)).astype(BF16)
        inner[:, columns] = mixed[edge : edge + own]
        weighted = first_pass(
            pieces, mean, inverse, gain, mask, (g_table, x_table), mixed, q, columns, scaled, sum_a, sum_b
        )
        gain_sum[:, columns] = jnp.sum(weighted, axis=0, keepdims=True)

    each_block(width, block)
    last_pass([(grads, 0, own)], pieces, mean, inverse, scaled, sum_a, sum_b, grad_x)
    for even in range(2):

        @pl.when(lax.rem(lax.axis_index("tm") + 1, 2) == even)
        def _():
            top, bottom = (far_edge, near_edge) if even else (near_edge, far_edge)
            top[...] = grad_x[pl.ds(0, edge), :]
            bottom[...] = grad_x[pl.ds(own - edge, edge), :]


def tap_term(go_table, t_table, m, mixed):
    g_own = dot(go_table[...], jnp.concatenate([mixed, mixed], axis=0))
    return transform(t_table, product_conj(m, g_own))


def put_taps(taps, tap, gain_sum, columns):
    row = lax.broadcasted_iota(jnp.int32, tap.shape, 0)
    taps[:, columns] = jnp.where(row == tap.shape[0] - 1, gain_sum, tap).astype(taps.dtype)


def first_taps_kernel(halo, masked, inner, gain_sum, m_table, go_table, t_table, taps):
    def block(columns):
        m = transform(m_table, joined(halo, masked, columns))
        put_taps(taps, tap_term(go_table, t_table, m, inner[:, columns]), gain_sum[:, columns], columns)

    each_block(masked.shape[1], block)


def added(mine, other):
    return (mine[...].astype(F32) + other[...].astype(F32)).astype(BF16)


def add_kernel(mine0, other0, mine1, other1, out0, out1):
    out0[...] = added(mine0, other0)
    out1[...] = added(mine1, other1)


def second_early_kernel(notes, saved, weights, q_table, masked, mean, inverse, q):
    own = masked.shape[0]
    slot, length, first = looked_up(notes, BACK1)
    norm_pieces([(saved.at[1], 0, own)], slot_row(weights, slot), first, length, masked, mean, inverse)

    def block(columns):
        q[:, columns] = tap_spectrum(q_table[...], weights[slot, :, columns])

    each_block(masked.shape[1], block)


def second_ready_kernel(
    reach, notes, far, near, weights, ahead0, masked, q, m_table, c_table, m_out, factor, conv_out, ahead, halo, halos
):
    left, right = sorted_halos(near, far, reach, halos)
    ahead[pl.ds(0, reach), :] = left[...]
    ahead[pl.ds(reach, reach), :] = right[...]
    ahead[pl.ds(2 * reach, ahead0.shape[0]), :] = ahead0[...]
    own, width = masked.shape
    slot, length, first = looked_up(notes, BACK1)
    left, right = sorted_halos(near, far, 0, halos)
    norm_halo(left, right, own, slot_row(weights, slot), first, length, halo)

    def block(columns):
        m = transform(m_table, joined(halo, masked, columns))
        conv = transform(c_table, product(m, q[:, columns]))
        m_out[:, columns] = m
        factor[:, columns] = gate_factor(conv)
        edge = (conv.shape[0] - own) // 2
        conv_out[:, columns] = conv[edge : edge + own]

    each_block(width, block)


def second_taps_kernel(
    notes, received, far, near, weights, m, factor, conv, taps0, go_table, t_table, mixed_out, taps, taps0_out, halos
):
    taps0_out[...] = taps0[...]
    own, width = conv.shape
    rows = factor.shape[0]
    edge = (rows - own) // 2
    gain = slot_row(weights, notes[BACK1])
    left, right = sorted_halos(near, far, 0, halos)
    pieces = [(left, 0, edge), (received, 0, own), (right, 0, edge)]

    def block(columns):
        mixed = (window(pieces, columns).astype(F32) * factor[:, columns]).astype(BF16)
        mixed_out[:, columns] = mixed
        inner = mixed[edge : edge + own]
        gain_sum = jnp.sum(inner.astype(F32) * conv[:, columns], axis=0, keepdims=True) / gain(columns)
        put_taps(taps, tap_term(go_table, t_table, m[:, columns], inner), gain_sum, columns)

    each_block(width, block)


def second_backward_kernel(
    notes, saved, received, weights, mixed, q, mean, inverse, g_table, x_table, grad_x, scaled, sum_a, sum_b
):
    own, width = grad_x.shape
    slot, length, first = looked_up(notes, BACK1)
    pieces = [(saved.at[1], 0, own)]
    mask = frame_mask(own, first, length)
    sum_a[...] = jnp.zeros_like(sum_a)
    sum_b[...] = jnp.zeros_like(sum_b)

    def block(columns):
        first_pass(
            pieces, mean, inverse, slot_row(weights, slot), mask, (g_table, x_table), mixed[:, columns], q[:, columns],
            columns, scaled, sum_a, sum_b,
        )

    each_block(width, block)
    last_pass([(received, 0, own)], pieces, mean, inverse, scaled, sum_a, sum_b, grad_x)


def row_gain(layer):
    last = layer.shape[0] - 1
    return lambda columns: layer[last : last + 1, columns].astype(F32)


def first_forward_kernel(reach, notes, act, ahead, m_table, q_table, c_table, out, halo, masked):
    own, width = act.shape
    middle = reach // 2
    _, length, first = looked_up(notes, AHEAD0)
    left, right = ahead.at[pl.ds(0, reach)], ahead.at[pl.ds(reach, reach)]
    layer = ahead.at[pl.ds(2 * reach, ahead.shape[0] - 2 * reach)]
    inner = [(left, middle, middle), (act, 0, own), (right, 0, middle)]
    norm_pieces([(act, 0, own)], row_gain(layer), first, length, masked)
    norm_halo(left, right, own, row_gain(layer), first, length, halo)

    def block(columns):
        q = tap_spectrum(q_table[...], layer[:, columns])
        conv = rounded_transform(c_table, product(rounded_transform(m_table, joined(halo, masked, columns)), q))
        out[:, columns] = (window(inner, columns).astype(F32) + conv * sigmoid(conv)).astype(BF16)

    each_block(width, block)


def second_forward_kernel(notes, between, layer, m_table, q_table, c_table, out, masked):
    own, width = out.shape
    rows = between.shape[0]
    edge = (rows - own) // 2
    _, length, first = looked_up(notes, AHEAD0)
    norm_pieces([(between, 0, rows)], row_gain(layer), first - edge, length, masked, chunk=rows // 2)

    def block(columns):
        q = tap_spectrum(q_table[...], layer[:, columns])
        conv = rounded_transform(c_table, product(rounded_transform(m_table, masked[:, columns]), q))
        out[:, columns] = (between[edge : edge + own, columns].astype(F32) + conv * sigmoid(conv)).astype(BF16)

    each_block(width, block)


def pack_kernel(
    reaches, saved, grad, back_lengths, ahead_lengths, back_slots, ahead_slots,
    near, far, notes, back_len, ahead_len, back_slot, ahead_slot, sems,
):
    own = grad.shape[1]
    even = lax.rem(lax.axis_index("tm") + 1, 2)
    copies = []
    at = 0
    for x, reach in zip((saved, grad), reaches):
        for out, tail in ((near, even), (far, 1 - even)):
            start = pl.multiple_of(tail * (own - reach), 16)
            copies.append((x.at[0, pl.ds(start, reach)], out.at[pl.ds(at, reach)]))
        at += reach
    small = [(back_lengths, back_len), (ahead_lengths, ahead_len), (back_slots, back_slot), (ahead_slots, ahead_slot)]
    copies = [pltpu.make_async_copy(a, b, sems.at[k]) for k, (a, b) in enumerate(small + copies)]
    for copy in copies:
        copy.start()
    for copy in copies:
        copy.wait()
    section, sections = lax.axis_index("section"), lax.axis_size("section")
    notes[FIRST] = lax.axis_index("tm") * own
    notes[FIRST + 1] = ahead_slot[1, section]
    notes[BACK0] = back_slot[0, section]
    notes[BACK0 + 1] = back_len[section]
    notes[BACK1] = back_slot[1, section]
    notes[BACK1 + 1] = back_len[lax.rem(section + 1, sections)]
    notes[AHEAD0] = ahead_slot[0, section]
    notes[AHEAD0 + 1] = ahead_len[lax.rem(section + sections - 2, sections)]


def final_kernel(notes, mine0, mine1, other0, other1, act, grad, act_out, grad_out, taps_out, gains_out, taps, gains, sems):
    copies = [
        pltpu.make_async_copy(act, act_out, sems.at[0]),
        pltpu.make_async_copy(grad, grad_out, sems.at[1]),
    ]
    for copy in copies:
        copy.start()
    count, slots, width = taps.shape
    step = width // 4
    for begin in range(0, width, step):
        columns = pl.ds(begin, step)
        pairs = (mine0, other0), (mine1, other1)
        ticks = [a[:, columns].astype(F32) + b[:, columns].astype(F32) for a, b in pairs]
        for slot in range(slots):
            use = [(notes[layer] == slot).astype(F32) for layer in (BACK0, BACK1)]
            both = use[0] * ticks[0] + use[1] * ticks[1]
            taps[:, slot, columns] = both[:count]
            gains[slot : slot + 1, columns] = both[count:]
        for source, target in ((taps.at[:, :, columns], taps_out.at[:, :, columns]),):
            copies.append(pltpu.make_async_copy(source, target, sems.at[len(copies)]))
            copies[-1].start()
    copies.append(pltpu.make_async_copy(gains, gains_out, sems.at[len(copies)]))
    copies[-1].start()
    for copy in copies:
        copy.wait()


def span(reach, own):
    return np.arange(-reach, own + reach)


VMEM = pl.BlockSpec(memory_space=pltpu.VMEM)
SMEM = pl.BlockSpec(memory_space=pltpu.SMEM)
ANY = pl.BlockSpec(memory_space=pl.ANY)
HBM = pl.BlockSpec(memory_space=pltpu.HBM)
LIMIT = 24 * 1024 * 1024
FULL = 127 * 512 * 1024


def call(kernel, outs, scratch, operands, micros, specs=None, out_specs=None, limit=LIMIT, after=()):
    if specs is None:
        specs = [SMEM if x.dtype == jnp.int32 else VMEM for x in operands]
    if after:
        inner, place = kernel, len(operands)
        operands, specs = [*operands, *after], [*specs, *[ANY] * len(after)]

        def kernel(*refs):
            return inner(*refs[:place], *refs[place + len(after) :])

    return pl.pallas_call(
        kernel,
        out_shape=outs,
        in_specs=specs,
        out_specs=jax.tree.map(lambda _: VMEM, outs) if out_specs is None else out_specs,
        scratch_shapes=scratch,
        compiler_params=pltpu.CompilerParams(vmem_limit_bytes=limit),
        cost_estimate=pl.CostEstimate(flops=int(micros * 1e9), bytes_accessed=0, transcendentals=0),
    )(*operands)


def like(rows, width, dtype):
    return jax.ShapeDtypeStruct((rows, width), dtype)


def up16(count):
    return -(-count // 16) * 16


def local(
    act_in, grad_in, saved_inputs, kernels, norm_gains,
    forward_lengths, backward_lengths, forward_slots, backward_slots,
):
    sections = lax.axis_size("section")
    shards = lax.axis_size("tm")
    act, grad, saved = act_in[0], grad_in[0], saved_inputs[0]
    own, width = act.shape
    tap_count = kernels.shape[2]
    half = (tap_count - 1) // 2
    one, two = up16(half), up16(2 * half)
    size, small = own + 2 * two, own + 2 * one

    def shifted(x, by):
        return lax.ppermute(x, "section", [(i, (i + by) % sections) for i in range(sections)])

    def swapped(near, far, by=0):
        results = []
        for x, begin in ((far, 1), (near, 0)):
            pairs = [(i, i + 1) for i in range(begin, shards - 1, 2)]
            pairs = [
                (s * shards + i, (s + by) % sections * shards + j)
                for s in range(sections)
                for a, b in pairs
                for i, j in ((a, b), (b, a))
            ]
            results.append(lax.ppermute(x, ("section", "tm"), pairs))
        return results[::-1]

    act_ahead = shifted(act, 2)
    lengths = pltpu.SMEM(backward_lengths.shape, jnp.int32)
    forward_slots, backward_slots = forward_slots.T, backward_slots.T
    slots = pltpu.SMEM(backward_slots.shape, jnp.int32)
    near0, far0, notes = call(
        functools.partial(pack_kernel, (two, one)),
        (like(two + one, width, BF16), like(two + one, width, BF16), jax.ShapeDtypeStruct((8,), jnp.int32)),
        [lengths, lengths, slots, slots, pltpu.SemaphoreType.DMA((8,))],
        (saved, grad_in, backward_lengths, forward_lengths, backward_slots, forward_slots),
        0, [HBM] * 6, (VMEM, VMEM, SMEM), FULL,
    )
    near0, far0 = swapped(near0, far0)
    tap_back = np.concatenate([from_freq(size, np.arange(tap_count) - half), np.zeros((1, size))], axis=0)
    m_table = stacked(to_freq(size, span(two, own)))
    q_table = tap_freq(size, tap_count)
    c_table = stacked(from_freq(size, span(one, own)))
    go_table = beside(to_freq(size, np.arange(own)))
    t_table = stacked(tap_back)

    def run(kernel, outs, scratch, operands, micros=0, *after):
        return call(kernel, outs, scratch, [jnp.asarray(x) for x in operands], micros, after=after)

    rows = [pltpu.VMEM((own, width), F32)] + [pltpu.VMEM((own, LANES), F32)] * 2
    layer = like(own, width, BF16), like(own, LANES, F32), like(own, LANES, F32)
    weights, ahead0, ahead1, near1, far1, *layer0 = run(
        functools.partial(prepare_kernel, two),
        (
            jax.ShapeDtypeStruct((kernels.shape[1], tap_count + 1, width), BF16), like(tap_count + 1, width, BF16),
            like(tap_count + 1, width, BF16), like(2 * two, width, BF16), like(2 * two, width, BF16), *layer,
        ),
        [],
        [notes, kernels[0].transpose(1, 0, 2), norm_gains[0], saved, act],
        0,
    )
    near1, far1 = swapped(near1, far1)
    ahead1 = shifted(ahead1, 1)
    g_table, x_table = stacked(to_freq(size, span(one, own))), stacked(from_freq(size, span(0, own)))
    grad_mid, near2, far2, halo0, inner0, gain0 = run(
        functools.partial(first_backward_kernel, two),
        (
            like(own, width, BF16), like(one, width, BF16), like(one, width, BF16),
            like(2 * two, width, BF16), like(own, width, BF16), like(1, width, F32),
        ),
        [pltpu.VMEM((2, two, width), BF16), pltpu.VMEM((2, one, width), BF16), *rows],
        [
            notes, saved, far0, near0, grad, weights, *layer0,
            m_table, q_table, c_table, g_table, x_table,
        ],
        4,
        act_ahead,
    )
    grad_mid = shifted(grad_mid, -1)
    near2, far2 = swapped(near2, far2, -1)
    taps0 = run(
        first_taps_kernel, like(tap_count + 1, width, BF16), [],
        [halo0, layer0[0], inner0, gain0, m_table, go_table, t_table],
        0,
    )
    masked1, mean1, inverse1, q1 = run(
        second_early_kernel, (*layer, like(size, width, F32)), [], [notes, saved, weights, q_table], 1, taps0
    )
    m1, factor1, conv1, ahead0 = run(
        functools.partial(second_ready_kernel, two),
        (
            like(size, width, F32), like(small, width, F32), like(own, width, F32),
            like(2 * two + tap_count + 1, width, BF16),
        ),
        [pltpu.VMEM((2 * two, width), BF16), pltpu.VMEM((2, two, width), BF16)],
        [notes, far1, near1, weights, ahead0, masked1, q1, m_table, c_table],
        5,
    )
    ahead0 = shifted(ahead0, 2)
    def partner(x, step):
        return lax.ppermute(x, "tm", [(i, i ^ step) for i in range(shards)])

    mixed1, taps1, taps0 = run(
        second_taps_kernel,
        (like(small, width, BF16), like(tap_count + 1, width, BF16), like(tap_count + 1, width, BF16)),
        [pltpu.VMEM((2, one, width), BF16)],
        [notes, grad_mid, far2, near2, weights, m1, factor1, conv1, taps0, go_table, t_table],
        2,
    )
    grad_out = run(
        second_backward_kernel,
        like(own, width, BF16),
        rows,
        [
            notes, saved, grad_mid, weights, mixed1, q1, mean1, inverse1,
            g_table, x_table,
        ],
        6,
    )
    grad_out = shifted(grad_out, -1)
    steps = [1 << i for i in range(shards.bit_length() - 1)]
    mine = taps0, taps1
    other = partner(taps0, steps[0]), partner(taps1, steps[-1])
    order = list(zip(steps, steps[::-1]))[1:]
    for count, pair in enumerate(order):
        operands = (mine[0], other[0], mine[1], other[1])
        mine = call(add_kernel, (like(*taps0.shape, BF16),) * 2, [], operands, 0 if count else 6)
        other = tuple(partner(x, step) for x, step in zip(mine, pair))
    between = run(
        functools.partial(first_forward_kernel, two),
        like(small, width, BF16),
        [pltpu.VMEM((2 * two, width), BF16), pltpu.VMEM((own, width), BF16)],
        [notes, act_ahead, ahead0, m_table, q_table, c_table],
        10,
        mine[0],
    )
    act_out = run(
        second_forward_kernel,
        like(own, width, BF16),
        [pltpu.VMEM((small, width), BF16)],
        [
            notes, between, ahead1,
            stacked(to_freq(small, span(one, own))), tap_freq(small, tap_count), stacked(from_freq(small, span(0, own))),
        ],
        10,
    )
    slots = kernels.shape[1]
    act_out, grad_out, taps, gains = call(
        final_kernel,
        (
            like(own, width, BF16), like(own, width, BF16),
            jax.ShapeDtypeStruct((tap_count, slots, width), F32), like(slots, width, F32),
        ),
        [
            pltpu.VMEM((tap_count, slots, width), F32), pltpu.VMEM((slots, width), F32),
            pltpu.SemaphoreType.DMA((7,)),
        ],
        (notes, *mine, *other, act_out, grad_out),
        0, [SMEM] + [VMEM] * 4 + [ANY] * 2, (ANY,) * 4,
    )
    return act_out[None], grad_out[None], taps.transpose(1, 0, 2)[None], gains[None]


def solution(mesh):
    in_specs = (
        P("section", "tm", None),
        P("section", "tm", None),
        P("section", None, "tm", None),
        P("section", None, None, None),
        P("section", None, None),
        P(),
        P(),
        P(),
        P(),
    )
    out_specs = (
        P("section", "tm", None),
        P("section", "tm", None),
        P("section", None, None, None),
        P("section", None, None),
    )
    return jax.shard_map(local, mesh=mesh, in_specs=in_specs, out_specs=out_specs, check_vma=False)
```

```python
import functools

import jax
import jax.numpy as jnp
import ml_dtypes
import numpy as np
from jax import lax
from jax.experimental import pallas as pl
from jax.experimental.pallas import tpu as pltpu
from jax.sharding import PartitionSpec as P

epsilon = 1e-05
BLOCK = 2048
LANES = 128
F32 = jnp.float32
BF16 = jnp.bfloat16


def split(matrix):
    high = matrix.astype(ml_dtypes.bfloat16)
    low = (matrix - high.astype(np.float64)).astype(ml_dtypes.bfloat16)
    return high, low


def angles(size, times):
    return 2.0 * np.pi / size * np.outer(np.arange(size // 2) + 0.5, np.asarray(times, np.float64))


def to_freq(size, times):
    phase = angles(size, times)
    return np.concatenate([np.cos(phase), -np.sin(phase)], axis=0)


def from_freq(size, times):
    phase = angles(size, times).T
    return 2.0 / size * np.concatenate([np.cos(phase), -np.sin(phase)], axis=1)


def stacked(matrix):
    return np.concatenate(split(matrix), axis=0)


def beside(matrix):
    return np.concatenate(split(matrix), axis=1)


def tap_freq(size, taps):
    phase = angles(size, np.arange(taps) - (taps - 1) // 2)
    table = np.concatenate([np.cos(phase), np.sin(phase)], axis=0)
    return beside(np.concatenate([table, np.zeros((size, 1))], axis=1))


def dot(a, b):
    return jnp.dot(a, b, preferred_element_type=F32)


def transform(table, values):
    return sum(halves(dot(table[...], values.astype(BF16))))


def rounded_transform(table, values):
    return dot(table[: table.shape[0] // 2], values.astype(BF16))


def halves(values):
    half = values.shape[0] // 2
    return values[:half], values[half:]


def product(a, b):
    ar, ai = halves(a)
    br, bi = halves(b)
    return jnp.concatenate([ar * br - ai * bi, ar * bi + ai * br], axis=0)


def product_conj(a, b):
    ar, ai = halves(a)
    br, bi = halves(b)
    return jnp.concatenate([ar * br + ai * bi, ai * br - ar * bi], axis=0)


def sigmoid(values):
    return 0.5 * jnp.tanh(0.5 * values) + 0.5


def wide(stat, count):
    return jnp.concatenate([stat] * (count // LANES), axis=1)


def norm_rows(ref, start, count, at, gain, first, length, masked_ref, mean_ref, inverse_ref):
    width = masked_ref.shape[1]
    rows = pl.ds(start, count)
    tiles = [pl.ds(i * LANES, LANES) for i in range(width // LANES)]

    def values(tile):
        return ref[rows, tile].astype(F32)

    total = values(tiles[0])
    for tile in tiles[1:]:
        total = total + values(tile)
    mean = jnp.sum(total, axis=1, keepdims=True) * (1.0 / width)
    mean = jnp.broadcast_to(mean, (count, LANES))
    square = jnp.zeros((count, LANES), F32)
    for tile in tiles:
        center = values(tile) - mean
        square = square + center * center
    var = jnp.sum(square, axis=1, keepdims=True) * (1.0 / width)
    inverse = jnp.broadcast_to(lax.rsqrt(var + epsilon), (count, LANES))
    frame = first + at + lax.broadcasted_iota(jnp.int32, (count, LANES), 0)
    mask = ((frame >= 0) & (frame < length)).astype(F32)
    scale = mask * inverse
    out = pl.ds(at, count)
    for tile in tiles:
        masked_ref[out, tile] = ((values(tile) - mean) * scale * gain(tile)).astype(BF16)
    if mean_ref is not None:
        mean_ref[out, :] = mean
        inverse_ref[out, :] = inverse


def norm_pieces(pieces, gain, first, length, masked_ref, mean_ref=None, inverse_ref=None, chunk=128):
    at = 0
    for ref, start, count in pieces:
        for begin in range(0, count, chunk):
            norm_rows(
                ref, start + begin, min(chunk, count - begin), at + begin,
                gain, first, length, masked_ref, mean_ref, inverse_ref,
            )
        at += count


def window(pieces, columns):
    parts = [ref[pl.ds(start, count), columns] for ref, start, count in pieces]
    return parts[0] if len(parts) == 1 else jnp.concatenate(parts, axis=0)


def each_block(width, body):
    for begin in range(0, width, BLOCK):
        body(pl.ds(begin, BLOCK))


def tap_spectrum(table, weights):
    return dot(table, jnp.concatenate([weights, weights], axis=0))


def gate_factor(conv):
    gate = sigmoid(conv)
    return gate * (1.0 + conv * (1.0 - gate))


FIRST, BACK0, BACK1, AHEAD0 = range(0, 8, 2)


def looked_up(notes, layer):
    return notes[layer], notes[layer + 1], notes[FIRST]


def sorted_halos(near, far, at, halos):
    even = lax.rem(lax.axis_index("tm") + 1, 2)
    rows = pl.ds(at, halos.shape[1])
    halos[even] = near[rows, :]
    halos[1 - even] = far[rows, :]
    return halos.at[0], halos.at[1]


def lane_sum(values):
    total = values[:, :LANES]
    for lane in range(LANES, values.shape[1], LANES):
        total = total + values[:, lane : lane + LANES]
    return total


def first_pass(pieces, mean, inverse, gain, mask, tables, mixed, q, columns, scaled, sum_a, sum_b):
    g_table, x_table = tables
    grad_masked = wide(mask, BLOCK) * rounded_transform(x_table, product_conj(transform(g_table, mixed), q))
    centered = window(pieces, columns).astype(F32) - wide(mean[...], BLOCK)
    weighted = grad_masked * (centered * wide(inverse[...], BLOCK))
    gain = gain(columns)
    by_gain = grad_masked * gain
    scaled[:, columns] = by_gain
    sum_a[...] += lane_sum(by_gain)
    sum_b[...] += lane_sum(weighted * gain)
    return weighted


def last_pass(grad_pieces, pieces, mean, inverse, scaled, sum_a, sum_b, grad_x, chunk=128):
    width = scaled.shape[1]
    at = 0
    for (ref, start, count), (saved, base, _) in zip(grad_pieces, pieces):
        for begin in range(0, count, chunk):
            here = min(chunk, count - begin)
            rows = pl.ds(at + begin, here)
            inv = inverse[rows, :]
            mean_a = jnp.sum(sum_a[rows, :], axis=1, keepdims=True) * (1.0 / width)
            mean_b = jnp.sum(sum_b[rows, :], axis=1, keepdims=True) * (1.0 / width)
            slope = inv * jnp.broadcast_to(mean_b, (here, LANES)) * inv
            fixed = inv * jnp.broadcast_to(mean_a, (here, LANES)) - slope * mean[rows, :]
            for lane in range(0, width, LANES):
                tile = pl.ds(lane, LANES)
                x = saved[pl.ds(base + begin, here), tile].astype(F32)
                change = inv * scaled[rows, tile] - fixed - slope * x
                grad_x[rows, tile] = (ref[pl.ds(start + begin, here), tile].astype(F32) + change).astype(BF16)
        at += count


def frame_mask(rows, first, length):
    frame = first + lax.broadcasted_iota(jnp.int32, (rows, LANES), 0)
    return ((frame >= 0) & (frame < length)).astype(F32)


def slot_row(weights, slot):
    last = weights.shape[1] - 1
    return lambda columns: weights[slot, last : last + 1, columns].astype(F32)


def prepare_kernel(
    reach, notes, kernels, gains, saved, act, weights, ahead0, ahead1, near, far, masked, mean, inverse
):
    own = act.shape[0]
    for even in range(2):

        @pl.when(lax.rem(lax.axis_index("tm") + 1, 2) == even)
        def _():
            for x, at in ((saved.at[1], 0), (act, reach)):
                tail, head = (near, far) if even else (far, near)
                tail[pl.ds(at, reach), :] = x[pl.ds(own - reach, reach), :]
                head[pl.ds(at, reach), :] = x[pl.ds(0, reach), :]

    count = kernels.shape[0]
    for slot in range(kernels.shape[1]):
        weights[slot, :count, :] = kernels[:, slot, :]
        weights[slot, count:, :] = gains[slot : slot + 1, :]
    ahead0[...] = weights[notes[AHEAD0]]
    ahead1[...] = weights[notes[FIRST + 1]]
    slot, length, first = looked_up(notes, BACK0)
    norm_pieces([(saved.at[0], 0, own)], slot_row(weights, slot), first, length, masked, mean, inverse)


def norm_halo(left, right, own, gain, first, length, halo):
    reach = left.shape[0]
    norm_pieces([(left, 0, reach)], gain, first - reach, length, halo)
    norm_pieces([(right, 0, reach)], gain, first + own, length, halo.at[pl.ds(reach, reach)])


def joined(halo, own, columns):
    reach = halo.shape[0] // 2
    return jnp.concatenate([halo[:reach, columns], own[:, columns], halo[reach:, columns]], axis=0)


def first_backward_kernel(
    reach, notes, saved, far, near, grads, weights, masked, mean, inverse,
    m_table, q_table, c_table, g_table, x_table,
    grad_x, near_edge, far_edge, halo, inner, gain_sum, halos, grad_halos, scaled, sum_a, sum_b,
):
    own, width = grads.shape
    edge = near_edge.shape[0]
    slot, length, first = looked_up(notes, BACK0)
    gain = slot_row(weights, slot)
    left, right = sorted_halos(near, far, 0, halos)
    grad_left, grad_right = sorted_halos(near, far, reach, grad_halos)
    norm_halo(left, right, own, gain, first, length, halo)
    grad_pieces = [(grad_left, 0, edge), (grads, 0, own), (grad_right, 0, edge)]
    pieces = [(saved.at[0], 0, own)]
    mask = frame_mask(own, first, length)
    sum_a[...] = jnp.zeros_like(sum_a)
    sum_b[...] = jnp.zeros_like(sum_b)

    def block(columns):
        m = transform(m_table, joined(halo, masked, columns))
        q = tap_spectrum(q_table[...], weights[slot, :, columns])
        conv = transform(c_table, product(m, q))
        mixed = (window(grad_pieces, columns).astype(F32) * gate_factor(conv)).astype(BF16)
        inner[:, columns] = mixed[edge : edge + own]
        weighted = first_pass(
            pieces, mean, inverse, gain, mask, (g_table, x_table), mixed, q, columns, scaled, sum_a, sum_b
        )
        gain_sum[:, columns] = jnp.sum(weighted, axis=0, keepdims=True)

    each_block(width, block)
    last_pass([(grads, 0, own)], pieces, mean, inverse, scaled, sum_a, sum_b, grad_x)
    for even in range(2):

        @pl.when(lax.rem(lax.axis_index("tm") + 1, 2) == even)
        def _():
            top, bottom = (far_edge, near_edge) if even else (near_edge, far_edge)
            top[...] = grad_x[pl.ds(0, edge), :]
            bottom[...] = grad_x[pl.ds(own - edge, edge), :]


def tap_term(go_table, t_table, m, mixed):
    g_own = dot(go_table[...], jnp.concatenate([mixed, mixed], axis=0))
    return transform(t_table, product_conj(m, g_own))


def put_taps(taps, tap, gain_sum, columns):
    row = lax.broadcasted_iota(jnp.int32, tap.shape, 0)
    taps[:, columns] = jnp.where(row == tap.shape[0] - 1, gain_sum, tap).astype(taps.dtype)


def first_taps_kernel(halo, masked, inner, gain_sum, m_table, go_table, t_table, taps):
    def block(columns):
        m = transform(m_table, joined(halo, masked, columns))
        put_taps(taps, tap_term(go_table, t_table, m, inner[:, columns]), gain_sum[:, columns], columns)

    each_block(masked.shape[1], block)


def added(mine, other):
    return (mine[...].astype(F32) + other[...].astype(F32)).astype(BF16)


def add_kernel(mine0, other0, mine1, other1, out0, out1):
    out0[...] = added(mine0, other0)
    out1[...] = added(mine1, other1)


def second_early_kernel(notes, saved, weights, q_table, masked, mean, inverse, q):
    own = masked.shape[0]
    slot, length, first = looked_up(notes, BACK1)
    norm_pieces([(saved.at[1], 0, own)], slot_row(weights, slot), first, length, masked, mean, inverse)

    def block(columns):
        q[:, columns] = tap_spectrum(q_table[...], weights[slot, :, columns])

    each_block(masked.shape[1], block)


def second_ready_kernel(
    reach, notes, far, near, weights, ahead0, masked, q, m_table, c_table, m_out, factor, conv_out, ahead, halo, halos
):
    left, right = sorted_halos(near, far, reach, halos)
    ahead[pl.ds(0, reach), :] = left[...]
    ahead[pl.ds(reach, reach), :] = right[...]
    ahead[pl.ds(2 * reach, ahead0.shape[0]), :] = ahead0[...]
    own, width = masked.shape
    slot, length, first = looked_up(notes, BACK1)
    left, right = sorted_halos(near, far, 0, halos)
    norm_halo(left, right, own, slot_row(weights, slot), first, length, halo)

    def block(columns):
        m = transform(m_table, joined(halo, masked, columns))
        conv = transform(c_table, product(m, q[:, columns]))
        m_out[:, columns] = m
        factor[:, columns] = gate_factor(conv)
        edge = (conv.shape[0] - own) // 2
        conv_out[:, columns] = conv[edge : edge + own]

    each_block(width, block)


def second_taps_kernel(
    notes, received, far, near, weights, m, factor, conv, taps0, go_table, t_table, mixed_out, taps, taps0_out, halos
):
    taps0_out[...] = taps0[...]
    own, width = conv.shape
    rows = factor.shape[0]
    edge = (rows - own) // 2
    gain = slot_row(weights, notes[BACK1])
    left, right = sorted_halos(near, far, 0, halos)
    pieces = [(left, 0, edge), (received, 0, own), (right, 0, edge)]

    def block(columns):
        mixed = (window(pieces, columns).astype(F32) * factor[:, columns]).astype(BF16)
        mixed_out[:, columns] = mixed
        inner = mixed[edge : edge + own]
        gain_sum = jnp.sum(inner.astype(F32) * conv[:, columns], axis=0, keepdims=True) / gain(columns)
        put_taps(taps, tap_term(go_table, t_table, m[:, columns], inner), gain_sum, columns)

    each_block(width, block)


def second_backward_kernel(
    notes, saved, received, weights, mixed, q, mean, inverse, g_table, x_table, grad_x, scaled, sum_a, sum_b
):
    own, width = grad_x.shape
    slot, length, first = looked_up(notes, BACK1)
    pieces = [(saved.at[1], 0, own)]
    mask = frame_mask(own, first, length)
    sum_a[...] = jnp.zeros_like(sum_a)
    sum_b[...] = jnp.zeros_like(sum_b)

    def block(columns):
        first_pass(
            pieces, mean, inverse, slot_row(weights, slot), mask, (g_table, x_table), mixed[:, columns], q[:, columns],
            columns, scaled, sum_a, sum_b,
        )

    each_block(width, block)
    last_pass([(received, 0, own)], pieces, mean, inverse, scaled, sum_a, sum_b, grad_x)


def row_gain(layer):
    last = layer.shape[0] - 1
    return lambda columns: layer[last : last + 1, columns].astype(F32)


def first_forward_kernel(reach, notes, act, ahead, m_table, q_table, c_table, out, halo, masked):
    own, width = act.shape
    middle = reach // 2
    _, length, first = looked_up(notes, AHEAD0)
    left, right = ahead.at[pl.ds(0, reach)], ahead.at[pl.ds(reach, reach)]
    layer = ahead.at[pl.ds(2 * reach, ahead.shape[0] - 2 * reach)]
    inner = [(left, middle, middle), (act, 0, own), (right, 0, middle)]
    norm_pieces([(act, 0, own)], row_gain(layer), first, length, masked)
    norm_halo(left, right, own, row_gain(layer), first, length, halo)

    def block(columns):
        q = tap_spectrum(q_table[...], layer[:, columns])
        conv = rounded_transform(c_table, product(rounded_transform(m_table, joined(halo, masked, columns)), q))
        out[:, columns] = (window(inner, columns).astype(F32) + conv * sigmoid(conv)).astype(BF16)

    each_block(width, block)


def second_forward_kernel(notes, between, layer, m_table, q_table, c_table, out, masked):
    own, width = out.shape
    rows = between.shape[0]
    edge = (rows - own) // 2
    _, length, first = looked_up(notes, AHEAD0)
    norm_pieces([(between, 0, rows)], row_gain(layer), first - edge, length, masked, chunk=rows // 2)

    def block(columns):
        q = tap_spectrum(q_table[...], layer[:, columns])
        conv = rounded_transform(c_table, product(rounded_transform(m_table, masked[:, columns]), q))
        out[:, columns] = (between[edge : edge + own, columns].astype(F32) + conv * sigmoid(conv)).astype(BF16)

    each_block(width, block)


def pack_kernel(
    reaches, saved, grad, back_lengths, ahead_lengths, back_slots, ahead_slots,
    near, far, notes, back_len, ahead_len, back_slot, ahead_slot, sems,
):
    own = grad.shape[1]
    even = lax.rem(lax.axis_index("tm") + 1, 2)
    copies = []
    at = 0
    for x, reach in zip((saved, grad), reaches):
        for out, tail in ((near, even), (far, 1 - even)):
            start = pl.multiple_of(tail * (own - reach), 16)
            copies.append((x.at[0, pl.ds(start, reach)], out.at[pl.ds(at, reach)]))
        at += reach
    small = [(back_lengths, back_len), (ahead_lengths, ahead_len), (back_slots, back_slot), (ahead_slots, ahead_slot)]
    copies = [pltpu.make_async_copy(a, b, sems.at[k]) for k, (a, b) in enumerate(small + copies)]
    for copy in copies:
        copy.start()
    for copy in copies:
        copy.wait()
    section, sections = lax.axis_index("section"), lax.axis_size("section")
    notes[FIRST] = lax.axis_index("tm") * own
    notes[FIRST + 1] = ahead_slot[1, section]
    notes[BACK0] = back_slot[0, section]
    notes[BACK0 + 1] = back_len[section]
    notes[BACK1] = back_slot[1, section]
    notes[BACK1 + 1] = back_len[lax.rem(section + 1, sections)]
    notes[AHEAD0] = ahead_slot[0, section]
    notes[AHEAD0 + 1] = ahead_len[lax.rem(section + sections - 2, sections)]


def final_kernel(notes, mine0, mine1, other0, other1, act, grad, act_out, grad_out, taps_out, gains_out, taps, gains, sems):
    copies = [
        pltpu.make_async_copy(act, act_out, sems.at[0]),
        pltpu.make_async_copy(grad, grad_out, sems.at[1]),
    ]
    for copy in copies:
        copy.start()
    count, slots, width = taps.shape
    step = width // 4
    for begin in range(0, width, step):
        columns = pl.ds(begin, step)
        pairs = (mine0, other0), (mine1, other1)
        ticks = [a[:, columns].astype(F32) + b[:, columns].astype(F32) for a, b in pairs]
        for slot in range(slots):
            use = [(notes[layer] == slot).astype(F32) for layer in (BACK0, BACK1)]
            both = use[0] * ticks[0] + use[1] * ticks[1]
            taps[:, slot, columns] = both[:count]
            gains[slot : slot + 1, columns] = both[count:]
        for source, target in ((taps.at[:, :, columns], taps_out.at[:, :, columns]),):
            copies.append(pltpu.make_async_copy(source, target, sems.at[len(copies)]))
            copies[-1].start()
    copies.append(pltpu.make_async_copy(gains, gains_out, sems.at[len(copies)]))
    copies[-1].start()
    for copy in copies:
        copy.wait()


def span(reach, own):
    return np.arange(-reach, own + reach)


VMEM = pl.BlockSpec(memory_space=pltpu.VMEM)
SMEM = pl.BlockSpec(memory_space=pltpu.SMEM)
ANY = pl.BlockSpec(memory_space=pl.ANY)
HBM = pl.BlockSpec(memory_space=pltpu.HBM)
LIMIT = 24 * 1024 * 1024
FULL = 127 * 512 * 1024


def call(kernel, outs, scratch, operands, micros, specs=None, out_specs=None, limit=LIMIT, after=()):
    if specs is None:
        specs = [SMEM if x.dtype == jnp.int32 else VMEM for x in operands]
    if after:
        inner, place = kernel, len(operands)
        operands, specs = [*operands, *after], [*specs, *[ANY] * len(after)]

        def kernel(*refs):
            return inner(*refs[:place], *refs[place + len(after) :])

    return pl.pallas_call(
        kernel,
        out_shape=outs,
        in_specs=specs,
        out_specs=jax.tree.map(lambda _: VMEM, outs) if out_specs is None else out_specs,
        scratch_shapes=scratch,
        compiler_params=pltpu.CompilerParams(vmem_limit_bytes=limit),
        cost_estimate=pl.CostEstimate(flops=int(micros * 1e9), bytes_accessed=0, transcendentals=0),
    )(*operands)


def like(rows, width, dtype):
    return jax.ShapeDtypeStruct((rows, width), dtype)


def up16(count):
    return -(-count // 16) * 16


def local(
    act_in, grad_in, saved_inputs, kernels, norm_gains,
    forward_lengths, backward_lengths, forward_slots, backward_slots,
):
    sections = lax.axis_size("section")
    shards = lax.axis_size("tm")
    act, grad, saved = act_in[0], grad_in[0], saved_inputs[0]
    own, width = act.shape
    tap_count = kernels.shape[2]
    half = (tap_count - 1) // 2
    one, two = up16(half), up16(2 * half)
    size, small = own + 2 * two, own + 2 * one

    def shifted(x, by):
        return lax.ppermute(x, "section", [(i, (i + by) % sections) for i in range(sections)])

    def swapped(near, far, by=0):
        results = []
        for x, begin in ((far, 1), (near, 0)):
            pairs = [(i, i + 1) for i in range(begin, shards - 1, 2)]
            pairs = [
                (s * shards + i, (s + by) % sections * shards + j)
                for s in range(sections)
                for a, b in pairs
                for i, j in ((a, b), (b, a))
            ]
            results.append(lax.ppermute(x, ("section", "tm"), pairs))
        return results[::-1]

    act_ahead = shifted(act, 2)
    lengths = pltpu.SMEM(backward_lengths.shape, jnp.int32)
    forward_slots, backward_slots = forward_slots.T, backward_slots.T
    slots = pltpu.SMEM(backward_slots.shape, jnp.int32)
    near0, far0, notes = call(
        functools.partial(pack_kernel, (two, one)),
        (like(two + one, width, BF16), like(two + one, width, BF16), jax.ShapeDtypeStruct((8,), jnp.int32)),
        [lengths, lengths, slots, slots, pltpu.SemaphoreType.DMA((8,))],
        (saved, grad_in, backward_lengths, forward_lengths, backward_slots, forward_slots),
        0, [HBM] * 6, (VMEM, VMEM, SMEM), FULL,
    )
    near0, far0 = swapped(near0, far0)
    tap_back = np.concatenate([from_freq(size, np.arange(tap_count) - half), np.zeros((1, size))], axis=0)
    m_table = stacked(to_freq(size, span(two, own)))
    q_table = tap_freq(size, tap_count)
    c_table = stacked(from_freq(size, span(one, own)))
    go_table = beside(to_freq(size, np.arange(own)))
    t_table = stacked(tap_back)

    def run(kernel, outs, scratch, operands, micros=0, *after):
        return call(kernel, outs, scratch, [jnp.asarray(x) for x in operands], micros, after=after)

    rows = [pltpu.VMEM((own, width), F32)] + [pltpu.VMEM((own, LANES), F32)] * 2
    layer = like(own, width, BF16), like(own, LANES, F32), like(own, LANES, F32)
    weights, ahead0, ahead1, near1, far1, *layer0 = run(
        functools.partial(prepare_kernel, two),
        (
            jax.ShapeDtypeStruct((kernels.shape[1], tap_count + 1, width), BF16), like(tap_count + 1, width, BF16),
            like(tap_count + 1, width, BF16), like(2 * two, width, BF16), like(2 * two, width, BF16), *layer,
        ),
        [],
        [notes, kernels[0].transpose(1, 0, 2), norm_gains[0], saved, act],
        0,
    )
    near1, far1 = swapped(near1, far1)
    ahead1 = shifted(ahead1, 1)
    g_table, x_table = stacked(to_freq(size, span(one, own))), stacked(from_freq(size, span(0, own)))
    grad_mid, near2, far2, halo0, inner0, gain0 = run(
        functools.partial(first_backward_kernel, two),
        (
            like(own, width, BF16), like(one, width, BF16), like(one, width, BF16),
            like(2 * two, width, BF16), like(own, width, BF16), like(1, width, F32),
        ),
        [pltpu.VMEM((2, two, width), BF16), pltpu.VMEM((2, one, width), BF16), *rows],
        [
            notes, saved, far0, near0, grad, weights, *layer0,
            m_table, q_table, c_table, g_table, x_table,
        ],
        4,
        act_ahead,
    )
    grad_mid = shifted(grad_mid, -1)
    near2, far2 = swapped(near2, far2, -1)
    taps0 = run(
        first_taps_kernel, like(tap_count + 1, width, BF16), [],
        [halo0, layer0[0], inner0, gain0, m_table, go_table, t_table],
        0,
    )
    masked1, mean1, inverse1, q1 = run(
        second_early_kernel, (*layer, like(size, width, F32)), [], [notes, saved, weights, q_table], 1, taps0
    )
    m1, factor1, conv1, ahead0 = run(
        functools.partial(second_ready_kernel, two),
        (
            like(size, width, F32), like(small, width, F32), like(own, width, F32),
            like(2 * two + tap_count + 1, width, BF16),
        ),
        [pltpu.VMEM((2 * two, width), BF16), pltpu.VMEM((2, two, width), BF16)],
        [notes, far1, near1, weights, ahead0, masked1, q1, m_table, c_table],
        5,
    )
    ahead0 = shifted(ahead0, 2)
    def partner(x, step):
        return lax.ppermute(x, "tm", [(i, i ^ step) for i in range(shards)])

    mixed1, taps1, taps0 = run(
        second_taps_kernel,
        (like(small, width, BF16), like(tap_count + 1, width, BF16), like(tap_count + 1, width, BF16)),
        [pltpu.VMEM((2, one, width), BF16)],
        [notes, grad_mid, far2, near2, weights, m1, factor1, conv1, taps0, go_table, t_table],
        2,
    )
    grad_out = run(
        second_backward_kernel,
        like(own, width, BF16),
        rows,
        [
            notes, saved, grad_mid, weights, mixed1, q1, mean1, inverse1,
            g_table, x_table,
        ],
        6,
    )
    grad_out = shifted(grad_out, -1)
    steps = [1 << i for i in range(shards.bit_length() - 1)]
    mine = taps0, taps1
    other = partner(taps0, steps[0]), partner(taps1, steps[-1])
    order = list(zip(steps, steps[::-1]))[1:]
    for count, pair in enumerate(order):
        operands = (mine[0], other[0], mine[1], other[1])
        mine = call(add_kernel, (like(*taps0.shape, BF16),) * 2, [], operands, 0 if count else 6)
        other = tuple(partner(x, step) for x, step in zip(mine, pair))
    between = run(
        functools.partial(first_forward_kernel, two),
        like(small, width, BF16),
        [pltpu.VMEM((2 * two, width), BF16), pltpu.VMEM((own, width), BF16)],
        [notes, act_ahead, ahead0, m_table, q_table, c_table],
        10,
        mine[0],
    )
    act_out = run(
        second_forward_kernel,
        like(own, width, BF16),
        [pltpu.VMEM((small, width), BF16)],
        [
            notes, between, ahead1,
            stacked(to_freq(small, span(one, own))), tap_freq(small, tap_count), stacked(from_freq(small, span(0, own))),
        ],
        10,
    )
    slots = kernels.shape[1]
    act_out, grad_out, taps, gains = call(
        final_kernel,
        (
            like(own, width, BF16), like(own, width, BF16),
            jax.ShapeDtypeStruct((tap_count, slots, width), F32), like(slots, width, F32),
        ),
        [
            pltpu.VMEM((tap_count, slots, width), F32), pltpu.VMEM((slots, width), F32),
            pltpu.SemaphoreType.DMA((7,)),
        ],
        (notes, *mine, *other, act_out, grad_out),
        0, [SMEM] + [VMEM] * 4 + [ANY] * 2, (ANY,) * 4,
    )
    return act_out[None], grad_out[None], taps.transpose(1, 0, 2)[None], gains[None]


def solution(mesh):
    in_specs = (
        P("section", "tm", None),
        P("section", "tm", None),
        P("section", None, "tm", None),
        P("section", None, None, None),
        P("section", None, None),
        P(),
        P(),
        P(),
        P(),
    )
    out_specs = (
        P("section", "tm", None),
        P("section", "tm", None),
        P("section", None, None, None),
        P("section", None, None),
    )
    return jax.shard_map(local, mesh=mesh, in_specs=in_specs, out_specs=out_specs, check_vma=False)
```
